32 devices in a mesh: seq: 8 (over y, x, core), tp: 4 (over z).
Axes of the slice: x: 2, y: 2, z: 4, core: 2. Of those that a mesh axis runs over, the one named last changes fastest.
Arguments:
- hidden_in: bfloat16 [4, 4096, 1024], P(None, 'seq'), may hold values from -6 to 6
- query_weight: bfloat16 [1024, 1024], P('seq', 'tp'), may hold values from -0.1875 to 0.1875
- key_weight: bfloat16 [1024, 1024], P('seq', 'tp'), may hold values from -0.1875 to 0.1875
- value_weight: bfloat16 [1024, 1024], P('seq', 'tp'), may hold values from -0.1875 to 0.1875
- gate_weight: bfloat16 [1024, 1024], P('seq', 'tp'), may hold values from -0.1875 to 0.1875
- out_weight: bfloat16 [1024, 1024], P('tp', 'seq'), may hold values from -0.1875 to 0.1875
- left_weight: bfloat16 [1024, 2816], P('seq', 'tp'), may hold values from -0.1875 to 0.1875
- right_weight: bfloat16 [1024, 2816], P('seq', 'tp'), may hold values from -0.1875 to 0.1875
- down_weight: bfloat16 [2816, 1024], P('tp', 'seq'), may hold values from -0.109375 to 0.109375
- decay_rate: float32 [8], P('tp'), may hold values from 0 to 1, as said below
- seq_bounds: int32 [4], replicated, may hold values from 1 to 4095, as said below
- out_cotangent: bfloat16 [4, 4096, 1024], P(None, 'seq'), may hold values from -6 to 6
Outputs:
- output: bfloat16 [4, 4096, 1024], P(None, 'seq')
- input_grad: float32 [4, 4096, 1024], P(None, 'seq')
- query_grad: float32 [1024, 1024], P('seq', 'tp')
- key_grad: float32 [1024, 1024], P('seq', 'tp')
- value_grad: float32 [1024, 1024], P('seq', 'tp')
- gate_grad: float32 [1024, 1024], P('seq', 'tp')
- out_grad: float32 [1024, 1024], P('tp', 'seq')
- left_grad: float32 [1024, 2816], P('seq', 'tp')
- right_grad: float32 [1024, 2816], P('seq', 'tp')
- down_grad: float32 [2816, 1024], P('tp', 'seq')
The draws below stay inside these ranges and needn't reach their ends.
Inputs may be any that keep to these rules, and one draw needn't show every extreme that they name: Micro-batch m holds two sequences, rows below seq_bounds[m] and the rest; the boundary lies within the first or the last 512 rows of the micro-batch and never on a multiple of 512. A head's state shrinks by exp(-decay_rate) a row.
All inputs are finite; a program needn't handle non-finite values.
Results may differ from the reference program's by a relative error of at most 0.014.
Values may be sent and summed in bfloat16 or wider, within the bound.
A program may use at most 192 MiB of HBM per device.

```python
import math
from functools import partial
import jax
import jax.numpy as jnp
from jax import lax

D = 1024
HEADS = 8
HEAD = 128
FF = 2816
GROUP = 512
MB = 4
L = 4096


def draw_decay_rate(key, part):
    key = jax.random.fold_in(key, 11)
    slow_key, fast_key, pick_key = jax.random.split(key, 3)
    slow_rates = jnp.exp(jax.random.uniform(slow_key, (HEADS,), jnp.float32, math.log(0.2), math.log(2.0))) / L
    fast_rates = jnp.exp(jax.random.uniform(fast_key, (HEADS,), jnp.float32, math.log(1.0 / 50.0), math.log(1.0 / 30.0)))
    ranking = jax.random.permutation(pick_key, HEADS)
    return jnp.where(ranking < HEADS // 2, fast_rates, slow_rates)


def draw_seq_bounds(key, part):
    key = jax.random.fold_in(key, 23)
    coin_key, early_key, late_key = jax.random.split(key, 3)
    coins = jax.random.randint(coin_key, (MB,), 0, 2)
    early = jax.random.randint(early_key, (MB,), 1, GROUP)
    late = jax.random.randint(late_key, (MB,), L - GROUP + 1, L)
    return jnp.where(coins == 1, early, late).astype(jnp.int32)


def block_scale(own_key, extent, shards, least, top_value):
    factor_of = 1.0
    for position, parts in shards:
        steps = jax.random.uniform(jax.random.fold_in(jax.random.fold_in(own_key, 6), position), (parts,), jnp.float32, least / len(shards), top_value / len(shards))
        factor_of = factor_of * jnp.repeat(jnp.exp(steps), extent[position] // parts).reshape((-1,) + (1,) * (len(extent) - 1 - position))
    return factor_of


def bell_draw(own_key, shape, width, limit, cuts=(), kind=jnp.bfloat16):
    gain = block_scale(own_key, shape, cuts, -0.22, 0.18) if cuts else 1.0
    drawn = jax.random.normal(own_key, shape, jnp.float32) * width * gain
    return jnp.minimum(jnp.maximum(drawn, -limit), limit).astype(kind)


def setup_inputs(seed: int = 0) -> dict:
    splits = jax.random.split(jax.random.key(seed), 13)
    return {
        "hidden_in": bell_draw(splits[0], (MB, L, D), 1.0, 6.0, ((1, 8),)),
        "query_weight": bell_draw(splits[1], (D, D), D ** -0.5, 0.1875, ((0, 8), (1, 4))),
        "key_weight": bell_draw(splits[2], (D, D), D ** -0.5, 0.1875, ((0, 8), (1, 4))),
        "value_weight": bell_draw(splits[3], (D, D), D ** -0.5, 0.1875, ((0, 8), (1, 4))),
        "gate_weight": bell_draw(splits[4], (D, D), D ** -0.5, 0.1875, ((0, 8), (1, 4))),
        "out_weight": bell_draw(splits[5], (D, D), D ** -0.5, 0.1875, ((0, 4), (1, 8))),
        "left_weight": bell_draw(splits[6], (D, FF), D ** -0.5, 0.1875, ((0, 8), (1, 4))),
        "right_weight": bell_draw(splits[7], (D, FF), D ** -0.5, 0.1875, ((0, 8), (1, 4))),
        "down_weight": bell_draw(splits[8], (FF, D), FF ** -0.5, 0.109375, ((0, 4), (1, 8))),
        "decay_rate": draw_decay_rate(jax.random.fold_in(splits[12], 71), 0),
        "seq_bounds": draw_seq_bounds(jax.random.fold_in(splits[12], 71), 0),
        "out_cotangent": bell_draw(splits[11], (MB, L, D), 1.0, 6.0, ((1, 8),)),
    }


EPSILON = 1e-06
HIGHEST_PRECISION = lax.Precision.HIGHEST

@jax.custom_vjp
def low(v):
    return lax.optimization_barrier(v.astype(jnp.bfloat16)).astype(jnp.float32)

@jax.custom_vjp
def low_back(v):
    return v

def low_keep(v):
    return (low(v), None)

def low_pass(kept, grad):
    return (grad,)

def back_keep(v):
    return (v, None)

def back_low(kept, grad):
    return (low(grad),)
low.defvjp(low_keep, low_pass)
low_back.defvjp(back_keep, back_low)

def swish(pre_act):
    return pre_act * jax.nn.sigmoid(pre_act)

def rotate(rows_in, cosine_table, sine_table, signed):
    halfway = rows_in.shape[-1] // 2
    front_half = rows_in[..., :halfway]
    back_half = rows_in[..., halfway:]
    return jnp.concatenate([front_half * cosine_table - signed * back_half * sine_table, signed * front_half * sine_table + back_half * cosine_table], axis=-1)

def matmul(left_side, right_side):
    return jnp.dot(left_side, right_side, precision=HIGHEST_PRECISION)

def srms(values):
    return values * lax.rsqrt(lax.optimization_barrier(jnp.mean(values * values, axis=-1, keepdims=True)) + EPSILON)

def block_step(rates, state, inputs):
    queries, keys_in, values, segment, before = inputs
    local_f = jnp.arange(GROUP, dtype=jnp.float32)
    distance = local_f[:, None] - local_f[None, :]
    allowed = (distance >= 0.0) & (segment[:, None] == segment[None, :])
    decay = jnp.where(allowed[None], jnp.exp(-rates[:, None, None] * jnp.maximum(distance, 0.0)[None]), 0.0)
    scores = jnp.einsum('ihe,jhe->hij', queries, keys_in, precision=HIGHEST_PRECISION)
    attn_weights = low(low_back(scores * decay))
    inner_out = jnp.einsum('hij,jhe->ihe', attn_weights, values, precision=HIGHEST_PRECISION)
    coef_in = jnp.exp(-rates[None, :] * (local_f[:, None] + 1.0)) * (segment == before).astype(jnp.float32)[:, None]
    outer_out = coef_in[:, :, None] * jnp.einsum('ihe,hef->ihf', queries, state, precision=HIGHEST_PRECISION)
    last_segment = segment[GROUP - 1]
    weight_loc = jnp.exp(-rates[None, :] * (GROUP - 1.0 - local_f)[:, None]) * (segment == last_segment).astype(jnp.float32)[:, None]
    factor = jnp.where(last_segment == before, jnp.exp(-rates * GROUP), 0.0)
    local_state = jnp.einsum('jhe,jhf->hef', keys_in * weight_loc[:, :, None], values, precision=HIGHEST_PRECISION)
    return (factor[:, None, None] * state + local_state, inner_out + outer_out)

def attend(query_rot, key_rot, value_rows, segment, rates):
    blocks = L // GROUP
    shape_in = (blocks, GROUP, HEADS, HEAD)
    seg_blocks = segment.reshape(blocks, GROUP)
    before = jnp.concatenate([jnp.zeros((1,), jnp.int32), seg_blocks[:-1, GROUP - 1].astype(jnp.int32)])
    stepper = jax.checkpoint(partial(block_step, rates))
    final_state, pieces = lax.scan(stepper, jnp.zeros((HEADS, HEAD, HEAD), jnp.float32), (query_rot.reshape(shape_in), key_rot.reshape(shape_in), value_rows.reshape(shape_in), seg_blocks, before))
    return pieces.reshape(L, HEADS * HEAD)

def layer(decay_rate, seq_bounds, hidden_in, query_weight, key_weight, value_weight, gate_weight, out_weight, left_weight, right_weight, down_weight):
    frequency = jnp.exp(jnp.arange(HEAD // 2, dtype=jnp.float32) * (-2.0 * math.log(10000.0) / HEAD))
    positions = jnp.arange(L, dtype=jnp.float32)
    angles = positions[:, None] * frequency[None, :]
    cosine_table = jnp.cos(angles)[:, None, :]
    sine_table = jnp.sin(angles)[:, None, :]
    heads_shape = (L, HEADS, HEAD)
    results = []
    for batch_index in range(MB):
        input_rows = hidden_in[batch_index]
        unit_first = srms(input_rows)
        normed_first = low(unit_first)
        query_pre = low_back(matmul(normed_first, query_weight))
        key_pre = low_back(matmul(normed_first, key_weight))
        value_rows = low(low_back(matmul(normed_first, value_weight))).reshape(heads_shape)
        gate_pre = low_back(matmul(normed_first, gate_weight))
        query_rot = low(rotate(swish(query_pre).reshape(heads_shape), cosine_table, sine_table, 1.0))
        key_rot = low(rotate(swish(key_pre).reshape(heads_shape), cosine_table, sine_table, 1.0))
        segment = (jnp.arange(L, dtype=jnp.int32) >= seq_bounds[batch_index]).astype(jnp.int32)
        mixed_heads = low_back(attend(query_rot, key_rot, value_rows, segment, decay_rate))
        unit_mix = srms(mixed_heads)
        gate_mix = low(unit_mix * gate_pre)
        resid_mid = input_rows + low_back(matmul(gate_mix, out_weight))
        unit_second = srms(resid_mid)
        normed_second = low(unit_second)
        left_pre = low_back(matmul(normed_second, left_weight))
        right_pre = low_back(matmul(normed_second, right_weight))
        glu_product = low(left_pre * right_pre)
        results.append(resid_mid + low_back(matmul(glu_product, down_weight)))
    return jnp.stack(results)

def reference(hidden_in, query_weight, key_weight, value_weight, gate_weight, out_weight, left_weight, right_weight, down_weight, decay_rate, seq_bounds, out_cotangent):
    primals = [operand.astype(jnp.float32) for operand in (hidden_in, query_weight, key_weight, value_weight, gate_weight, out_weight, left_weight, right_weight, down_weight)]
    result, pullback = jax.vjp(partial(layer, decay_rate.astype(jnp.float32), seq_bounds.astype(jnp.int32)), *primals)
    grads = pullback(out_cotangent.astype(jnp.float32))
    return (result.astype(jnp.bfloat16), grads[0], grads[1], grads[2], grads[3], grads[4], grads[5], grads[6], grads[7], grads[8])
```

```python
import functools
import math

import jax
import jax.numpy as jnp
from jax import lax
from jax.experimental import pallas as pl
from jax.experimental.pallas import tpu as pltpu
from jax.sharding import PartitionSpec as P

D = 1024
HEAD = 128


EPSILON = 1e-06
HIGHEST_PRECISION = lax.Precision.HIGHEST
MESH = pl.DeviceIdType.MESH
BF16 = jnp.bfloat16
F32 = jnp.float32

SEQ = 8
TP = 4
STRIPE = 128


def place():
    s, t = lax.axis_index("seq"), lax.axis_index("tp")
    core = s % 2
    column = (s // 2) % 2
    line = s // 4
    other = s + 1 - 2 * core
    across_x = s + 2 * (1 - 2 * column)
    across_y = s + 4 * (1 - 2 * line)
    first = across_x + core * (across_y - across_x)
    second = across_y + core * (across_x - across_y)
    diagonal = across_x + across_y - s
    return s, t, other, first, second, diagonal


def nearest(t, step):
    flip = t // 2
    low = t + flip * (3 - 2 * t)
    swap = low * (1 - step // 2)
    index = step + swap * (1 - 2 * step)
    return index + flip * (3 - 2 * index)


def stripe(index):
    return pl.ds(pl.multiple_of(index * STRIPE, STRIPE), STRIPE)


def greet(devices):
    barrier = pltpu.get_barrier_semaphore()
    for device in devices:
        pl.semaphore_signal(barrier, inc=1, device_id=device, device_id_type=MESH)


def greet_line(t, s, here):
    barrier = pltpu.get_barrier_semaphore()

    @pl.when(t > 0)
    def _():
        pl.semaphore_signal(barrier, inc=1, device_id=(s, t - 1), device_id_type=MESH)

    @pl.when(t < TP - 1)
    def _():
        pl.semaphore_signal(barrier, inc=1, device_id=(s, t + 1), device_id_type=MESH)

    for device in here:
        pl.semaphore_signal(barrier, inc=1, device_id=(device, t), device_id_type=MESH)
    inner = jnp.where((t > 0) & (t < TP - 1), 1, 0)
    pl.semaphore_wait(barrier, len(here) + 1 + inner)


SENDS = ("first", "second", "other", "relay", "relay_other", "third_other", "fourth_other")


def gather_kernel(count, *refs):
    ins, outs = refs[:count], refs[count : 2 * count]
    local_sem, up_sem, down_sem, line_sem, send_sem, first_sem, second_sem, other_sem = refs[2 * count :]
    s, t, other, first, second, diagonal = place()
    other_first = first + (second - s) + (other - s) - (first - s)
    other_second = second + (first - s) + (other - s) - (second - s)
    other_diagonal = diagonal + other - s
    greet_line(t, s, (other, first, second))

    def remote(src, w, owner, column, send, receive, device):
        return pltpu.make_async_remote_copy(
            src_ref=src,
            dst_ref=outs[w].at[owner, :, stripe(column)],
            send_sem=send,
            recv_sem=receive,
            device_id=device,
            device_id_type=MESH,
        )

    def spot(w, owner, column):
        return outs[w].at[owner, :, stripe(column)]

    waits = []
    items = [(w, step) for w in range(count) for step in range(TP)]

    def own(w):
        return pltpu.make_async_copy(ins[w], spot(w, t, s), local_sem.at[w])

    def line_copies(w, owner, src):
        up = remote(src, w, owner, s, up_sem.at[w, owner], line_sem.at[w, owner], (s, t + 1))
        down = remote(src, w, owner, s, down_sem.at[w, owner], line_sem.at[w, owner], (s, t - 1))
        return up, down

    def plane_copies(index, w, owner, src):
        return (
            remote(src, w, owner, s, send_sem.at[index, 0], first_sem.at[index], (first, t)),
            remote(src, w, owner, s, send_sem.at[index, 1], second_sem.at[index, 0], (second, t)),
            remote(src, w, owner, s, send_sem.at[index, 2], other_sem.at[index, 0], (other, t)),
        )

    def relay_copies(index, w, owner):
        src = spot(w, owner, first)
        return (
            remote(src, w, owner, first, send_sem.at[index, 3], second_sem.at[index, 1], (second, t)),
            remote(src, w, owner, first, send_sem.at[index, 4], other_sem.at[index, 1], (other, t)),
        )

    def last_copies(index, w, owner):
        return (
            remote(spot(w, owner, second), w, owner, second, send_sem.at[index, 5], other_sem.at[index, 2], (other, t)),
            remote(spot(w, owner, diagonal), w, owner, diagonal, send_sem.at[index, 6], other_sem.at[index, 3], (other, t)),
        )

    for index in range(len(items) + 2):
        if index < len(items):
            w, step = items[index]
            owner = nearest(t, step)
            if step == 0:
                own(w).start()
                src = ins[w]
                up, down = line_copies(w, owner, src)
                pl.when(t < TP - 1)(up.start)
                pl.when(t > 0)(down.start)
            else:
                src = spot(w, owner, s)
                up, down = line_copies(w, owner, src)
                up.wait_recv()
                pl.when((owner < t) & (t < TP - 1))(up.start)
                pl.when((owner > t) & (t > 0))(down.start)
            for copy in plane_copies(index, w, owner, src):
                copy.start()
        if 1 <= index <= len(items):
            w, step = items[index - 1]
            owner = nearest(t, step)
            remote(spot(w, owner, first), w, owner, first, send_sem.at[index - 1, 0], first_sem.at[index - 1], (first, t)).wait_recv()
            for copy in relay_copies(index - 1, w, owner):
                copy.start()
        if index >= 2:
            w, step = items[index - 2]
            owner = nearest(t, step)
            for part, column in enumerate((second, diagonal)):
                remote(spot(w, owner, column), w, owner, column, send_sem.at[index - 2, 1], second_sem.at[index - 2, part], (second, t)).wait_recv()
            for copy in last_copies(index - 2, w, owner):
                copy.start()
    for index, (w, step) in enumerate(items):
        owner = nearest(t, step)
        for part, column in enumerate((other, other_first, other_second, other_diagonal)):
            remote(spot(w, owner, column), w, owner, column, send_sem.at[index, 2], other_sem.at[index, part], (other, t)).wait_recv()
        src = ins[w] if step == 0 else spot(w, owner, s)
        up, down = line_copies(w, owner, src)
        if step == 0:
            own(w).wait()
            pl.when(t < TP - 1)(up.wait_send)
            pl.when(t > 0)(down.wait_send)
        else:
            pl.when((owner < t) & (t < TP - 1))(up.wait_send)
            pl.when((owner > t) & (t > 0))(down.wait_send)
        for copy in plane_copies(index, w, owner, src) + relay_copies(index, w, owner) + last_copies(index, w, owner):
            copy.wait_send()


def gather_weights(shards):
    count = len(shards)
    items = count * TP
    dma = pltpu.SemaphoreType.DMA
    return pl.pallas_call(
        functools.partial(gather_kernel, count),
        out_shape=[jax.ShapeDtypeStruct((TP, shard.shape[0], D), BF16) for shard in shards],
        in_specs=[pl.BlockSpec(memory_space=pl.ANY)] * count,
        out_specs=[pl.BlockSpec(memory_space=pl.ANY)] * count,
        scratch_shapes=[
            dma((count,)),
            dma((count, TP)),
            dma((count, TP)),
            dma((count, TP)),
            dma((items, 7)),
            dma((items,)),
            dma((items, 2)),
            dma((items, 4)),
        ],
        compiler_params=pltpu.CompilerParams(collective_id=0, has_side_effects=True),
        name="gather_weights",
    )(*shards)


ROWS_STEP = 64
PIECES = 4


def add_rows(target, *terms):
    rows = target.shape[0]

    @pl.loop(0, rows // ROWS_STEP)
    def _(block):
        part = pl.ds(pl.multiple_of(block * ROWS_STEP, ROWS_STEP), ROWS_STEP)
        total = terms[0][part, :].astype(F32)
        for term in terms[1:]:
            total = total + term[part, :].astype(F32)
        target[part, :] = total.astype(target.dtype)


def reduce_kernel(count, spread, *refs):
    grads, refs = refs[:count], refs[count:]
    shares, refs = refs[:spread], refs[spread:]
    outs, refs = refs[:count], refs[count:]
    wholes, refs = refs[:spread], refs[spread:]
    own, refs = refs[0], refs[1:]
    other_land, refs = refs[:count], refs[count:]
    second_land, refs = refs[:count], refs[count:]
    first_land, refs = refs[:count], refs[count:]
    below_land, refs = refs[:count], refs[count:]
    above_land, refs = refs[:count], refs[count:]
    (own_sem, other_send, other_recv, second_send, second_recv, first_send, first_recv,
     line_send, below_recv, above_recv, share_local, share_up, share_down, share_recv) = refs
    s, t, other, first, second, diagonal = place()
    core = s % 2
    greet_line(t, s, (other, first, second))

    def remote(src, dst, send, receive, device):
        return pltpu.make_async_remote_copy(
            src_ref=src, dst_ref=dst, send_sem=send, recv_sem=receive, device_id=device, device_id_type=MESH
        )

    piece_rows = shares[0].shape[0] // PIECES
    pieces = [(a, p) for p in range(PIECES) for a in range(spread)]

    def piece(a, owner, p):
        return wholes[a].at[owner, pl.ds(p * piece_rows, piece_rows), :]

    def share_copies(a, p, owner, src):
        sem = (a, p, owner)
        return (
            remote(src, piece(a, owner, p), share_up.at[sem], share_recv.at[sem], (s, t + 1)),
            remote(src, piece(a, owner, p), share_down.at[sem], share_recv.at[sem], (s, t - 1)),
        )

    def own_piece(a, p):
        return shares[a].at[pl.ds(p * piece_rows, piece_rows), :]

    for a, p in pieces:
        up, down = share_copies(a, p, t, own_piece(a, p))
        pl.when(t < TP - 1)(up.start)
        pl.when(t > 0)(down.start)
        pltpu.make_async_copy(own_piece(a, p), piece(a, t, p), share_local.at[a, p]).start()

    relays = [(a, p, step) for a, p in pieces for step in range(1, TP)]

    def relay(index):
        a, p, step = relays[index]
        owner = nearest(t, step)
        up, down = share_copies(a, p, owner, piece(a, owner, p))
        up.wait_recv()
        pl.when((owner < t) & (t < TP - 1))(up.start)
        pl.when((owner > t) & (t > 0))(down.start)

    items = [(w, step) for w in range(count) for step in reversed(range(TP))]
    slots = own.shape[0]

    def sends(index, w, owner):
        return [
            remote(
                grads[w].at[owner, :, stripe(2 * chip + 1 - core)],
                other_land[w].at[owner, chip],
                other_send.at[index, chip],
                other_recv.at[index, chip],
                (other, t),
            )
            for chip in range(4)
        ]

    def loads(index, w, owner):
        rows = grads[w].shape[1]
        return [
            pltpu.make_async_copy(
                grads[w].at[owner, :, stripe(2 * chip + core)],
                own.at[index % slots, chip, pl.ds(0, rows), :],
                own_sem.at[index % slots, chip],
            )
            for chip in range(4)
        ]

    def to_second(index, w, owner):
        return [
            remote(
                other_land[w].at[owner, column // 2],
                second_land[w].at[owner, part],
                second_send.at[index, part],
                second_recv.at[index, part],
                (second, t),
            )
            for part, column in enumerate((diagonal, second))
        ]

    def to_first(index, w, owner):
        return remote(
            second_land[w].at[owner, 0], first_land[w].at[owner], first_send.at[index], first_recv.at[index], (first, t)
        )

    def along(index, w, owner):
        up = remote(
            first_land[w].at[owner], below_land[w].at[owner], line_send.at[index], below_recv.at[w, owner], (s, t + 1)
        )
        down = remote(
            first_land[w].at[owner], above_land[w].at[owner], line_send.at[index], above_recv.at[w, owner], (s, t - 1)
        )
        return up, down

    total = len(items)
    for tick in range(total + 4):
        index = tick
        if index < total:
            w, step = items[index]
            owner = nearest(t, step)
            for copy in sends(index, w, owner) + loads(index, w, owner):
                copy.start()
        index = tick - 1
        if 0 <= index < total:
            w, step = items[index]
            owner = nearest(t, step)
            rows = grads[w].shape[1]
            for copy in loads(index, w, owner):
                copy.wait()
            for copy in sends(index, w, owner):
                copy.wait_recv()
            for chip in range(4):
                add_rows(
                    other_land[w].at[owner, chip],
                    other_land[w].at[owner, chip],
                    own.at[index % slots, chip, pl.ds(0, rows), :],
                )
            for copy in to_second(index, w, owner):
                copy.start()
        index = tick - 2
        if 0 <= index < total:
            w, step = items[index]
            owner = nearest(t, step)
            for copy in to_second(index, w, owner):
                copy.wait_recv()
            add_rows(second_land[w].at[owner, 0], second_land[w].at[owner, 0], other_land[w].at[owner, first // 2])
            to_first(index, w, owner).start()
        index = tick - 3
        if 0 <= index < total:
            w, step = items[index]
            owner = nearest(t, step)
            to_first(index, w, owner).wait_recv()
            add_rows(
                first_land[w].at[owner],
                first_land[w].at[owner],
                other_land[w].at[owner, s // 2],
                second_land[w].at[owner, 1],
            )
        index = tick - 4
        if 0 <= index < total:
            w, step = items[index]
            owner = nearest(t, step)
            up, down = along(index, w, owner)
            if step:

                @pl.when((owner > t) & (t > 0))
                def _():
                    up.wait_recv()
                    add_rows(first_land[w].at[owner], first_land[w].at[owner], below_land[w].at[owner])

                @pl.when((owner < t) & (t < TP - 1))
                def _():
                    down.wait_recv()
                    add_rows(first_land[w].at[owner], first_land[w].at[owner], above_land[w].at[owner])

                pl.when(owner > t)(up.start)
                pl.when(owner < t)(down.start)
            else:

                @pl.when(t == 0)
                def _():
                    down.wait_recv()
                    add_rows(outs[w], first_land[w].at[owner], above_land[w].at[owner])

                @pl.when(t == TP - 1)
                def _():
                    up.wait_recv()
                    add_rows(outs[w], first_land[w].at[owner], below_land[w].at[owner])

                @pl.when((t > 0) & (t < TP - 1))
                def _():
                    up.wait_recv()
                    down.wait_recv()
                    add_rows(outs[w], first_land[w].at[owner], below_land[w].at[owner], above_land[w].at[owner])

        if tick < len(relays):
            relay(tick)

    for index, (w, step) in enumerate(items):
        owner = nearest(t, step)
        for copy in sends(index, w, owner) + to_second(index, w, owner):
            copy.wait_send()
        to_first(index, w, owner).wait_send()
        if step:
            along(index, w, owner)[0].wait_send()
    for a, p in pieces:
        up, down = share_copies(a, p, t, own_piece(a, p))
        pl.when(t < TP - 1)(up.wait_send)
        pl.when(t > 0)(down.wait_send)
        pltpu.make_async_copy(own_piece(a, p), piece(a, t, p), share_local.at[a, p]).wait()
    for a, p, step in relays:
        owner = nearest(t, step)
        up, down = share_copies(a, p, owner, piece(a, owner, p))
        pl.when((owner < t) & (t < TP - 1))(up.wait_send)
        pl.when((owner > t) & (t > 0))(down.wait_send)


def reduce_gradients(grads, shares):
    count, spread = len(grads), len(shares)
    items = count * TP
    dma = pltpu.SemaphoreType.DMA
    rows = [grad.shape[1] for grad in grads]
    vmem = pl.BlockSpec(memory_space=pltpu.VMEM)
    anywhere = pl.BlockSpec(memory_space=pl.ANY)
    results = pl.pallas_call(
        functools.partial(reduce_kernel, count, spread),
        out_shape=[jax.ShapeDtypeStruct((r, STRIPE), F32) for r in rows]
        + [jax.ShapeDtypeStruct((TP, *share.shape), share.dtype) for share in shares],
        in_specs=[anywhere] * (count + spread),
        out_specs=[vmem] * count + [anywhere] * spread,
        scratch_shapes=[pltpu.VMEM((3, 4, max(rows), STRIPE), BF16)]
        + [pltpu.VMEM((TP, 4, r, STRIPE), BF16) for r in rows]
        + [pltpu.VMEM((TP, 2, r, STRIPE), BF16) for r in rows]
        + [pltpu.VMEM((TP, r, STRIPE), BF16) for r in rows]
        + [pltpu.VMEM((TP, r, STRIPE), BF16) for r in rows]
        + [pltpu.VMEM((TP, r, STRIPE), BF16) for r in rows]
        + [
            dma((3, 4)),
            dma((items, 4)),
            dma((items, 4)),
            dma((items, 2)),
            dma((items, 2)),
            dma((items,)),
            dma((items,)),
            dma((items,)),
            dma((count, TP)),
            dma((count, TP)),
            dma((spread, PIECES)),
            dma((spread, PIECES, TP)),
            dma((spread, PIECES, TP)),
            dma((spread, PIECES, TP)),
        ],
        compiler_params=pltpu.CompilerParams(
            collective_id=1, has_side_effects=True, vmem_limit_bytes=56 * 2**20
        ),
        name="reduce_gradients",
    )(*grads, *shares)
    return results[:count], results[count:]


def entering(value, axis, join, neutral, backward):
    count, mine = (lax.axis_size(axis), lax.axis_index(axis))
    pieces = jax.tree.map(lambda part: lax.all_gather(part, axis), value)
    if backward:
        pieces = jax.tree.map(lambda part: part[::-1], pieces)
        mine = count - 1 - mine
    subtotal = jax.tree.map(
        lambda part, zero: jnp.full_like(part, 0) + jnp.asarray(zero, part.dtype), value, neutral
    )

    def step(position, subtotal):
        longer = join(subtotal, jax.tree.map(lambda part: part[position], pieces))
        return jax.tree.map(lambda new, old: jnp.where(position < mine, new, old), longer, subtotal)

    return lax.fori_loop(0, count - 1, step, subtotal)


def swish_parts(pre_act):
    logistic = jax.nn.sigmoid(pre_act)
    return (pre_act * logistic, logistic * (1.0 + pre_act * (1.0 - logistic)))


def rotate(rows_in, cosine_table, sine_table, signed):
    halfway = rows_in.shape[-1] // 2
    front_half = rows_in[..., :halfway]
    back_half = rows_in[..., halfway:]
    return jnp.concatenate(
        [
            front_half * cosine_table - signed * back_half * sine_table,
            signed * front_half * sine_table + back_half * cosine_table,
        ],
        axis=-1,
    )


def combine_forward(earlier, following):
    return (earlier[0] * following[0], following[0][:, None, None] * earlier[1] + following[1])


def combine_backward(farther, nearer):
    return (farther[0] * nearer[0], nearer[1] + nearer[0][:, None, None] * farther[1])


def collect_weights(
    query_weight,
    key_weight,
    value_weight,
    gate_weight,
    out_weight,
    left_weight,
    right_weight,
    down_weight,
):
    return (
        lax.all_gather(query_weight, "seq", axis=0, tiled=True),
        lax.all_gather(key_weight, "seq", axis=0, tiled=True),
        lax.all_gather(value_weight, "seq", axis=0, tiled=True),
        lax.all_gather(gate_weight, "seq", axis=0, tiled=True),
        lax.all_gather(out_weight, "seq", axis=1, tiled=True),
        lax.all_gather(left_weight, "seq", axis=0, tiled=True),
        lax.all_gather(right_weight, "seq", axis=0, tiled=True),
        lax.all_gather(down_weight, "seq", axis=1, tiled=True),
    )


def state_prefix(factor, local_state):
    neutral = (jnp.ones_like(factor), jnp.zeros_like(local_state))
    return entering((factor, local_state), "seq", combine_forward, neutral, False)[1]


def state_suffix(factor, state_grad):
    neutral = (jnp.ones_like(factor), jnp.zeros_like(state_grad))
    return entering((factor, state_grad), "seq", combine_backward, neutral, True)[1]


def body(
    hidden_in,
    query_weight,
    key_weight,
    value_weight,
    gate_weight,
    out_weight,
    left_weight,
    right_weight,
    down_weight,
    decay_rate,
    seq_bounds,
    out_cotangent,
):
    row_count = hidden_in.shape[1]
    batch_count = hidden_in.shape[0]
    local_heads = decay_rate.shape[0]
    heads_shape = (row_count, local_heads, HEAD)
    device = lax.axis_index("seq")
    offsets = jnp.arange(row_count, dtype=jnp.int32)
    positions = device * row_count + offsets
    frequency = jnp.exp(
        jnp.arange(HEAD // 2, dtype=jnp.float32) * (-2.0 * math.log(10000.0) / HEAD)
    )
    angles = positions.astype(jnp.float32)[:, None] * frequency[None, :]
    cosine_table = jnp.cos(angles)[:, None, :]
    sine_table = jnp.sin(angles)[:, None, :]
    local_f = offsets.astype(jnp.float32)
    distance = local_f[:, None] - local_f[None, :]
    causal = distance >= 0.0
    distance_pos = jnp.maximum(distance, 0.0)
    accum = None
    outputs = []
    in_grads = []
    for batch_index in range(batch_count):
        gathered = collect_weights(
            query_weight,
            key_weight,
            value_weight,
            gate_weight,
            out_weight,
            left_weight,
            right_weight,
            down_weight,
        )
        query_full, key_full, value_full, gate_full, out_full, left_full, right_full, down_full = (
            gathered
        )
        boundary = seq_bounds[batch_index]
        segment = (positions >= boundary).astype(jnp.int32)
        before = (device * row_count - 1 >= boundary).astype(jnp.int32)
        last_segment = segment[row_count - 1]
        allowed = causal & (segment[:, None] == segment[None, :])
        decay = jnp.where(
            allowed[None], jnp.exp(-decay_rate[:, None, None] * distance_pos[None]), 0.0
        )
        coef_in = (
            jnp.exp(-decay_rate[None, :] * (local_f[:, None] + 1.0))
            * (segment == before).astype(jnp.float32)[:, None]
        )
        weight_loc = (
            jnp.exp(-decay_rate[None, :] * (row_count - 1.0 - local_f)[:, None])
            * (segment == last_segment).astype(jnp.float32)[:, None]
        )
        factor = jnp.where(last_segment == before, jnp.exp(-decay_rate * row_count), 0.0)
        input_rows = hidden_in[batch_index].astype(jnp.float32)
        inv_first = lax.rsqrt(jnp.mean(input_rows * input_rows, axis=-1, keepdims=True) + EPSILON)
        unit_first = input_rows * inv_first
        normed_first = unit_first.astype(jnp.bfloat16)
        query_pre = jnp.dot(normed_first, query_full, preferred_element_type=jnp.float32)
        key_pre = jnp.dot(normed_first, key_full, preferred_element_type=jnp.float32)
        value_pre = jnp.dot(normed_first, value_full, preferred_element_type=jnp.float32)
        gate_pre = jnp.dot(normed_first, gate_full, preferred_element_type=jnp.float32)
        query_act, query_slope = swish_parts(query_pre)
        key_act, key_slope = swish_parts(key_pre)
        query_rot = rotate(query_act.reshape(heads_shape), cosine_table, sine_table, 1.0).astype(
            jnp.bfloat16
        )
        key_rot = rotate(key_act.reshape(heads_shape), cosine_table, sine_table, 1.0).astype(
            jnp.bfloat16
        )
        value_rows = value_pre.astype(jnp.bfloat16).reshape(heads_shape)
        query_wide = query_rot.astype(jnp.float32)
        key_wide = key_rot.astype(jnp.float32)
        value_wide = value_rows.astype(jnp.float32)
        scores = jnp.einsum("ihe,jhe->hij", query_rot, key_rot, preferred_element_type=jnp.float32)
        attn_weights = (scores * decay).astype(jnp.bfloat16)
        inner_out = jnp.einsum(
            "hij,jhe->ihe", attn_weights, value_rows, preferred_element_type=jnp.float32
        )
        local_state = jnp.einsum(
            "jhe,jhf->hef",
            key_wide * weight_loc[:, :, None],
            value_wide,
            precision=HIGHEST_PRECISION,
        )
        incoming = state_prefix(factor, local_state)
        outer_out = coef_in[:, :, None] * jnp.einsum(
            "ihe,hef->ihf", query_wide, incoming, precision=HIGHEST_PRECISION
        )
        mixed_heads = (inner_out + outer_out).reshape(row_count, local_heads * HEAD)
        total_sq = lax.psum(jnp.sum(mixed_heads * mixed_heads, axis=-1), "tp")
        inv_mix = lax.rsqrt(total_sq / D + EPSILON)[:, None]
        unit_mix = mixed_heads * inv_mix
        gate_mix = (unit_mix * gate_pre).astype(jnp.bfloat16)
        attn_sum = lax.psum(jnp.dot(gate_mix, out_full, preferred_element_type=jnp.float32), "tp")
        resid_mid = input_rows + attn_sum
        inv_second = lax.rsqrt(jnp.mean(resid_mid * resid_mid, axis=-1, keepdims=True) + EPSILON)
        unit_second = resid_mid * inv_second
        normed_second = unit_second.astype(jnp.bfloat16)
        left_pre = jnp.dot(normed_second, left_full, preferred_element_type=jnp.float32)
        right_pre = jnp.dot(normed_second, right_full, preferred_element_type=jnp.float32)
        glu_product = (left_pre * right_pre).astype(jnp.bfloat16)
        glu_out = lax.psum(
            jnp.dot(glu_product, down_full, preferred_element_type=jnp.float32), "tp"
        )
        outputs.append((resid_mid + glu_out).astype(jnp.bfloat16))
        glu_cot = out_cotangent[batch_index]
        product_grad = jnp.einsum(
            "cd,fd->cf", glu_cot, down_full, preferred_element_type=jnp.float32
        )
        left_back = (product_grad * right_pre).astype(jnp.bfloat16)
        right_back = (product_grad * left_pre).astype(jnp.bfloat16)
        second_part = jnp.einsum(
            "cf,df->cd", left_back, left_full, preferred_element_type=jnp.float32
        ) + jnp.einsum("cf,df->cd", right_back, right_full, preferred_element_type=jnp.float32)
        second_back = lax.psum(second_part, "tp")
        mid_grad = glu_cot.astype(jnp.float32) + inv_second * (
            second_back - unit_second * jnp.mean(second_back * unit_second, axis=-1, keepdims=True)
        )
        attn_cot = mid_grad.astype(jnp.bfloat16)
        gate_mix_grad = jnp.einsum(
            "cd,kd->ck", attn_cot, out_full, preferred_element_type=jnp.float32
        )
        gate_back = (gate_mix_grad * unit_mix).astype(jnp.bfloat16)
        unit_mix_grad = gate_mix_grad * gate_pre
        mix_dot = lax.psum(jnp.sum(unit_mix_grad * unit_mix, axis=-1), "tp")
        heads_grad = (
            (inv_mix * (unit_mix_grad - unit_mix * (mix_dot / D)[:, None]))
            .astype(jnp.bfloat16)
            .reshape(heads_shape)
        )
        pair_grad = jnp.einsum(
            "ihe,jhe->hij", heads_grad, value_rows, preferred_element_type=jnp.float32
        ).astype(jnp.bfloat16)
        score_grad = pair_grad.astype(jnp.float32) * decay
        query_inner = jnp.einsum("hij,jhe->ihe", score_grad, key_wide, precision=HIGHEST_PRECISION)
        key_inner = jnp.einsum("hij,ihe->jhe", score_grad, query_wide, precision=HIGHEST_PRECISION)
        value_inner = jnp.einsum(
            "hij,ihe->jhe", attn_weights, heads_grad, preferred_element_type=jnp.float32
        )
        scaled_grad = heads_grad.astype(jnp.float32) * coef_in[:, :, None]
        query_outer = jnp.einsum("ihf,hef->ihe", scaled_grad, incoming, precision=HIGHEST_PRECISION)
        state_grad = jnp.einsum(
            "ihe,ihf->hef", query_wide, scaled_grad, precision=HIGHEST_PRECISION
        )
        later_grad = state_suffix(factor, state_grad)
        key_state = weight_loc[:, :, None] * jnp.einsum(
            "jhf,hef->jhe", value_wide, later_grad, precision=HIGHEST_PRECISION
        )
        value_state = weight_loc[:, :, None] * jnp.einsum(
            "jhe,hef->jhf", key_wide, later_grad, precision=HIGHEST_PRECISION
        )
        query_back = (
            rotate(query_inner + query_outer, cosine_table, sine_table, -1.0).reshape(row_count, -1)
            * query_slope
        ).astype(jnp.bfloat16)
        key_back = (
            rotate(key_inner + key_state, cosine_table, sine_table, -1.0).reshape(row_count, -1)
            * key_slope
        ).astype(jnp.bfloat16)
        value_back = (value_inner + value_state).reshape(row_count, -1).astype(jnp.bfloat16)
        fresh = (
            jnp.einsum("cd,ck->dk", normed_first, query_back, preferred_element_type=jnp.float32),
            jnp.einsum("cd,ck->dk", normed_first, key_back, preferred_element_type=jnp.float32),
            jnp.einsum("cd,ck->dk", normed_first, value_back, preferred_element_type=jnp.float32),
            jnp.einsum("cd,ck->dk", normed_first, gate_back, preferred_element_type=jnp.float32),
            jnp.einsum("ck,cd->kd", gate_mix, attn_cot, preferred_element_type=jnp.float32),
            jnp.einsum("cd,cf->df", normed_second, left_back, preferred_element_type=jnp.float32),
            jnp.einsum("cd,cf->df", normed_second, right_back, preferred_element_type=jnp.float32),
            jnp.einsum("cf,cd->fd", glu_product, glu_cot, preferred_element_type=jnp.float32),
        )
        if accum is None:
            accum = list(fresh)
        else:
            accum = [older + newer for older, newer in zip(accum, fresh)]
        total = jnp.einsum("ck,dk->cd", query_back, query_full, preferred_element_type=jnp.float32)
        total = total + jnp.einsum(
            "ck,dk->cd", key_back, key_full, preferred_element_type=jnp.float32
        )
        total = total + jnp.einsum(
            "ck,dk->cd", value_back, value_full, preferred_element_type=jnp.float32
        )
        first_back = lax.psum(
            total
            + jnp.einsum("ck,dk->cd", gate_back, gate_full, preferred_element_type=jnp.float32),
            "tp",
        )
        input_back = mid_grad + inv_first * (
            first_back - unit_first * jnp.mean(first_back * unit_first, axis=-1, keepdims=True)
        )
        in_grads.append(input_back)
    summed = (
        lax.psum_scatter(accum[0], "seq", scatter_dimension=0, tiled=True),
        lax.psum_scatter(accum[1], "seq", scatter_dimension=0, tiled=True),
        lax.psum_scatter(accum[2], "seq", scatter_dimension=0, tiled=True),
        lax.psum_scatter(accum[3], "seq", scatter_dimension=0, tiled=True),
        lax.psum_scatter(accum[4], "seq", scatter_dimension=1, tiled=True),
        lax.psum_scatter(accum[5], "seq", scatter_dimension=0, tiled=True),
        lax.psum_scatter(accum[6], "seq", scatter_dimension=0, tiled=True),
        lax.psum_scatter(accum[7], "seq", scatter_dimension=1, tiled=True),
    )
    return (
        jnp.stack(outputs),
        jnp.stack(in_grads),
        summed[0],
        summed[1],
        summed[2],
        summed[3],
        summed[4],
        summed[5],
        summed[6],
        summed[7],
    )


def dots(left, right, dims):
    return lax.dot_general(left, right, (dims, ((), ())), preferred_element_type=F32)


NN = ((1,), (0,))
NT = ((1,), (1,))
TN = ((0,), (0,))


def fused_body(
    hidden_in,
    query_weight,
    key_weight,
    value_weight,
    gate_weight,
    out_weight,
    left_weight,
    right_weight,
    down_weight,
    decay_rate,
    seq_bounds,
    out_cotangent,
):
    row_count = hidden_in.shape[1]
    device, batch = lax.axis_index("seq"), lax.axis_index("tp")
    rates = lax.all_gather(decay_rate, "tp", axis=0, tiled=True)
    heads = rates.shape[0]
    shards = [
        query_weight.T,
        key_weight.T,
        value_weight.T,
        gate_weight.T,
        out_weight,
        left_weight.T,
        right_weight.T,
        down_weight,
    ]
    query_full, key_full, value_full, gate_full, out_full, left_full, right_full, down_full = [
        whole.reshape(-1, D) for whole in gather_weights(shards)
    ]
    heads_shape = (row_count, heads, HEAD)
    offsets = jnp.arange(row_count, dtype=jnp.int32)
    positions = device * row_count + offsets
    frequency = jnp.exp(
        jnp.arange(HEAD // 2, dtype=F32) * (-2.0 * math.log(10000.0) / HEAD)
    )
    angles = positions.astype(F32)[:, None] * frequency[None, :]
    cosine_table = jnp.cos(angles)[:, None, :]
    sine_table = jnp.sin(angles)[:, None, :]
    local_f = offsets.astype(F32)
    distance = local_f[:, None] - local_f[None, :]
    boundary = lax.dynamic_index_in_dim(seq_bounds, batch, 0, keepdims=False)
    segment = (positions >= boundary).astype(jnp.int32)
    before = (device * row_count - 1 >= boundary).astype(jnp.int32)
    last_segment = segment[row_count - 1]
    allowed = (distance >= 0.0) & (segment[:, None] == segment[None, :])
    decay = jnp.where(allowed[None], jnp.exp(-rates[:, None, None] * jnp.maximum(distance, 0.0)[None]), 0.0)
    coef_in = (
        jnp.exp(-rates[None, :] * (local_f[:, None] + 1.0)) * (segment == before).astype(F32)[:, None]
    )
    weight_loc = (
        jnp.exp(-rates[None, :] * (row_count - 1.0 - local_f)[:, None])
        * (segment == last_segment).astype(F32)[:, None]
    )
    blocks = jnp.arange(SEQ)
    ends = ((blocks + 1) * row_count - 1 >= boundary).astype(jnp.int32)
    gap = (device - 1 - blocks).astype(F32)
    prefix_coef = jnp.where(
        ((blocks < device) & (ends == before))[:, None],
        jnp.exp(-rates[None, :] * row_count * jnp.maximum(gap, 0.0)[:, None]),
        0.0,
    )
    later_before = (blocks * row_count - 1 >= boundary).astype(jnp.int32)
    later_gap = (blocks - 1 - device).astype(F32)
    suffix_coef = jnp.where(
        ((blocks > device) & (later_before == last_segment))[:, None],
        jnp.exp(-rates[None, :] * row_count * jnp.maximum(later_gap, 0.0)[:, None]),
        0.0,
    )

    def states(local, coef):
        every = lax.all_gather(local.astype(BF16), "seq").astype(F32)
        return jnp.sum(coef[:, :, None, None] * every, axis=0)

    input_rows = lax.dynamic_index_in_dim(hidden_in, batch, 0, keepdims=False).astype(F32)
    glu_cot = lax.dynamic_index_in_dim(out_cotangent, batch, 0, keepdims=False)
    inv_first = lax.rsqrt(jnp.mean(input_rows * input_rows, axis=-1, keepdims=True) + EPSILON)
    unit_first = input_rows * inv_first
    normed_first = unit_first.astype(BF16)
    query_pre = dots(normed_first, query_full, NT)
    key_pre = dots(normed_first, key_full, NT)
    value_pre = dots(normed_first, value_full, NT)
    gate_pre = dots(normed_first, gate_full, NT)
    query_act, query_slope = swish_parts(query_pre)
    key_act, key_slope = swish_parts(key_pre)
    query_rot = rotate(query_act.reshape(heads_shape), cosine_table, sine_table, 1.0).astype(BF16)
    key_rot = rotate(key_act.reshape(heads_shape), cosine_table, sine_table, 1.0).astype(BF16)
    value_rows = value_pre.astype(BF16).reshape(heads_shape)
    scores = jnp.einsum("ihe,jhe->hij", query_rot, key_rot, preferred_element_type=F32)
    attn_weights = (scores * decay).astype(BF16)
    inner_out = jnp.einsum("hij,jhe->ihe", attn_weights, value_rows, preferred_element_type=F32)
    key_decayed = (key_rot.astype(F32) * weight_loc[:, :, None]).astype(BF16)
    local_state = jnp.einsum("jhe,jhf->hef", key_decayed, value_rows, preferred_element_type=F32)
    incoming = states(local_state, prefix_coef).astype(BF16)
    outer_out = coef_in[:, :, None] * jnp.einsum("ihe,hef->ihf", query_rot, incoming, preferred_element_type=F32)
    mixed_heads = (inner_out + outer_out).reshape(row_count, D)
    inv_mix = lax.rsqrt(jnp.mean(mixed_heads * mixed_heads, axis=-1, keepdims=True) + EPSILON)
    unit_mix = mixed_heads * inv_mix
    gate_mix = (unit_mix * gate_pre).astype(BF16)
    resid_mid = input_rows + dots(gate_mix, out_full, NN)
    inv_second = lax.rsqrt(jnp.mean(resid_mid * resid_mid, axis=-1, keepdims=True) + EPSILON)
    unit_second = resid_mid * inv_second
    normed_second = unit_second.astype(BF16)
    left_pre = dots(normed_second, left_full, NT)
    right_pre = dots(normed_second, right_full, NT)
    glu_product = (left_pre * right_pre).astype(BF16)
    output = (resid_mid + dots(glu_product, down_full, NN)).astype(BF16)

    product_grad = dots(glu_cot, down_full, NT)
    left_back = (product_grad * right_pre).astype(BF16)
    right_back = (product_grad * left_pre).astype(BF16)
    second_back = dots(left_back, left_full, NN) + dots(right_back, right_full, NN)
    mid_grad = glu_cot.astype(F32) + inv_second * (
        second_back - unit_second * jnp.mean(second_back * unit_second, axis=-1, keepdims=True)
    )
    attn_cot = mid_grad.astype(BF16)
    gate_mix_grad = dots(attn_cot, out_full, NT)
    gate_back = (gate_mix_grad * unit_mix).astype(BF16)
    unit_mix_grad = gate_mix_grad * gate_pre
    mix_dot = jnp.mean(unit_mix_grad * unit_mix, axis=-1, keepdims=True)
    heads_grad = (inv_mix * (unit_mix_grad - unit_mix * mix_dot)).astype(BF16).reshape(heads_shape)
    pair_grad = jnp.einsum("ihe,jhe->hij", heads_grad, value_rows, preferred_element_type=F32).astype(BF16)
    score_grad = (pair_grad.astype(F32) * decay).astype(BF16)
    query_inner = jnp.einsum("hij,jhe->ihe", score_grad, key_rot, preferred_element_type=F32)
    key_inner = jnp.einsum("hij,ihe->jhe", score_grad, query_rot, preferred_element_type=F32)
    value_inner = jnp.einsum("hij,ihe->jhe", attn_weights, heads_grad, preferred_element_type=F32)
    scaled_grad = (heads_grad.astype(F32) * coef_in[:, :, None]).astype(BF16)
    query_outer = jnp.einsum("ihf,hef->ihe", scaled_grad, incoming, preferred_element_type=F32)
    state_grad = jnp.einsum("ihe,ihf->hef", query_rot, scaled_grad, preferred_element_type=F32)
    later_grad = states(state_grad, suffix_coef).astype(BF16)
    key_state = weight_loc[:, :, None] * jnp.einsum("jhf,hef->jhe", value_rows, later_grad, preferred_element_type=F32)
    value_state = weight_loc[:, :, None] * jnp.einsum("jhe,hef->jhf", key_rot, later_grad, preferred_element_type=F32)
    query_back = (
        rotate(query_inner + query_outer, cosine_table, sine_table, -1.0).reshape(row_count, D) * query_slope
    ).astype(BF16)
    key_back = (
        rotate(key_inner + key_state, cosine_table, sine_table, -1.0).reshape(row_count, D) * key_slope
    ).astype(BF16)
    value_back = (value_inner + value_state).reshape(row_count, D).astype(BF16)
    first_back = (
        dots(query_back, query_full, NN)
        + dots(key_back, key_full, NN)
        + dots(value_back, value_full, NN)
        + dots(gate_back, gate_full, NN)
    )
    input_back = mid_grad + inv_first * (
        first_back - unit_first * jnp.mean(first_back * unit_first, axis=-1, keepdims=True)
    )
    grads = [
        dots(glu_product, glu_cot, TN),
        dots(left_back, normed_second, TN),
        dots(right_back, normed_second, TN),
        dots(gate_mix, attn_cot, TN),
        dots(query_back, normed_first, TN),
        dots(key_back, normed_first, TN),
        dots(value_back, normed_first, TN),
        dots(gate_back, normed_first, TN),
    ]
    sums, wholes = reduce_gradients(
        [grad.astype(BF16).reshape(TP, -1, D) for grad in grads], [output, input_back.astype(BF16)]
    )
    down_grad, left_grad, right_grad, out_grad, query_grad, key_grad, value_grad, gate_grad = sums
    return (
        wholes[0],
        wholes[1].astype(F32),
        query_grad.T,
        key_grad.T,
        value_grad.T,
        gate_grad.T,
        out_grad,
        left_grad.T,
        right_grad.T,
        down_grad,
    )


def solution(mesh):
    fits = mesh.shape["seq"] == SEQ and mesh.shape["tp"] == TP
    return jax.shard_map(
        fused_body if fits else body,
        mesh=mesh,
        in_specs=(
            P(None, "seq", None),
            P("seq", "tp"),
            P("seq", "tp"),
            P("seq", "tp"),
            P("seq", "tp"),
            P("tp", "seq"),
            P("seq", "tp"),
            P("seq", "tp"),
            P("tp", "seq"),
            P("tp"),
            P(),
            P(None, "seq", None),
        ),
        out_specs=(
            P(None, "seq", None),
            P(None, "seq", None),
            P("seq", "tp"),
            P("seq", "tp"),
            P("seq", "tp"),
            P("seq", "tp"),
            P("tp", "seq"),
            P("seq", "tp"),
            P("seq", "tp"),
            P("tp", "seq"),
        ),
        check_vma=False,
    )
```

```python
import functools
import math

import jax
import jax.numpy as jnp
from jax import lax
from jax.experimental import pallas as pl
from jax.experimental.pallas import tpu as pltpu
from jax.sharding import PartitionSpec as P

D = 1024
HEAD = 128


EPSILON = 1e-06
HIGHEST_PRECISION = lax.Precision.HIGHEST
MESH = pl.DeviceIdType.MESH
BF16 = jnp.bfloat16
F32 = jnp.float32

SEQ = 8
TP = 4
STRIPE = 128
PAIR = 2 * HEAD
BLOCK = 32

NN = ((1,), (0,))
NT = ((1,), (1,))
TN = ((0,), (0,))


def dots(left, right, dims):
    return lax.dot_general(left, right, (dims, ((), ())), preferred_element_type=F32)


def place():
    s, t = lax.axis_index("seq"), lax.axis_index("tp")
    core = s % 2
    column = (s // 2) % 2
    line = s // 4
    other = s + 1 - 2 * core
    across_x = s + 2 * (1 - 2 * column)
    across_y = s + 4 * (1 - 2 * line)
    first = across_x + core * (across_y - across_x)
    second = across_y + core * (across_x - across_y)
    diagonal = across_x + across_y - s
    return s, t, other, first, second, diagonal


def nearest(t, step):
    flip = t // 2
    low = t + flip * (3 - 2 * t)
    swap = low * (1 - step // 2)
    index = step + swap * (1 - 2 * step)
    return index + flip * (3 - 2 * index)


def stripe(index):
    return pl.ds(pl.multiple_of(index * STRIPE, STRIPE), STRIPE)


def rows_of(index, size):
    return pl.ds(pl.multiple_of(index * size, size), size)


def remote(src, dst, send, receive, device):
    return pltpu.make_async_remote_copy(
        src_ref=src, dst_ref=dst, send_sem=send, recv_sem=receive, device_id=device, device_id_type=MESH
    )


def greet(s, t, around):
    barrier = pltpu.get_barrier_semaphore()
    for step in range(1, TP):
        pl.semaphore_signal(barrier, inc=1, device_id=(s, (t + step) % TP), device_id_type=MESH)
    for device in around:
        pl.semaphore_signal(barrier, inc=1, device_id=(device, t), device_id_type=MESH)
    pl.semaphore_wait(barrier, TP - 1 + len(around))


def every_rows(count, body, size=BLOCK):
    @pl.loop(0, count // size)
    def _(block):
        body(pl.ds(pl.multiple_of(block * size, size), size), block * size)


def flag(condition):
    return jnp.where(condition, 1.0, 0.0).astype(F32)


def rotated(values, cosine, sine):
    return values * cosine + pltpu.roll(values, HEAD // 2, 1) * sine


LAG_B, LAG_C = 2, 4
WEIGHTS = ("qkvg", "out", "left", "right", "down")


def forward_kernel(rows, sizes, *refs):
    (shards, refs) = refs[:5], refs[5:]
    (hidden, cosine, sine, rate_in, bounds), refs = refs[:5], refs[5:]
    whole_out, refs = refs[:5], refs[5:]
    (acts_out, slope_out, normed_out, unit_out, gated_out, second_out, left_out, right_out, glu_out,
     incoming_out, inv_mix_out, inv_second_out, rate_out, result_out), refs = refs[:14], refs[14:]
    whole, refs = refs[:5], refs[5:]
    (acts, slopes, normed, unit, gated, second_normed, sides, glu, wide, mixed, distance, scores, weights,
     state, state_land, mine, partial, partial_land, incoming, inv_mix, inv_second, rates), refs = refs[:22], refs[22:]
    (local_sem, up_sem, down_sem, line_sem, send_sem, first_sem, second_sem, other_sem, rate_send, rate_recv,
     state_send, state_recv, partial_sem, copy_sem, side_sem) = refs
    s, t, other, first, second, diagonal = place()
    units, beside = sizes[2], wide.shape[1] // 2
    shift = other - s
    greet(s, t, (other, first, second, diagonal))

    pairs = [(2, step) for step in range(TP)], [(3, step) for step in range(TP)]
    items = (
        [(0, step) for step in range(TP)]
        + [(1, step) for step in range(TP)]
        + [item for both in zip(*pairs) for item in both]
        + [(4, step) for step in range(TP)]
    )

    def spot(w, owner, column):
        return whole[w].at[rows_of(owner, sizes[w]), stripe(column)]

    def source(w, step, owner):
        return shards[w] if step == 0 else spot(w, owner, s)

    def up_copy(w, step, owner):
        return remote(source(w, step, owner), spot(w, owner, s), up_sem.at[w, owner], line_sem.at[w, owner], (s, t + 1))

    def down_copy(w, step, owner):
        return remote(source(w, step, owner), spot(w, owner, s), down_sem.at[w, owner], line_sem.at[w, owner], (s, t - 1))

    def own_copy(w):
        return pltpu.make_async_copy(shards[w], spot(w, t, s), local_sem.at[w])

    def plane_copies(index, w, step, owner):
        src, dst = source(w, step, owner), spot(w, owner, s)
        return (
            remote(src, dst, send_sem.at[index, 0], first_sem.at[index], (first, t)),
            remote(src, dst, send_sem.at[index, 1], second_sem.at[index, 0], (second, t)),
            remote(src, dst, send_sem.at[index, 2], other_sem.at[index, 0], (other, t)),
        )

    def relay_copies(index, w, owner):
        src = spot(w, owner, first)
        return (
            remote(src, src, send_sem.at[index, 3], second_sem.at[index, 1], (second, t)),
            remote(src, src, send_sem.at[index, 4], other_sem.at[index, 1], (other, t)),
        )

    def last_copies(index, w, owner):
        near, far = spot(w, owner, second), spot(w, owner, diagonal)
        return (
            remote(near, near, send_sem.at[index, 5], other_sem.at[index, 2], (other, t)),
            remote(far, far, send_sem.at[index, 6], other_sem.at[index, 3], (other, t)),
        )

    def tick(now):
        index = now
        if index < len(items):
            w, step = items[index]
            owner = nearest(t, step)
            if step == 0:
                own_copy(w).start()

                @pl.when(t < TP - 1)
                def _():
                    up_copy(w, step, owner).start()

                @pl.when(t > 0)
                def _():
                    down_copy(w, step, owner).start()
            else:
                up_copy(w, step, owner).wait_recv()

                @pl.when((owner < t) & (t < TP - 1))
                def _():
                    up_copy(w, step, owner).start()

                @pl.when((owner > t) & (t > 0))
                def _():
                    down_copy(w, step, owner).start()
            for copy in plane_copies(index, w, step, owner):
                copy.start()
        index = now - LAG_B
        if 0 <= index < len(items):
            w, step = items[index]
            owner = nearest(t, step)
            here = spot(w, owner, first)
            remote(here, here, send_sem.at[index, 0], first_sem.at[index], (first, t)).wait_recv()
            for copy in relay_copies(index, w, owner):
                copy.start()
        index = now - LAG_C
        if 0 <= index < len(items):
            w, step = items[index]
            owner = nearest(t, step)
            for part, column in enumerate((second, diagonal)):
                here = spot(w, owner, column)
                remote(here, here, send_sem.at[index, 1], second_sem.at[index, part], (second, t)).wait_recv()
            for copy in last_copies(index, w, owner):
                copy.start()

    keeps = []

    def keep(src, dst):
        copy = functools.partial(pltpu.make_async_copy, src, dst, copy_sem.at[len(keeps)])
        copy().start()
        keeps.append(copy)

    def ready(index):
        w, step = items[index]
        owner = nearest(t, step)
        if step == 0:
            own_copy(w).wait()
        for part, column in enumerate((other, second + shift, first + shift, diagonal + shift)):
            here = spot(w, owner, column)
            remote(here, here, send_sem.at[index, 2], other_sem.at[index, part], (other, t)).wait_recv()
        block = rows_of(owner, sizes[w])
        keep(whole[w].at[block, :], whole_out[w].at[block, :])
        return owner, block

    def rate_copy(step):
        return remote(rate_in, rates.at[t], rate_send.at[step - 1], rate_recv.at[step - 1], (s, (t + step) % TP))

    for step in range(1, TP):
        rate_copy(step).start()
    rates[t] = rate_in[...]

    tick(0)
    tick(1)
    boundary = bounds[t]
    edge = boundary - s * rows

    def prepare(part, start):
        values = hidden[part, :].astype(F32)
        scale = lax.rsqrt(jnp.mean(values * values, axis=-1, keepdims=True) + EPSILON)
        normed[part, :] = (values * scale).astype(BF16)
        row = lax.broadcasted_iota(jnp.int32, (BLOCK, rows), 0) + start
        column = lax.broadcasted_iota(jnp.int32, (BLOCK, rows), 1)
        apart = (column > row) | ((row >= edge) & (column < edge))
        distance[part, :] = jnp.where(apart, -1, row - column).astype(F32)

    every_rows(rows, prepare)
    keep(normed, normed_out)
    for step in range(1, TP):
        here = rates.at[t]
        remote(here, here, rate_send.at[step - 1], rate_recv.at[step - 1], (s, t)).wait_recv()
    keep(rates, rate_out)

    before = jnp.where(s * rows - 1 >= boundary, 1, 0)
    last = jnp.where(s * rows + rows - 1 >= boundary, 1, 0)

    def rate_of(block, half):
        return rates[block, half : half + 1, :]

    def row_numbers(start, count=BLOCK):
        return lax.broadcasted_iota(jnp.int32, (count, HEAD), 0) + start

    def project(index):
        owner, block = ready(index)
        wide[:, 0:D] = dots(normed[...], whole[0][block, :], NT)

        def shape_rows(part, start):
            turn, lean = cosine[part, :], sine[part, :]
            for kind in range(2):
                for half in range(2):
                    at = kind * PAIR + half * HEAD
                    values = wide[part, at : at + HEAD]
                    logistic = 1.0 / (1.0 + jnp.exp(-values))
                    acts[owner, part, at : at + HEAD] = rotated(values * logistic, turn, lean).astype(BF16)
                    slopes[owner, part, at : at + HEAD] = (
                        logistic * (1.0 + values * (1.0 - logistic))
                    ).astype(BF16)
            acts[owner, part, 2 * PAIR : 4 * PAIR] = wide[part, 2 * PAIR : 4 * PAIR].astype(BF16)
            number = row_numbers(start)
            valid = jnp.where(jnp.where(number >= edge, 1, 0) == last, 1.0, 0.0)
            for half in range(2):
                fade = jnp.exp(-rate_of(owner, half) * (rows - 1 - number).astype(F32)) * valid
                keys = acts[owner, part, PAIR + half * HEAD : PAIR + half * HEAD + HEAD].astype(F32)
                weights[part, half * HEAD : half * HEAD + HEAD] = (keys * fade).astype(BF16)

        every_rows(rows, shape_rows)
        for half in range(2):
            at = half * HEAD
            state[owner * 2 + half] = dots(
                weights[:, at : at + HEAD], acts[owner, :, 2 * PAIR + at : 2 * PAIR + at + HEAD], TN
            ).astype(BF16)

    def attend(step):
        owner = nearest(t, step)
        for half in range(2):
            at = half * HEAD
            rate = rates[owner, half : half + 1, :]
            for top in range(0, rows, PAIR):
                width = top + PAIR
                scores[0:PAIR, 0:width] = dots(
                    acts[owner, top : top + PAIR, at : at + HEAD], acts[owner, 0:width, PAIR + at : PAIR + at + HEAD], NT
                )

                def weigh(part, start, width=width, top=top, rate=rate):
                    for left in range(0, width, HEAD):
                        apart = distance[pl.ds(pl.multiple_of(start + top, BLOCK), BLOCK), left : left + HEAD]
                        fade = jnp.where(apart >= 0.0, jnp.exp(-rate * apart), 0.0)
                        weights[part, left : left + HEAD] = (scores[part, left : left + HEAD] * fade).astype(BF16)

                every_rows(PAIR, weigh)
                column = pl.ds(pl.multiple_of(owner * PAIR + at, HEAD), HEAD)
                mixed[top : top + PAIR, column] = dots(
                    weights[0:PAIR, 0:width], acts[owner, 0:width, 2 * PAIR + at : 2 * PAIR + at + HEAD], NN
                )

    around = (first, second, diagonal)

    def state_copy(part):
        return remote(state, state_land.at[part], state_send.at[part], state_recv.at[part], (around[part], t))

    def prefix_scale(block, source_block, rate):
        same = jnp.where((source_block + 1) * rows - 1 >= boundary, 1, 0) == jnp.where(block * rows - 1 >= boundary, 1, 0)
        usable = flag(source_block < block) * flag(same)
        gap = jnp.maximum(block - 1 - source_block, 0).astype(F32)
        return jnp.exp(-rate * (rows * gap)) * usable

    def partial_copy():
        return remote(partial, partial_land, partial_sem.at[0], partial_sem.at[1], (other, t))

    def collect():
        for part in range(3):
            state_copy(part).wait_recv()

        @pl.loop(0, 2 * TP)
        def _(head):
            rate = rates[head // 2, pl.ds(head % 2, 1), :]
            here = jnp.zeros((HEAD, HEAD), F32)
            there = prefix_scale(other, s, rate) * state[head].astype(F32)
            for part in range(3):
                values = state_land[part, head].astype(F32)
                here += prefix_scale(s, around[part], rate) * values
                there += prefix_scale(other, around[part], rate) * values
            mine[head] = here
            partial[head] = there

        partial_copy().start()

    def mix():
        partial_copy().wait_recv()

        @pl.loop(0, 2 * TP)
        def _(head):
            incoming[head] = (mine[head] + partial_land[head]).astype(BF16)

        keep(incoming, incoming_out)
        for block in range(TP):
            for half in range(2):
                at = half * HEAD
                scores[:, at : at + HEAD] = dots(acts[block, :, at : at + HEAD], incoming[2 * block + half], NN)

            def add_outer(part, start, block=block):
                number = row_numbers(start)
                valid = jnp.where(jnp.where(number >= edge, 1, 0) == before, 1.0, 0.0)
                for half in range(2):
                    fade = jnp.exp(-rate_of(block, half) * (number + 1).astype(F32)) * valid
                    column = slice(block * PAIR + half * HEAD, block * PAIR + half * HEAD + HEAD)
                    mixed[part, column] += fade * scores[part, half * HEAD : half * HEAD + HEAD]

            every_rows(rows, add_outer)

        def gate_rows(part, start):
            values = mixed[part, :]
            scale = lax.rsqrt(jnp.mean(values * values, axis=-1, keepdims=True) + EPSILON)
            inv_mix[part, :] = jnp.broadcast_to(scale, (BLOCK, HEAD))
            values = values * scale
            unit[part, :] = values.astype(BF16)
            for block in range(TP):
                column = slice(block * PAIR, block * PAIR + PAIR)
                gate = acts[block, part, 3 * PAIR : 4 * PAIR].astype(F32)
                gated[part, column] = (values[:, column] * gate).astype(BF16)

        every_rows(rows, gate_rows, BLOCK)
        keep(acts, acts_out)
        keep(slopes, slope_out)
        keep(unit, unit_out)
        keep(gated, gated_out)
        keep(inv_mix, inv_mix_out)

    def project_out():
        wide[:, 0:D] = dots(gated[...], whole[1][...], NN)

        def norm_rows(part, start):
            values = hidden[part, :].astype(F32) + wide[part, 0:D]
            mixed[part, :] = values
            scale = lax.rsqrt(jnp.mean(values * values, axis=-1, keepdims=True) + EPSILON)
            inv_second[part, :] = jnp.broadcast_to(scale, (BLOCK, HEAD))
            second_normed[part, :] = (values * scale).astype(BF16)

        every_rows(rows, norm_rows)
        keep(second_normed, second_out)
        keep(inv_second, inv_second_out)

    def left_side(index):
        owner, block = ready(index)
        wide[:, 0:units] = dots(second_normed[...], whole[2][block, :], NT)

    def side_copies(slot, owner):
        return (
            pltpu.make_async_copy(sides.at[slot, 0], left_out.at[owner], side_sem.at[slot, 0]),
            pltpu.make_async_copy(sides.at[slot, 1], right_out.at[owner], side_sem.at[slot, 1]),
        )

    def right_side(index):
        owner, block = ready(index)
        wide[:, beside : beside + units] = dots(second_normed[...], whole[3][block, :], NT)
        step = items[index][1]
        slot = step % 2
        if step >= 2:
            for copy in side_copies(slot, nearest(t, step - 2)):
                copy.wait()

        def multiply(part, start):
            left, right = wide[part, 0:units], wide[part, beside : beside + units]
            glu[owner, part, :] = (left * right).astype(BF16)
            sides[slot, 0, part, :] = left.astype(BF16)
            sides[slot, 1, part, :] = right.astype(BF16)

        every_rows(rows, multiply)
        for copy in side_copies(slot, owner):
            copy.start()
        keep(glu.at[owner], glu_out.at[owner])

    def down(index):
        owner, block = ready(index)
        mixed[...] += dots(glu[owner], whole[4][block, :], NN)

    for now in range(2, 6):
        tick(now)
    for step in range(TP):
        project(step)
        tick(6 + step)
    for part in range(3):
        state_copy(part).start()
    for step in range(TP):
        attend(step)
        if step < 2:
            tick(10 + step)
    collect()
    for index in range(TP, 2 * TP):
        ready(index)
    tick(12)
    mix()
    tick(13)
    project_out()
    for index in range(2 * TP, len(items)):
        if index + 6 < len(items) + LAG_C:
            tick(index + 6)
        w = items[index][0]
        (left_side, right_side, down)[w - 2](index)

    def finish(part, start):
        result_out[part, :] = mixed[part, :].astype(BF16)

    every_rows(rows, finish)

    for step in range(1, TP):
        rate_copy(step).wait_send()
    for part in range(3):
        state_copy(part).wait_send()
    partial_copy().wait_send()
    for copy in keeps:
        copy().wait()
    for step in (2, 3):
        for copy in side_copies(step % 2, nearest(t, step)):
            copy.wait()
    for index, (w, step) in enumerate(items):
        owner = nearest(t, step)
        if step == 0:

            @pl.when(t < TP - 1)
            def _():
                up_copy(w, step, owner).wait_send()

            @pl.when(t > 0)
            def _():
                down_copy(w, step, owner).wait_send()
        else:

            @pl.when((owner < t) & (t < TP - 1))
            def _():
                up_copy(w, step, owner).wait_send()

            @pl.when((owner > t) & (t > 0))
            def _():
                down_copy(w, step, owner).wait_send()
        for copy in plane_copies(index, w, step, owner) + relay_copies(index, w, owner) + last_copies(index, w, owner):
            copy.wait_send()


KEPT = 34


def forward(shards, hidden, cosine, sine, rate, bounds):
    rows = hidden.shape[0]
    sizes = tuple(shard.shape[0] for shard in shards)
    units = sizes[2]
    beside = -(-units // HEAD) * HEAD
    items = 5 * TP
    dma = pltpu.SemaphoreType.DMA
    vmem = pl.BlockSpec(memory_space=pltpu.VMEM)
    anywhere = pl.BlockSpec(memory_space=pl.ANY)
    heads = 2 * TP
    outs = [jax.ShapeDtypeStruct((TP * size, D), BF16) for size in sizes] + [
        jax.ShapeDtypeStruct((TP, rows, 4 * PAIR), BF16),
        jax.ShapeDtypeStruct((TP, rows, 2 * PAIR), BF16),
        jax.ShapeDtypeStruct((rows, D), BF16),
        jax.ShapeDtypeStruct((rows, D), BF16),
        jax.ShapeDtypeStruct((rows, D), BF16),
        jax.ShapeDtypeStruct((rows, D), BF16),
        jax.ShapeDtypeStruct((TP, rows, units), BF16),
        jax.ShapeDtypeStruct((TP, rows, units), BF16),
        jax.ShapeDtypeStruct((TP, rows, units), BF16),
        jax.ShapeDtypeStruct((heads, HEAD, HEAD), BF16),
        jax.ShapeDtypeStruct((rows, HEAD), F32),
        jax.ShapeDtypeStruct((rows, HEAD), F32),
        jax.ShapeDtypeStruct((TP, 8, HEAD), F32),
        jax.ShapeDtypeStruct((rows, D), BF16),
    ]
    return pl.pallas_call(
        functools.partial(forward_kernel, rows, sizes),
        out_shape=outs,
        in_specs=[anywhere] * 5 + [vmem] * 4 + [pl.BlockSpec(memory_space=pltpu.SMEM)],
        out_specs=[anywhere] * (len(outs) - 1) + [vmem],
        scratch_shapes=[pltpu.VMEM((TP * size, D), BF16) for size in sizes]
        + [
            pltpu.VMEM((TP, rows, 4 * PAIR), BF16),
            pltpu.VMEM((TP, rows, 2 * PAIR), BF16),
            pltpu.VMEM((rows, D), BF16),
            pltpu.VMEM((rows, D), BF16),
            pltpu.VMEM((rows, D), BF16),
            pltpu.VMEM((rows, D), BF16),
            pltpu.VMEM((2, 2, rows, units), BF16),
            pltpu.VMEM((TP, rows, units), BF16),
            pltpu.VMEM((rows, max(2 * beside, D)), F32),
            pltpu.VMEM((rows, D), F32),
            pltpu.VMEM((rows, rows), F32),
            pltpu.VMEM((rows, rows), F32),
            pltpu.VMEM((rows, rows), BF16),
            pltpu.VMEM((heads, HEAD, HEAD), BF16),
            pltpu.VMEM((3, heads, HEAD, HEAD), BF16),
            pltpu.VMEM((heads, HEAD, HEAD), F32),
            pltpu.VMEM((heads, HEAD, HEAD), F32),
            pltpu.VMEM((heads, HEAD, HEAD), F32),
            pltpu.VMEM((heads, HEAD, HEAD), BF16),
            pltpu.VMEM((rows, HEAD), F32),
            pltpu.VMEM((rows, HEAD), F32),
            pltpu.VMEM((TP, 8, HEAD), F32),
            dma((5,)),
            dma((5, TP)),
            dma((5, TP)),
            dma((5, TP)),
            dma((items, 7)),
            dma((items,)),
            dma((items, 2)),
            dma((items, 4)),
            dma((TP - 1,)),
            dma((TP - 1,)),
            dma((3,)),
            dma((3,)),
            dma((2,)),
            dma((KEPT,)),
            dma((2, 2)),
        ],
        compiler_params=pltpu.CompilerParams(
            collective_id=0, has_side_effects=True, vmem_limit_bytes=60 * 2**20
        ),
        name="forward",
    )(*shards, hidden, cosine, sine, rate, bounds)


ROWS_STEP = 64
PIECES = 4
LAG_1, LAG_2, LAG_3, LAG_4 = 2, 4, 6, 8
SLOTS = 4


def add_rows(target, *terms):
    rows = target.shape[0]

    @pl.loop(0, rows // ROWS_STEP)
    def _(block):
        part = pl.ds(pl.multiple_of(block * ROWS_STEP, ROWS_STEP), ROWS_STEP)
        total = terms[0][part, :].astype(F32)
        for term in terms[1:]:
            total = total + term[part, :].astype(F32)
        target[part, :] = total.astype(target.dtype)


def reduce_kernel(count, spread, *refs):
    grads, refs = refs[:count], refs[count:]
    shares, refs = refs[:spread], refs[spread:]
    outs, refs = refs[:count], refs[count:]
    wholes, refs = refs[:spread], refs[spread:]
    own, refs = refs[0], refs[1:]
    other_land, refs = refs[:count], refs[count:]
    second_land, refs = refs[:count], refs[count:]
    first_land, refs = refs[:count], refs[count:]
    below_land, refs = refs[:count], refs[count:]
    above_land, refs = refs[:count], refs[count:]
    (own_sem, other_send, other_recv, second_send, second_recv, first_send, first_recv,
     line_send, below_recv, above_recv, share_local, share_up, share_down, share_recv) = refs
    s, t, other, first, second, diagonal = place()
    core = s % 2
    greet(s, t, (other, first, second))

    piece_rows = shares[0].shape[0] // PIECES
    pieces = [(a, p) for p in range(PIECES) for a in range(spread)]

    def piece(a, owner, p):
        return wholes[a].at[owner, pl.ds(p * piece_rows, piece_rows), :]

    def share_copies(a, p, owner, src):
        sem = (a, p, owner)
        return (
            remote(src, piece(a, owner, p), share_up.at[sem], share_recv.at[sem], (s, t + 1)),
            remote(src, piece(a, owner, p), share_down.at[sem], share_recv.at[sem], (s, t - 1)),
        )

    def own_piece(a, p):
        return shares[a].at[pl.ds(p * piece_rows, piece_rows), :]

    for a, p in pieces:
        up, down = share_copies(a, p, t, own_piece(a, p))
        pl.when(t < TP - 1)(up.start)
        pl.when(t > 0)(down.start)
        pltpu.make_async_copy(own_piece(a, p), piece(a, t, p), share_local.at[a, p]).start()

    relays = [(a, p, step) for a, p in pieces for step in range(1, TP)]

    def relay(index):
        a, p, step = relays[index]
        owner = nearest(t, step)
        up, down = share_copies(a, p, owner, piece(a, owner, p))
        up.wait_recv()
        pl.when((owner < t) & (t < TP - 1))(up.start)
        pl.when((owner > t) & (t > 0))(down.start)

    items = [(w, step) for w in range(count) for step in reversed(range(TP))]
    slots = own.shape[0]

    def sends(index, w, owner):
        return [
            remote(
                grads[w].at[owner, :, stripe(2 * chip + 1 - core)],
                other_land[w].at[owner, chip],
                other_send.at[index, chip],
                other_recv.at[index, chip],
                (other, t),
            )
            for chip in range(4)
        ]

    def loads(index, w, owner):
        rows = grads[w].shape[1]
        return [
            pltpu.make_async_copy(
                grads[w].at[owner, :, stripe(2 * chip + core)],
                own.at[index % slots, chip, pl.ds(0, rows), :],
                own_sem.at[index % slots, chip],
            )
            for chip in range(4)
        ]

    def to_second(index, w, owner):
        return [
            remote(
                other_land[w].at[owner, column // 2],
                second_land[w].at[owner, part],
                second_send.at[index, part],
                second_recv.at[index, part],
                (second, t),
            )
            for part, column in enumerate((diagonal, second))
        ]

    def to_first(index, w, owner):
        return remote(
            second_land[w].at[owner, 0], first_land[w].at[owner], first_send.at[index], first_recv.at[index], (first, t)
        )

    def along(index, w, owner):
        up = remote(
            first_land[w].at[owner], below_land[w].at[owner], line_send.at[index], below_recv.at[w, owner], (s, t + 1)
        )
        down = remote(
            first_land[w].at[owner], above_land[w].at[owner], line_send.at[index], above_recv.at[w, owner], (s, t - 1)
        )
        return up, down

    total = len(items)
    for tick in range(total + LAG_4):
        index = tick
        if index < total:
            w, step = items[index]
            owner = nearest(t, step)
            for copy in sends(index, w, owner) + loads(index, w, owner):
                copy.start()
        index = tick - LAG_1
        if 0 <= index < total:
            w, step = items[index]
            owner = nearest(t, step)
            rows = grads[w].shape[1]
            for copy in loads(index, w, owner):
                copy.wait()
            for copy in sends(index, w, owner):
                copy.wait_recv()
            for chip in range(4):
                add_rows(
                    other_land[w].at[owner, chip],
                    other_land[w].at[owner, chip],
                    own.at[index % slots, chip, pl.ds(0, rows), :],
                )
            for copy in to_second(index, w, owner):
                copy.start()
        index = tick - LAG_2
        if 0 <= index < total:
            w, step = items[index]
            owner = nearest(t, step)
            for copy in to_second(index, w, owner):
                copy.wait_recv()
            add_rows(second_land[w].at[owner, 0], second_land[w].at[owner, 0], other_land[w].at[owner, first // 2])
            to_first(index, w, owner).start()
        index = tick - LAG_3
        if 0 <= index < total:
            w, step = items[index]
            owner = nearest(t, step)
            to_first(index, w, owner).wait_recv()
            add_rows(
                first_land[w].at[owner],
                first_land[w].at[owner],
                other_land[w].at[owner, s // 2],
                second_land[w].at[owner, 1],
            )
        index = tick - LAG_4
        if 0 <= index < total:
            w, step = items[index]
            owner = nearest(t, step)
            up, down = along(index, w, owner)
            if step:

                @pl.when((owner > t) & (t > 0))
                def _():
                    up.wait_recv()
                    add_rows(first_land[w].at[owner], first_land[w].at[owner], below_land[w].at[owner])

                @pl.when((owner < t) & (t < TP - 1))
                def _():
                    down.wait_recv()
                    add_rows(first_land[w].at[owner], first_land[w].at[owner], above_land[w].at[owner])

                pl.when(owner > t)(up.start)
                pl.when(owner < t)(down.start)
            else:

                @pl.when(t == 0)
                def _():
                    down.wait_recv()
                    add_rows(outs[w], first_land[w].at[owner], above_land[w].at[owner])

                @pl.when(t == TP - 1)
                def _():
                    up.wait_recv()
                    add_rows(outs[w], first_land[w].at[owner], below_land[w].at[owner])

                @pl.when((t > 0) & (t < TP - 1))
                def _():
                    up.wait_recv()
                    down.wait_recv()
                    add_rows(outs[w], first_land[w].at[owner], below_land[w].at[owner], above_land[w].at[owner])

        if tick < len(relays):
            relay(tick)

    for index, (w, step) in enumerate(items):
        owner = nearest(t, step)
        for copy in sends(index, w, owner) + to_second(index, w, owner):
            copy.wait_send()
        to_first(index, w, owner).wait_send()
        if step:
            along(index, w, owner)[0].wait_send()
    for a, p in pieces:
        up, down = share_copies(a, p, t, own_piece(a, p))
        pl.when(t < TP - 1)(up.wait_send)
        pl.when(t > 0)(down.wait_send)
        pltpu.make_async_copy(own_piece(a, p), piece(a, t, p), share_local.at[a, p]).wait()
    for a, p, step in relays:
        owner = nearest(t, step)
        up, down = share_copies(a, p, owner, piece(a, owner, p))
        pl.when((owner < t) & (t < TP - 1))(up.wait_send)
        pl.when((owner > t) & (t > 0))(down.wait_send)


def reduce_gradients(grads, shares):
    count, spread = len(grads), len(shares)
    items = count * TP
    dma = pltpu.SemaphoreType.DMA
    rows = [grad.shape[1] for grad in grads]
    vmem = pl.BlockSpec(memory_space=pltpu.VMEM)
    anywhere = pl.BlockSpec(memory_space=pl.ANY)
    results = pl.pallas_call(
        functools.partial(reduce_kernel, count, spread),
        out_shape=[jax.ShapeDtypeStruct((r, STRIPE), F32) for r in rows]
        + [jax.ShapeDtypeStruct((TP, *share.shape), share.dtype) for share in shares],
        in_specs=[anywhere] * (count + spread),
        out_specs=[vmem] * count + [anywhere] * spread,
        scratch_shapes=[pltpu.VMEM((SLOTS, 4, max(rows), STRIPE), BF16)]
        + [pltpu.VMEM((TP, 4, r, STRIPE), BF16) for r in rows]
        + [pltpu.VMEM((TP, 2, r, STRIPE), BF16) for r in rows]
        + [pltpu.VMEM((TP, r, STRIPE), BF16) for r in rows]
        + [pltpu.VMEM((TP, r, STRIPE), BF16) for r in rows]
        + [pltpu.VMEM((TP, r, STRIPE), BF16) for r in rows]
        + [
            dma((SLOTS, 4)),
            dma((items, 4)),
            dma((items, 4)),
            dma((items, 2)),
            dma((items, 2)),
            dma((items,)),
            dma((items,)),
            dma((items,)),
            dma((count, TP)),
            dma((count, TP)),
            dma((spread, PIECES)),
            dma((spread, PIECES, TP)),
            dma((spread, PIECES, TP)),
            dma((spread, PIECES, TP)),
        ],
        compiler_params=pltpu.CompilerParams(
            collective_id=1, has_side_effects=True, vmem_limit_bytes=56 * 2**20
        ),
        name="reduce_gradients",
    )(*grads, *shares)
    return results[:count], results[count:]


def entering(value, axis, join, neutral, backward):
    count, mine = (lax.axis_size(axis), lax.axis_index(axis))
    pieces = jax.tree.map(lambda part: lax.all_gather(part, axis), value)
    if backward:
        pieces = jax.tree.map(lambda part: part[::-1], pieces)
        mine = count - 1 - mine
    subtotal = jax.tree.map(
        lambda part, zero: jnp.full_like(part, 0) + jnp.asarray(zero, part.dtype), value, neutral
    )

    def step(position, subtotal):
        longer = join(subtotal, jax.tree.map(lambda part: part[position], pieces))
        return jax.tree.map(lambda new, old: jnp.where(position < mine, new, old), longer, subtotal)

    return lax.fori_loop(0, count - 1, step, subtotal)


def swish_parts(pre_act):
    logistic = jax.nn.sigmoid(pre_act)
    return (pre_act * logistic, logistic * (1.0 + pre_act * (1.0 - logistic)))


def rotate(rows_in, cosine_table, sine_table, signed):
    halfway = rows_in.shape[-1] // 2
    front_half = rows_in[..., :halfway]
    back_half = rows_in[..., halfway:]
    return jnp.concatenate(
        [
            front_half * cosine_table - signed * back_half * sine_table,
            signed * front_half * sine_table + back_half * cosine_table,
        ],
        axis=-1,
    )


def combine_forward(earlier, following):
    return (earlier[0] * following[0], following[0][:, None, None] * earlier[1] + following[1])


def combine_backward(farther, nearer):
    return (farther[0] * nearer[0], nearer[1] + nearer[0][:, None, None] * farther[1])


def collect_weights(
    query_weight,
    key_weight,
    value_weight,
    gate_weight,
    out_weight,
    left_weight,
    right_weight,
    down_weight,
):
    return (
        lax.all_gather(query_weight, "seq", axis=0, tiled=True),
        lax.all_gather(key_weight, "seq", axis=0, tiled=True),
        lax.all_gather(value_weight, "seq", axis=0, tiled=True),
        lax.all_gather(gate_weight, "seq", axis=0, tiled=True),
        lax.all_gather(out_weight, "seq", axis=1, tiled=True),
        lax.all_gather(left_weight, "seq", axis=0, tiled=True),
        lax.all_gather(right_weight, "seq", axis=0, tiled=True),
        lax.all_gather(down_weight, "seq", axis=1, tiled=True),
    )


def state_prefix(factor, local_state):
    neutral = (jnp.ones_like(factor), jnp.zeros_like(local_state))
    return entering((factor, local_state), "seq", combine_forward, neutral, False)[1]


def state_suffix(factor, state_grad):
    neutral = (jnp.ones_like(factor), jnp.zeros_like(state_grad))
    return entering((factor, state_grad), "seq", combine_backward, neutral, True)[1]


def body(
    hidden_in,
    query_weight,
    key_weight,
    value_weight,
    gate_weight,
    out_weight,
    left_weight,
    right_weight,
    down_weight,
    decay_rate,
    seq_bounds,
    out_cotangent,
):
    row_count = hidden_in.shape[1]
    batch_count = hidden_in.shape[0]
    local_heads = decay_rate.shape[0]
    heads_shape = (row_count, local_heads, HEAD)
    device = lax.axis_index("seq")
    offsets = jnp.arange(row_count, dtype=jnp.int32)
    positions = device * row_count + offsets
    frequency = jnp.exp(
        jnp.arange(HEAD // 2, dtype=jnp.float32) * (-2.0 * math.log(10000.0) / HEAD)
    )
    angles = positions.astype(jnp.float32)[:, None] * frequency[None, :]
    cosine_table = jnp.cos(angles)[:, None, :]
    sine_table = jnp.sin(angles)[:, None, :]
    local_f = offsets.astype(jnp.float32)
    distance = local_f[:, None] - local_f[None, :]
    causal = distance >= 0.0
    distance_pos = jnp.maximum(distance, 0.0)
    accum = None
    outputs = []
    in_grads = []
    for batch_index in range(batch_count):
        gathered = collect_weights(
            query_weight,
            key_weight,
            value_weight,
            gate_weight,
            out_weight,
            left_weight,
            right_weight,
            down_weight,
        )
        query_full, key_full, value_full, gate_full, out_full, left_full, right_full, down_full = (
            gathered
        )
        boundary = seq_bounds[batch_index]
        segment = (positions >= boundary).astype(jnp.int32)
        before = (device * row_count - 1 >= boundary).astype(jnp.int32)
        last_segment = segment[row_count - 1]
        allowed = causal & (segment[:, None] == segment[None, :])
        decay = jnp.where(
            allowed[None], jnp.exp(-decay_rate[:, None, None] * distance_pos[None]), 0.0
        )
        coef_in = (
            jnp.exp(-decay_rate[None, :] * (local_f[:, None] + 1.0))
            * (segment == before).astype(jnp.float32)[:, None]
        )
        weight_loc = (
            jnp.exp(-decay_rate[None, :] * (row_count - 1.0 - local_f)[:, None])
            * (segment == last_segment).astype(jnp.float32)[:, None]
        )
        factor = jnp.where(last_segment == before, jnp.exp(-decay_rate * row_count), 0.0)
        input_rows = hidden_in[batch_index].astype(jnp.float32)
        inv_first = lax.rsqrt(jnp.mean(input_rows * input_rows, axis=-1, keepdims=True) + EPSILON)
        unit_first = input_rows * inv_first
        normed_first = unit_first.astype(jnp.bfloat16)
        query_pre = jnp.dot(normed_first, query_full, preferred_element_type=jnp.float32)
        key_pre = jnp.dot(normed_first, key_full, preferred_element_type=jnp.float32)
        value_pre = jnp.dot(normed_first, value_full, preferred_element_type=jnp.float32)
        gate_pre = jnp.dot(normed_first, gate_full, preferred_element_type=jnp.float32)
        query_act, query_slope = swish_parts(query_pre)
        key_act, key_slope = swish_parts(key_pre)
        query_rot = rotate(query_act.reshape(heads_shape), cosine_table, sine_table, 1.0).astype(
            jnp.bfloat16
        )
        key_rot = rotate(key_act.reshape(heads_shape), cosine_table, sine_table, 1.0).astype(
            jnp.bfloat16
        )
        value_rows = value_pre.astype(jnp.bfloat16).reshape(heads_shape)
        query_wide = query_rot.astype(jnp.float32)
        key_wide = key_rot.astype(jnp.float32)
        value_wide = value_rows.astype(jnp.float32)
        scores = jnp.einsum("ihe,jhe->hij", query_rot, key_rot, preferred_element_type=jnp.float32)
        attn_weights = (scores * decay).astype(jnp.bfloat16)
        inner_out = jnp.einsum(
            "hij,jhe->ihe", attn_weights, value_rows, preferred_element_type=jnp.float32
        )
        local_state = jnp.einsum(
            "jhe,jhf->hef",
            key_wide * weight_loc[:, :, None],
            value_wide,
            precision=HIGHEST_PRECISION,
        )
        incoming = state_prefix(factor, local_state)
        outer_out = coef_in[:, :, None] * jnp.einsum(
            "ihe,hef->ihf", query_wide, incoming, precision=HIGHEST_PRECISION
        )
        mixed_heads = (inner_out + outer_out).reshape(row_count, local_heads * HEAD)
        total_sq = lax.psum(jnp.sum(mixed_heads * mixed_heads, axis=-1), "tp")
        inv_mix = lax.rsqrt(total_sq / D + EPSILON)[:, None]
        unit_mix = mixed_heads * inv_mix
        gate_mix = (unit_mix * gate_pre).astype(jnp.bfloat16)
        attn_sum = lax.psum(jnp.dot(gate_mix, out_full, preferred_element_type=jnp.float32), "tp")
        resid_mid = input_rows + attn_sum
        inv_second = lax.rsqrt(jnp.mean(resid_mid * resid_mid, axis=-1, keepdims=True) + EPSILON)
        unit_second = resid_mid * inv_second
        normed_second = unit_second.astype(jnp.bfloat16)
        left_pre = jnp.dot(normed_second, left_full, preferred_element_type=jnp.float32)
        right_pre = jnp.dot(normed_second, right_full, preferred_element_type=jnp.float32)
        glu_product = (left_pre * right_pre).astype(jnp.bfloat16)
        glu_out = lax.psum(
            jnp.dot(glu_product, down_full, preferred_element_type=jnp.float32), "tp"
        )
        outputs.append((resid_mid + glu_out).astype(jnp.bfloat16))
        glu_cot = out_cotangent[batch_index]
        product_grad = jnp.einsum(
            "cd,fd->cf", glu_cot, down_full, preferred_element_type=jnp.float32
        )
        left_back = (product_grad * right_pre).astype(jnp.bfloat16)
        right_back = (product_grad * left_pre).astype(jnp.bfloat16)
        second_part = jnp.einsum(
            "cf,df->cd", left_back, left_full, preferred_element_type=jnp.float32
        ) + jnp.einsum("cf,df->cd", right_back, right_full, preferred_element_type=jnp.float32)
        second_back = lax.psum(second_part, "tp")
        mid_grad = glu_cot.astype(jnp.float32) + inv_second * (
            second_back - unit_second * jnp.mean(second_back * unit_second, axis=-1, keepdims=True)
        )
        attn_cot = mid_grad.astype(jnp.bfloat16)
        gate_mix_grad = jnp.einsum(
            "cd,kd->ck", attn_cot, out_full, preferred_element_type=jnp.float32
        )
        gate_back = (gate_mix_grad * unit_mix).astype(jnp.bfloat16)
        unit_mix_grad = gate_mix_grad * gate_pre
        mix_dot = lax.psum(jnp.sum(unit_mix_grad * unit_mix, axis=-1), "tp")
        heads_grad = (
            (inv_mix * (unit_mix_grad - unit_mix * (mix_dot / D)[:, None]))
            .astype(jnp.bfloat16)
            .reshape(heads_shape)
        )
        pair_grad = jnp.einsum(
            "ihe,jhe->hij", heads_grad, value_rows, preferred_element_type=jnp.float32
        ).astype(jnp.bfloat16)
        score_grad = pair_grad.astype(jnp.float32) * decay
        query_inner = jnp.einsum("hij,jhe->ihe", score_grad, key_wide, precision=HIGHEST_PRECISION)
        key_inner = jnp.einsum("hij,ihe->jhe", score_grad, query_wide, precision=HIGHEST_PRECISION)
        value_inner = jnp.einsum(
            "hij,ihe->jhe", attn_weights, heads_grad, preferred_element_type=jnp.float32
        )
        scaled_grad = heads_grad.astype(jnp.float32) * coef_in[:, :, None]
        query_outer = jnp.einsum("ihf,hef->ihe", scaled_grad, incoming, precision=HIGHEST_PRECISION)
        state_grad = jnp.einsum(
            "ihe,ihf->hef", query_wide, scaled_grad, precision=HIGHEST_PRECISION
        )
        later_grad = state_suffix(factor, state_grad)
        key_state = weight_loc[:, :, None] * jnp.einsum(
            "jhf,hef->jhe", value_wide, later_grad, precision=HIGHEST_PRECISION
        )
        value_state = weight_loc[:, :, None] * jnp.einsum(
            "jhe,hef->jhf", key_wide, later_grad, precision=HIGHEST_PRECISION
        )
        query_back = (
            rotate(query_inner + query_outer, cosine_table, sine_table, -1.0).reshape(row_count, -1)
            * query_slope
        ).astype(jnp.bfloat16)
        key_back = (
            rotate(key_inner + key_state, cosine_table, sine_table, -1.0).reshape(row_count, -1)
            * key_slope
        ).astype(jnp.bfloat16)
        value_back = (value_inner + value_state).reshape(row_count, -1).astype(jnp.bfloat16)
        fresh = (
            jnp.einsum("cd,ck->dk", normed_first, query_back, preferred_element_type=jnp.float32),
            jnp.einsum("cd,ck->dk", normed_first, key_back, preferred_element_type=jnp.float32),
            jnp.einsum("cd,ck->dk", normed_first, value_back, preferred_element_type=jnp.float32),
            jnp.einsum("cd,ck->dk", normed_first, gate_back, preferred_element_type=jnp.float32),
            jnp.einsum("ck,cd->kd", gate_mix, attn_cot, preferred_element_type=jnp.float32),
            jnp.einsum("cd,cf->df", normed_second, left_back, preferred_element_type=jnp.float32),
            jnp.einsum("cd,cf->df", normed_second, right_back, preferred_element_type=jnp.float32),
            jnp.einsum("cf,cd->fd", glu_product, glu_cot, preferred_element_type=jnp.float32),
        )
        if accum is None:
            accum = list(fresh)
        else:
            accum = [older + newer for older, newer in zip(accum, fresh)]
        total = jnp.einsum("ck,dk->cd", query_back, query_full, preferred_element_type=jnp.float32)
        total = total + jnp.einsum(
            "ck,dk->cd", key_back, key_full, preferred_element_type=jnp.float32
        )
        total = total + jnp.einsum(
            "ck,dk->cd", value_back, value_full, preferred_element_type=jnp.float32
        )
        first_back = lax.psum(
            total
            + jnp.einsum("ck,dk->cd", gate_back, gate_full, preferred_element_type=jnp.float32),
            "tp",
        )
        input_back = mid_grad + inv_first * (
            first_back - unit_first * jnp.mean(first_back * unit_first, axis=-1, keepdims=True)
        )
        in_grads.append(input_back)
    summed = (
        lax.psum_scatter(accum[0], "seq", scatter_dimension=0, tiled=True),
        lax.psum_scatter(accum[1], "seq", scatter_dimension=0, tiled=True),
        lax.psum_scatter(accum[2], "seq", scatter_dimension=0, tiled=True),
        lax.psum_scatter(accum[3], "seq", scatter_dimension=0, tiled=True),
        lax.psum_scatter(accum[4], "seq", scatter_dimension=1, tiled=True),
        lax.psum_scatter(accum[5], "seq", scatter_dimension=0, tiled=True),
        lax.psum_scatter(accum[6], "seq", scatter_dimension=0, tiled=True),
        lax.psum_scatter(accum[7], "seq", scatter_dimension=1, tiled=True),
    )
    return (
        jnp.stack(outputs),
        jnp.stack(in_grads),
        summed[0],
        summed[1],
        summed[2],
        summed[3],
        summed[4],
        summed[5],
        summed[6],
        summed[7],
    )


def fused_body(
    hidden_in,
    query_weight,
    key_weight,
    value_weight,
    gate_weight,
    out_weight,
    left_weight,
    right_weight,
    down_weight,
    decay_rate,
    seq_bounds,
    out_cotangent,
):
    row_count = hidden_in.shape[1]
    device, batch = lax.axis_index("seq"), lax.axis_index("tp")
    rates = None
    units = left_weight.shape[1]
    shards = [
        jnp.concatenate([query_weight.T, key_weight.T, value_weight.T, gate_weight.T], axis=0),
        out_weight,
        left_weight.T,
        right_weight.T,
        down_weight,
    ]
    heads = 2 * TP
    heads_shape = (row_count, heads, HEAD)
    offsets = jnp.arange(row_count, dtype=jnp.int32)
    positions = device * row_count + offsets
    frequency = jnp.exp(
        jnp.arange(HEAD // 2, dtype=F32) * (-2.0 * math.log(10000.0) / HEAD)
    )
    angles = positions.astype(F32)[:, None] * frequency[None, :]
    cosine, sine = jnp.cos(angles), jnp.sin(angles)
    cosine_table, sine_table = cosine[:, None, :], sine[:, None, :]
    input_bf = lax.dynamic_index_in_dim(hidden_in, batch, 0, keepdims=False)
    glu_cot = lax.dynamic_index_in_dim(out_cotangent, batch, 0, keepdims=False)
    results = forward(
        shards,
        input_bf,
        jnp.concatenate([cosine, cosine], axis=1),
        jnp.concatenate([-sine, sine], axis=1),
        jnp.broadcast_to(jnp.pad(decay_rate, (0, 6))[:, None], (8, HEAD)),
        seq_bounds,
    )
    qkvg_full, out_full, left_full, right_full, down_full = results[:5]
    (acts, slopes, normed_first, unit_mix, gate_mix, normed_second, left_pre, right_pre, glu_parts, incoming,
     inv_mix, inv_second, rates, output) = results[5:]
    rates = rates[:, :2, 0].reshape(heads)
    local_f = offsets.astype(F32)
    distance = local_f[:, None] - local_f[None, :]
    boundary = lax.dynamic_index_in_dim(seq_bounds, batch, 0, keepdims=False)
    segment = (positions >= boundary).astype(jnp.int32)
    before = (device * row_count - 1 >= boundary).astype(jnp.int32)
    last_segment = segment[row_count - 1]
    allowed = (distance >= 0.0) & (segment[:, None] == segment[None, :])
    decay = jnp.where(allowed[None], jnp.exp(-rates[:, None, None] * jnp.maximum(distance, 0.0)[None]), 0.0)
    coef_in = (
        jnp.exp(-rates[None, :] * (local_f[:, None] + 1.0)) * (segment == before).astype(F32)[:, None]
    )
    weight_loc = (
        jnp.exp(-rates[None, :] * (row_count - 1.0 - local_f)[:, None])
        * (segment == last_segment).astype(F32)[:, None]
    )
    blocks = jnp.arange(SEQ)
    ends = ((blocks + 1) * row_count - 1 >= boundary).astype(jnp.int32)
    gap = (device - 1 - blocks).astype(F32)
    prefix_coef = jnp.where(
        ((blocks < device) & (ends == before))[:, None],
        jnp.exp(-rates[None, :] * row_count * jnp.maximum(gap, 0.0)[:, None]),
        0.0,
    )
    later_before = (blocks * row_count - 1 >= boundary).astype(jnp.int32)
    later_gap = (blocks - 1 - device).astype(F32)
    suffix_coef = jnp.where(
        ((blocks > device) & (later_before == last_segment))[:, None],
        jnp.exp(-rates[None, :] * row_count * jnp.maximum(later_gap, 0.0)[:, None]),
        0.0,
    )

    def states(local, coef):
        every = lax.all_gather(local.astype(BF16), "seq").astype(F32)
        return jnp.sum(coef[:, :, None, None] * every, axis=0)

    def side(parts):
        return parts.transpose(1, 0, 2).reshape(row_count, -1)

    def kind(parts, index, size):
        return side(parts[:, :, index * size : index * size + size])

    query_rot, key_rot, value_rows = [kind(acts, index, PAIR).reshape(heads_shape) for index in range(3)]
    gate_pre = kind(acts, 3, PAIR).astype(F32)
    query_slope, key_slope = [kind(slopes, index, PAIR).astype(F32) for index in range(2)]
    query_full, key_full, value_full, gate_full = [
        qkvg_full.reshape(TP, 4, PAIR, D)[:, index].reshape(D, D) for index in range(4)
    ]
    left_pre, right_pre, glu_product = side(left_pre).astype(F32), side(right_pre).astype(F32), side(glu_parts)
    inv_mix, inv_second = inv_mix[:, :1], inv_second[:, :1]
    unit_mix, unit_second = unit_mix.astype(F32), normed_second.astype(F32)
    input_rows = input_bf.astype(F32)
    inv_first = lax.rsqrt(jnp.mean(input_rows * input_rows, axis=-1, keepdims=True) + EPSILON)
    unit_first = input_rows * inv_first
    scores = jnp.einsum("ihe,jhe->hij", query_rot, key_rot, preferred_element_type=F32)
    attn_weights = (scores * decay).astype(BF16)

    product_grad = dots(glu_cot, down_full, NT)
    left_back = (product_grad * right_pre).astype(BF16)
    right_back = (product_grad * left_pre).astype(BF16)
    second_back = dots(left_back, left_full, NN) + dots(right_back, right_full, NN)
    mid_grad = glu_cot.astype(F32) + inv_second * (
        second_back - unit_second * jnp.mean(second_back * unit_second, axis=-1, keepdims=True)
    )
    attn_cot = mid_grad.astype(BF16)
    gate_mix_grad = dots(attn_cot, out_full, NT)
    gate_back = (gate_mix_grad * unit_mix).astype(BF16)
    unit_mix_grad = gate_mix_grad * gate_pre
    mix_dot = jnp.mean(unit_mix_grad * unit_mix, axis=-1, keepdims=True)
    heads_grad = (inv_mix * (unit_mix_grad - unit_mix * mix_dot)).astype(BF16).reshape(heads_shape)
    pair_grad = jnp.einsum("ihe,jhe->hij", heads_grad, value_rows, preferred_element_type=F32).astype(BF16)
    score_grad = (pair_grad.astype(F32) * decay).astype(BF16)
    query_inner = jnp.einsum("hij,jhe->ihe", score_grad, key_rot, preferred_element_type=F32)
    key_inner = jnp.einsum("hij,ihe->jhe", score_grad, query_rot, preferred_element_type=F32)
    value_inner = jnp.einsum("hij,ihe->jhe", attn_weights, heads_grad, preferred_element_type=F32)
    scaled_grad = (heads_grad.astype(F32) * coef_in[:, :, None]).astype(BF16)
    query_outer = jnp.einsum("ihf,hef->ihe", scaled_grad, incoming, preferred_element_type=F32)
    state_grad = jnp.einsum("ihe,ihf->hef", query_rot, scaled_grad, preferred_element_type=F32)
    later_grad = states(state_grad, suffix_coef).astype(BF16)
    key_state = weight_loc[:, :, None] * jnp.einsum("jhf,hef->jhe", value_rows, later_grad, preferred_element_type=F32)
    value_state = weight_loc[:, :, None] * jnp.einsum("jhe,hef->jhf", key_rot, later_grad, preferred_element_type=F32)
    query_back = (
        rotate(query_inner + query_outer, cosine_table, sine_table, -1.0).reshape(row_count, D) * query_slope
    ).astype(BF16)
    key_back = (
        rotate(key_inner + key_state, cosine_table, sine_table, -1.0).reshape(row_count, D) * key_slope
    ).astype(BF16)
    value_back = (value_inner + value_state).reshape(row_count, D).astype(BF16)
    first_back = (
        dots(query_back, query_full, NN)
        + dots(key_back, key_full, NN)
        + dots(value_back, value_full, NN)
        + dots(gate_back, gate_full, NN)
    )
    input_back = mid_grad + inv_first * (
        first_back - unit_first * jnp.mean(first_back * unit_first, axis=-1, keepdims=True)
    )
    grads = [
        dots(glu_product, glu_cot, TN),
        dots(left_back, normed_second, TN),
        dots(right_back, normed_second, TN),
        dots(gate_mix, attn_cot, TN),
        dots(query_back, normed_first, TN),
        dots(key_back, normed_first, TN),
        dots(value_back, normed_first, TN),
        dots(gate_back, normed_first, TN),
    ]
    sums, wholes = reduce_gradients(
        [grad.astype(BF16).reshape(TP, -1, D) for grad in grads], [output, input_back.astype(BF16)]
    )
    down_grad, left_grad, right_grad, out_grad, query_grad, key_grad, value_grad, gate_grad = sums
    return (
        wholes[0],
        wholes[1].astype(F32),
        query_grad.T,
        key_grad.T,
        value_grad.T,
        gate_grad.T,
        out_grad,
        left_grad.T,
        right_grad.T,
        down_grad,
    )


def solution(mesh):
    fits = mesh.shape["seq"] == SEQ and mesh.shape["tp"] == TP
    return jax.shard_map(
        fused_body if fits else body,
        mesh=mesh,
        in_specs=(
            P(None, "seq", None),
            P("seq", "tp"),
            P("seq", "tp"),
            P("seq", "tp"),
            P("seq", "tp"),
            P("tp", "seq"),
            P("seq", "tp"),
            P("seq", "tp"),
            P("tp", "seq"),
            P("tp"),
            P(),
            P(None, "seq", None),
        ),
        out_specs=(
            P(None, "seq", None),
            P(None, "seq", None),
            P("seq", "tp"),
            P("seq", "tp"),
            P("seq", "tp"),
            P("seq", "tp"),
            P("tp", "seq"),
            P("seq", "tp"),
            P("seq", "tp"),
            P("tp", "seq"),
        ),
        check_vma=False,
    )
```

```python
import functools
import math

import jax
import jax.numpy as jnp
from jax import lax
from jax.experimental import pallas as pl
from jax.experimental.pallas import tpu as pltpu
from jax.sharding import PartitionSpec as P

D = 1024
HEAD = 128


EPSILON = 1e-06
HIGHEST_PRECISION = lax.Precision.HIGHEST
MESH = pl.DeviceIdType.MESH
BF16 = jnp.bfloat16
F32 = jnp.float32

SEQ = 8
TP = 4
STRIPE = 128
PAIR = 2 * HEAD
BLOCK = 32

NN = ((1,), (0,))
NT = ((1,), (1,))
TN = ((0,), (0,))


def dots(left, right, dims):
    return lax.dot_general(left, right, (dims, ((), ())), preferred_element_type=F32)


def place():
    s, t = lax.axis_index("seq"), lax.axis_index("tp")
    core = s % 2
    column = (s // 2) % 2
    line = s // 4
    other = s + 1 - 2 * core
    across_x = s + 2 * (1 - 2 * column)
    across_y = s + 4 * (1 - 2 * line)
    first = across_x + core * (across_y - across_x)
    second = across_y + core * (across_x - across_y)
    diagonal = across_x + across_y - s
    return s, t, other, first, second, diagonal


def nearest(t, step):
    flip = t // 2
    low = t + flip * (3 - 2 * t)
    swap = low * (1 - step // 2)
    index = step + swap * (1 - 2 * step)
    return index + flip * (3 - 2 * index)


def stripe(index):
    return pl.ds(pl.multiple_of((index % 2 * (SEQ // 2) + index // 2) * STRIPE, STRIPE), STRIPE)


def plain(index):
    return slice(index * STRIPE, index * STRIPE + STRIPE)


def place_of(index):
    at = (index % 2 * (SEQ // 2) + index // 2) * STRIPE
    return slice(at, at + STRIPE)


def rows_of(index, size):
    return pl.ds(pl.multiple_of(index * size, size), size)


def remote(src, dst, send, receive, device):
    return pltpu.make_async_remote_copy(
        src_ref=src, dst_ref=dst, send_sem=send, recv_sem=receive, device_id=device, device_id_type=MESH
    )


def greet(s, t, around):
    barrier = pltpu.get_barrier_semaphore()
    for step in range(1, TP):
        pl.semaphore_signal(barrier, inc=1, device_id=(s, (t + step) % TP), device_id_type=MESH)
    for device in around:
        pl.semaphore_signal(barrier, inc=1, device_id=(device, t), device_id_type=MESH)
    pl.semaphore_wait(barrier, TP - 1 + len(around))


def every_rows(count, body, size=BLOCK):
    @pl.loop(0, count // size)
    def _(block):
        body(pl.ds(pl.multiple_of(block * size, size), size), block * size)


def flag(condition):
    return jnp.where(condition, 1.0, 0.0).astype(F32)


def rotated(values, cosine, sine):
    return values * cosine + pltpu.roll(values, HEAD // 2, 1) * sine


LAG_B, LAG_C = 2, 4
WEIGHTS = ("qkvg", "out", "left", "right", "down")


def forward_kernel(rows, sizes, *refs):
    (shards, refs) = refs[:5], refs[5:]
    (hidden_in, cosine, sine, rate_in, bounds), refs = refs[:5], refs[5:]
    whole_out, refs = refs[:5], refs[5:]
    (acts_out, pack_out, normed_out, second_out, left_out, right_out, glu_out,
     incoming_out, inv_mix_out, inv_second_out, rate_out, result_out), refs = refs[:12], refs[12:]
    whole, refs = refs[:5], refs[5:]
    (acts, pack, normed, hidden, second_normed, sides, glu, wide, mixed, distance, scores, weights,
     state, state_land, mine, partial, partial_land, incoming, inv_mix, inv_second, rates), refs = refs[:21], refs[21:]
    (local_sem, up_sem, down_sem, line_sem, send_sem, first_sem, second_sem, other_sem, rate_send, rate_recv,
     state_send, state_recv, partial_sem, copy_sem, side_sem, hidden_sem) = refs
    s, t, other, first, second, diagonal = place()
    units, beside = sizes[2], wide.shape[1] // 2
    shift = other - s
    greet(s, t, (other, first, second, diagonal))

    for index in range(SEQ):
        pltpu.make_async_copy(
            hidden_in.at[t, :, plain(index)], hidden.at[:, place_of(index)], hidden_sem.at[index]
        ).start()

    pairs = [(2, step) for step in range(TP)], [(3, step) for step in range(TP)]
    items = (
        [(0, step) for step in range(TP)]
        + [(1, step) for step in range(TP)]
        + [item for both in zip(*pairs) for item in both]
        + [(4, step) for step in range(TP)]
    )

    def spot(w, owner, column):
        return whole[w].at[rows_of(owner, sizes[w]), stripe(column)]

    def source(w, step, owner):
        return shards[w] if step == 0 else spot(w, owner, s)

    def up_copy(w, step, owner):
        return remote(source(w, step, owner), spot(w, owner, s), up_sem.at[w, owner], line_sem.at[w, owner], (s, t + 1))

    def down_copy(w, step, owner):
        return remote(source(w, step, owner), spot(w, owner, s), down_sem.at[w, owner], line_sem.at[w, owner], (s, t - 1))

    def own_copy(w):
        return pltpu.make_async_copy(shards[w], spot(w, t, s), local_sem.at[w])

    def plane_copies(index, w, step, owner):
        src, dst = source(w, step, owner), spot(w, owner, s)
        return (
            remote(src, dst, send_sem.at[index, 0], first_sem.at[index], (first, t)),
            remote(src, dst, send_sem.at[index, 1], second_sem.at[index, 0], (second, t)),
            remote(src, dst, send_sem.at[index, 2], other_sem.at[index, 0], (other, t)),
        )

    def relay_copies(index, w, owner):
        src = spot(w, owner, first)
        return (
            remote(src, src, send_sem.at[index, 3], second_sem.at[index, 1], (second, t)),
            remote(src, src, send_sem.at[index, 4], other_sem.at[index, 1], (other, t)),
        )

    def last_copies(index, w, owner):
        near, far = spot(w, owner, second), spot(w, owner, diagonal)
        return (
            remote(near, near, send_sem.at[index, 5], other_sem.at[index, 2], (other, t)),
            remote(far, far, send_sem.at[index, 6], other_sem.at[index, 3], (other, t)),
        )

    def tick(now):
        index = now
        if index < len(items):
            w, step = items[index]
            owner = nearest(t, step)
            if step == 0:
                own_copy(w).start()

                @pl.when(t < TP - 1)
                def _():
                    up_copy(w, step, owner).start()

                @pl.when(t > 0)
                def _():
                    down_copy(w, step, owner).start()
            else:
                up_copy(w, step, owner).wait_recv()

                @pl.when((owner < t) & (t < TP - 1))
                def _():
                    up_copy(w, step, owner).start()

                @pl.when((owner > t) & (t > 0))
                def _():
                    down_copy(w, step, owner).start()
            for copy in plane_copies(index, w, step, owner):
                copy.start()
        index = now - LAG_B
        if 0 <= index < len(items):
            w, step = items[index]
            owner = nearest(t, step)
            here = spot(w, owner, first)
            remote(here, here, send_sem.at[index, 0], first_sem.at[index], (first, t)).wait_recv()
            for copy in relay_copies(index, w, owner):
                copy.start()
        index = now - LAG_C
        if 0 <= index < len(items):
            w, step = items[index]
            owner = nearest(t, step)
            for part, column in enumerate((second, diagonal)):
                here = spot(w, owner, column)
                remote(here, here, send_sem.at[index, 1], second_sem.at[index, part], (second, t)).wait_recv()
            for copy in last_copies(index, w, owner):
                copy.start()

    keeps = []

    def keep(src, dst):
        copy = functools.partial(pltpu.make_async_copy, src, dst, copy_sem.at[len(keeps)])
        copy().start()
        keeps.append(copy)

    def ready(index):
        w, step = items[index]
        owner = nearest(t, step)
        if step == 0:
            own_copy(w).wait()
        for part, column in enumerate((other, second + shift, first + shift, diagonal + shift)):
            here = spot(w, owner, column)
            remote(here, here, send_sem.at[index, 2], other_sem.at[index, part], (other, t)).wait_recv()
        block = rows_of(owner, sizes[w])
        keep(whole[w].at[block, :], whole_out[w].at[block, :])
        return owner, block

    def rate_copy(step):
        return remote(rate_in, rates.at[t], rate_send.at[step - 1], rate_recv.at[step - 1], (s, (t + step) % TP))

    for step in range(1, TP):
        rate_copy(step).start()
    rates[t] = rate_in[...]

    tick(0)
    tick(1)
    boundary = bounds[t]
    edge = boundary - s * rows

    for index in range(SEQ):
        pltpu.make_async_copy(
            hidden_in.at[t, :, plain(index)], hidden.at[:, place_of(index)], hidden_sem.at[index]
        ).wait()

    def prepare(part, start):
        values = hidden[part, :].astype(F32)
        scale = lax.rsqrt(jnp.mean(values * values, axis=-1, keepdims=True) + EPSILON)
        normed[part, :] = (values * scale).astype(BF16)
        row = lax.broadcasted_iota(jnp.int32, (BLOCK, rows), 0) + start
        column = lax.broadcasted_iota(jnp.int32, (BLOCK, rows), 1)
        apart = (column > row) | ((row >= edge) & (column < edge))
        distance[part, :] = jnp.where(apart, -1, row - column).astype(F32)

    every_rows(rows, prepare)
    keep(normed, normed_out)
    for step in range(1, TP):
        here = rates.at[t]
        remote(here, here, rate_send.at[step - 1], rate_recv.at[step - 1], (s, t)).wait_recv()
    keep(rates, rate_out)

    before = jnp.where(s * rows - 1 >= boundary, 1, 0)
    last = jnp.where(s * rows + rows - 1 >= boundary, 1, 0)

    def rate_of(block, half):
        return rates[block, half : half + 1, :]

    def row_numbers(start, count=BLOCK):
        return lax.broadcasted_iota(jnp.int32, (count, HEAD), 0) + start

    def project(index):
        owner, block = ready(index)
        wide[:, 0:D] = dots(normed[...], whole[0][block, :], NT)

        def shape_rows(part, start):
            turn, lean = cosine[part, :], sine[part, :]
            for kind in range(2):
                for half in range(2):
                    at = kind * PAIR + half * HEAD
                    values = wide[part, at : at + HEAD]
                    logistic = 1.0 / (1.0 + jnp.exp(-values))
                    acts[owner, part, at : at + HEAD] = rotated(values * logistic, turn, lean).astype(BF16)
                    pack[owner, part, at : at + HEAD] = (
                        logistic * (1.0 + values * (1.0 - logistic))
                    ).astype(BF16)
            acts[owner, part, 2 * PAIR : 4 * PAIR] = wide[part, 2 * PAIR : 4 * PAIR].astype(BF16)
            number = row_numbers(start)
            valid = jnp.where(jnp.where(number >= edge, 1, 0) == last, 1.0, 0.0)
            for half in range(2):
                fade = jnp.exp(-rate_of(owner, half) * (rows - 1 - number).astype(F32)) * valid
                keys = acts[owner, part, PAIR + half * HEAD : PAIR + half * HEAD + HEAD].astype(F32)
                weights[part, half * HEAD : half * HEAD + HEAD] = (keys * fade).astype(BF16)

        every_rows(rows, shape_rows)
        for half in range(2):
            at = half * HEAD
            state[owner * 2 + half] = dots(
                weights[:, at : at + HEAD], acts[owner, :, 2 * PAIR + at : 2 * PAIR + at + HEAD], TN
            ).astype(BF16)

    def attend(step):
        owner = nearest(t, step)
        for half in range(2):
            at = half * HEAD
            rate = rates[owner, half : half + 1, :]
            for top in range(0, rows, PAIR):
                width = top + PAIR
                scores[0:PAIR, 0:width] = dots(
                    acts[owner, top : top + PAIR, at : at + HEAD], acts[owner, 0:width, PAIR + at : PAIR + at + HEAD], NT
                )

                def weigh(part, start, width=width, top=top, rate=rate):
                    for left in range(0, width, HEAD):
                        apart = distance[pl.ds(pl.multiple_of(start + top, BLOCK), BLOCK), left : left + HEAD]
                        fade = jnp.where(apart >= 0.0, jnp.exp(-rate * apart), 0.0)
                        weights[part, left : left + HEAD] = (scores[part, left : left + HEAD] * fade).astype(BF16)

                every_rows(PAIR, weigh)
                column = pl.ds(pl.multiple_of(owner * PAIR + at, HEAD), HEAD)
                mixed[top : top + PAIR, column] = dots(
                    weights[0:PAIR, 0:width], acts[owner, 0:width, 2 * PAIR + at : 2 * PAIR + at + HEAD], NN
                )

    around = (first, second, diagonal)

    def state_copy(part):
        return remote(state, state_land.at[part], state_send.at[part], state_recv.at[part], (around[part], t))

    def prefix_scale(block, source_block, rate):
        same = jnp.where((source_block + 1) * rows - 1 >= boundary, 1, 0) == jnp.where(block * rows - 1 >= boundary, 1, 0)
        usable = flag(source_block < block) * flag(same)
        gap = jnp.maximum(block - 1 - source_block, 0).astype(F32)
        return jnp.exp(-rate * (rows * gap)) * usable

    def partial_copy():
        return remote(partial, partial_land, partial_sem.at[0], partial_sem.at[1], (other, t))

    def collect():
        for part in range(3):
            state_copy(part).wait_recv()

        @pl.loop(0, 2 * TP)
        def _(head):
            rate = rates[head // 2, pl.ds(head % 2, 1), :]
            here = jnp.zeros((HEAD, HEAD), F32)
            there = prefix_scale(other, s, rate) * state[head].astype(F32)
            for part in range(3):
                values = state_land[part, head].astype(F32)
                here += prefix_scale(s, around[part], rate) * values
                there += prefix_scale(other, around[part], rate) * values
            mine[head] = here
            partial[head] = there

        partial_copy().start()

    def mix():
        partial_copy().wait_recv()

        @pl.loop(0, 2 * TP)
        def _(head):
            incoming[head] = (mine[head] + partial_land[head]).astype(BF16)

        keep(incoming, incoming_out)
        for block in range(TP):
            for half in range(2):
                at = half * HEAD
                scores[:, at : at + HEAD] = dots(acts[block, :, at : at + HEAD], incoming[2 * block + half], NN)

            def add_outer(part, start, block=block):
                number = row_numbers(start)
                valid = jnp.where(jnp.where(number >= edge, 1, 0) == before, 1.0, 0.0)
                for half in range(2):
                    fade = jnp.exp(-rate_of(block, half) * (number + 1).astype(F32)) * valid
                    column = slice(block * PAIR + half * HEAD, block * PAIR + half * HEAD + HEAD)
                    mixed[part, column] += fade * scores[part, half * HEAD : half * HEAD + HEAD]

            every_rows(rows, add_outer)

        def gate_rows(part, start):
            values = mixed[part, :]
            scale = lax.rsqrt(jnp.mean(values * values, axis=-1, keepdims=True) + EPSILON)
            inv_mix[part, :] = jnp.broadcast_to(scale, (BLOCK, HEAD))
            values = values * scale
            for block in range(TP):
                column = slice(block * PAIR, block * PAIR + PAIR)
                gate = acts[block, part, 3 * PAIR : 4 * PAIR].astype(F32)
                pack[block, part, 2 * PAIR : 3 * PAIR] = (values[:, column] * gate).astype(BF16)
                pack[block, part, 3 * PAIR : 4 * PAIR] = values[:, column].astype(BF16)

        every_rows(rows, gate_rows, BLOCK)
        keep(acts, acts_out)
        keep(pack, pack_out)
        keep(inv_mix, inv_mix_out)

    def project_out():
        for block in range(TP):
            term = dots(pack[block, :, 2 * PAIR : 3 * PAIR], whole[1][block * PAIR : block * PAIR + PAIR, :], NN)
            if block:
                wide[:, 0:D] += term
            else:
                wide[:, 0:D] = term

        def norm_rows(part, start):
            values = hidden[part, :].astype(F32) + wide[part, 0:D]
            mixed[part, :] = values
            scale = lax.rsqrt(jnp.mean(values * values, axis=-1, keepdims=True) + EPSILON)
            inv_second[part, :] = jnp.broadcast_to(scale, (BLOCK, HEAD))
            second_normed[part, :] = (values * scale).astype(BF16)

        every_rows(rows, norm_rows)
        keep(second_normed, second_out)
        keep(inv_second, inv_second_out)

    def left_side(index):
        owner, block = ready(index)
        wide[:, 0:units] = dots(second_normed[...], whole[2][block, :], NT)

    def side_copies(slot, owner):
        return (
            pltpu.make_async_copy(sides.at[slot, 0], left_out.at[owner], side_sem.at[slot, 0]),
            pltpu.make_async_copy(sides.at[slot, 1], right_out.at[owner], side_sem.at[slot, 1]),
        )

    def right_side(index):
        owner, block = ready(index)
        wide[:, beside : beside + units] = dots(second_normed[...], whole[3][block, :], NT)
        step = items[index][1]
        slot = step % 2
        if step >= 2:
            for copy in side_copies(slot, nearest(t, step - 2)):
                copy.wait()

        def multiply(part, start):
            left, right = wide[part, 0:units], wide[part, beside : beside + units]
            glu[owner, part, :] = (left * right).astype(BF16)
            sides[slot, 0, part, :] = left.astype(BF16)
            sides[slot, 1, part, :] = right.astype(BF16)

        every_rows(rows, multiply)
        for copy in side_copies(slot, owner):
            copy.start()
        keep(glu.at[owner], glu_out.at[owner])

    def down(index):
        owner, block = ready(index)
        mixed[...] += dots(glu[owner], whole[4][block, :], NN)

    for now in range(2, 6):
        tick(now)
    for step in range(TP):
        project(step)
        tick(6 + step)
    for part in range(3):
        state_copy(part).start()
    for step in range(TP):
        attend(step)
        if step < 2:
            tick(10 + step)
    collect()
    for index in range(TP, 2 * TP):
        ready(index)
    tick(12)
    mix()
    tick(13)
    project_out()
    for index in range(2 * TP, len(items)):
        if index + 6 < len(items) + LAG_C:
            tick(index + 6)
        w = items[index][0]
        (left_side, right_side, down)[w - 2](index)

    def finish(part, start):
        for index in range(SEQ):
            result_out[part, plain(index)] = mixed[part, place_of(index)].astype(BF16)

    every_rows(rows, finish)

    for step in range(1, TP):
        rate_copy(step).wait_send()
    for part in range(3):
        state_copy(part).wait_send()
    partial_copy().wait_send()
    for copy in keeps:
        copy().wait()
    for step in (2, 3):
        for copy in side_copies(step % 2, nearest(t, step)):
            copy.wait()
    for index, (w, step) in enumerate(items):
        owner = nearest(t, step)
        if step == 0:

            @pl.when(t < TP - 1)
            def _():
                up_copy(w, step, owner).wait_send()

            @pl.when(t > 0)
            def _():
                down_copy(w, step, owner).wait_send()
        else:

            @pl.when((owner < t) & (t < TP - 1))
            def _():
                up_copy(w, step, owner).wait_send()

            @pl.when((owner > t) & (t > 0))
            def _():
                down_copy(w, step, owner).wait_send()
        for copy in plane_copies(index, w, step, owner) + relay_copies(index, w, owner) + last_copies(index, w, owner):
            copy.wait_send()


KEPT = 34


def forward(shards, hidden, cosine, sine, rate, bounds):
    rows = hidden.shape[1]
    sizes = tuple(shard.shape[0] for shard in shards)
    units = sizes[2]
    beside = -(-units // HEAD) * HEAD
    items = 5 * TP
    dma = pltpu.SemaphoreType.DMA
    vmem = pl.BlockSpec(memory_space=pltpu.VMEM)
    anywhere = pl.BlockSpec(memory_space=pl.ANY)
    heads = 2 * TP
    outs = [jax.ShapeDtypeStruct((TP * size, D), BF16) for size in sizes] + [
        jax.ShapeDtypeStruct((TP, rows, 4 * PAIR), BF16),
        jax.ShapeDtypeStruct((TP, rows, 4 * PAIR), BF16),
        jax.ShapeDtypeStruct((rows, D), BF16),
        jax.ShapeDtypeStruct((rows, D), BF16),
        jax.ShapeDtypeStruct((TP, rows, units), BF16),
        jax.ShapeDtypeStruct((TP, rows, units), BF16),
        jax.ShapeDtypeStruct((TP, rows, units), BF16),
        jax.ShapeDtypeStruct((heads, HEAD, HEAD), BF16),
        jax.ShapeDtypeStruct((rows, HEAD), F32),
        jax.ShapeDtypeStruct((rows, HEAD), F32),
        jax.ShapeDtypeStruct((TP, 8, HEAD), F32),
        jax.ShapeDtypeStruct((rows, D), BF16),
    ]
    return pl.pallas_call(
        functools.partial(forward_kernel, rows, sizes),
        out_shape=outs,
        in_specs=[anywhere] * 6 + [vmem] * 3 + [pl.BlockSpec(memory_space=pltpu.SMEM)],
        out_specs=[anywhere] * (len(outs) - 1) + [vmem],
        scratch_shapes=[pltpu.VMEM((TP * size, D), BF16) for size in sizes]
        + [
            pltpu.VMEM((TP, rows, 4 * PAIR), BF16),
            pltpu.VMEM((TP, rows, 4 * PAIR), BF16),
            pltpu.VMEM((rows, D), BF16),
            pltpu.VMEM((rows, D), BF16),
            pltpu.VMEM((rows, D), BF16),
            pltpu.VMEM((2, 2, rows, units), BF16),
            pltpu.VMEM((TP, rows, units), BF16),
            pltpu.VMEM((rows, max(2 * beside, D)), F32),
            pltpu.VMEM((rows, D), F32),
            pltpu.VMEM((rows, rows), F32),
            pltpu.VMEM((rows, rows), F32),
            pltpu.VMEM((rows, rows), BF16),
            pltpu.VMEM((heads, HEAD, HEAD), BF16),
            pltpu.VMEM((3, heads, HEAD, HEAD), BF16),
            pltpu.VMEM((heads, HEAD, HEAD), F32),
            pltpu.VMEM((heads, HEAD, HEAD), F32),
            pltpu.VMEM((heads, HEAD, HEAD), F32),
            pltpu.VMEM((heads, HEAD, HEAD), BF16),
            pltpu.VMEM((rows, HEAD), F32),
            pltpu.VMEM((rows, HEAD), F32),
            pltpu.VMEM((TP, 8, HEAD), F32),
            dma((5,)),
            dma((5, TP)),
            dma((5, TP)),
            dma((5, TP)),
            dma((items, 7)),
            dma((items,)),
            dma((items, 2)),
            dma((items, 4)),
            dma((TP - 1,)),
            dma((TP - 1,)),
            dma((3,)),
            dma((3,)),
            dma((2,)),
            dma((KEPT,)),
            dma((2, 2)),
            dma((SEQ,)),
        ],
        compiler_params=pltpu.CompilerParams(
            collective_id=0, has_side_effects=True, vmem_limit_bytes=60 * 2**20
        ),
        name="forward",
    )(*shards, hidden, cosine, sine, rate, bounds)


ROWS_STEP = 64
PIECES = 4
HELD = 6
LAG_2, LAG_3, LAG_4 = 2, 4, 7
KINDS = 6
ITEMS = KINDS * TP


def add_rows(target, *terms):
    rows = target.shape[0]

    @pl.loop(0, rows // ROWS_STEP)
    def _(block):
        part = pl.ds(pl.multiple_of(block * ROWS_STEP, ROWS_STEP), ROWS_STEP)
        total = terms[0][part, :].astype(F32)
        for term in terms[1:]:
            total = total + term[part, :].astype(F32)
        target[part, :] = total.astype(target.dtype)


def backward_kernel(rows, sizes, *refs):
    whole, refs = refs[:5], refs[5:]
    (acts_in, pack_in, normed_in, second_in, left_in, right_in, glu_in, output_in, hidden_in, cot_in,
     incoming, inv_mix, inv_second, rates, cosine, sine, bounds), refs = refs[:17], refs[17:]
    (down_grad, left_grad, right_grad, out_grad, qkvg_grad, output_whole, input_whole,
     left_own, right_own, glu_other, left_other, right_other, gated_other, backs_own, backs_other), refs = refs[:15], refs[15:]
    (tiles, sides, cot, second_normed, normed, attn_cot, halves, acts, pack, backs, mid, wide, distance, scores,
     weights, slopes, faded, state, state_land, mine, partial, partial_land, later, lhs, held), refs = refs[:25], refs[25:]
    lands, refs = refs[:9], refs[9:]
    (tile_sem, side_load, side_keep, side_send, side_recv, glu_send, glu_recv, half_send, half_recv, gated_sem,
     backs_keep, backs_send, backs_recv, load_sem, cot_sem, hidden_sem, lhs_sem, second_send, second_recv,
     first_send, first_recv, line_send, below_recv, above_recv, share_local, share_up, share_down, share_recv,
     state_send, state_recv, partial_sem) = refs
    s, t, other, first, second, diagonal = place()
    core = s % 2
    units = sizes[2]
    half_d = D // 2
    ours, theirs = rows_of(core, half_d), rows_of(1 - core, half_d)
    boundary = bounds[t]
    edge = boundary - s * rows
    before = jnp.where(s * rows - 1 >= boundary, 1, 0)
    last = jnp.where(s * rows + rows - 1 >= boundary, 1, 0)
    around = (first, second, diagonal)
    order = [3, 2, 1, 0]
    local = pltpu.make_async_copy

    done = set()

    def once(key, wait):
        if key not in done:
            done.add(key)
            wait()

    greet(s, t, (other, first, second, diagonal))

    def cot_load(index):
        return local(cot_in.at[t, :, plain(index)], cot.at[:, place_of(index)], cot_sem.at[index])

    def hidden_load(index):
        return local(hidden_in.at[t, :, plain(index)], acts.at[0, :, place_of(index)], hidden_sem.at[index])

    def second_load():
        return local(second_in, second_normed, load_sem.at[0])

    def normed_load():
        return local(normed_in, normed, load_sem.at[1])

    def acts_load():
        return local(acts_in, acts, load_sem.at[2])

    def pack_load():
        return local(pack_in, pack, load_sem.at[3])

    def glu_copy(block):
        return remote(glu_in.at[block], glu_other.at[block], glu_send.at[block], glu_recv.at[block], (other, t))

    def gated_copy():
        return remote(
            pack_in.at[:, :, 2 * PAIR : 3 * PAIR], gated_other, gated_sem.at[0], gated_sem.at[1], (other, t)
        )

    def half_copy(part):
        src = (cot, second_normed, normed, attn_cot)[part]
        return remote(src.at[:, theirs], halves.at[part], half_send.at[part], half_recv.at[part], (other, t))

    tile_list = (
        [(w, step) for step in order for w in (4, 2, 3)]
        + [(1, part) for part in range(2)]
        + [(0, part) for part in range(2 * TP)]
    )

    def tile_load(index):
        w, at = tile_list[index]
        size = units if w >= 2 else half_d
        start = nearest(t, at) * units if w >= 2 else at * half_d
        src = whole[w].at[pl.ds(pl.multiple_of(start, 16), size), :]
        return local(src, tiles.at[index % 3, pl.ds(0, size), :], tile_sem.at[index % 3])

    def tile(index):
        tile_load(index).wait()
        size = units if tile_list[index][0] >= 2 else half_d
        return tiles[index % 3, 0:size, :]

    def tile_next(index):
        if index + 3 < len(tile_list):
            tile_load(index + 3).start()

    def side_loads(number):
        owner = nearest(t, order[number])
        slot = number % 2
        return (
            local(left_in.at[owner], sides.at[slot, 0], side_load.at[slot, 0]),
            local(right_in.at[owner], sides.at[slot, 1], side_load.at[slot, 1]),
        )

    def side_keeps(number):
        owner = nearest(t, order[number])
        slot = number % 2
        return (
            local(sides.at[slot, 0], left_own.at[owner], side_keep.at[slot, 0]),
            local(sides.at[slot, 1], right_own.at[owner], side_keep.at[slot, 1]),
        )

    def side_copies(number):
        owner = nearest(t, order[number])
        slot = number % 2
        return (
            remote(sides.at[slot, 0], left_other.at[owner], side_send.at[slot, 0], side_recv.at[0, number], (other, t)),
            remote(sides.at[slot, 1], right_other.at[owner], side_send.at[slot, 1], side_recv.at[1, number], (other, t)),
        )

    def backs_keep_copy(block):
        return local(backs.at[block], backs_own.at[block], backs_keep.at[block])

    def backs_copy(block):
        return remote(backs.at[block], backs_other.at[block], backs_send.at[block], backs_recv.at[block], (other, t))

    piece_rows = rows // PIECES
    shares = ((output_in, output_whole), (acts.at[1], input_whole))

    def piece(a, owner, p):
        return shares[a][1].at[owner, pl.ds(p * piece_rows, piece_rows), :]

    def own_piece(a, p):
        return shares[a][0].at[pl.ds(p * piece_rows, piece_rows), :]

    def share_copy(a, p, owner, src, up):
        sem, target = (share_up, t + 1) if up else (share_down, t - 1)
        return remote(src, piece(a, owner, p), sem.at[a, p, owner], share_recv.at[a, p, owner], (s, target))

    def share_keep(a, p):
        return local(own_piece(a, p), piece(a, t, p), share_local.at[a, p])

    def share_start(a, p):
        @pl.when(t < TP - 1)
        def _():
            share_copy(a, p, t, own_piece(a, p), True).start()

        @pl.when(t > 0)
        def _():
            share_copy(a, p, t, own_piece(a, p), False).start()

        share_keep(a, p).start()

    relays = [(a, p, step) for a in range(2) for step in range(1, TP) for p in range(PIECES)]
    relayed = []

    def relay(limit=1, until=None):
        for _ in range(limit):
            if len(relayed) >= (len(relays) if until is None else until):
                return
            a, p, step = relays[len(relayed)]
            relayed.append(1)
            owner = nearest(t, step)
            share_copy(a, p, owner, piece(a, owner, p), True).wait_recv()

            @pl.when((owner < t) & (t < TP - 1))
            def _(a=a, p=p, owner=owner):
                share_copy(a, p, owner, piece(a, owner, p), True).start()

            @pl.when((owner > t) & (t > 0))
            def _(a=a, p=p, owner=owner):
                share_copy(a, p, owner, piece(a, owner, p), False).start()

    items = (
        [(0, step) for step in order]
        + [(kind, step) for step in order for kind in (1, 2)]
        + [(3, step) for step in order]
        + [(kind, step) for step in order for kind in (4, 5)]
    )
    heights = (units, units, units, sizes[1], half_d, half_d)

    def lands_of(index):
        kind, step = items[index]
        owner = nearest(t, step)
        group, base, extra = ((0, kind * TP, 3 * TP + kind), (1, 0, TP), (2, (kind - 4) * TP, 2 * TP + kind - 4))[
            0 if kind < 3 else 1 if kind == 3 else 2
        ]
        return owner, lands[3 * group : 3 * group + 3], base + owner, extra

    def own_source(kind, owner):
        if kind == 0:
            return glu_in.at[owner], glu_other.at[owner]
        if kind == 1:
            return left_own.at[owner], left_other.at[owner]
        if kind == 2:
            return right_own.at[owner], right_other.at[owner]
        if kind == 3:
            return pack_in.at[owner, :, 2 * PAIR : 3 * PAIR], gated_other.at[owner]
        part = slice((kind - 4) * half_d, (kind - 3) * half_d)
        return backs_own.at[owner, :, part], backs_other.at[owner, :, part]

    def lhs_loads(index):
        kind, step = items[index]
        slot = index % 2
        return [
            local(src, lhs.at[slot, part, :, pl.ds(0, heights[kind])], lhs_sem.at[slot, part])
            for part, src in enumerate(own_source(kind, nearest(t, step)))
        ]

    def prefetch(index):
        kind, step = items[index]
        owner = nearest(t, step)
        if kind == 0:
            once(("glu", step), lambda: glu_copy(owner).wait_recv())
        elif kind < 3:
            number = order.index(step)
            once(("keep", number, kind - 1), lambda: side_keeps(number)[kind - 1].wait())
            once(("side", number, kind - 1), lambda: side_copies(number)[kind - 1].wait_recv())
        elif kind == 3:
            once("gated", lambda: gated_copy().wait_recv())
        else:
            once(("backs", step), lambda: backs_keep_copy(owner).wait())
            once(("backs_other", step), lambda: backs_copy(owner).wait_recv())
        for copy in lhs_loads(index):
            copy.start()

    def to_second(index):
        kind = items[index][0]
        owner, (second_land, first_land, line_land), at, extra = lands_of(index)
        return [
            remote(
                held.at[index % HELD, column // 2, pl.ds(0, heights[kind]), :],
                second_land.at[at, part],
                second_send.at[index, part],
                second_recv.at[index, part],
                (second, t),
            )
            for part, column in enumerate((diagonal, second))
        ]

    def to_first(index):
        owner, (second_land, first_land, line_land), at, extra = lands_of(index)
        return remote(second_land.at[at, 0], first_land.at[at], first_send.at[index], first_recv.at[index], (first, t))

    def along(index, up):
        kind = items[index][0]
        owner, (second_land, first_land, line_land), at, extra = lands_of(index)
        if up:
            return remote(
                first_land.at[at], line_land.at[at], line_send.at[index], below_recv.at[kind, owner], (s, t + 1)
            )
        final = jnp.where(owner == t - 1, 1, 0)
        return remote(
            first_land.at[at],
            line_land.at[at + final * (extra - at)],
            line_send.at[index],
            above_recv.at[kind, owner],
            (s, t - 1),
        )

    def held_rows(index, chip):
        return held.at[index % HELD, chip, pl.ds(0, heights[items[index][0]]), :]

    def advance(now):
        index = now - LAG_2
        if 0 <= index < ITEMS:
            owner, (second_land, first_land, line_land), at, extra = lands_of(index)
            for copy in to_second(index):
                copy.wait_recv()
            add_rows(second_land.at[at, 0], second_land.at[at, 0], held_rows(index, first // 2))
            to_first(index).start()
        index = now - LAG_3
        if 0 <= index < ITEMS:
            owner, (second_land, first_land, line_land), at, extra = lands_of(index)
            to_first(index).wait_recv()
            add_rows(first_land.at[at], first_land.at[at], held_rows(index, s // 2), second_land.at[at, 1])
        index = now - LAG_4
        if 0 <= index < ITEMS:
            kind, step = items[index]
            owner, (second_land, first_land, line_land), at, extra = lands_of(index)
            if step:

                @pl.when((owner > t) & (t > 0))
                def _():
                    along(index, True).wait_recv()
                    add_rows(first_land.at[at], first_land.at[at], line_land.at[at])

                @pl.when((owner < t) & (t < TP - 1))
                def _():
                    along(index, False).wait_recv()
                    add_rows(first_land.at[at], first_land.at[at], line_land.at[at])

                @pl.when(owner > t)
                def _():
                    along(index, True).start()

                @pl.when(owner < t)
                def _():
                    along(index, False).start()
            else:
                target = (down_grad, left_grad, right_grad, out_grad, qkvg_grad, qkvg_grad)[kind]
                if kind >= 4:
                    target = target.at[(kind - 4) * half_d : (kind - 3) * half_d]

                @pl.when(t == 0)
                def _():
                    along(index, False).wait_recv()
                    add_rows(target, first_land.at[at], line_land.at[extra])

                @pl.when(t == TP - 1)
                def _():
                    along(index, True).wait_recv()
                    add_rows(target, first_land.at[at], line_land.at[at])

                @pl.when((t > 0) & (t < TP - 1))
                def _():
                    along(index, True).wait_recv()
                    along(index, False).wait_recv()
                    add_rows(target, first_land.at[at], line_land.at[at], line_land.at[extra])

    def produce(index):
        kind, step = items[index]
        height = heights[kind]
        right, part = ((cot, 0), (second_normed, 1), (second_normed, 1), (attn_cot, 3), (normed, 2), (normed, 2))[kind]
        once(("half", part), lambda: half_copy(part).wait_recv())
        for copy in lhs_loads(index):
            copy.wait()
        if index >= HELD:
            for copy in to_second(index - HELD):
                copy.wait_send()
        slot = index % 2
        product = dots(lhs[slot, 0, :, 0:height], right[:, ours], TN) + dots(lhs[slot, 1, :, 0:height], halves[part], TN)
        for chip in range(4):
            held[index % HELD, chip, 0:height, :] = product[:, chip * STRIPE : chip * STRIPE + STRIPE].astype(BF16)
        for copy in to_second(index):
            copy.start()
        advance(index)

    for index in range(SEQ):
        cot_load(index).start()
    for index in range(3):
        tile_load(index).start()
    for copy in side_loads(0):
        copy.start()
    for p in range(PIECES):
        share_start(0, p)
    second_load().start()
    for step in order:
        glu_copy(nearest(t, step)).start()
    for copy in side_loads(1):
        copy.start()
    normed_load().start()
    acts_load().start()
    pack_load().start()
    gated_copy().start()
    for index in range(SEQ):
        cot_load(index).wait()
    half_copy(0).start()

    def feed_forward(number):
        index = 3 * number
        slot = number % 2
        wide[:, 0:units] = dots(cot[...], tile(index), NT)
        tile_next(index)
        for copy in side_loads(number):
            copy.wait()

        def multiply(part, start):
            product = wide[part, 0:units]
            left, right = sides[slot, 0, part, :].astype(F32), sides[slot, 1, part, :].astype(F32)
            sides[slot, 0, part, :] = (product * right).astype(BF16)
            sides[slot, 1, part, :] = (product * left).astype(BF16)

        every_rows(rows, multiply)
        for copy in side_keeps(number) + side_copies(number):
            copy.start()
        term = dots(sides[slot, 0], tile(index + 1), NN)
        if number:
            mid[...] += term
        else:
            mid[...] = term
        tile_next(index + 1)
        mid[...] += dots(sides[slot, 1], tile(index + 2), NN)
        tile_next(index + 2)

    def side_refill(number):
        for part in range(2):
            once(("keep", number, part), lambda: side_keeps(number)[part].wait())
            side_copies(number)[part].wait_send()
        for copy in side_loads(number + 2):
            copy.start()

    feed_forward(0)
    prefetch(0)
    second_load().wait()
    half_copy(1).start()
    side_refill(0)
    feed_forward(1)
    produce(0)
    prefetch(1)
    relay()
    side_refill(1)
    feed_forward(2)
    produce(1)
    prefetch(2)
    relay()
    feed_forward(3)
    produce(2)
    prefetch(3)
    relay()
    normed_load().wait()
    half_copy(2).start()

    def middle(part, start):
        unit = second_normed[part, :].astype(F32)
        values = mid[part, :]
        inner = jnp.mean(values * unit, axis=-1, keepdims=True)
        values = cot[part, :].astype(F32) + inv_second[part, 0:1] * (values - unit * inner)
        mid[part, :] = values
        attn_cot[part, :] = values.astype(BF16)

    every_rows(rows, middle)
    half_copy(3).start()
    at_tile = 3 * TP
    for part in range(2):
        wide[:, part * half_d : part * half_d + half_d] = dots(attn_cot[...], tile(at_tile + part), NT)
        tile_next(at_tile + part)
    at_tile += 2
    produce(3)
    prefetch(4)
    relay()
    acts_load().wait()
    pack_load().wait()

    def head_rows(part, start):
        total = jnp.zeros((BLOCK, 1), F32)
        for block in range(TP):
            values = wide[part, block * PAIR : block * PAIR + PAIR]
            gate = acts[block, part, 3 * PAIR : 4 * PAIR].astype(F32)
            unit = pack[block, part, 3 * PAIR : 4 * PAIR].astype(F32)
            total += jnp.sum(values * gate * unit, axis=-1, keepdims=True)
        total = total * (1.0 / D)
        scale = inv_mix[part, 0:1]
        for block in range(TP):
            values = wide[part, block * PAIR : block * PAIR + PAIR]
            gate = acts[block, part, 3 * PAIR : 4 * PAIR].astype(F32)
            unit = pack[block, part, 3 * PAIR : 4 * PAIR].astype(F32)
            backs[block, part, 3 * PAIR : 4 * PAIR] = (values * unit).astype(BF16)
            backs[block, part, 2 * PAIR : 3 * PAIR] = (scale * (values * gate - unit * total)).astype(BF16)
        row = lax.broadcasted_iota(jnp.int32, (BLOCK, rows), 0) + start
        column = lax.broadcasted_iota(jnp.int32, (BLOCK, rows), 1)
        apart = (column > row) | ((row >= edge) & (column < edge))
        distance[part, :] = jnp.where(apart, -1, row - column).astype(F32)

    every_rows(rows, head_rows)
    produce(4)
    prefetch(5)
    relay()

    def rate_of(block, half):
        return rates[block, half : half + 1, :]

    def row_numbers(start):
        return lax.broadcasted_iota(jnp.int32, (BLOCK, HEAD), 0) + start

    for block in range(TP):
        for half in range(2):
            at = half * HEAD

            def fade_rows(part, start, block=block, half=half, at=at):
                number = row_numbers(start)
                valid = jnp.where(jnp.where(number >= edge, 1, 0) == before, 1.0, 0.0)
                fade = jnp.exp(-rate_of(block, half) * (number + 1).astype(F32)) * valid
                values = backs[block, part, 2 * PAIR + at : 2 * PAIR + at + HEAD].astype(F32)
                faded[part, :] = (values * fade).astype(BF16)

            every_rows(rows, fade_rows)
            head = 2 * block + half
            state[head] = dots(acts[block, :, at : at + HEAD], faded[...], TN).astype(BF16)
            wide[:, head * HEAD : head * HEAD + HEAD] = dots(faded[...], incoming[head], NT)

    def state_copy(part):
        return remote(state, state_land.at[part], state_send.at[part], state_recv.at[part], (around[part], t))

    for part in range(3):
        state_copy(part).start()
    produce(5)
    prefetch(6)
    relay()
    weights[0:PAIR, PAIR:rows] = jnp.zeros((PAIR, rows - PAIR), BF16)
    slopes[0:PAIR, PAIR:rows] = jnp.zeros((PAIR, rows - PAIR), BF16)

    def attend(block):
        for half in range(2):
            at = half * HEAD
            head = 2 * block + half
            rate = rate_of(block, half)
            query, key, value = [slice(kind * PAIR + at, kind * PAIR + at + HEAD) for kind in range(3)]
            mine_columns = slice(head * HEAD, head * HEAD + HEAD)
            for top in range(0, rows, PAIR):
                width = top + PAIR
                scores[0:PAIR, 0:width] = dots(acts[block, top:width, query], acts[block, 0:width, key], NT)
                scores[PAIR : 2 * PAIR, 0:width] = dots(backs[block, top:width, value], acts[block, 0:width, value], NT)

                def weigh(part, start, width=width, top=top):
                    below = pl.ds(pl.multiple_of(start + PAIR, BLOCK), BLOCK)
                    there = pl.ds(pl.multiple_of(start + top, BLOCK), BLOCK)
                    for left in range(0, width, HEAD):
                        apart = distance[there, left : left + HEAD]
                        fade = jnp.where(apart >= 0.0, jnp.exp(-rate * apart), 0.0)
                        weights[there, left : left + HEAD] = (scores[part, left : left + HEAD] * fade).astype(BF16)
                        grad = scores[below, left : left + HEAD].astype(BF16).astype(F32)
                        slopes[there, left : left + HEAD] = (grad * fade).astype(BF16)

                every_rows(PAIR, weigh)
                wide[top:width, mine_columns] += dots(slopes[top:width, 0:width], acts[block, 0:width, key], NN)
            inner = dots(weights[...], backs[block, :, value], TN)
            acts[block, :, 3 * PAIR + at : 3 * PAIR + at + HEAD] = inner.astype(BF16)
            inner = dots(slopes[...], acts[block, :, query], TN)
            backs[block, :, key] = inner.astype(BF16)

            def turn_back(part, start):
                turned = rotated(wide[part, mine_columns], cosine[part, :], -sine[part, :])
                backs[block, part, query] = (turned * pack[block, part, query].astype(F32)).astype(BF16)

            every_rows(rows, turn_back)

    for block in range(TP):
        attend(block)
        produce(6 + block)
        prefetch(7 + block)
        relay()

    def suffix_scale(block, source_block, rate):
        same = jnp.where(source_block * rows - 1 >= boundary, 1, 0) == jnp.where(block * rows + rows - 1 >= boundary, 1, 0)
        usable = flag(source_block > block) * flag(same)
        gap = jnp.maximum(source_block - 1 - block, 0).astype(F32)
        return jnp.exp(-rate * (rows * gap)) * usable

    def partial_copy():
        return remote(partial, partial_land, partial_sem.at[0], partial_sem.at[1], (other, t))

    for part in range(3):
        state_copy(part).wait_recv()

    @pl.loop(0, 2 * TP)
    def _(head):
        rate = rates[head // 2, pl.ds(head % 2, 1), :]
        here = jnp.zeros((HEAD, HEAD), F32)
        there = suffix_scale(other, s, rate) * state[head].astype(F32)
        for part in range(3):
            values = state_land[part, head].astype(F32)
            here += suffix_scale(s, around[part], rate) * values
            there += suffix_scale(other, around[part], rate) * values
        mine[head] = here
        partial[head] = there

    partial_copy().start()
    produce(10)
    prefetch(11)
    relay()
    partial_copy().wait_recv()

    @pl.loop(0, 2 * TP)
    def _(head):
        later[head] = (mine[head] + partial_land[head]).astype(BF16)

    for block in range(TP):
        for half in range(2):
            at = half * HEAD
            head = 2 * block + half
            query, key, value = [slice(kind * PAIR + at, kind * PAIR + at + HEAD) for kind in range(3)]
            scores[:, 0:HEAD] = dots(acts[block, :, value], later[head], NT)
            scores[:, HEAD : 2 * HEAD] = dots(acts[block, :, key], later[head], NN)

            def finish_rows(part, start, block=block, half=half, at=at, key=key, value=value):
                number = row_numbers(start)
                valid = jnp.where(jnp.where(number >= edge, 1, 0) == last, 1.0, 0.0)
                fade = jnp.exp(-rate_of(block, half) * (rows - 1 - number).astype(F32)) * valid
                keys = backs[block, part, key].astype(F32) + fade * scores[part, 0:HEAD]
                turned = rotated(keys, cosine[part, :], -sine[part, :])
                backs[block, part, key] = (turned * pack[block, part, key].astype(F32)).astype(BF16)
                values = acts[block, part, 3 * PAIR + at : 3 * PAIR + at + HEAD].astype(F32)
                backs[block, part, value] = (values + fade * scores[part, HEAD : 2 * HEAD]).astype(BF16)

            every_rows(rows, finish_rows)
        backs_keep_copy(block).start()
        backs_copy(block).start()
        for part in range(2):
            index = at_tile + 2 * block + part
            term = dots(backs[block, :, part * half_d : part * half_d + half_d], tile(index), NN)
            if block or part:
                wide[...] += term
            else:
                wide[...] = term
            tile_next(index)
        if block == 0:
            for index in range(SEQ):
                hidden_load(index).start()
        if block == 1:
            produce(11)
            prefetch(12)
    relay(12, 12)
    for index in range(SEQ):
        hidden_load(index).wait()

    def input_rows(part, start):
        values = acts[0, part, :].astype(F32)
        scale = lax.rsqrt(jnp.mean(values * values, axis=-1, keepdims=True) + EPSILON)
        unit = values * scale
        grad = wide[part, :]
        inner = jnp.mean(grad * unit, axis=-1, keepdims=True)
        grad = mid[part, :] + scale * (grad - unit * inner)
        for index in range(SEQ):
            acts[1, part, plain(index)] = grad[:, place_of(index)].astype(BF16)

    for p in range(PIECES):

        @pl.loop(0, piece_rows // BLOCK)
        def _(block, p=p):
            start = p * piece_rows + block * BLOCK
            input_rows(pl.ds(pl.multiple_of(start, BLOCK), BLOCK), start)

        share_start(1, p)
    for index in range(12, ITEMS):
        produce(index)
        if index + 1 < ITEMS:
            prefetch(index + 1)
        if index >= 14:
            relay()
    for now in range(ITEMS, ITEMS + LAG_4):
        advance(now)
        relay()
    relay(len(relays))

    for step in order:
        glu_copy(nearest(t, step)).wait_send()
    for part in range(4):
        half_copy(part).wait_send()
    gated_copy().wait_send()
    for number in (2, 3):
        for copy in side_copies(number):
            copy.wait_send()
    for block in range(TP):
        backs_copy(block).wait_send()
    for part in range(3):
        state_copy(part).wait_send()
    partial_copy().wait_send()
    for index, (kind, step) in enumerate(items):
        if index >= ITEMS - HELD:
            for copy in to_second(index):
                copy.wait_send()
        to_first(index).wait_send()
        if step:
            along(index, True).wait_send()
    for a in range(2):
        for p in range(PIECES):
            share_keep(a, p).wait()

            @pl.when(t < TP - 1)
            def _(a=a, p=p):
                share_copy(a, p, t, own_piece(a, p), True).wait_send()

            @pl.when(t > 0)
            def _(a=a, p=p):
                share_copy(a, p, t, own_piece(a, p), False).wait_send()
    for a, p, step in relays:
        owner = nearest(t, step)

        @pl.when((owner < t) & (t < TP - 1))
        def _(a=a, p=p, owner=owner):
            share_copy(a, p, owner, piece(a, owner, p), True).wait_send()

        @pl.when((owner > t) & (t > 0))
        def _(a=a, p=p, owner=owner):
            share_copy(a, p, owner, piece(a, owner, p), False).wait_send()


def backward(whole, kept, output, hidden_in, out_cotangent, incoming, inv_mix, inv_second, rates, cosine, sine, bounds):
    rows = output.shape[0]
    sizes = tuple(weight.shape[0] // TP for weight in whole)
    units = sizes[2]
    dma = pltpu.SemaphoreType.DMA
    vmem = pl.BlockSpec(memory_space=pltpu.VMEM)
    anywhere = pl.BlockSpec(memory_space=pl.ANY)
    heads = 2 * TP
    half_d = D // 2
    shape = jax.ShapeDtypeStruct
    tall = lambda height: shape((height, STRIPE), F32)
    scratch = [
        pltpu.VMEM((3, units, D), BF16),
        pltpu.VMEM((2, 2, rows, units), BF16),
        *[pltpu.VMEM((rows, D), BF16)] * 4,
        pltpu.VMEM((4, rows, half_d), BF16),
        *[pltpu.VMEM((TP, rows, 4 * PAIR), BF16)] * 3,
        pltpu.VMEM((rows, D), F32),
        pltpu.VMEM((rows, D), F32),
        pltpu.VMEM((rows, rows), F32),
        pltpu.VMEM((rows, rows), F32),
        pltpu.VMEM((rows, rows), BF16),
        pltpu.VMEM((rows, rows), BF16),
        pltpu.VMEM((rows, HEAD), BF16),
        pltpu.VMEM((heads, HEAD, HEAD), BF16),
        pltpu.VMEM((3, heads, HEAD, HEAD), BF16),
        *[pltpu.VMEM((heads, HEAD, HEAD), F32)] * 3,
        pltpu.VMEM((heads, HEAD, HEAD), BF16),
        pltpu.VMEM((2, 2, rows, units), BF16),
        pltpu.VMEM((HELD, 4, units, STRIPE), BF16),
    ]
    for count, height, extra in ((3 * TP, units, 3), (TP, sizes[1], 1), (2 * TP, half_d, 2)):
        scratch += [
            pltpu.VMEM((count, 2, height, STRIPE), BF16),
            pltpu.VMEM((count, height, STRIPE), BF16),
            pltpu.VMEM((count + extra, height, STRIPE), BF16),
        ]
    scratch += [
        dma((3,)),
        dma((2, 2)),
        dma((2, 2)),
        dma((2, 2)),
        dma((2, TP)),
        dma((TP,)),
        dma((TP,)),
        dma((4,)),
        dma((4,)),
        dma((2,)),
        dma((TP,)),
        dma((TP,)),
        dma((TP,)),
        dma((4,)),
        dma((SEQ,)),
        dma((SEQ,)),
        dma((2, 2)),
        dma((ITEMS, 2)),
        dma((ITEMS, 2)),
        dma((ITEMS,)),
        dma((ITEMS,)),
        dma((ITEMS,)),
        dma((KINDS, TP)),
        dma((KINDS, TP)),
        dma((2, PIECES)),
        dma((2, PIECES, TP)),
        dma((2, PIECES, TP)),
        dma((2, PIECES, TP)),
        dma((3,)),
        dma((3,)),
        dma((2,)),
    ]
    return pl.pallas_call(
        functools.partial(backward_kernel, rows, sizes),
        out_shape=[tall(units), tall(units), tall(units), tall(sizes[1]), tall(sizes[0])]
        + [shape((TP, rows, D), BF16)] * 2
        + [shape((TP, rows, units), BF16)] * 5
        + [shape((TP, rows, PAIR), BF16)]
        + [shape((TP, rows, 4 * PAIR), BF16)] * 2,
        in_specs=[anywhere] * 15 + [vmem] * 6 + [pl.BlockSpec(memory_space=pltpu.SMEM)],
        out_specs=[vmem] * 5 + [anywhere] * 10,
        scratch_shapes=scratch,
        compiler_params=pltpu.CompilerParams(
            collective_id=1, has_side_effects=True, vmem_limit_bytes=63 * 2**20
        ),
        name="backward",
    )(*whole, *kept, output, hidden_in, out_cotangent, incoming, inv_mix, inv_second, rates, cosine, sine, bounds)


def entering(value, axis, join, neutral, backward):
    count, mine = (lax.axis_size(axis), lax.axis_index(axis))
    pieces = jax.tree.map(lambda part: lax.all_gather(part, axis), value)
    if backward:
        pieces = jax.tree.map(lambda part: part[::-1], pieces)
        mine = count - 1 - mine
    subtotal = jax.tree.map(
        lambda part, zero: jnp.full_like(part, 0) + jnp.asarray(zero, part.dtype), value, neutral
    )

    def step(position, subtotal):
        longer = join(subtotal, jax.tree.map(lambda part: part[position], pieces))
        return jax.tree.map(lambda new, old: jnp.where(position < mine, new, old), longer, subtotal)

    return lax.fori_loop(0, count - 1, step, subtotal)


def swish_parts(pre_act):
    logistic = jax.nn.sigmoid(pre_act)
    return (pre_act * logistic, logistic * (1.0 + pre_act * (1.0 - logistic)))


def rotate(rows_in, cosine_table, sine_table, signed):
    halfway = rows_in.shape[-1] // 2
    front_half = rows_in[..., :halfway]
    back_half = rows_in[..., halfway:]
    return jnp.concatenate(
        [
            front_half * cosine_table - signed * back_half * sine_table,
            signed * front_half * sine_table + back_half * cosine_table,
        ],
        axis=-1,
    )


def combine_forward(earlier, following):
    return (earlier[0] * following[0], following[0][:, None, None] * earlier[1] + following[1])


def combine_backward(farther, nearer):
    return (farther[0] * nearer[0], nearer[1] + nearer[0][:, None, None] * farther[1])


def collect_weights(
    query_weight,
    key_weight,
    value_weight,
    gate_weight,
    out_weight,
    left_weight,
    right_weight,
    down_weight,
):
    return (
        lax.all_gather(query_weight, "seq", axis=0, tiled=True),
        lax.all_gather(key_weight, "seq", axis=0, tiled=True),
        lax.all_gather(value_weight, "seq", axis=0, tiled=True),
        lax.all_gather(gate_weight, "seq", axis=0, tiled=True),
        lax.all_gather(out_weight, "seq", axis=1, tiled=True),
        lax.all_gather(left_weight, "seq", axis=0, tiled=True),
        lax.all_gather(right_weight, "seq", axis=0, tiled=True),
        lax.all_gather(down_weight, "seq", axis=1, tiled=True),
    )


def state_prefix(factor, local_state):
    neutral = (jnp.ones_like(factor), jnp.zeros_like(local_state))
    return entering((factor, local_state), "seq", combine_forward, neutral, False)[1]


def state_suffix(factor, state_grad):
    neutral = (jnp.ones_like(factor), jnp.zeros_like(state_grad))
    return entering((factor, state_grad), "seq", combine_backward, neutral, True)[1]


def body(
    hidden_in,
    query_weight,
    key_weight,
    value_weight,
    gate_weight,
    out_weight,
    left_weight,
    right_weight,
    down_weight,
    decay_rate,
    seq_bounds,
    out_cotangent,
):
    row_count = hidden_in.shape[1]
    batch_count = hidden_in.shape[0]
    local_heads = decay_rate.shape[0]
    heads_shape = (row_count, local_heads, HEAD)
    device = lax.axis_index("seq")
    offsets = jnp.arange(row_count, dtype=jnp.int32)
    positions = device * row_count + offsets
    frequency = jnp.exp(
        jnp.arange(HEAD // 2, dtype=jnp.float32) * (-2.0 * math.log(10000.0) / HEAD)
    )
    angles = positions.astype(jnp.float32)[:, None] * frequency[None, :]
    cosine_table = jnp.cos(angles)[:, None, :]
    sine_table = jnp.sin(angles)[:, None, :]
    local_f = offsets.astype(jnp.float32)
    distance = local_f[:, None] - local_f[None, :]
    causal = distance >= 0.0
    distance_pos = jnp.maximum(distance, 0.0)
    accum = None
    outputs = []
    in_grads = []
    for batch_index in range(batch_count):
        gathered = collect_weights(
            query_weight,
            key_weight,
            value_weight,
            gate_weight,
            out_weight,
            left_weight,
            right_weight,
            down_weight,
        )
        query_full, key_full, value_full, gate_full, out_full, left_full, right_full, down_full = (
            gathered
        )
        boundary = seq_bounds[batch_index]
        segment = (positions >= boundary).astype(jnp.int32)
        before = (device * row_count - 1 >= boundary).astype(jnp.int32)
        last_segment = segment[row_count - 1]
        allowed = causal & (segment[:, None] == segment[None, :])
        decay = jnp.where(
            allowed[None], jnp.exp(-decay_rate[:, None, None] * distance_pos[None]), 0.0
        )
        coef_in = (
            jnp.exp(-decay_rate[None, :] * (local_f[:, None] + 1.0))
            * (segment == before).astype(jnp.float32)[:, None]
        )
        weight_loc = (
            jnp.exp(-decay_rate[None, :] * (row_count - 1.0 - local_f)[:, None])
            * (segment == last_segment).astype(jnp.float32)[:, None]
        )
        factor = jnp.where(last_segment == before, jnp.exp(-decay_rate * row_count), 0.0)
        input_rows = hidden_in[batch_index].astype(jnp.float32)
        inv_first = lax.rsqrt(jnp.mean(input_rows * input_rows, axis=-1, keepdims=True) + EPSILON)
        unit_first = input_rows * inv_first
        normed_first = unit_first.astype(jnp.bfloat16)
        query_pre = jnp.dot(normed_first, query_full, preferred_element_type=jnp.float32)
        key_pre = jnp.dot(normed_first, key_full, preferred_element_type=jnp.float32)
        value_pre = jnp.dot(normed_first, value_full, preferred_element_type=jnp.float32)
        gate_pre = jnp.dot(normed_first, gate_full, preferred_element_type=jnp.float32)
        query_act, query_slope = swish_parts(query_pre)
        key_act, key_slope = swish_parts(key_pre)
        query_rot = rotate(query_act.reshape(heads_shape), cosine_table, sine_table, 1.0).astype(
            jnp.bfloat16
        )
        key_rot = rotate(key_act.reshape(heads_shape), cosine_table, sine_table, 1.0).astype(
            jnp.bfloat16
        )
        value_rows = value_pre.astype(jnp.bfloat16).reshape(heads_shape)
        query_wide = query_rot.astype(jnp.float32)
        key_wide = key_rot.astype(jnp.float32)
        value_wide = value_rows.astype(jnp.float32)
        scores = jnp.einsum("ihe,jhe->hij", query_rot, key_rot, preferred_element_type=jnp.float32)
        attn_weights = (scores * decay).astype(jnp.bfloat16)
        inner_out = jnp.einsum(
            "hij,jhe->ihe", attn_weights, value_rows, preferred_element_type=jnp.float32
        )
        local_state = jnp.einsum(
            "jhe,jhf->hef",
            key_wide * weight_loc[:, :, None],
            value_wide,
            precision=HIGHEST_PRECISION,
        )
        incoming = state_prefix(factor, local_state)
        outer_out = coef_in[:, :, None] * jnp.einsum(
            "ihe,hef->ihf", query_wide, incoming, precision=HIGHEST_PRECISION
        )
        mixed_heads = (inner_out + outer_out).reshape(row_count, local_heads * HEAD)
        total_sq = lax.psum(jnp.sum(mixed_heads * mixed_heads, axis=-1), "tp")
        inv_mix = lax.rsqrt(total_sq / D + EPSILON)[:, None]
        unit_mix = mixed_heads * inv_mix
        gate_mix = (unit_mix * gate_pre).astype(jnp.bfloat16)
        attn_sum = lax.psum(jnp.dot(gate_mix, out_full, preferred_element_type=jnp.float32), "tp")
        resid_mid = input_rows + attn_sum
        inv_second = lax.rsqrt(jnp.mean(resid_mid * resid_mid, axis=-1, keepdims=True) + EPSILON)
        unit_second = resid_mid * inv_second
        normed_second = unit_second.astype(jnp.bfloat16)
        left_pre = jnp.dot(normed_second, left_full, preferred_element_type=jnp.float32)
        right_pre = jnp.dot(normed_second, right_full, preferred_element_type=jnp.float32)
        glu_product = (left_pre * right_pre).astype(jnp.bfloat16)
        glu_out = lax.psum(
            jnp.dot(glu_product, down_full, preferred_element_type=jnp.float32), "tp"
        )
        outputs.append((resid_mid + glu_out).astype(jnp.bfloat16))
        glu_cot = out_cotangent[batch_index]
        product_grad = jnp.einsum(
            "cd,fd->cf", glu_cot, down_full, preferred_element_type=jnp.float32
        )
        left_back = (product_grad * right_pre).astype(jnp.bfloat16)
        right_back = (product_grad * left_pre).astype(jnp.bfloat16)
        second_part = jnp.einsum(
            "cf,df->cd", left_back, left_full, preferred_element_type=jnp.float32
        ) + jnp.einsum("cf,df->cd", right_back, right_full, preferred_element_type=jnp.float32)
        second_back = lax.psum(second_part, "tp")
        mid_grad = glu_cot.astype(jnp.float32) + inv_second * (
            second_back - unit_second * jnp.mean(second_back * unit_second, axis=-1, keepdims=True)
        )
        attn_cot = mid_grad.astype(jnp.bfloat16)
        gate_mix_grad = jnp.einsum(
            "cd,kd->ck", attn_cot, out_full, preferred_element_type=jnp.float32
        )
        gate_back = (gate_mix_grad * unit_mix).astype(jnp.bfloat16)
        unit_mix_grad = gate_mix_grad * gate_pre
        mix_dot = lax.psum(jnp.sum(unit_mix_grad * unit_mix, axis=-1), "tp")
        heads_grad = (
            (inv_mix * (unit_mix_grad - unit_mix * (mix_dot / D)[:, None]))
            .astype(jnp.bfloat16)
            .reshape(heads_shape)
        )
        pair_grad = jnp.einsum(
            "ihe,jhe->hij", heads_grad, value_rows, preferred_element_type=jnp.float32
        ).astype(jnp.bfloat16)
        score_grad = pair_grad.astype(jnp.float32) * decay
        query_inner = jnp.einsum("hij,jhe->ihe", score_grad, key_wide, precision=HIGHEST_PRECISION)
        key_inner = jnp.einsum("hij,ihe->jhe", score_grad, query_wide, precision=HIGHEST_PRECISION)
        value_inner = jnp.einsum(
            "hij,ihe->jhe", attn_weights, heads_grad, preferred_element_type=jnp.float32
        )
        scaled_grad = heads_grad.astype(jnp.float32) * coef_in[:, :, None]
        query_outer = jnp.einsum("ihf,hef->ihe", scaled_grad, incoming, precision=HIGHEST_PRECISION)
        state_grad = jnp.einsum(
            "ihe,ihf->hef", query_wide, scaled_grad, precision=HIGHEST_PRECISION
        )
        later_grad = state_suffix(factor, state_grad)
        key_state = weight_loc[:, :, None] * jnp.einsum(
            "jhf,hef->jhe", value_wide, later_grad, precision=HIGHEST_PRECISION
        )
        value_state = weight_loc[:, :, None] * jnp.einsum(
            "jhe,hef->jhf", key_wide, later_grad, precision=HIGHEST_PRECISION
        )
        query_back = (
            rotate(query_inner + query_outer, cosine_table, sine_table, -1.0).reshape(row_count, -1)
            * query_slope
        ).astype(jnp.bfloat16)
        key_back = (
            rotate(key_inner + key_state, cosine_table, sine_table, -1.0).reshape(row_count, -1)
            * key_slope
        ).astype(jnp.bfloat16)
        value_back = (value_inner + value_state).reshape(row_count, -1).astype(jnp.bfloat16)
        fresh = (
            jnp.einsum("cd,ck->dk", normed_first, query_back, preferred_element_type=jnp.float32),
            jnp.einsum("cd,ck->dk", normed_first, key_back, preferred_element_type=jnp.float32),
            jnp.einsum("cd,ck->dk", normed_first, value_back, preferred_element_type=jnp.float32),
            jnp.einsum("cd,ck->dk", normed_first, gate_back, preferred_element_type=jnp.float32),
            jnp.einsum("ck,cd->kd", gate_mix, attn_cot, preferred_element_type=jnp.float32),
            jnp.einsum("cd,cf->df", normed_second, left_back, preferred_element_type=jnp.float32),
            jnp.einsum("cd,cf->df", normed_second, right_back, preferred_element_type=jnp.float32),
            jnp.einsum("cf,cd->fd", glu_product, glu_cot, preferred_element_type=jnp.float32),
        )
        if accum is None:
            accum = list(fresh)
        else:
            accum = [older + newer for older, newer in zip(accum, fresh)]
        total = jnp.einsum("ck,dk->cd", query_back, query_full, preferred_element_type=jnp.float32)
        total = total + jnp.einsum(
            "ck,dk->cd", key_back, key_full, preferred_element_type=jnp.float32
        )
        total = total + jnp.einsum(
            "ck,dk->cd", value_back, value_full, preferred_element_type=jnp.float32
        )
        first_back = lax.psum(
            total
            + jnp.einsum("ck,dk->cd", gate_back, gate_full, preferred_element_type=jnp.float32),
            "tp",
        )
        input_back = mid_grad + inv_first * (
            first_back - unit_first * jnp.mean(first_back * unit_first, axis=-1, keepdims=True)
        )
        in_grads.append(input_back)
    summed = (
        lax.psum_scatter(accum[0], "seq", scatter_dimension=0, tiled=True),
        lax.psum_scatter(accum[1], "seq", scatter_dimension=0, tiled=True),
        lax.psum_scatter(accum[2], "seq", scatter_dimension=0, tiled=True),
        lax.psum_scatter(accum[3], "seq", scatter_dimension=0, tiled=True),
        lax.psum_scatter(accum[4], "seq", scatter_dimension=1, tiled=True),
        lax.psum_scatter(accum[5], "seq", scatter_dimension=0, tiled=True),
        lax.psum_scatter(accum[6], "seq", scatter_dimension=0, tiled=True),
        lax.psum_scatter(accum[7], "seq", scatter_dimension=1, tiled=True),
    )
    return (
        jnp.stack(outputs),
        jnp.stack(in_grads),
        summed[0],
        summed[1],
        summed[2],
        summed[3],
        summed[4],
        summed[5],
        summed[6],
        summed[7],
    )


def fused_body(
    hidden_in,
    query_weight,
    key_weight,
    value_weight,
    gate_weight,
    out_weight,
    left_weight,
    right_weight,
    down_weight,
    decay_rate,
    seq_bounds,
    out_cotangent,
):
    row_count = hidden_in.shape[1]
    device = lax.axis_index("seq")
    positions = device * row_count + jnp.arange(row_count, dtype=jnp.int32)
    frequency = jnp.exp(jnp.arange(HEAD // 2, dtype=F32) * (-2.0 * math.log(10000.0) / HEAD))
    angles = positions.astype(F32)[:, None] * frequency[None, :]
    cosine, sine = jnp.cos(angles), jnp.sin(angles)
    cosine = jnp.concatenate([cosine, cosine], axis=1)
    sine = jnp.concatenate([-sine, sine], axis=1)
    rate = jnp.broadcast_to(jnp.pad(decay_rate, (0, 8 - decay_rate.shape[0]))[:, None], (8, HEAD))
    shards = [
        jnp.concatenate([query_weight.T, key_weight.T, value_weight.T, gate_weight.T], axis=0),
        out_weight,
        left_weight.T,
        right_weight.T,
        down_weight,
    ]
    results = forward(shards, hidden_in, cosine, sine, rate, seq_bounds)
    whole, (incoming, inv_mix, inv_second, rates, output) = results[:5], results[12:]
    down_grad, left_grad, right_grad, out_grad, qkvg_grad, output, input_grad = backward(
        whole,
        results[5:12],
        output,
        hidden_in,
        out_cotangent,
        incoming,
        inv_mix,
        inv_second,
        rates,
        cosine,
        sine,
        seq_bounds,
    )[:7]
    query_grad, key_grad, value_grad, gate_grad = [
        qkvg_grad[index * PAIR : index * PAIR + PAIR].T for index in range(4)
    ]
    return (
        output,
        input_grad.astype(F32),
        query_grad,
        key_grad,
        value_grad,
        gate_grad,
        out_grad,
        left_grad.T,
        right_grad.T,
        down_grad,
    )


def solution(mesh):
    fits = mesh.shape["seq"] == SEQ and mesh.shape["tp"] == TP
    return jax.shard_map(
        fused_body if fits else body,
        mesh=mesh,
        in_specs=(
            P(None, "seq", None),
            P("seq", "tp"),
            P("seq", "tp"),
            P("seq", "tp"),
            P("seq", "tp"),
            P("tp", "seq"),
            P("seq", "tp"),
            P("seq", "tp"),
            P("tp", "seq"),
            P("tp"),
            P(),
            P(None, "seq", None),
        ),
        out_specs=(
            P(None, "seq", None),
            P(None, "seq", None),
            P("seq", "tp"),
            P("seq", "tp"),
            P("seq", "tp"),
            P("seq", "tp"),
            P("tp", "seq"),
            P("seq", "tp"),
            P("seq", "tp"),
            P("tp", "seq"),
        ),
        check_vma=False,
    )
```

```python
import functools
import math

import jax
import jax.numpy as jnp
from jax import lax
from jax.experimental import pallas as pl
from jax.experimental.pallas import tpu as pltpu
from jax.sharding import PartitionSpec as P

D = 1024
HEAD = 128


EPSILON = 1e-06
HIGHEST_PRECISION = lax.Precision.HIGHEST
MESH = pl.DeviceIdType.MESH
BF16 = jnp.bfloat16
F32 = jnp.float32

SEQ = 8
TP = 4
STRIPE = 128
PAIR = 2 * HEAD
BLOCK = 32

NN = ((1,), (0,))
NT = ((1,), (1,))
TN = ((0,), (0,))


def dots(left, right, dims):
    return lax.dot_general(left, right, (dims, ((), ())), preferred_element_type=F32)


def place():
    s, t = lax.axis_index("seq"), lax.axis_index("tp")
    core = s % 2
    column = (s // 2) % 2
    line = s // 4
    other = s + 1 - 2 * core
    across_x = s + 2 * (1 - 2 * column)
    across_y = s + 4 * (1 - 2 * line)
    first = across_x + core * (across_y - across_x)
    second = across_y + core * (across_x - across_y)
    diagonal = across_x + across_y - s
    return s, t, other, first, second, diagonal


def nearest(t, step):
    flip = t // 2
    low = t + flip * (3 - 2 * t)
    swap = low * (1 - step // 2)
    index = step + swap * (1 - 2 * step)
    return index + flip * (3 - 2 * index)


def stripe(index):
    return pl.ds(pl.multiple_of((index % 2 * (SEQ // 2) + index // 2) * STRIPE, STRIPE), STRIPE)


def plain(index):
    return slice(index * STRIPE, index * STRIPE + STRIPE)


def place_of(index):
    at = (index % 2 * (SEQ // 2) + index // 2) * STRIPE
    return slice(at, at + STRIPE)


def rows_of(index, size):
    return pl.ds(pl.multiple_of(index * size, size), size)


def remote(src, dst, send, receive, device):
    return pltpu.make_async_remote_copy(
        src_ref=src, dst_ref=dst, send_sem=send, recv_sem=receive, device_id=device, device_id_type=MESH
    )


def greet(s, t, around):
    barrier = pltpu.get_barrier_semaphore()
    for step in range(1, TP):
        pl.semaphore_signal(barrier, inc=1, device_id=(s, (t + step) % TP), device_id_type=MESH)
    for device in around:
        pl.semaphore_signal(barrier, inc=1, device_id=(device, t), device_id_type=MESH)
    pl.semaphore_wait(barrier, TP - 1 + len(around))


def every_rows(count, body, size=BLOCK):
    @pl.loop(0, count // size)
    def _(block):
        body(pl.ds(pl.multiple_of(block * size, size), size), block * size)


def flag(condition):
    return jnp.where(condition, 1.0, 0.0).astype(F32)


def rotated(values, cosine, sine):
    return values * cosine + pltpu.roll(values, HEAD // 2, 1) * sine


def state_exchange(rows, boundary, refs, rates, scale, toward, source_of):
    state, pair_land, chip_state, chip_land, partial, result, pair_sem, chip_send, chip_recv, partial_sem = refs
    s, t, other, first, second, diagonal = place()
    core, half = s % 2, TP
    around = (first, second, diagonal)
    ours, theirs = pl.ds(core * half, half), pl.ds((1 - core) * half, half)

    def pair_copy():
        return remote(state.at[theirs], pair_land, pair_sem.at[0], pair_sem.at[1], (other, t))

    def chip_copy(part):
        return remote(chip_state, chip_land.at[part], chip_send.at[part], chip_recv.at[part], (around[part], t))

    def partial_copy():
        return remote(partial, result.at[ours], partial_sem.at[0], partial_sem.at[1], (other, t))

    def rate_of(number):
        head = core * half + number
        return rates[head // 2, pl.ds(head % 2, 1), :]

    def begin():
        pair_copy().start()

    def add_pair():
        pair_copy().wait_recv()

        @pl.loop(0, half)
        def _(number):
            rate, target = rate_of(number), toward(s // 2)
            total = scale(target, s, rate) * state[core * half + number].astype(F32)
            total += scale(target, other, rate) * pair_land[number].astype(F32)
            chip_state[number] = total.astype(BF16)

        for part in range(3):
            chip_copy(part).start()

    def add_chips():
        for part in range(3):
            chip_copy(part).wait_recv()

        @pl.loop(0, half)
        def _(number):
            rate = rate_of(number)
            mine, its = state[core * half + number].astype(F32), pair_land[number].astype(F32)
            here = scale(s, s, rate) * mine + scale(s, other, rate) * its
            there = scale(other, s, rate) * mine + scale(other, other, rate) * its
            for part in range(3):
                values = chip_land[part, number].astype(F32)
                source = source_of(around[part] // 2)
                here += scale(s, source, rate) * values
                there += scale(other, source, rate) * values
            result[core * half + number] = here.astype(BF16)
            partial[number] = there.astype(BF16)

        partial_copy().start()

    def finish():
        partial_copy().wait_recv()

    def close():
        pair_copy().wait_send()
        for part in range(3):
            chip_copy(part).wait_send()
        partial_copy().wait_send()

    return begin, add_pair, add_chips, finish, close


def state_scratch():
    dma = pltpu.SemaphoreType.DMA
    return [
        pltpu.VMEM((2 * TP, HEAD, HEAD), BF16),
        pltpu.VMEM((TP, HEAD, HEAD), BF16),
        pltpu.VMEM((TP, HEAD, HEAD), BF16),
        pltpu.VMEM((3, TP, HEAD, HEAD), BF16),
        pltpu.VMEM((TP, HEAD, HEAD), BF16),
        pltpu.VMEM((2 * TP, HEAD, HEAD), BF16),
        dma((2,)),
        dma((3,)),
        dma((3,)),
        dma((2,)),
    ]


LAG_B, LAG_C = 2, 4
LINE_STARTS = {1: (4,), 2: (2, 3)}


def forward_kernel(rows, sizes, *refs):
    heads_in, refs = refs[:4], refs[4:]
    shards, refs = refs[:4], refs[4:]
    (hidden_in, cot_in, cosine, sine, rate_in, bounds), refs = refs[:6], refs[6:]
    whole_out, refs = refs[:2], refs[2:]
    (acts_out, pack_out, normed_out, second_out, glu_out, left_out, right_out, glu_other, left_other, right_other,
     gated_other, normed_other, second_other, cot_other, back_out,
     incoming_out, inv_mix_out, inv_second_out, rate_out, result_out), refs = refs[:20], refs[20:]
    whole, refs = refs[:5], refs[5:]
    (acts, pack, normed, hidden, cot, second_normed, sides, back, wide, mixed, distance, scores, weights,
     inv_mix, inv_second, rates, heads_shard), refs = refs[:17], refs[17:]
    exchange, refs = refs[:10], refs[10:]
    state, incoming = exchange[0], exchange[5]
    shards = (heads_shard, *shards)
    (local_sem, up_sem, down_sem, line_sem, send_sem, first_sem, second_sem, other_sem, rate_send, rate_recv,
     copy_sem, side_sem, side_send, side_recv, half_send, half_recv,
     hidden_sem, cot_sem) = refs
    s, t, other, first, second, diagonal = place()
    units, beside = sizes[2], wide.shape[1] // 3
    theirs = rows_of(1 - s % 2, D // 2)
    shift = other - s
    for kind in range(4):
        heads_shard[kind * PAIR : kind * PAIR + PAIR, :] = heads_in[kind][...].T
    greet(s, t, (other, first, second, diagonal))

    def hidden_load(index):
        return pltpu.make_async_copy(
            hidden_in.at[t, :, plain(index)], hidden.at[:, place_of(index)], hidden_sem.at[index]
        )

    def cot_load(index):
        return pltpu.make_async_copy(cot_in.at[t, :, plain(index)], cot.at[:, place_of(index)], cot_sem.at[index])

    def half_copy(part):
        src, dst = (
            (normed.at[:, theirs], normed_other),
            (second_normed.at[:, theirs], second_other),
            (cot.at[:, theirs], cot_other),
            (pack.at[:, :, 2 * PAIR : 3 * PAIR], gated_other),
        )[part]
        return remote(src, dst, half_send.at[part], half_recv.at[part], (other, t))

    for index in range(SEQ):
        hidden_load(index).start()

    pairs = [(2, step) for step in range(TP)], [(3, step) for step in range(TP)]
    items = (
        [(0, step) for step in range(TP)]
        + [(1, step) for step in range(TP)]
        + [(4, step) for step in range(TP)]
        + [item for both in zip(*pairs) for item in both]
    )

    def spot(w, owner, column):
        return whole[w].at[rows_of(owner, sizes[w]), stripe(column)]

    def source(w, step, owner):
        return shards[w] if step == 0 else spot(w, owner, s)

    def up_copy(w, step, owner):
        return remote(source(w, step, owner), spot(w, owner, s), up_sem.at[w, owner], line_sem.at[w, owner], (s, t + 1))

    def down_copy(w, step, owner):
        return remote(source(w, step, owner), spot(w, owner, s), down_sem.at[w, owner], line_sem.at[w, owner], (s, t - 1))

    def own_copy(w):
        return pltpu.make_async_copy(shards[w], spot(w, t, s), local_sem.at[w])

    def plane_copies(index, w, step, owner):
        src, dst = source(w, step, owner), spot(w, owner, s)
        return (
            remote(src, dst, send_sem.at[index, 0], first_sem.at[index], (first, t)),
            remote(src, dst, send_sem.at[index, 1], second_sem.at[index, 0], (second, t)),
            remote(src, dst, send_sem.at[index, 2], other_sem.at[index, 0], (other, t)),
        )

    def relay_copies(index, w, owner):
        src = spot(w, owner, first)
        return (
            remote(src, src, send_sem.at[index, 3], second_sem.at[index, 1], (second, t)),
            remote(src, src, send_sem.at[index, 4], other_sem.at[index, 1], (other, t)),
        )

    def last_copies(index, w, owner):
        near, far = spot(w, owner, second), spot(w, owner, diagonal)
        return (
            remote(near, near, send_sem.at[index, 5], other_sem.at[index, 2], (other, t)),
            remote(far, far, send_sem.at[index, 6], other_sem.at[index, 3], (other, t)),
        )

    def line_start(w):
        own_copy(w).start()

        @pl.when(t < TP - 1)
        def _():
            up_copy(w, 0, t).start()

        @pl.when(t > 0)
        def _():
            down_copy(w, 0, t).start()

    def line_pass(index):
        if index >= len(items):
            return
        w, step = items[index]
        if step:
            owner = nearest(t, step)
            up_copy(w, step, owner).wait_recv()

            @pl.when((owner < t) & (t < TP - 1))
            def _():
                up_copy(w, step, owner).start()

            @pl.when((owner > t) & (t > 0))
            def _():
                down_copy(w, step, owner).start()

    def stage_a(index):
        w, step = items[index]
        for copy in plane_copies(index, w, step, nearest(t, step)):
            copy.start()

    relayed, ended = [], []

    def stage_b(until):
        while len(relayed) <= min(until, len(items) - 1):
            index = len(relayed)
            relayed.append(index)
            w, step = items[index]
            owner = nearest(t, step)
            here = spot(w, owner, first)
            remote(here, here, send_sem.at[index, 0], first_sem.at[index], (first, t)).wait_recv()
            for copy in relay_copies(index, w, owner):
                copy.start()

    def stage_c(until):
        while len(ended) <= min(until, len(items) - 1):
            index = len(ended)
            ended.append(index)
            w, step = items[index]
            owner = nearest(t, step)
            for part, column in enumerate((second, diagonal)):
                here = spot(w, owner, column)
                remote(here, here, send_sem.at[index, 1], second_sem.at[index, part], (second, t)).wait_recv()
            for copy in last_copies(index, w, owner):
                copy.start()

    def tick(now):
        stage_b(now - LAG_B)
        if now < len(items):
            stage_a(now)
        stage_c(now - LAG_C)
        if now % TP == 0:
            for w in LINE_STARTS.get(now // TP, ()):
                line_start(w)
        line_pass(now + 2)

    keeps = []

    def keep(src, dst):
        copy = functools.partial(pltpu.make_async_copy, src, dst, copy_sem.at[len(keeps)])
        copy().start()
        keeps.append(copy)

    def ready(index):
        w, step = items[index]
        owner = nearest(t, step)
        if step == 0:
            own_copy(w).wait()
        for part, column in enumerate((other, second + shift, first + shift, diagonal + shift)):
            here = spot(w, owner, column)
            remote(here, here, send_sem.at[index, 2], other_sem.at[index, part], (other, t)).wait_recv()
        block = rows_of(owner, sizes[w])
        if w < 2:
            keep(whole[w].at[block, :], whole_out[w].at[block, :])
        return owner, block

    def rate_copy(step):
        return remote(rates.at[t], rates.at[t], rate_send.at[step - 1], rate_recv.at[step - 1], (s, (t + step) % TP))

    row = lax.broadcasted_iota(jnp.int32, (8, HEAD), 0)
    rates[t] = jnp.where(row == 0, rate_in[0], rate_in[1])
    for step in range(1, TP):
        rate_copy(step).start()
    stage_a(0)
    line_start(0)
    line_start(1)
    boundary = bounds[t]
    edge = boundary - s * rows

    for index in range(SEQ):
        hidden_load(index).wait()
        cot_load(index).start()

    def prepare(part, start):
        values = hidden[part, :].astype(F32)
        scale = lax.rsqrt(jnp.mean(values * values, axis=-1, keepdims=True) + EPSILON)
        normed[part, :] = (values * scale).astype(BF16)
        row = lax.broadcasted_iota(jnp.int32, (BLOCK, rows), 0) + start
        column = lax.broadcasted_iota(jnp.int32, (BLOCK, rows), 1)
        apart = (column > row) | ((row >= edge) & (column < edge))
        distance[part, :] = jnp.where(apart, -1, row - column).astype(F32)

    every_rows(rows, prepare)
    keep(normed, normed_out)
    half_copy(0).start()
    for step in range(1, TP):
        here = rates.at[t]
        remote(here, here, rate_send.at[step - 1], rate_recv.at[step - 1], (s, t)).wait_recv()
    keep(rates, rate_out)

    before = jnp.where(s * rows - 1 >= boundary, 1, 0)
    last = jnp.where(s * rows + rows - 1 >= boundary, 1, 0)

    def rate_of(block, half):
        return rates[block, half : half + 1, :]

    def row_numbers(start, count=BLOCK):
        return lax.broadcasted_iota(jnp.int32, (count, HEAD), 0) + start

    def project(index):
        owner, block = ready(index)
        wide[:, 0:D] = dots(normed[...], whole[0][block, :], NT)

        def shape_rows(part, start):
            turn, lean = cosine[part, :], sine[part, :]
            for kind in range(2):
                for half in range(2):
                    at = kind * PAIR + half * HEAD
                    values = wide[part, at : at + HEAD]
                    logistic = 1.0 / (1.0 + jnp.exp(-values))
                    acts[owner, part, at : at + HEAD] = rotated(values * logistic, turn, lean).astype(BF16)
                    pack[owner, part, at : at + HEAD] = (
                        logistic * (1.0 + values * (1.0 - logistic))
                    ).astype(BF16)
            acts[owner, part, 2 * PAIR : 4 * PAIR] = wide[part, 2 * PAIR : 4 * PAIR].astype(BF16)
            number = row_numbers(start)
            valid = jnp.where(jnp.where(number >= edge, 1, 0) == last, 1.0, 0.0)
            for half in range(2):
                fade = jnp.exp(-rate_of(owner, half) * (rows - 1 - number).astype(F32)) * valid
                keys = acts[owner, part, PAIR + half * HEAD : PAIR + half * HEAD + HEAD].astype(F32)
                weights[part, half * HEAD : half * HEAD + HEAD] = (keys * fade).astype(BF16)

        every_rows(rows, shape_rows)
        for half in range(2):
            at = half * HEAD
            state[owner * 2 + half] = dots(
                weights[:, at : at + HEAD], acts[owner, :, 2 * PAIR + at : 2 * PAIR + at + HEAD], TN
            ).astype(BF16)

    def attend(step):
        owner = nearest(t, step)
        for half in range(2):
            at = half * HEAD
            rate = rates[owner, half : half + 1, :]
            for top in range(0, rows, PAIR):
                width = top + PAIR
                scores[0:PAIR, 0:width] = dots(
                    acts[owner, top : top + PAIR, at : at + HEAD], acts[owner, 0:width, PAIR + at : PAIR + at + HEAD], NT
                )

                def weigh(part, start, width=width, top=top, rate=rate):
                    for left in range(0, width, HEAD):
                        apart = distance[pl.ds(pl.multiple_of(start + top, BLOCK), BLOCK), left : left + HEAD]
                        fade = jnp.where(apart >= 0.0, jnp.exp(-rate * apart), 0.0)
                        weights[part, left : left + HEAD] = (scores[part, left : left + HEAD] * fade).astype(BF16)

                every_rows(PAIR, weigh)
                column = pl.ds(pl.multiple_of(owner * PAIR + at, HEAD), HEAD)
                mixed[top : top + PAIR, column] = dots(
                    weights[0:PAIR, 0:width], acts[owner, 0:width, 2 * PAIR + at : 2 * PAIR + at + HEAD], NN
                )

    def prefix_scale(block, source_block, rate):
        same = jnp.where((source_block + 1) * rows - 1 >= boundary, 1, 0) == jnp.where(block * rows - 1 >= boundary, 1, 0)
        usable = flag(source_block < block) * flag(same)
        gap = jnp.maximum(block - 1 - source_block, 0).astype(F32)
        return jnp.exp(-rate * (rows * gap)) * usable

    begin_states, add_pair, add_chips, finish_states, close_states = state_exchange(
        rows, boundary, exchange, rates, prefix_scale, lambda chip: 2 * chip + 2, lambda chip: 2 * chip + 1
    )

    def mix():
        finish_states()
        keep(incoming, incoming_out)
        for block in range(TP):
            for half in range(2):
                at = half * HEAD
                scores[:, at : at + HEAD] = dots(acts[block, :, at : at + HEAD], incoming[2 * block + half], NN)

            def add_outer(part, start, block=block):
                number = row_numbers(start)
                valid = jnp.where(jnp.where(number >= edge, 1, 0) == before, 1.0, 0.0)
                for half in range(2):
                    fade = jnp.exp(-rate_of(block, half) * (number + 1).astype(F32)) * valid
                    column = slice(block * PAIR + half * HEAD, block * PAIR + half * HEAD + HEAD)
                    mixed[part, column] += fade * scores[part, half * HEAD : half * HEAD + HEAD]

            every_rows(rows, add_outer)

        def gate_rows(part, start):
            values = mixed[part, :]
            scale = lax.rsqrt(jnp.mean(values * values, axis=-1, keepdims=True) + EPSILON)
            inv_mix[part, :] = jnp.broadcast_to(scale, (BLOCK, HEAD))
            values = values * scale
            for block in range(TP):
                column = slice(block * PAIR, block * PAIR + PAIR)
                gate = acts[block, part, 3 * PAIR : 4 * PAIR].astype(F32)
                pack[block, part, 2 * PAIR : 3 * PAIR] = (values[:, column] * gate).astype(BF16)
                pack[block, part, 3 * PAIR : 4 * PAIR] = values[:, column].astype(BF16)

        every_rows(rows, gate_rows, BLOCK)
        keep(acts, acts_out)
        keep(pack, pack_out)
        half_copy(3).start()
        keep(inv_mix, inv_mix_out)

    def project_out():
        for block in range(TP):
            term = dots(pack[block, :, 2 * PAIR : 3 * PAIR], whole[1][block * PAIR : block * PAIR + PAIR, :], NN)
            if block:
                wide[:, 0:D] += term
            else:
                wide[:, 0:D] = term

        def norm_rows(part, start):
            values = hidden[part, :].astype(F32) + wide[part, 0:D]
            mixed[part, :] = values
            scale = lax.rsqrt(jnp.mean(values * values, axis=-1, keepdims=True) + EPSILON)
            inv_second[part, :] = jnp.broadcast_to(scale, (BLOCK, HEAD))
            second_normed[part, :] = (values * scale).astype(BF16)

        every_rows(rows, norm_rows)
        keep(second_normed, second_out)
        half_copy(1).start()
        keep(inv_second, inv_second_out)

    def left_side(index):
        owner, block = ready(index)
        wide[:, 0:units] = dots(second_normed[...], whole[2][block, :], NT)
        wide[:, 2 * beside : 2 * beside + units] = dots(cot[...], whole[4][block, :], NT)

    def side_copies(slot, owner):
        return [
            pltpu.make_async_copy(sides.at[slot, part], out.at[owner], side_sem.at[slot, part])
            for part, out in enumerate((glu_out, left_out, right_out))
        ]

    def side_remotes(slot, step):
        owner = nearest(t, step)
        return [
            remote(sides.at[slot, part], out.at[owner], side_send.at[slot, part], side_recv.at[step, part], (other, t))
            for part, out in enumerate((glu_other, left_other, right_other))
        ]

    def right_side(index):
        owner, block = ready(index)
        wide[:, beside : beside + units] = dots(second_normed[...], whole[3][block, :], NT)
        step = items[index][1]
        slot = step % 2
        if step >= 2:
            for copy in side_copies(slot, nearest(t, step - 2)):
                copy.wait()
            for copy in side_remotes(slot, step - 2):
                copy.wait_send()

        def multiply(part, start):
            left, right = wide[part, 0:units], wide[part, beside : beside + units]
            grad = wide[part, 2 * beside : 2 * beside + units]
            sides[slot, 0, part, :] = (left * right).astype(BF16)
            sides[slot, 1, part, :] = (grad * right).astype(BF16)
            sides[slot, 2, part, :] = (grad * left).astype(BF16)

        every_rows(rows, multiply)
        for copy in side_copies(slot, owner) + side_remotes(slot, step):
            copy.start()
        mixed[...] += dots(sides[slot, 0], whole[4][block, :], NN)
        term = dots(sides[slot, 1], whole[2][block, :], NN) + dots(sides[slot, 2], whole[3][block, :], NN)
        if step:
            back[...] += term
        else:
            back[...] = term

    stage_b(0)
    line_pass(1)
    stage_a(1)
    stage_b(1)
    line_pass(2)
    stage_a(2)
    stage_c(0)
    line_pass(3)
    stage_a(3)
    stage_b(2)
    line_pass(4)
    line_pass(5)
    for step in range(TP):
        tick(TP + step)
        project(step)
    begin_states()
    for index in range(SEQ):
        cot_load(index).wait()
    half_copy(2).start()
    tick(8)
    add_pair()
    for step in range(TP):
        attend(step)
        tick(9 + step)
    add_chips()
    for index in range(TP, 2 * TP):
        ready(index)
    tick(13)
    mix()
    tick(14)
    project_out()
    tick(15)
    for index in range(2 * TP, 3 * TP):
        ready(index)
    for index in range(3 * TP, len(items)):
        tick(index + LAG_C)
        (left_side, right_side)[items[index][0] - 2](index)

    def finish(part, start):
        for index in range(SEQ):
            result_out[part, plain(index)] = mixed[part, place_of(index)].astype(BF16)

    keep(back, back_out)
    every_rows(rows, finish)

    for step in range(1, TP):
        rate_copy(step).wait_send()
    close_states()
    for copy in keeps:
        copy().wait()
    for part in range(4):
        half_copy(part).wait()
    for step in range(TP):
        for copy in side_remotes(step % 2, step):
            copy.wait_recv()
            if step >= 2:
                copy.wait_send()
        if step >= 2:
            for copy in side_copies(step % 2, nearest(t, step)):
                copy.wait()
    for index, (w, step) in enumerate(items):
        owner = nearest(t, step)
        if step == 0:

            @pl.when(t < TP - 1)
            def _():
                up_copy(w, step, owner).wait_send()

            @pl.when(t > 0)
            def _():
                down_copy(w, step, owner).wait_send()
        else:

            @pl.when((owner < t) & (t < TP - 1))
            def _():
                up_copy(w, step, owner).wait_send()

            @pl.when((owner > t) & (t > 0))
            def _():
                down_copy(w, step, owner).wait_send()
        for copy in plane_copies(index, w, step, owner) + relay_copies(index, w, owner) + last_copies(index, w, owner):
            copy.wait_send()


KEPT = 20


def forward(heads_in, shards, hidden, cot, cosine, sine, rate, bounds):
    rows = hidden.shape[1]
    sizes = (4 * PAIR, *(shard.shape[0] for shard in shards))
    units = sizes[2]
    beside = -(-units // HEAD) * HEAD
    items = 5 * TP
    dma = pltpu.SemaphoreType.DMA
    vmem = pl.BlockSpec(memory_space=pltpu.VMEM)
    anywhere = pl.BlockSpec(memory_space=pl.ANY)
    heads = 2 * TP
    shape = jax.ShapeDtypeStruct
    outs = [
        *[shape((TP * size, D), BF16) for size in sizes[:2]],
        *[shape((TP, rows, 4 * PAIR), BF16)] * 2,
        *[shape((rows, D), BF16)] * 2,
        *[shape((TP, rows, units), BF16)] * 6,
        shape((TP, rows, PAIR), BF16),
        *[shape((rows, D // 2), BF16)] * 3,
        shape((rows, D), F32),
        shape((heads, HEAD, HEAD), BF16),
        shape((rows, HEAD), F32),
        shape((rows, HEAD), F32),
        shape((TP, 8, HEAD), F32),
        shape((rows, D), BF16),
    ]
    return pl.pallas_call(
        functools.partial(forward_kernel, rows, sizes),
        out_shape=outs,
        in_specs=[vmem] * 4 + [anywhere] * 6 + [vmem] * 2 + [pl.BlockSpec(memory_space=pltpu.SMEM)] * 2,
        out_specs=[anywhere] * (len(outs) - 1) + [vmem],
        scratch_shapes=[pltpu.VMEM((TP * size, D), BF16) for size in sizes]
        + [
            *[pltpu.VMEM((TP, rows, 4 * PAIR), BF16)] * 2,
            *[pltpu.VMEM((rows, D), BF16)] * 4,
            pltpu.VMEM((2, 3, rows, units), BF16),
            pltpu.VMEM((rows, D), F32),
            pltpu.VMEM((rows, 3 * beside), F32),
            pltpu.VMEM((rows, D), F32),
            pltpu.VMEM((rows, rows), F32),
            pltpu.VMEM((rows, rows), F32),
            pltpu.VMEM((rows, rows), BF16),
            pltpu.VMEM((rows, HEAD), F32),
            pltpu.VMEM((rows, HEAD), F32),
            pltpu.VMEM((TP, 8, HEAD), F32),
            pltpu.VMEM((4 * PAIR, STRIPE), BF16),
            *state_scratch(),
            dma((5,)),
            dma((5, TP)),
            dma((5, TP)),
            dma((5, TP)),
            dma((items, 7)),
            dma((items,)),
            dma((items, 2)),
            dma((items, 4)),
            dma((TP - 1,)),
            dma((TP - 1,)),
            dma((KEPT,)),
            dma((2, 3)),
            dma((2, 3)),
            dma((TP, 3)),
            dma((4,)),
            dma((4,)),
            dma((SEQ,)),
            dma((SEQ,)),
        ],
        compiler_params=pltpu.CompilerParams(
            collective_id=0, has_side_effects=True, vmem_limit_bytes=63 * 2**20
        ),
        name="forward",
    )(*heads_in, *shards, hidden, cot, cosine, sine, rate, bounds)


ROWS_STEP = 64
PIECES = 4
HELD = 6
LAG_2, LAG_3, LAG_4, LAG_5 = 2, 4, 8, 14
KINDS = 6
ITEMS = KINDS * TP


def add_rows(target, *terms):
    rows = target.shape[0]

    @pl.loop(0, rows // ROWS_STEP)
    def _(block):
        part = pl.ds(pl.multiple_of(block * ROWS_STEP, ROWS_STEP), ROWS_STEP)
        total = terms[0][part, :].astype(F32)
        for term in terms[1:]:
            total = total + term[part, :].astype(F32)
        target[part, :] = total.astype(target.dtype)


def backward_kernel(rows, sizes, *refs):
    whole, refs = refs[:2], refs[2:]
    (acts_in, pack_in, normed_in, second_in, glu_own, left_own, right_own, glu_other, left_other, right_other,
     gated_other, normed_other, second_other, cot_other, back_in, output_in, hidden_in, cot_in,
     incoming, inv_mix, inv_second, rates, cosine, sine, bounds), refs = refs[:25], refs[25:]
    (down_grad, left_grad, right_grad, out_grad, qkvg_grad, output_whole, input_whole,
     backs_own, backs_other), refs = refs[:9], refs[9:]
    (tiles, cot, second_normed, normed, attn_cot, halves, acts, pack, backs, mid, wide, distance, scores,
     weights, slopes, faded, lhs, held), refs = refs[:18], refs[18:]
    exchange, refs = refs[:10], refs[10:]
    state, later = exchange[0], exchange[5]
    lands, refs = refs[:9], refs[9:]
    (tile_sem, half_sem, half_load_sem, backs_keep, backs_send, backs_recv, load_sem, cot_sem, hidden_sem, lhs_sem, second_send, second_recv,
     first_send, first_recv, line_send, below_recv, above_recv, share_local, share_up, share_down, share_recv) = refs
    s, t, other, first, second, diagonal = place()
    core = s % 2
    units = sizes[2]
    half_d = D // 2
    ours, theirs = rows_of(core, half_d), rows_of(1 - core, half_d)
    boundary = bounds[t]
    edge = boundary - s * rows
    before = jnp.where(s * rows - 1 >= boundary, 1, 0)
    last = jnp.where(s * rows + rows - 1 >= boundary, 1, 0)
    around = (first, second, diagonal)
    order = [3, 2, 1, 0]
    local = pltpu.make_async_copy

    done = set()

    def once(key, wait):
        if key not in done:
            done.add(key)
            wait()

    greet(s, t, (other, first, second, diagonal))

    def cot_load(index):
        return local(cot_in.at[t, :, plain(index)], cot.at[:, place_of(index)], cot_sem.at[index])

    def hidden_load(index):
        return local(hidden_in.at[t, :, plain(index)], acts.at[0, :, place_of(index)], hidden_sem.at[index])

    def second_load():
        return local(second_in, second_normed, load_sem.at[0])

    def normed_load():
        return local(normed_in, normed, load_sem.at[1])

    def acts_load():
        return local(acts_in, acts, load_sem.at[2])

    def pack_load():
        return local(pack_in, pack, load_sem.at[3])

    def back_load():
        return local(back_in, mid, load_sem.at[4])

    def half_load(part):
        return local((cot_other, second_other, normed_other)[part], halves.at[part], half_load_sem.at[part])

    def half_copy():
        return remote(attn_cot.at[:, theirs], halves.at[3], half_sem.at[0], half_sem.at[1], (other, t))

    tile_list = [(1, part) for part in range(2)] + [(0, part) for part in range(2 * TP)]

    def tile_load(index):
        w, at = tile_list[index]
        return local(whole[w].at[pl.ds(at * half_d, half_d), :], tiles.at[index % 3], tile_sem.at[index % 3])

    def tile(index):
        tile_load(index).wait()
        return tiles[index % 3]

    def tile_next(index):
        if index + 3 < len(tile_list):
            tile_load(index + 3).start()

    def backs_keep_copy(block):
        return local(backs.at[block], backs_own.at[block], backs_keep.at[block])

    def backs_copy(block):
        return remote(backs.at[block], backs_other.at[block], backs_send.at[block], backs_recv.at[block], (other, t))

    piece_rows = rows // PIECES
    shares = ((output_in, output_whole), (acts.at[1], input_whole))

    def piece(a, owner, p):
        return shares[a][1].at[owner, pl.ds(p * piece_rows, piece_rows), :]

    def own_piece(a, p):
        return shares[a][0].at[pl.ds(p * piece_rows, piece_rows), :]

    def share_copy(a, p, owner, src, up):
        sem, target = (share_up, t + 1) if up else (share_down, t - 1)
        return remote(src, piece(a, owner, p), sem.at[a, p, owner], share_recv.at[a, p, owner], (s, target))

    def share_keep(a, p):
        return local(own_piece(a, p), piece(a, t, p), share_local.at[a, p])

    def share_start(a, p):
        @pl.when(t < TP - 1)
        def _():
            share_copy(a, p, t, own_piece(a, p), True).start()

        @pl.when(t > 0)
        def _():
            share_copy(a, p, t, own_piece(a, p), False).start()

        share_keep(a, p).start()

    relays = [
        (a, p, step) for a in range(2) for steps in ((1, 2), (3,)) for p in range(PIECES) for step in steps
    ]
    relayed = []

    def passes(owner, up):
        return (owner < t) & (t < TP - 1) if up else (owner > t) & (t > 0)

    def relay(limit, until=len(relays)):
        for _ in range(limit):
            if len(relayed) >= until:
                return
            a, p, step = relays[len(relayed)]
            relayed.append(1)
            owner = nearest(t, step)
            for up in (True, False):

                @pl.when(passes(owner, up))
                def _(up=up):
                    share_copy(a, p, owner, piece(a, owner, p), up).wait_recv()
                    share_copy(a, p, owner, piece(a, owner, p), up).start()

    items = (
        [(0, step) for step in order]
        + [(kind, step) for step in order for kind in (1, 2)]
        + [(3, step) for step in order]
        + [(kind, step) for step in order for kind in (4, 5)]
    )
    heights = (units, units, units, sizes[1], half_d, half_d)

    def lands_of(index):
        kind, step = items[index]
        owner = nearest(t, step)
        group, base, extra = ((0, kind * TP, 3 * TP + kind), (1, 0, TP), (2, (kind - 4) * TP, 2 * TP + kind - 4))[
            0 if kind < 3 else 1 if kind == 3 else 2
        ]
        return owner, lands[3 * group : 3 * group + 3], base + owner, extra

    def own_source(kind, owner):
        if kind == 0:
            return glu_own.at[owner], glu_other.at[owner]
        if kind == 1:
            return left_own.at[owner], left_other.at[owner]
        if kind == 2:
            return right_own.at[owner], right_other.at[owner]
        if kind == 3:
            return pack_in.at[owner, :, 2 * PAIR : 3 * PAIR], gated_other.at[owner]
        part = slice((kind - 4) * half_d, (kind - 3) * half_d)
        return backs_own.at[owner, :, part], backs_other.at[owner, :, part]

    def lhs_loads(index):
        kind, step = items[index]
        slot = index % 2
        return [
            local(src, lhs.at[slot, part, :, pl.ds(0, heights[kind])], lhs_sem.at[slot, part])
            for part, src in enumerate(own_source(kind, nearest(t, step)))
        ]

    def prefetch(index):
        kind, step = items[index]
        owner = nearest(t, step)
        if kind >= 4:
            once(("backs", step), lambda: backs_keep_copy(owner).wait())
            once(("backs_other", step), lambda: backs_copy(owner).wait_recv())
        for copy in lhs_loads(index):
            copy.start()

    def to_second(index):
        kind = items[index][0]
        owner, (second_land, first_land, line_land), at, extra = lands_of(index)
        return [
            remote(
                held.at[index % HELD, column // 2, pl.ds(0, heights[kind]), :],
                second_land.at[at, part],
                second_send.at[index, part],
                second_recv.at[index, part],
                (second, t),
            )
            for part, column in enumerate((diagonal, second))
        ]

    def to_first(index):
        owner, (second_land, first_land, line_land), at, extra = lands_of(index)
        return remote(second_land.at[at, 0], first_land.at[at], first_send.at[index], first_recv.at[index], (first, t))

    def along(index, up):
        kind = items[index][0]
        owner, (second_land, first_land, line_land), at, extra = lands_of(index)
        if up:
            return remote(
                first_land.at[at], line_land.at[at], line_send.at[index], below_recv.at[kind, owner], (s, t + 1)
            )
        final = jnp.where(owner == t - 1, 1, 0)
        return remote(
            first_land.at[at],
            line_land.at[at + final * (extra - at)],
            line_send.at[index],
            above_recv.at[kind, owner],
            (s, t - 1),
        )

    def held_rows(index, chip):
        return held.at[index % HELD, chip, pl.ds(0, heights[items[index][0]]), :]

    def advance(now):
        index = now - LAG_2
        if 0 <= index < ITEMS:
            owner, (second_land, first_land, line_land), at, extra = lands_of(index)
            for copy in to_second(index):
                copy.wait_recv()
            add_rows(second_land.at[at, 0], second_land.at[at, 0], held_rows(index, first // 2))
            to_first(index).start()
        index = now - LAG_3
        if 0 <= index < ITEMS:
            owner, (second_land, first_land, line_land), at, extra = lands_of(index)
            to_first(index).wait_recv()
            add_rows(first_land.at[at], first_land.at[at], held_rows(index, s // 2), second_land.at[at, 1])
        index = now - LAG_4
        if 0 <= index < ITEMS:
            kind, step = items[index]
            owner, (second_land, first_land, line_land), at, extra = lands_of(index)
            if step:

                @pl.when((owner > t) & (t > 0))
                def _():
                    along(index, True).wait_recv()
                    add_rows(first_land.at[at], first_land.at[at], line_land.at[at])

                @pl.when((owner < t) & (t < TP - 1))
                def _():
                    along(index, False).wait_recv()
                    add_rows(first_land.at[at], first_land.at[at], line_land.at[at])

                @pl.when(owner > t)
                def _():
                    along(index, True).start()

                @pl.when(owner < t)
                def _():
                    along(index, False).start()
        index = now - LAG_5
        if 0 <= index < ITEMS:
            kind, step = items[index]
            owner, (second_land, first_land, line_land), at, extra = lands_of(index)
            if step == 0:
                target = (down_grad, left_grad, right_grad, out_grad, qkvg_grad, qkvg_grad)[kind]
                if kind >= 4:
                    target = target.at[(kind - 4) * half_d : (kind - 3) * half_d]

                @pl.when(t == 0)
                def _():
                    along(index, False).wait_recv()
                    add_rows(target, first_land.at[at], line_land.at[extra])

                @pl.when(t == TP - 1)
                def _():
                    along(index, True).wait_recv()
                    add_rows(target, first_land.at[at], line_land.at[at])

                @pl.when((t > 0) & (t < TP - 1))
                def _():
                    along(index, True).wait_recv()
                    along(index, False).wait_recv()
                    add_rows(target, first_land.at[at], line_land.at[at], line_land.at[extra])

    def produce(index):
        kind, step = items[index]
        height = heights[kind]
        right, part = ((cot, 0), (second_normed, 1), (second_normed, 1), (attn_cot, 3), (normed, 2), (normed, 2))[kind]
        once(("half", part), lambda: half_copy().wait_recv() if part == 3 else half_load(part).wait())
        if kind >= 4:
            once("normed", lambda: normed_load().wait())
        for copy in lhs_loads(index):
            copy.wait()
        if index >= HELD:
            for copy in to_second(index - HELD):
                copy.wait_send()
        slot = index % 2
        product = dots(lhs[slot, 0, :, 0:height], right[:, ours], TN) + dots(lhs[slot, 1, :, 0:height], halves[part], TN)
        for chip in range(4):
            held[index % HELD, chip, 0:height, :] = product[:, chip * STRIPE : chip * STRIPE + STRIPE].astype(BF16)
        for copy in to_second(index):
            copy.start()
        advance(index)

    for index in range(SEQ):
        cot_load(index).start()
    half_load(0).start()
    prefetch(0)
    for p in range(PIECES):
        share_start(0, p)
    back_load().start()
    second_load().start()
    half_load(1).start()
    for index in range(3):
        tile_load(index).start()
    acts_load().start()
    pack_load().start()
    normed_load().start()
    half_load(2).start()
    for index in range(SEQ):
        cot_load(index).wait()
    produce(0)
    prefetch(1)
    back_load().wait()
    second_load().wait()

    def middle(part, start):
        unit = second_normed[part, :].astype(F32)
        values = mid[part, :]
        inner = jnp.mean(values * unit, axis=-1, keepdims=True)
        values = cot[part, :].astype(F32) + inv_second[part, 0:1] * (values - unit * inner)
        mid[part, :] = values
        attn_cot[part, :] = values.astype(BF16)

    every_rows(rows, middle)
    half_copy().start()
    produce(1)
    prefetch(2)
    at_tile = 0
    for part in range(2):
        wide[:, part * half_d : part * half_d + half_d] = dots(attn_cot[...], tile(at_tile + part), NT)
        tile_next(at_tile + part)
    at_tile += 2
    acts_load().wait()
    pack_load().wait()

    def head_rows(part, start):
        total = jnp.zeros((BLOCK, 1), F32)
        for block in range(TP):
            values = wide[part, block * PAIR : block * PAIR + PAIR]
            gate = acts[block, part, 3 * PAIR : 4 * PAIR].astype(F32)
            unit = pack[block, part, 3 * PAIR : 4 * PAIR].astype(F32)
            total += jnp.sum(values * gate * unit, axis=-1, keepdims=True)
        total = total * (1.0 / D)
        scale = inv_mix[part, 0:1]
        for block in range(TP):
            values = wide[part, block * PAIR : block * PAIR + PAIR]
            gate = acts[block, part, 3 * PAIR : 4 * PAIR].astype(F32)
            unit = pack[block, part, 3 * PAIR : 4 * PAIR].astype(F32)
            backs[block, part, 3 * PAIR : 4 * PAIR] = (values * unit).astype(BF16)
            backs[block, part, 2 * PAIR : 3 * PAIR] = (scale * (values * gate - unit * total)).astype(BF16)
        row = lax.broadcasted_iota(jnp.int32, (BLOCK, rows), 0) + start
        column = lax.broadcasted_iota(jnp.int32, (BLOCK, rows), 1)
        apart = (column > row) | ((row >= edge) & (column < edge))
        distance[part, :] = jnp.where(apart, -1, row - column).astype(F32)

    every_rows(rows, head_rows)
    produce(2)
    prefetch(3)
    relay(2, 12)

    def rate_of(block, half):
        return rates[block, half : half + 1, :]

    def row_numbers(start):
        return lax.broadcasted_iota(jnp.int32, (BLOCK, HEAD), 0) + start

    for block in range(TP):
        for half in range(2):
            at = half * HEAD

            def fade_rows(part, start, block=block, half=half, at=at):
                number = row_numbers(start)
                valid = jnp.where(jnp.where(number >= edge, 1, 0) == before, 1.0, 0.0)
                fade = jnp.exp(-rate_of(block, half) * (number + 1).astype(F32)) * valid
                values = backs[block, part, 2 * PAIR + at : 2 * PAIR + at + HEAD].astype(F32)
                faded[part, :] = (values * fade).astype(BF16)

            every_rows(rows, fade_rows)
            head = 2 * block + half
            state[head] = dots(acts[block, :, at : at + HEAD], faded[...], TN).astype(BF16)
            wide[:, head * HEAD : head * HEAD + HEAD] = dots(faded[...], incoming[head], NT)

    def suffix_scale(block, source_block, rate):
        same = jnp.where(source_block * rows - 1 >= boundary, 1, 0) == jnp.where(block * rows + rows - 1 >= boundary, 1, 0)
        usable = flag(source_block > block) * flag(same)
        gap = jnp.maximum(source_block - 1 - block, 0).astype(F32)
        return jnp.exp(-rate * (rows * gap)) * usable

    begin_states, add_pair, add_chips, finish_states, close_states = state_exchange(
        rows, boundary, exchange, rates, suffix_scale, lambda chip: 2 * chip - 1, lambda chip: 2 * chip
    )
    begin_states()
    produce(3)
    prefetch(4)
    relay(2, 12)
    add_pair()
    weights[0:PAIR, PAIR:rows] = jnp.zeros((PAIR, rows - PAIR), BF16)
    slopes[0:PAIR, PAIR:rows] = jnp.zeros((PAIR, rows - PAIR), BF16)

    def attend(block):
        for half in range(2):
            at = half * HEAD
            head = 2 * block + half
            rate = rate_of(block, half)
            query, key, value = [slice(kind * PAIR + at, kind * PAIR + at + HEAD) for kind in range(3)]
            mine_columns = slice(head * HEAD, head * HEAD + HEAD)
            for top in range(0, rows, PAIR):
                width = top + PAIR
                scores[0:PAIR, 0:width] = dots(acts[block, top:width, query], acts[block, 0:width, key], NT)
                scores[PAIR : 2 * PAIR, 0:width] = dots(backs[block, top:width, value], acts[block, 0:width, value], NT)

                def weigh(part, start, width=width, top=top):
                    below = pl.ds(pl.multiple_of(start + PAIR, BLOCK), BLOCK)
                    there = pl.ds(pl.multiple_of(start + top, BLOCK), BLOCK)
                    for left in range(0, width, HEAD):
                        apart = distance[there, left : left + HEAD]
                        fade = jnp.where(apart >= 0.0, jnp.exp(-rate * apart), 0.0)
                        weights[there, left : left + HEAD] = (scores[part, left : left + HEAD] * fade).astype(BF16)
                        grad = scores[below, left : left + HEAD].astype(BF16).astype(F32)
                        slopes[there, left : left + HEAD] = (grad * fade).astype(BF16)

                every_rows(PAIR, weigh)
                wide[top:width, mine_columns] += dots(slopes[top:width, 0:width], acts[block, 0:width, key], NN)
            inner = dots(weights[...], backs[block, :, value], TN)
            acts[block, :, 3 * PAIR + at : 3 * PAIR + at + HEAD] = inner.astype(BF16)
            inner = dots(slopes[...], acts[block, :, query], TN)
            backs[block, :, key] = inner.astype(BF16)

            def turn_back(part, start):
                turned = rotated(wide[part, mine_columns], cosine[part, :], -sine[part, :])
                backs[block, part, query] = (turned * pack[block, part, query].astype(F32)).astype(BF16)

            every_rows(rows, turn_back)

    for block in range(TP):
        attend(block)
        produce(4 + block)
        prefetch(5 + block)
        relay(2, 12)

    add_chips()
    produce(8)
    prefetch(9)
    relay(2, 12)
    finish_states()

    for block in range(TP):
        for half in range(2):
            at = half * HEAD
            head = 2 * block + half
            query, key, value = [slice(kind * PAIR + at, kind * PAIR + at + HEAD) for kind in range(3)]
            scores[:, 0:HEAD] = dots(acts[block, :, value], later[head], NT)
            scores[:, HEAD : 2 * HEAD] = dots(acts[block, :, key], later[head], NN)

            def finish_rows(part, start, block=block, half=half, at=at, key=key, value=value):
                number = row_numbers(start)
                valid = jnp.where(jnp.where(number >= edge, 1, 0) == last, 1.0, 0.0)
                fade = jnp.exp(-rate_of(block, half) * (rows - 1 - number).astype(F32)) * valid
                keys = backs[block, part, key].astype(F32) + fade * scores[part, 0:HEAD]
                turned = rotated(keys, cosine[part, :], -sine[part, :])
                backs[block, part, key] = (turned * pack[block, part, key].astype(F32)).astype(BF16)
                values = acts[block, part, 3 * PAIR + at : 3 * PAIR + at + HEAD].astype(F32)
                backs[block, part, value] = (values + fade * scores[part, HEAD : 2 * HEAD]).astype(BF16)

            every_rows(rows, finish_rows)
        backs_keep_copy(block).start()
        backs_copy(block).start()
        for part in range(2):
            index = at_tile + 2 * block + part
            term = dots(backs[block, :, part * half_d : part * half_d + half_d], tile(index), NN)
            if block or part:
                wide[...] += term
            else:
                wide[...] = term
            tile_next(index)
        if block == 0:
            for index in range(SEQ):
                hidden_load(index).start()
        if block == 1:
            produce(9)
            prefetch(10)
    relay(12, 12)
    for index in range(SEQ):
        hidden_load(index).wait()

    def input_rows(part, start):
        values = acts[0, part, :].astype(F32)
        scale = lax.rsqrt(jnp.mean(values * values, axis=-1, keepdims=True) + EPSILON)
        unit = values * scale
        grad = wide[part, :]
        inner = jnp.mean(grad * unit, axis=-1, keepdims=True)
        grad = mid[part, :] + scale * (grad - unit * inner)
        for index in range(SEQ):
            acts[1, part, plain(index)] = grad[:, place_of(index)].astype(BF16)

    for p in range(PIECES):

        @pl.loop(0, piece_rows // BLOCK)
        def _(block, p=p):
            start = p * piece_rows + block * BLOCK
            input_rows(pl.ds(pl.multiple_of(start, BLOCK), BLOCK), start)

        share_start(1, p)
    for index in range(10, ITEMS):
        produce(index)
        if index + 1 < ITEMS:
            prefetch(index + 1)
        if index >= 13:
            relay(2, 20)
        if index >= 19:
            relay(1)
    relay(len(relays))
    for now in range(ITEMS, ITEMS + LAG_5):
        advance(now)

    half_copy().wait_send()
    for block in range(TP):
        backs_copy(block).wait_send()
    close_states()
    for index, (kind, step) in enumerate(items):
        if index >= ITEMS - HELD:
            for copy in to_second(index):
                copy.wait_send()
        to_first(index).wait_send()
        if step:
            along(index, True).wait_send()
    for a in range(2):
        for p in range(PIECES):
            share_keep(a, p).wait()

            @pl.when(t < TP - 1)
            def _(a=a, p=p):
                share_copy(a, p, t, own_piece(a, p), True).wait_send()

            @pl.when(t > 0)
            def _(a=a, p=p):
                share_copy(a, p, t, own_piece(a, p), False).wait_send()
    for a, p, step in relays:
        owner = nearest(t, step)
        passed = passes(owner, True) | passes(owner, False)

        @pl.when(jnp.logical_not(passed))
        def _(a=a, p=p, owner=owner):
            share_copy(a, p, owner, piece(a, owner, p), True).wait_recv()

        for up in (True, False):

            @pl.when(passes(owner, up))
            def _(a=a, p=p, owner=owner, up=up):
                share_copy(a, p, owner, piece(a, owner, p), up).wait_send()


def backward(units, whole, kept, output, hidden_in, out_cotangent, incoming, inv_mix, inv_second, rates, cosine, sine, bounds):
    rows = output.shape[0]
    sizes = tuple(weight.shape[0] // TP for weight in whole) + (units,)
    dma = pltpu.SemaphoreType.DMA
    vmem = pl.BlockSpec(memory_space=pltpu.VMEM)
    anywhere = pl.BlockSpec(memory_space=pl.ANY)
    half_d = D // 2
    shape = jax.ShapeDtypeStruct
    tall = lambda height: shape((height, STRIPE), F32)
    scratch = [
        pltpu.VMEM((3, half_d, D), BF16),
        *[pltpu.VMEM((rows, D), BF16)] * 4,
        pltpu.VMEM((4, rows, half_d), BF16),
        *[pltpu.VMEM((TP, rows, 4 * PAIR), BF16)] * 3,
        pltpu.VMEM((rows, D), F32),
        pltpu.VMEM((rows, D), F32),
        pltpu.VMEM((rows, rows), F32),
        pltpu.VMEM((rows, rows), F32),
        pltpu.VMEM((rows, rows), BF16),
        pltpu.VMEM((rows, rows), BF16),
        pltpu.VMEM((rows, HEAD), BF16),
        pltpu.VMEM((2, 2, rows, units), BF16),
        pltpu.VMEM((HELD, 4, units, STRIPE), BF16),
        *state_scratch(),
    ]
    for count, height, extra in ((3 * TP, units, 3), (TP, sizes[1], 1), (2 * TP, half_d, 2)):
        scratch += [
            pltpu.VMEM((count, 2, height, STRIPE), BF16),
            pltpu.VMEM((count, height, STRIPE), BF16),
            pltpu.VMEM((count + extra, height, STRIPE), BF16),
        ]
    scratch += [
        dma((3,)),
        dma((2,)),
        dma((3,)),
        dma((TP,)),
        dma((TP,)),
        dma((TP,)),
        dma((5,)),
        dma((SEQ,)),
        dma((SEQ,)),
        dma((2, 2)),
        dma((ITEMS, 2)),
        dma((ITEMS, 2)),
        dma((ITEMS,)),
        dma((ITEMS,)),
        dma((ITEMS,)),
        dma((KINDS, TP)),
        dma((KINDS, TP)),
        dma((2, PIECES)),
        dma((2, PIECES, TP)),
        dma((2, PIECES, TP)),
        dma((2, PIECES, TP)),
    ]
    return pl.pallas_call(
        functools.partial(backward_kernel, rows, sizes),
        out_shape=[tall(units), tall(units), tall(units), tall(sizes[1]), tall(sizes[0])]
        + [shape((TP, rows, D), BF16)] * 2
        + [shape((TP, rows, 4 * PAIR), BF16)] * 2,
        in_specs=[anywhere] * 20 + [vmem] * 6 + [pl.BlockSpec(memory_space=pltpu.SMEM)],
        out_specs=[vmem] * 5 + [anywhere] * 4,
        scratch_shapes=scratch,
        compiler_params=pltpu.CompilerParams(
            collective_id=1, has_side_effects=True, vmem_limit_bytes=63 * 2**20
        ),
        name="backward",
    )(*whole, *kept, output, hidden_in, out_cotangent, incoming, inv_mix, inv_second, rates, cosine, sine, bounds)


def finish_kernel(output_in, input_in, qkvg_in, tall_in, output, input_grad, *refs):
    output[...] = output_in[...]
    input_grad[...] = input_in[...].astype(F32)

    @pl.when(pl.program_id(0) == 0)
    def _():
        for kind in range(4):
            refs[kind][...] = qkvg_in[kind * PAIR : kind * PAIR + PAIR, :].T
        refs[4][...] = tall_in[...]


def finish(output, input_grad, qkvg_grad, out_grad):
    rows = output.shape[1]
    steps = 2
    block = lambda: pl.BlockSpec((1, rows // steps, D), lambda step: (step // steps, step % steps, 0))
    fixed = lambda *shape: pl.BlockSpec(shape, lambda step: (0, 0))
    shape = jax.ShapeDtypeStruct
    return pl.pallas_call(
        finish_kernel,
        grid=(TP * steps,),
        out_shape=[
            shape(output.shape, BF16),
            shape(input_grad.shape, F32),
            *[shape((STRIPE, PAIR), F32)] * 4,
            shape(out_grad.shape, F32),
        ],
        in_specs=[block(), block(), fixed(4 * PAIR, STRIPE), fixed(*out_grad.shape)],
        out_specs=[block(), block(), *[fixed(STRIPE, PAIR)] * 4, fixed(*out_grad.shape)],
        name="finish",
    )(output, input_grad, qkvg_grad, out_grad)


def entering(value, axis, join, neutral, backward):
    count, mine = (lax.axis_size(axis), lax.axis_index(axis))
    pieces = jax.tree.map(lambda part: lax.all_gather(part, axis), value)
    if backward:
        pieces = jax.tree.map(lambda part: part[::-1], pieces)
        mine = count - 1 - mine
    subtotal = jax.tree.map(
        lambda part, zero: jnp.full_like(part, 0) + jnp.asarray(zero, part.dtype), value, neutral
    )

    def step(position, subtotal):
        longer = join(subtotal, jax.tree.map(lambda part: part[position], pieces))
        return jax.tree.map(lambda new, old: jnp.where(position < mine, new, old), longer, subtotal)

    return lax.fori_loop(0, count - 1, step, subtotal)


def swish_parts(pre_act):
    logistic = jax.nn.sigmoid(pre_act)
    return (pre_act * logistic, logistic * (1.0 + pre_act * (1.0 - logistic)))


def rotate(rows_in, cosine_table, sine_table, signed):
    halfway = rows_in.shape[-1] // 2
    front_half = rows_in[..., :halfway]
    back_half = rows_in[..., halfway:]
    return jnp.concatenate(
        [
            front_half * cosine_table - signed * back_half * sine_table,
            signed * front_half * sine_table + back_half * cosine_table,
        ],
        axis=-1,
    )


def combine_forward(earlier, following):
    return (earlier[0] * following[0], following[0][:, None, None] * earlier[1] + following[1])


def combine_backward(farther, nearer):
    return (farther[0] * nearer[0], nearer[1] + nearer[0][:, None, None] * farther[1])


def collect_weights(
    query_weight,
    key_weight,
    value_weight,
    gate_weight,
    out_weight,
    left_weight,
    right_weight,
    down_weight,
):
    return (
        lax.all_gather(query_weight, "seq", axis=0, tiled=True),
        lax.all_gather(key_weight, "seq", axis=0, tiled=True),
        lax.all_gather(value_weight, "seq", axis=0, tiled=True),
        lax.all_gather(gate_weight, "seq", axis=0, tiled=True),
        lax.all_gather(out_weight, "seq", axis=1, tiled=True),
        lax.all_gather(left_weight, "seq", axis=0, tiled=True),
        lax.all_gather(right_weight, "seq", axis=0, tiled=True),
        lax.all_gather(down_weight, "seq", axis=1, tiled=True),
    )


def state_prefix(factor, local_state):
    neutral = (jnp.ones_like(factor), jnp.zeros_like(local_state))
    return entering((factor, local_state), "seq", combine_forward, neutral, False)[1]


def state_suffix(factor, state_grad):
    neutral = (jnp.ones_like(factor), jnp.zeros_like(state_grad))
    return entering((factor, state_grad), "seq", combine_backward, neutral, True)[1]


def body(
    hidden_in,
    query_weight,
    key_weight,
    value_weight,
    gate_weight,
    out_weight,
    left_weight,
    right_weight,
    down_weight,
    decay_rate,
    seq_bounds,
    out_cotangent,
):
    row_count = hidden_in.shape[1]
    batch_count = hidden_in.shape[0]
    local_heads = decay_rate.shape[0]
    heads_shape = (row_count, local_heads, HEAD)
    device = lax.axis_index("seq")
    offsets = jnp.arange(row_count, dtype=jnp.int32)
    positions = device * row_count + offsets
    frequency = jnp.exp(
        jnp.arange(HEAD // 2, dtype=jnp.float32) * (-2.0 * math.log(10000.0) / HEAD)
    )
    angles = positions.astype(jnp.float32)[:, None] * frequency[None, :]
    cosine_table = jnp.cos(angles)[:, None, :]
    sine_table = jnp.sin(angles)[:, None, :]
    local_f = offsets.astype(jnp.float32)
    distance = local_f[:, None] - local_f[None, :]
    causal = distance >= 0.0
    distance_pos = jnp.maximum(distance, 0.0)
    accum = None
    outputs = []
    in_grads = []
    for batch_index in range(batch_count):
        gathered = collect_weights(
            query_weight,
            key_weight,
            value_weight,
            gate_weight,
            out_weight,
            left_weight,
            right_weight,
            down_weight,
        )
        query_full, key_full, value_full, gate_full, out_full, left_full, right_full, down_full = (
            gathered
        )
        boundary = seq_bounds[batch_index]
        segment = (positions >= boundary).astype(jnp.int32)
        before = (device * row_count - 1 >= boundary).astype(jnp.int32)
        last_segment = segment[row_count - 1]
        allowed = causal & (segment[:, None] == segment[None, :])
        decay = jnp.where(
            allowed[None], jnp.exp(-decay_rate[:, None, None] * distance_pos[None]), 0.0
        )
        coef_in = (
            jnp.exp(-decay_rate[None, :] * (local_f[:, None] + 1.0))
            * (segment == before).astype(jnp.float32)[:, None]
        )
        weight_loc = (
            jnp.exp(-decay_rate[None, :] * (row_count - 1.0 - local_f)[:, None])
            * (segment == last_segment).astype(jnp.float32)[:, None]
        )
        factor = jnp.where(last_segment == before, jnp.exp(-decay_rate * row_count), 0.0)
        input_rows = hidden_in[batch_index].astype(jnp.float32)
        inv_first = lax.rsqrt(jnp.mean(input_rows * input_rows, axis=-1, keepdims=True) + EPSILON)
        unit_first = input_rows * inv_first
        normed_first = unit_first.astype(jnp.bfloat16)
        query_pre = jnp.dot(normed_first, query_full, preferred_element_type=jnp.float32)
        key_pre = jnp.dot(normed_first, key_full, preferred_element_type=jnp.float32)
        value_pre = jnp.dot(normed_first, value_full, preferred_element_type=jnp.float32)
        gate_pre = jnp.dot(normed_first, gate_full, preferred_element_type=jnp.float32)
        query_act, query_slope = swish_parts(query_pre)
        key_act, key_slope = swish_parts(key_pre)
        query_rot = rotate(query_act.reshape(heads_shape), cosine_table, sine_table, 1.0).astype(
            jnp.bfloat16
        )
        key_rot = rotate(key_act.reshape(heads_shape), cosine_table, sine_table, 1.0).astype(
            jnp.bfloat16
        )
        value_rows = value_pre.astype(jnp.bfloat16).reshape(heads_shape)
        query_wide = query_rot.astype(jnp.float32)
        key_wide = key_rot.astype(jnp.float32)
        value_wide = value_rows.astype(jnp.float32)
        scores = jnp.einsum("ihe,jhe->hij", query_rot, key_rot, preferred_element_type=jnp.float32)
        attn_weights = (scores * decay).astype(jnp.bfloat16)
        inner_out = jnp.einsum(
            "hij,jhe->ihe", attn_weights, value_rows, preferred_element_type=jnp.float32
        )
        local_state = jnp.einsum(
            "jhe,jhf->hef",
            key_wide * weight_loc[:, :, None],
            value_wide,
            precision=HIGHEST_PRECISION,
        )
        incoming = state_prefix(factor, local_state)
        outer_out = coef_in[:, :, None] * jnp.einsum(
            "ihe,hef->ihf", query_wide, incoming, precision=HIGHEST_PRECISION
        )
        mixed_heads = (inner_out + outer_out).reshape(row_count, local_heads * HEAD)
        total_sq = lax.psum(jnp.sum(mixed_heads * mixed_heads, axis=-1), "tp")
        inv_mix = lax.rsqrt(total_sq / D + EPSILON)[:, None]
        unit_mix = mixed_heads * inv_mix
        gate_mix = (unit_mix * gate_pre).astype(jnp.bfloat16)
        attn_sum = lax.psum(jnp.dot(gate_mix, out_full, preferred_element_type=jnp.float32), "tp")
        resid_mid = input_rows + attn_sum
        inv_second = lax.rsqrt(jnp.mean(resid_mid * resid_mid, axis=-1, keepdims=True) + EPSILON)
        unit_second = resid_mid * inv_second
        normed_second = unit_second.astype(jnp.bfloat16)
        left_pre = jnp.dot(normed_second, left_full, preferred_element_type=jnp.float32)
        right_pre = jnp.dot(normed_second, right_full, preferred_element_type=jnp.float32)
        glu_product = (left_pre * right_pre).astype(jnp.bfloat16)
        glu_out = lax.psum(
            jnp.dot(glu_product, down_full, preferred_element_type=jnp.float32), "tp"
        )
        outputs.append((resid_mid + glu_out).astype(jnp.bfloat16))
        glu_cot = out_cotangent[batch_index]
        product_grad = jnp.einsum(
            "cd,fd->cf", glu_cot, down_full, preferred_element_type=jnp.float32
        )
        left_back = (product_grad * right_pre).astype(jnp.bfloat16)
        right_back = (product_grad * left_pre).astype(jnp.bfloat16)
        second_part = jnp.einsum(
            "cf,df->cd", left_back, left_full, preferred_element_type=jnp.float32
        ) + jnp.einsum("cf,df->cd", right_back, right_full, preferred_element_type=jnp.float32)
        second_back = lax.psum(second_part, "tp")
        mid_grad = glu_cot.astype(jnp.float32) + inv_second * (
            second_back - unit_second * jnp.mean(second_back * unit_second, axis=-1, keepdims=True)
        )
        attn_cot = mid_grad.astype(jnp.bfloat16)
        gate_mix_grad = jnp.einsum(
            "cd,kd->ck", attn_cot, out_full, preferred_element_type=jnp.float32
        )
        gate_back = (gate_mix_grad * unit_mix).astype(jnp.bfloat16)
        unit_mix_grad = gate_mix_grad * gate_pre
        mix_dot = lax.psum(jnp.sum(unit_mix_grad * unit_mix, axis=-1), "tp")
        heads_grad = (
            (inv_mix * (unit_mix_grad - unit_mix * (mix_dot / D)[:, None]))
            .astype(jnp.bfloat16)
            .reshape(heads_shape)
        )
        pair_grad = jnp.einsum(
            "ihe,jhe->hij", heads_grad, value_rows, preferred_element_type=jnp.float32
        ).astype(jnp.bfloat16)
        score_grad = pair_grad.astype(jnp.float32) * decay
        query_inner = jnp.einsum("hij,jhe->ihe", score_grad, key_wide, precision=HIGHEST_PRECISION)
        key_inner = jnp.einsum("hij,ihe->jhe", score_grad, query_wide, precision=HIGHEST_PRECISION)
        value_inner = jnp.einsum(
            "hij,ihe->jhe", attn_weights, heads_grad, preferred_element_type=jnp.float32
        )
        scaled_grad = heads_grad.astype(jnp.float32) * coef_in[:, :, None]
        query_outer = jnp.einsum("ihf,hef->ihe", scaled_grad, incoming, precision=HIGHEST_PRECISION)
        state_grad = jnp.einsum(
            "ihe,ihf->hef", query_wide, scaled_grad, precision=HIGHEST_PRECISION
        )
        later_grad = state_suffix(factor, state_grad)
        key_state = weight_loc[:, :, None] * jnp.einsum(
            "jhf,hef->jhe", value_wide, later_grad, precision=HIGHEST_PRECISION
        )
        value_state = weight_loc[:, :, None] * jnp.einsum(
            "jhe,hef->jhf", key_wide, later_grad, precision=HIGHEST_PRECISION
        )
        query_back = (
            rotate(query_inner + query_outer, cosine_table, sine_table, -1.0).reshape(row_count, -1)
            * query_slope
        ).astype(jnp.bfloat16)
        key_back = (
            rotate(key_inner + key_state, cosine_table, sine_table, -1.0).reshape(row_count, -1)
            * key_slope
        ).astype(jnp.bfloat16)
        value_back = (value_inner + value_state).reshape(row_count, -1).astype(jnp.bfloat16)
        fresh = (
            jnp.einsum("cd,ck->dk", normed_first, query_back, preferred_element_type=jnp.float32),
            jnp.einsum("cd,ck->dk", normed_first, key_back, preferred_element_type=jnp.float32),
            jnp.einsum("cd,ck->dk", normed_first, value_back, preferred_element_type=jnp.float32),
            jnp.einsum("cd,ck->dk", normed_first, gate_back, preferred_element_type=jnp.float32),
            jnp.einsum("ck,cd->kd", gate_mix, attn_cot, preferred_element_type=jnp.float32),
            jnp.einsum("cd,cf->df", normed_second, left_back, preferred_element_type=jnp.float32),
            jnp.einsum("cd,cf->df", normed_second, right_back, preferred_element_type=jnp.float32),
            jnp.einsum("cf,cd->fd", glu_product, glu_cot, preferred_element_type=jnp.float32),
        )
        if accum is None:
            accum = list(fresh)
        else:
            accum = [older + newer for older, newer in zip(accum, fresh)]
        total = jnp.einsum("ck,dk->cd", query_back, query_full, preferred_element_type=jnp.float32)
        total = total + jnp.einsum(
            "ck,dk->cd", key_back, key_full, preferred_element_type=jnp.float32
        )
        total = total + jnp.einsum(
            "ck,dk->cd", value_back, value_full, preferred_element_type=jnp.float32
        )
        first_back = lax.psum(
            total
            + jnp.einsum("ck,dk->cd", gate_back, gate_full, preferred_element_type=jnp.float32),
            "tp",
        )
        input_back = mid_grad + inv_first * (
            first_back - unit_first * jnp.mean(first_back * unit_first, axis=-1, keepdims=True)
        )
        in_grads.append(input_back)
    summed = (
        lax.psum_scatter(accum[0], "seq", scatter_dimension=0, tiled=True),
        lax.psum_scatter(accum[1], "seq", scatter_dimension=0, tiled=True),
        lax.psum_scatter(accum[2], "seq", scatter_dimension=0, tiled=True),
        lax.psum_scatter(accum[3], "seq", scatter_dimension=0, tiled=True),
        lax.psum_scatter(accum[4], "seq", scatter_dimension=1, tiled=True),
        lax.psum_scatter(accum[5], "seq", scatter_dimension=0, tiled=True),
        lax.psum_scatter(accum[6], "seq", scatter_dimension=0, tiled=True),
        lax.psum_scatter(accum[7], "seq", scatter_dimension=1, tiled=True),
    )
    return (
        jnp.stack(outputs),
        jnp.stack(in_grads),
        summed[0],
        summed[1],
        summed[2],
        summed[3],
        summed[4],
        summed[5],
        summed[6],
        summed[7],
    )


def fused_body(
    hidden_in,
    query_weight,
    key_weight,
    value_weight,
    gate_weight,
    out_weight,
    left_weight,
    right_weight,
    down_weight,
    decay_rate,
    seq_bounds,
    out_cotangent,
):
    row_count = hidden_in.shape[1]
    device = lax.axis_index("seq")
    positions = device * row_count + jnp.arange(row_count, dtype=jnp.int32)
    frequency = jnp.exp(jnp.arange(HEAD // 2, dtype=F32) * (-2.0 * math.log(10000.0) / HEAD))
    angles = positions.astype(F32)[:, None] * jnp.tile(frequency, 2)[None, :]
    sign = jnp.where(jnp.arange(HEAD) < HEAD // 2, -1.0, 1.0).astype(F32)
    cosine, sine = jnp.cos(angles), jnp.sin(angles) * sign[None, :]
    results = forward(
        (query_weight, key_weight, value_weight, gate_weight),
        (out_weight, left_weight.T, right_weight.T, down_weight),
        hidden_in,
        out_cotangent,
        cosine,
        sine,
        decay_rate,
        seq_bounds,
    )
    whole, kept, (incoming, inv_mix, inv_second, rates, output) = results[:2], results[2:17], results[17:]
    down_grad, left_grad, right_grad, out_grad, qkvg_grad, output, input_grad = backward(
        down_weight.shape[0],
        whole,
        kept,
        output,
        hidden_in,
        out_cotangent,
        incoming,
        inv_mix,
        inv_second,
        rates,
        cosine,
        sine,
        seq_bounds,
    )[:7]
    output, input_grad, query_grad, key_grad, value_grad, gate_grad, out_grad = finish(
        output, input_grad, qkvg_grad, out_grad
    )
    return (
        output,
        input_grad,
        query_grad,
        key_grad,
        value_grad,
        gate_grad,
        out_grad,
        left_grad.T,
        right_grad.T,
        down_grad,
    )


def solution(mesh):
    fits = mesh.shape["seq"] == SEQ and mesh.shape["tp"] == TP
    return jax.shard_map(
        fused_body if fits else body,
        mesh=mesh,
        in_specs=(
            P(None, "seq", None),
            P("seq", "tp"),
            P("seq", "tp"),
            P("seq", "tp"),
            P("seq", "tp"),
            P("tp", "seq"),
            P("seq", "tp"),
            P("seq", "tp"),
            P("tp", "seq"),
            P("tp"),
            P(),
            P(None, "seq", None),
        ),
        out_specs=(
            P(None, "seq", None),
            P(None, "seq", None),
            P("seq", "tp"),
            P("seq", "tp"),
            P("seq", "tp"),
            P("seq", "tp"),
            P("tp", "seq"),
            P("seq", "tp"),
            P("seq", "tp"),
            P("tp", "seq"),
        ),
        check_vma=False,
    )
```

```python
import functools
import math

import jax
import jax.numpy as jnp
from jax import lax
from jax.experimental import pallas as pl
from jax.experimental.pallas import tpu as pltpu
from jax.sharding import PartitionSpec as P

D = 1024
HEAD = 128


EPSILON = 1e-06
HIGHEST_PRECISION = lax.Precision.HIGHEST
MESH = pl.DeviceIdType.MESH
BF16 = jnp.bfloat16
F32 = jnp.float32

SEQ = 8
TP = 4
STRIPE = 128
PAIR = 2 * HEAD
BLOCK = 32

NN = ((1,), (0,))
NT = ((1,), (1,))
TN = ((0,), (0,))


def dots(left, right, dims):
    return lax.dot_general(left, right, (dims, ((), ())), preferred_element_type=F32)


def place():
    s, t = lax.axis_index("seq"), lax.axis_index("tp")
    core = s % 2
    column = (s // 2) % 2
    line = s // 4
    other = s + 1 - 2 * core
    across_x = s + 2 * (1 - 2 * column)
    across_y = s + 4 * (1 - 2 * line)
    first = across_x + core * (across_y - across_x)
    second = across_y + core * (across_x - across_y)
    diagonal = across_x + across_y - s
    return s, t, other, first, second, diagonal


def nearest(t, step):
    flip = t // 2
    low = t + flip * (3 - 2 * t)
    swap = low * (1 - step // 2)
    index = step + swap * (1 - 2 * step)
    return index + flip * (3 - 2 * index)


def stripe(index):
    return pl.ds(pl.multiple_of((index % 2 * (SEQ // 2) + index // 2) * STRIPE, STRIPE), STRIPE)


def plain(index):
    return slice(index * STRIPE, index * STRIPE + STRIPE)


def place_of(index):
    at = (index % 2 * (SEQ // 2) + index // 2) * STRIPE
    return slice(at, at + STRIPE)


def rows_of(index, size):
    return pl.ds(pl.multiple_of(index * size, size), size)


def remote(src, dst, send, receive, device):
    return pltpu.make_async_remote_copy(
        src_ref=src, dst_ref=dst, send_sem=send, recv_sem=receive, device_id=device, device_id_type=MESH
    )


def greet(s, t, around):
    barrier = pltpu.get_barrier_semaphore()
    for step in range(1, TP):
        pl.semaphore_signal(barrier, inc=1, device_id=(s, (t + step) % TP), device_id_type=MESH)
    for device in around:
        pl.semaphore_signal(barrier, inc=1, device_id=(device, t), device_id_type=MESH)
    pl.semaphore_wait(barrier, TP - 1 + len(around))


def every_rows(count, body, size=BLOCK):
    @pl.loop(0, count // size)
    def _(block):
        body(pl.ds(pl.multiple_of(block * size, size), size), block * size)


def flag(condition):
    return jnp.where(condition, 1.0, 0.0).astype(F32)


def rotated(values, cosine, sine):
    return values * cosine + pltpu.roll(values, HEAD // 2, 1) * sine


def state_exchange(rows, boundary, refs, rates, scale, toward, source_of):
    state, pair_land, chip_state, chip_land, partial, result, pair_sem, chip_send, chip_recv, partial_sem = refs
    s, t, other, first, second, diagonal = place()
    core, half = s % 2, TP
    around = (first, second, diagonal)
    ours, theirs = pl.ds(core * half, half), pl.ds((1 - core) * half, half)

    def pair_copy():
        return remote(state.at[theirs], pair_land, pair_sem.at[0], pair_sem.at[1], (other, t))

    def chip_copy(part):
        return remote(chip_state, chip_land.at[part], chip_send.at[part], chip_recv.at[part], (around[part], t))

    def partial_copy():
        return remote(partial, result.at[ours], partial_sem.at[0], partial_sem.at[1], (other, t))

    def rate_of(number):
        head = core * half + number
        return rates[head // 2, pl.ds(head % 2, 1), :]

    def begin():
        pair_copy().start()

    def add_pair():
        pair_copy().wait_recv()

        @pl.loop(0, half)
        def _(number):
            rate, target = rate_of(number), toward(s // 2)
            total = scale(target, s, rate) * state[core * half + number].astype(F32)
            total += scale(target, other, rate) * pair_land[number].astype(F32)
            chip_state[number] = total.astype(BF16)

        for part in range(3):
            chip_copy(part).start()

    def add_chips():
        for part in range(3):
            chip_copy(part).wait_recv()

        @pl.loop(0, half)
        def _(number):
            rate = rate_of(number)
            mine, its = state[core * half + number].astype(F32), pair_land[number].astype(F32)
            here = scale(s, s, rate) * mine + scale(s, other, rate) * its
            there = scale(other, s, rate) * mine + scale(other, other, rate) * its
            for part in range(3):
                values = chip_land[part, number].astype(F32)
                source = source_of(around[part] // 2)
                here += scale(s, source, rate) * values
                there += scale(other, source, rate) * values
            result[core * half + number] = here.astype(BF16)
            partial[number] = there.astype(BF16)

        partial_copy().start()

    def finish():
        partial_copy().wait_recv()

    def close():
        pair_copy().wait_send()
        for part in range(3):
            chip_copy(part).wait_send()
        partial_copy().wait_send()

    return begin, add_pair, add_chips, finish, close


def state_scratch():
    dma = pltpu.SemaphoreType.DMA
    return [
        pltpu.VMEM((2 * TP, HEAD, HEAD), BF16),
        pltpu.VMEM((TP, HEAD, HEAD), BF16),
        pltpu.VMEM((TP, HEAD, HEAD), BF16),
        pltpu.VMEM((3, TP, HEAD, HEAD), BF16),
        pltpu.VMEM((TP, HEAD, HEAD), BF16),
        pltpu.VMEM((2 * TP, HEAD, HEAD), BF16),
        dma((2,)),
        dma((3,)),
        dma((3,)),
        dma((2,)),
    ]


LAG_B, LAG_C = 2, 4

def forward_kernel(rows, sizes, *refs):
    heads_in, refs = refs[:4], refs[4:]
    shards, refs = refs[:4], refs[4:]
    (hidden_in, cot_in, cosine, sine, rate_in, bounds), refs = refs[:6], refs[6:]
    whole_out, refs = refs[:2], refs[2:]
    (acts_out, pack_out, normed_out, second_out, glu_out, left_out, right_out, glu_other, left_other, right_other,
     gated_other, normed_other, second_other, cot_other, back_out,
     incoming_out, inv_mix_out, inv_second_out, rate_out, result_out), refs = refs[:20], refs[20:]
    whole, refs = refs[:5], refs[5:]
    (acts, pack, normed, hidden, cot, second_normed, sides, back, wide, mixed, distance, scores, weights,
     inv_mix, inv_second, rates, heads_shard), refs = refs[:17], refs[17:]
    exchange, refs = refs[:10], refs[10:]
    state, incoming = exchange[0], exchange[5]
    shards = (heads_shard, *shards)
    (local_sem, up_sem, down_sem, line_sem, down_send, down_recv, send_sem, first_sem, second_sem, other_sem, rate_send, rate_recv,
     copy_sem, side_sem, side_send, side_recv, half_send, half_recv,
     hidden_sem, cot_sem) = refs
    s, t, other, first, second, diagonal = place()
    units, beside = sizes[2], wide.shape[1] // 3
    theirs = rows_of(1 - s % 2, D // 2)
    shift = other - s
    for kind in range(4):
        heads_shard[kind * PAIR : kind * PAIR + PAIR, :] = heads_in[kind][...].T
    greet(s, t, (other, first, second, diagonal))

    def hidden_load(index):
        return pltpu.make_async_copy(
            hidden_in.at[t, :, plain(index)], hidden.at[:, place_of(index)], hidden_sem.at[index]
        )

    def cot_load(index):
        return pltpu.make_async_copy(cot_in.at[t, :, plain(index)], cot.at[:, place_of(index)], cot_sem.at[index])

    def half_copy(part):
        src, dst = (
            (normed.at[:, theirs], normed_other),
            (second_normed.at[:, theirs], second_other),
            (cot.at[:, theirs], cot_other),
            (pack.at[:, :, 2 * PAIR : 3 * PAIR], gated_other),
        )[part]
        return remote(src, dst, half_send.at[part], half_recv.at[part], (other, t))

    for index in range(SEQ):
        hidden_load(index).start()

    cut = -(-units // (2 * HEAD)) * HEAD
    items = (
        [(0, 0), (4, 0)]
        + [(0, step) for step in range(1, TP)]
        + [(1, step) for step in range(TP)]
        + [(w, step) for step in range(TP) for w in (2, 3)]
    )
    items = [(w, step, 0, sizes[w]) for w, step in items]
    items[-1:] = [(3, TP - 1, 0, cut), (3, TP - 1, cut, units)]
    columns = (s, first, second, diagonal)

    def spot(w, owner, column, low=0, high=None):
        high = sizes[w] if high is None else high
        return whole[w].at[pl.ds(pl.multiple_of(owner * sizes[w] + low, 16), high - low), stripe(column)]

    def source(w, step, owner, low=0, high=None):
        if step:
            return spot(w, owner, s, low, high)
        return shards[w].at[pl.ds(low, (sizes[w] if high is None else high) - low), :]

    def own_copy(w):
        return pltpu.make_async_copy(shards[w], spot(w, t, s), local_sem.at[w])

    def plane_copies(index):
        w, step, low, high = items[index]
        owner = nearest(t, step)
        src, dst = source(w, step, owner, low, high), spot(w, owner, s, low, high)
        return (
            remote(src, dst, send_sem.at[index, 0], first_sem.at[index], (first, t)),
            remote(src, dst, send_sem.at[index, 1], second_sem.at[index, 0], (second, t)),
            remote(src, dst, send_sem.at[index, 2], other_sem.at[index, 0], (other, t)),
        )

    def found(index, column):
        w, step, low, high = items[index]
        return spot(w, nearest(t, step), column, low, high)

    def relay_copies(index):
        src = found(index, first)
        return (
            remote(src, src, send_sem.at[index, 3], second_sem.at[index, 1], (second, t)),
            remote(src, src, send_sem.at[index, 4], other_sem.at[index, 1], (other, t)),
        )

    def last_copies(index):
        near, far = found(index, second), found(index, diagonal)
        return (
            remote(near, near, send_sem.at[index, 5], other_sem.at[index, 2], (other, t)),
            remote(far, far, send_sem.at[index, 6], other_sem.at[index, 3], (other, t)),
        )

    def parcel(w, step, column, up):
        owner = nearest(t, step)
        dst = spot(w, owner, columns[column])
        src = shards[w] if step == 0 and column == 0 else dst
        sem, device = (up_sem, t + 1) if up else (down_sem, t - 1)
        return remote(src, dst, sem.at[w, owner, column], line_sem.at[w, owner, column], (s, device))

    def across(step, column):
        block = spot(4, nearest(t, step), columns[column])
        return remote(block, block, down_send.at[step, column], down_recv.at[step, column], (other, t))

    def goes(step, up):
        owner = nearest(t, step)
        if step == 0:
            return t < TP - 1 if up else t > 0
        return (owner < t) & (t < TP - 1) if up else (owner > t) & (t > 0)

    def set_out(w, column=0):
        for up in (True, False):

            @pl.when(goes(0, up))
            def _(up=up):
                parcel(w, 0, column, up).start()

    inside = (t > 0) & (t < TP - 1)

    def pass_on(w, step, column=0, where=None):
        def act():
            parcel(w, step, column, True).wait_recv()
            for up in (True, False):

                @pl.when(goes(step, up))
                def _(up=up):
                    parcel(w, step, column, up).start()

            if w == 4:
                across(step, column).start()

        if where is None:
            act()
        else:
            pl.when(where)(act)

    down_parcels = [(step, column) for step in range(1, TP) for column in range(4)]

    def line_pass(now, where):
        if now + 2 < len(items):
            w, step, low, high = items[now + 2]
            if step and low == 0:
                pass_on(w, step, 0, where)

    def down_pass(now):
        for at, where in ((now - 6, inside), (now - 8, jnp.logical_not(inside))):
            if 0 <= at < len(down_parcels):
                pass_on(4, *down_parcels[at], where)

    relayed, ended = [], []

    def stage_a(index):
        if items[index][1] == 0:
            own_copy(items[index][0]).start()
        for copy in plane_copies(index):
            copy.start()

    def stage_b(until):
        while len(relayed) <= min(until, len(items) - 1):
            index = len(relayed)
            relayed.append(index)
            block = found(index, first)
            remote(block, block, send_sem.at[index, 0], first_sem.at[index], (first, t)).wait_recv()
            for copy in relay_copies(index):
                copy.start()

    def stage_c(until):
        while len(ended) <= min(until, len(items) - 1):
            index = len(ended)
            ended.append(index)
            for part, column in enumerate((second, diagonal)):
                block = found(index, column)
                remote(block, block, send_sem.at[index, 1], second_sem.at[index, part], (second, t)).wait_recv()
            for copy in last_copies(index):
                copy.start()

    def tick(now):
        stage_b(now - LAG_B)
        if now < len(items):
            stage_a(now)
        stage_c(now - LAG_C)
        if now == 5:
            set_out(2)
            set_out(3)
            line_pass(now - 1, None)
            line_pass(now, inside)
        line_pass(now + 1, inside)
        line_pass(now, jnp.logical_not(inside))
        down_pass(now)

    keeps = []

    def keep(src, dst):
        copy = functools.partial(pltpu.make_async_copy, src, dst, copy_sem.at[len(keeps)])
        copy().start()
        keeps.append(copy)

    def ready(index):
        w, step, low, high = items[index]
        owner = nearest(t, step)
        if step == 0:
            own_copy(w).wait()
        for part, column in enumerate((other, second + shift, first + shift, diagonal + shift)):
            block = found(index, column)
            remote(block, block, send_sem.at[index, 2], other_sem.at[index, part], (other, t)).wait_recv()
        block = rows_of(owner, sizes[w])
        if w < 2:
            keep(whole[w].at[block, :], whole_out[w].at[block, :])
        return owner, block

    def down_ready(step):
        if step == 0:
            ready(1)
            return
        for column, index in enumerate((other, second + shift, first + shift, diagonal + shift)):
            block = spot(4, nearest(t, step), index)
            remote(block, block, down_send.at[step, column], down_recv.at[step, column], (other, t)).wait_recv()

    def rate_copy(step):
        return remote(rates.at[t], rates.at[t], rate_send.at[step - 1], rate_recv.at[step - 1], (s, (t + step) % TP))

    row = lax.broadcasted_iota(jnp.int32, (8, HEAD), 0)
    rates[t] = jnp.where(row == 0, rate_in[0], rate_in[1])
    for step in range(1, TP):
        rate_copy(step).start()
    stage_a(0)
    set_out(0)
    set_out(1)
    set_out(4)
    stage_a(1)
    boundary = bounds[t]
    edge = boundary - s * rows

    for index in range(SEQ):
        hidden_load(index).wait()
        cot_load(index).start()

    def prepare(part, start):
        values = hidden[part, :].astype(F32)
        scale = lax.rsqrt(jnp.mean(values * values, axis=-1, keepdims=True) + EPSILON)
        normed[part, :] = (values * scale).astype(BF16)
        row = lax.broadcasted_iota(jnp.int32, (BLOCK, rows), 0) + start
        column = lax.broadcasted_iota(jnp.int32, (BLOCK, rows), 1)
        apart = (column > row) | ((row >= edge) & (column < edge))
        distance[part, :] = jnp.where(apart, -1, row - column).astype(F32)

    every_rows(rows, prepare)
    keep(normed, normed_out)
    half_copy(0).start()
    for step in range(1, TP):
        here = rates.at[t]
        remote(here, here, rate_send.at[step - 1], rate_recv.at[step - 1], (s, t)).wait_recv()
    keep(rates, rate_out)

    before = jnp.where(s * rows - 1 >= boundary, 1, 0)
    last = jnp.where(s * rows + rows - 1 >= boundary, 1, 0)

    def rate_of(block, half):
        return rates[block, half : half + 1, :]

    def row_numbers(start, count=BLOCK):
        return lax.broadcasted_iota(jnp.int32, (count, HEAD), 0) + start

    def project(step, index):
        owner, block = ready(index)
        wide[:, 0:D] = dots(normed[...], whole[0][block, :], NT)

        def shape_rows(part, start):
            turn, lean = cosine[part, :], sine[part, :]
            for kind in range(2):
                for half in range(2):
                    at = kind * PAIR + half * HEAD
                    values = wide[part, at : at + HEAD]
                    logistic = 1.0 / (1.0 + jnp.exp(-values))
                    acts[owner, part, at : at + HEAD] = rotated(values * logistic, turn, lean).astype(BF16)
                    pack[owner, part, at : at + HEAD] = (
                        logistic * (1.0 + values * (1.0 - logistic))
                    ).astype(BF16)
            acts[owner, part, 2 * PAIR : 4 * PAIR] = wide[part, 2 * PAIR : 4 * PAIR].astype(BF16)
            number = row_numbers(start)
            valid = jnp.where(jnp.where(number >= edge, 1, 0) == last, 1.0, 0.0)
            for half in range(2):
                fade = jnp.exp(-rate_of(owner, half) * (rows - 1 - number).astype(F32)) * valid
                keys = acts[owner, part, PAIR + half * HEAD : PAIR + half * HEAD + HEAD].astype(F32)
                weights[part, half * HEAD : half * HEAD + HEAD] = (keys * fade).astype(BF16)

        every_rows(rows, shape_rows)
        for half in range(2):
            at = half * HEAD
            state[owner * 2 + half] = dots(
                weights[:, at : at + HEAD], acts[owner, :, 2 * PAIR + at : 2 * PAIR + at + HEAD], TN
            ).astype(BF16)

    def attend(step):
        owner = nearest(t, step)
        for half in range(2):
            at = half * HEAD
            rate = rates[owner, half : half + 1, :]
            for top in range(0, rows, PAIR):
                width = top + PAIR
                scores[0:PAIR, 0:width] = dots(
                    acts[owner, top : top + PAIR, at : at + HEAD], acts[owner, 0:width, PAIR + at : PAIR + at + HEAD], NT
                )

                def weigh(part, start, width=width, top=top, rate=rate):
                    for left in range(0, width, HEAD):
                        apart = distance[pl.ds(pl.multiple_of(start + top, BLOCK), BLOCK), left : left + HEAD]
                        fade = jnp.where(apart >= 0.0, jnp.exp(-rate * apart), 0.0)
                        weights[part, left : left + HEAD] = (scores[part, left : left + HEAD] * fade).astype(BF16)

                every_rows(PAIR, weigh)
                column = pl.ds(pl.multiple_of(owner * PAIR + at, HEAD), HEAD)
                mixed[top : top + PAIR, column] = dots(
                    weights[0:PAIR, 0:width], acts[owner, 0:width, 2 * PAIR + at : 2 * PAIR + at + HEAD], NN
                )

    def prefix_scale(block, source_block, rate):
        same = jnp.where((source_block + 1) * rows - 1 >= boundary, 1, 0) == jnp.where(block * rows - 1 >= boundary, 1, 0)
        usable = flag(source_block < block) * flag(same)
        gap = jnp.maximum(block - 1 - source_block, 0).astype(F32)
        return jnp.exp(-rate * (rows * gap)) * usable

    begin_states, add_pair, add_chips, finish_states, close_states = state_exchange(
        rows, boundary, exchange, rates, prefix_scale, lambda chip: 2 * chip + 2, lambda chip: 2 * chip + 1
    )

    def mix():
        finish_states()
        keep(incoming, incoming_out)
        for block in range(TP):
            for half in range(2):
                at = half * HEAD
                scores[:, at : at + HEAD] = dots(acts[block, :, at : at + HEAD], incoming[2 * block + half], NN)

            def add_outer(part, start, block=block):
                number = row_numbers(start)
                valid = jnp.where(jnp.where(number >= edge, 1, 0) == before, 1.0, 0.0)
                for half in range(2):
                    fade = jnp.exp(-rate_of(block, half) * (number + 1).astype(F32)) * valid
                    column = slice(block * PAIR + half * HEAD, block * PAIR + half * HEAD + HEAD)
                    mixed[part, column] += fade * scores[part, half * HEAD : half * HEAD + HEAD]

            every_rows(rows, add_outer)

        def gate_rows(part, start):
            values = mixed[part, :]
            scale = lax.rsqrt(jnp.mean(values * values, axis=-1, keepdims=True) + EPSILON)
            inv_mix[part, :] = jnp.broadcast_to(scale, (BLOCK, HEAD))
            values = values * scale
            for block in range(TP):
                column = slice(block * PAIR, block * PAIR + PAIR)
                gate = acts[block, part, 3 * PAIR : 4 * PAIR].astype(F32)
                pack[block, part, 2 * PAIR : 3 * PAIR] = (values[:, column] * gate).astype(BF16)
                pack[block, part, 3 * PAIR : 4 * PAIR] = values[:, column].astype(BF16)

        every_rows(rows, gate_rows, BLOCK)
        keep(acts, acts_out)
        keep(pack, pack_out)
        half_copy(3).start()
        keep(inv_mix, inv_mix_out)

    def project_out():
        for block in range(TP):
            term = dots(pack[block, :, 2 * PAIR : 3 * PAIR], whole[1][block * PAIR : block * PAIR + PAIR, :], NN)
            if block:
                wide[:, 0:D] += term
            else:
                wide[:, 0:D] = term

        def norm_rows(part, start):
            values = hidden[part, :].astype(F32) + wide[part, 0:D]
            mixed[part, :] = values
            scale = lax.rsqrt(jnp.mean(values * values, axis=-1, keepdims=True) + EPSILON)
            inv_second[part, :] = jnp.broadcast_to(scale, (BLOCK, HEAD))
            second_normed[part, :] = (values * scale).astype(BF16)

        every_rows(rows, norm_rows)
        keep(second_normed, second_out)
        half_copy(1).start()
        keep(inv_second, inv_second_out)

    def left_side(index):
        owner, block = ready(index)
        down_ready(items[index][1])
        wide[:, 0:units] = dots(second_normed[...], whole[2][block, :], NT)
        wide[:, 2 * beside : 2 * beside + units] = dots(cot[...], whole[4][block, :], NT)

    def side_copies(slot, owner):
        return [
            pltpu.make_async_copy(sides.at[slot, part], out.at[owner], side_sem.at[slot, part])
            for part, out in enumerate((glu_out, left_out, right_out))
        ]

    def side_remotes(slot, step):
        owner = nearest(t, step)
        return [
            remote(sides.at[slot, part], out.at[owner], side_send.at[slot, part], side_recv.at[step, part], (other, t))
            for part, out in enumerate((glu_other, left_other, right_other))
        ]

    def right_side(index):
        owner, block = ready(index)
        w, step, low, high = items[index]
        part_rows = pl.ds(pl.multiple_of(owner * units + low, 16), high - low)
        wide[:, beside + low : beside + high] = dots(second_normed[...], whole[3][part_rows, :], NT)
        slot = step % 2
        if step >= 2 and low == 0:
            for copy in side_copies(slot, nearest(t, step - 2)):
                copy.wait()
            for copy in side_remotes(slot, step - 2):
                copy.wait_send()

        def multiply(part, start):
            left, right = wide[part, low:high], wide[part, beside + low : beside + high]
            grad = wide[part, 2 * beside + low : 2 * beside + high]
            sides[slot, 0, part, low:high] = (left * right).astype(BF16)
            sides[slot, 1, part, low:high] = (grad * right).astype(BF16)
            sides[slot, 2, part, low:high] = (grad * left).astype(BF16)

        every_rows(rows, multiply)
        if high == units:
            for copy in side_copies(slot, owner) + side_remotes(slot, step):
                copy.start()
        mixed[...] += dots(sides[slot, 0, :, low:high], whole[4][part_rows, :], NN)
        term = dots(sides[slot, 1, :, low:high], whole[2][part_rows, :], NN) + dots(
            sides[slot, 2, :, low:high], whole[3][part_rows, :], NN
        )
        if step:
            back[...] += term
        else:
            back[...] = term

    stage_b(0)
    pass_on(0, 1)
    stage_a(2)
    stage_b(1)
    set_out(4, 1)
    stage_c(0)
    pass_on(0, 2)
    stage_a(3)
    stage_b(2)
    stage_c(1)
    set_out(4, 2)
    set_out(4, 3)
    pass_on(0, 3)
    stage_a(4)
    project(0, 0)
    tick(5)
    for step in range(1, TP):
        tick(5 + step)
        project(step, 1 + step)
    begin_states()
    for index in range(SEQ):
        cot_load(index).wait()
    half_copy(2).start()
    tick(9)
    add_pair()
    attend(0)
    tick(10)
    attend(1)
    tick(11)
    attend(2)
    attend(3)
    add_chips()
    tick(12)
    for index in range(5, 5 + TP):
        ready(index)
    mix()
    tick(13)
    project_out()
    for index in range(5 + TP, len(items)):
        if index > 5 + TP:
            tick(index + LAG_C)
        (left_side, right_side)[items[index][0] - 2](index)

    def finish(part, start):
        for index in range(SEQ):
            result_out[part, plain(index)] = mixed[part, place_of(index)].astype(BF16)

    keep(back, back_out)
    every_rows(rows, finish)

    for step in range(1, TP):
        rate_copy(step).wait_send()
    close_states()
    for copy in keeps:
        copy().wait()
    for part in range(4):
        half_copy(part).wait()
    for step in range(TP):
        for copy in side_remotes(step % 2, step):
            copy.wait_recv()
            if step >= 2:
                copy.wait_send()
        if step >= 2:
            for copy in side_copies(step % 2, nearest(t, step)):
                copy.wait()
    for index in range(len(items)):
        for copy in plane_copies(index) + relay_copies(index) + last_copies(index):
            copy.wait_send()
    for w in range(5):
        for step in range(TP):
            for column in range(4 if w == 4 else 1):
                for up in (True, False):

                    @pl.when(goes(step, up))
                    def _(w=w, step=step, column=column, up=up):
                        parcel(w, step, column, up).wait_send()

                if w == 4 and step:
                    across(step, column).wait_send()


KEPT = 20


def forward(heads_in, shards, hidden, cot, cosine, sine, rate, bounds):
    rows = hidden.shape[1]
    sizes = (4 * PAIR, *(shard.shape[0] for shard in shards))
    units = sizes[2]
    beside = -(-units // HEAD) * HEAD
    items = 4 * TP + 2
    dma = pltpu.SemaphoreType.DMA
    vmem = pl.BlockSpec(memory_space=pltpu.VMEM)
    anywhere = pl.BlockSpec(memory_space=pl.ANY)
    heads = 2 * TP
    shape = jax.ShapeDtypeStruct
    outs = [
        *[shape((TP * size, D), BF16) for size in sizes[:2]],
        *[shape((TP, rows, 4 * PAIR), BF16)] * 2,
        *[shape((rows, D), BF16)] * 2,
        *[shape((TP, rows, units), BF16)] * 6,
        shape((TP, rows, PAIR), BF16),
        *[shape((rows, D // 2), BF16)] * 3,
        shape((rows, D), F32),
        shape((heads, HEAD, HEAD), BF16),
        shape((rows, HEAD), F32),
        shape((rows, HEAD), F32),
        shape((TP, 8, HEAD), F32),
        shape((rows, D), BF16),
    ]
    return pl.pallas_call(
        functools.partial(forward_kernel, rows, sizes),
        out_shape=outs,
        in_specs=[vmem] * 4 + [anywhere] * 6 + [vmem] * 2 + [pl.BlockSpec(memory_space=pltpu.SMEM)] * 2,
        out_specs=[anywhere] * (len(outs) - 1) + [vmem],
        scratch_shapes=[pltpu.VMEM((TP * size, D), BF16) for size in sizes]
        + [
            *[pltpu.VMEM((TP, rows, 4 * PAIR), BF16)] * 2,
            *[pltpu.VMEM((rows, D), BF16)] * 4,
            pltpu.VMEM((2, 3, rows, units), BF16),
            pltpu.VMEM((rows, D), F32),
            pltpu.VMEM((rows, 3 * beside), F32),
            pltpu.VMEM((rows, D), F32),
            pltpu.VMEM((rows, rows), F32),
            pltpu.VMEM((rows, rows), F32),
            pltpu.VMEM((rows, rows), BF16),
            pltpu.VMEM((rows, HEAD), F32),
            pltpu.VMEM((rows, HEAD), F32),
            pltpu.VMEM((TP, 8, HEAD), F32),
            pltpu.VMEM((4 * PAIR, STRIPE), BF16),
            *state_scratch(),
            dma((5,)),
            dma((5, TP, 4)),
            dma((5, TP, 4)),
            dma((5, TP, 4)),
            dma((TP, 4)),
            dma((TP, 4)),
            dma((items, 7)),
            dma((items,)),
            dma((items, 2)),
            dma((items, 4)),
            dma((TP - 1,)),
            dma((TP - 1,)),
            dma((KEPT,)),
            dma((2, 3)),
            dma((2, 3)),
            dma((TP, 3)),
            dma((4,)),
            dma((4,)),
            dma((SEQ,)),
            dma((SEQ,)),
        ],
        compiler_params=pltpu.CompilerParams(
            collective_id=0, has_side_effects=True, vmem_limit_bytes=63 * 2**20
        ),
        name="forward",
    )(*heads_in, *shards, hidden, cot, cosine, sine, rate, bounds)


ROWS_STEP = 64
PIECES = 4
HELD = 6
LAG_2, LAG_3, LAG_4, HOP, LAG_5 = 2, 4, 6, 2, 13
KINDS = 6
BEFORE, EARLY, WAIT_1, WAIT_2 = 10, 2, 3, 9
ITEMS = KINDS * TP


def add_rows(target, *terms):
    rows = target.shape[0]

    @pl.loop(0, rows // ROWS_STEP)
    def _(block):
        part = pl.ds(pl.multiple_of(block * ROWS_STEP, ROWS_STEP), ROWS_STEP)
        total = terms[0][part, :].astype(F32)
        for term in terms[1:]:
            total = total + term[part, :].astype(F32)
        target[part, :] = total.astype(target.dtype)


def backward_kernel(rows, sizes, *refs):
    whole, refs = refs[:2], refs[2:]
    (acts_in, pack_in, normed_in, second_in, glu_own, left_own, right_own, glu_other, left_other, right_other,
     gated_other, normed_other, second_other, cot_other, back_in, output_in, hidden_in, cot_in,
     incoming, inv_mix, inv_second, rates, cosine, sine, bounds), refs = refs[:25], refs[25:]
    (down_grad, left_grad, right_grad, out_grad, qkvg_grad, output_whole, input_whole,
     backs_own, backs_other), refs = refs[:9], refs[9:]
    (tiles, cot, second_normed, normed, attn_cot, halves, acts, pack, backs, mid, wide, distance, scores,
     weights, slopes, faded, lhs, held), refs = refs[:18], refs[18:]
    exchange, refs = refs[:10], refs[10:]
    state, later = exchange[0], exchange[5]
    lands, refs = refs[:9], refs[9:]
    (tile_sem, half_sem, half_load_sem, backs_keep, backs_send, backs_recv, load_sem, cot_sem, hidden_sem, lhs_sem, second_send, second_recv,
     first_send, first_recv, line_send, below_recv, above_recv, share_local, share_up, share_down, share_recv) = refs
    s, t, other, first, second, diagonal = place()
    core = s % 2
    units = sizes[2]
    half_d = D // 2
    ours, theirs = rows_of(core, half_d), rows_of(1 - core, half_d)
    boundary = bounds[t]
    edge = boundary - s * rows
    before = jnp.where(s * rows - 1 >= boundary, 1, 0)
    last = jnp.where(s * rows + rows - 1 >= boundary, 1, 0)
    around = (first, second, diagonal)
    order = [3, 2, 1, 0]
    local = pltpu.make_async_copy

    done = set()

    def once(key, wait):
        if key not in done:
            done.add(key)
            wait()

    greet(s, t, (other, first, second, diagonal))

    def cot_load(index):
        return local(cot_in.at[t, :, plain(index)], cot.at[:, place_of(index)], cot_sem.at[index])

    def hidden_load(index):
        return local(hidden_in.at[t, :, plain(index)], acts.at[0, :, place_of(index)], hidden_sem.at[index])

    def second_load():
        return local(second_in, second_normed, load_sem.at[0])

    def normed_load():
        return local(normed_in, normed, load_sem.at[1])

    def acts_load():
        return local(acts_in, acts, load_sem.at[2])

    def pack_load():
        return local(pack_in, pack, load_sem.at[3])

    def back_load():
        return local(back_in, mid, load_sem.at[4])

    def half_load(part):
        return local((cot_other, second_other, normed_other)[part], halves.at[part], half_load_sem.at[part])

    def half_copy():
        return remote(attn_cot.at[:, theirs], halves.at[3], half_sem.at[0], half_sem.at[1], (other, t))

    tile_list = [(1, part) for part in range(2)] + [(0, part) for part in range(2 * TP)]

    def tile_load(index):
        w, at = tile_list[index]
        return local(whole[w].at[pl.ds(at * half_d, half_d), :], tiles.at[index % 3], tile_sem.at[index % 3])

    def tile(index):
        tile_load(index).wait()
        return tiles[index % 3]

    def tile_next(index):
        if index + 3 < len(tile_list):
            tile_load(index + 3).start()

    def backs_keep_copy(block):
        return local(backs.at[block], backs_own.at[block], backs_keep.at[block])

    def backs_copy(block):
        return remote(backs.at[block], backs_other.at[block], backs_send.at[block], backs_recv.at[block], (other, t))

    piece_rows = rows // PIECES
    shares = ((output_in, output_whole), (acts.at[1], input_whole))

    def piece(a, owner, p):
        return shares[a][1].at[owner, pl.ds(p * piece_rows, piece_rows), :]

    def own_piece(a, p):
        return shares[a][0].at[pl.ds(p * piece_rows, piece_rows), :]

    def share_copy(a, p, owner, src, up):
        sem, target = (share_up, t + 1) if up else (share_down, t - 1)
        return remote(src, piece(a, owner, p), sem.at[a, p, owner], share_recv.at[a, p, owner], (s, target))

    def share_keep(a, p):
        return local(own_piece(a, p), piece(a, t, p), share_local.at[a, p])

    def share_start(a, p):
        @pl.when(t < TP - 1)
        def _():
            share_copy(a, p, t, own_piece(a, p), True).start()

        @pl.when(t > 0)
        def _():
            share_copy(a, p, t, own_piece(a, p), False).start()

        share_keep(a, p).start()

    relays = [
        (a, p, step) for a in range(2) for steps in ((1, 2), (3,)) for p in range(PIECES) for step in steps
    ]
    relayed = []

    def passes(owner, up):
        return (owner < t) & (t < TP - 1) if up else (owner > t) & (t > 0)

    def relay(limit, until=len(relays)):
        for _ in range(limit):
            if len(relayed) >= until:
                return
            a, p, step = relays[len(relayed)]
            relayed.append(1)
            owner = nearest(t, step)
            for up in (True, False):

                @pl.when(passes(owner, up))
                def _(up=up):
                    share_copy(a, p, owner, piece(a, owner, p), up).wait_recv()
                    share_copy(a, p, owner, piece(a, owner, p), up).start()

    items = (
        [(0, step) for step in order]
        + [(kind, step) for step in order for kind in (1, 2)]
        + [(3, step) for step in order]
        + [(kind, step) for step in order for kind in (4, 5)]
    )
    heights = (units, units, units, sizes[1], half_d, half_d)

    def lands_of(index):
        kind, step = items[index]
        owner = nearest(t, step)
        group, base, extra = ((0, kind * TP, 3 * TP + kind), (1, 0, TP), (2, (kind - 4) * TP, 2 * TP + kind - 4))[
            0 if kind < 3 else 1 if kind == 3 else 2
        ]
        return owner, lands[3 * group : 3 * group + 3], base + owner, extra

    def own_source(kind, owner):
        if kind == 0:
            return glu_own.at[owner], glu_other.at[owner]
        if kind == 1:
            return left_own.at[owner], left_other.at[owner]
        if kind == 2:
            return right_own.at[owner], right_other.at[owner]
        if kind == 3:
            return pack_in.at[owner, :, 2 * PAIR : 3 * PAIR], gated_other.at[owner]
        part = slice((kind - 4) * half_d, (kind - 3) * half_d)
        return backs_own.at[owner, :, part], backs_other.at[owner, :, part]

    def lhs_loads(index):
        kind, step = items[index]
        slot = index % 2
        return [
            local(src, lhs.at[slot, part, :, pl.ds(0, heights[kind])], lhs_sem.at[slot, part])
            for part, src in enumerate(own_source(kind, nearest(t, step)))
        ]

    def prefetch(index):
        kind, step = items[index]
        owner = nearest(t, step)
        if kind >= 4:
            once(("backs", step), lambda: backs_keep_copy(owner).wait())
            once(("backs_other", step), lambda: backs_copy(owner).wait_recv())
        for copy in lhs_loads(index):
            copy.start()

    def to_second(index):
        kind = items[index][0]
        owner, (second_land, first_land, line_land), at, extra = lands_of(index)
        return [
            remote(
                held.at[index % HELD, column // 2, pl.ds(0, heights[kind]), :],
                second_land.at[at, part],
                second_send.at[index, part],
                second_recv.at[index, part],
                (second, t),
            )
            for part, column in enumerate((diagonal, second))
        ]

    def to_first(index):
        owner, (second_land, first_land, line_land), at, extra = lands_of(index)
        return remote(second_land.at[at, 0], first_land.at[at], first_send.at[index], first_recv.at[index], (first, t))

    def along(index, up):
        kind = items[index][0]
        owner, (second_land, first_land, line_land), at, extra = lands_of(index)
        if up:
            return remote(
                first_land.at[at], line_land.at[at], line_send.at[index], below_recv.at[kind, owner], (s, t + 1)
            )
        final = jnp.where(owner == t - 1, 1, 0)
        return remote(
            first_land.at[at],
            line_land.at[at + final * (extra - at)],
            line_send.at[index],
            above_recv.at[kind, owner],
            (s, t - 1),
        )

    def held_rows(index, chip):
        return held.at[index % HELD, chip, pl.ds(0, heights[items[index][0]]), :]

    def advance(now):
        index = now - LAG_2
        if 0 <= index < ITEMS:
            owner, (second_land, first_land, line_land), at, extra = lands_of(index)
            for copy in to_second(index):
                copy.wait_recv()
            add_rows(second_land.at[at, 0], second_land.at[at, 0], held_rows(index, first // 2))
            to_first(index).start()
        index = now - LAG_3
        if 0 <= index < ITEMS:
            owner, (second_land, first_land, line_land), at, extra = lands_of(index)
            to_first(index).wait_recv()
            add_rows(first_land.at[at], first_land.at[at], held_rows(index, s // 2), second_land.at[at, 1])
        for hop in range(TP - 1):
            index = now - LAG_4 - HOP * hop
            if not 0 <= index < ITEMS or items[index][1] == 0:
                continue
            owner, (second_land, first_land, line_land), at, extra = lands_of(index)
            for up in (True, False):

                @pl.when((t == hop) & (owner > t) if up else (t == TP - 1 - hop) & (owner < t))
                def _(index=index, at=at, up=up, first_land=first_land, line_land=line_land, hop=hop):
                    if hop:
                        along(index, up).wait_recv()
                        add_rows(first_land.at[at], first_land.at[at], line_land.at[at])
                    along(index, up).start()

        index = now - LAG_5
        if 0 <= index < ITEMS:
            kind, step = items[index]
            owner, (second_land, first_land, line_land), at, extra = lands_of(index)
            if step == 0:
                target = (down_grad, left_grad, right_grad, out_grad, qkvg_grad, qkvg_grad)[kind]
                if kind >= 4:
                    target = target.at[(kind - 4) * half_d : (kind - 3) * half_d]

                @pl.when(t == 0)
                def _():
                    along(index, False).wait_recv()
                    add_rows(target, first_land.at[at], line_land.at[extra])

                @pl.when(t == TP - 1)
                def _():
                    along(index, True).wait_recv()
                    add_rows(target, first_land.at[at], line_land.at[at])

                @pl.when((t > 0) & (t < TP - 1))
                def _():
                    along(index, True).wait_recv()
                    along(index, False).wait_recv()
                    add_rows(target, first_land.at[at], line_land.at[at], line_land.at[extra])

    def produce(index):
        kind, step = items[index]
        height = heights[kind]
        right, part = ((cot, 0), (second_normed, 1), (second_normed, 1), (attn_cot, 3), (normed, 2), (normed, 2))[kind]
        once(("half", part), lambda: half_copy().wait_recv() if part == 3 else half_load(part).wait())
        if kind >= 4:
            once("normed", lambda: normed_load().wait())
        for copy in lhs_loads(index):
            copy.wait()
        if index >= HELD:
            for copy in to_second(index - HELD):
                copy.wait_send()
        slot = index % 2
        product = dots(lhs[slot, 0, :, 0:height], right[:, ours], TN) + dots(lhs[slot, 1, :, 0:height], halves[part], TN)
        for chip in range(4):
            held[index % HELD, chip, 0:height, :] = product[:, chip * STRIPE : chip * STRIPE + STRIPE].astype(BF16)
        for copy in to_second(index):
            copy.start()
        advance(index)

    for index in range(SEQ):
        cot_load(index).start()
    half_load(0).start()
    prefetch(0)
    for p in range(PIECES):
        share_start(0, p)
    back_load().start()
    second_load().start()
    half_load(1).start()
    for index in range(3):
        tile_load(index).start()
    acts_load().start()
    pack_load().start()
    normed_load().start()
    half_load(2).start()
    for index in range(SEQ):
        cot_load(index).wait()
    produce(0)
    prefetch(1)
    back_load().wait()
    second_load().wait()

    def middle(part, start):
        unit = second_normed[part, :].astype(F32)
        values = mid[part, :]
        inner = jnp.mean(values * unit, axis=-1, keepdims=True)
        values = cot[part, :].astype(F32) + inv_second[part, 0:1] * (values - unit * inner)
        mid[part, :] = values
        attn_cot[part, :] = values.astype(BF16)

    every_rows(rows, middle)
    half_copy().start()
    produce(1)
    prefetch(2)
    at_tile = 0
    for part in range(2):
        wide[:, part * half_d : part * half_d + half_d] = dots(attn_cot[...], tile(at_tile + part), NT)
        tile_next(at_tile + part)
    at_tile += 2
    acts_load().wait()
    pack_load().wait()

    def head_rows(part, start):
        total = jnp.zeros((BLOCK, 1), F32)
        for block in range(TP):
            values = wide[part, block * PAIR : block * PAIR + PAIR]
            gate = acts[block, part, 3 * PAIR : 4 * PAIR].astype(F32)
            unit = pack[block, part, 3 * PAIR : 4 * PAIR].astype(F32)
            total += jnp.sum(values * gate * unit, axis=-1, keepdims=True)
        total = total * (1.0 / D)
        scale = inv_mix[part, 0:1]
        for block in range(TP):
            values = wide[part, block * PAIR : block * PAIR + PAIR]
            gate = acts[block, part, 3 * PAIR : 4 * PAIR].astype(F32)
            unit = pack[block, part, 3 * PAIR : 4 * PAIR].astype(F32)
            backs[block, part, 3 * PAIR : 4 * PAIR] = (values * unit).astype(BF16)
            backs[block, part, 2 * PAIR : 3 * PAIR] = (scale * (values * gate - unit * total)).astype(BF16)
        row = lax.broadcasted_iota(jnp.int32, (BLOCK, rows), 0) + start
        column = lax.broadcasted_iota(jnp.int32, (BLOCK, rows), 1)
        apart = (column > row) | ((row >= edge) & (column < edge))
        distance[part, :] = jnp.where(apart, -1, row - column).astype(F32)

    every_rows(rows, head_rows)
    produce(2)
    prefetch(3)
    relay(2, 12)

    def rate_of(block, half):
        return rates[block, half : half + 1, :]

    def row_numbers(start):
        return lax.broadcasted_iota(jnp.int32, (BLOCK, HEAD), 0) + start

    for block in range(TP):
        for half in range(2):
            at = half * HEAD

            def fade_rows(part, start, block=block, half=half, at=at):
                number = row_numbers(start)
                valid = jnp.where(jnp.where(number >= edge, 1, 0) == before, 1.0, 0.0)
                fade = jnp.exp(-rate_of(block, half) * (number + 1).astype(F32)) * valid
                values = backs[block, part, 2 * PAIR + at : 2 * PAIR + at + HEAD].astype(F32)
                faded[part, :] = (values * fade).astype(BF16)

            every_rows(rows, fade_rows)
            head = 2 * block + half
            state[head] = dots(acts[block, :, at : at + HEAD], faded[...], TN).astype(BF16)
            wide[:, head * HEAD : head * HEAD + HEAD] = dots(faded[...], incoming[head], NT)

    def suffix_scale(block, source_block, rate):
        same = jnp.where(source_block * rows - 1 >= boundary, 1, 0) == jnp.where(block * rows + rows - 1 >= boundary, 1, 0)
        usable = flag(source_block > block) * flag(same)
        gap = jnp.maximum(source_block - 1 - block, 0).astype(F32)
        return jnp.exp(-rate * (rows * gap)) * usable

    begin_states, add_pair, add_chips, finish_states, close_states = state_exchange(
        rows, boundary, exchange, rates, suffix_scale, lambda chip: 2 * chip - 1, lambda chip: 2 * chip
    )
    begin_states()
    produce(3)
    prefetch(4)
    relay(2, 12)
    add_pair()
    weights[0:PAIR, PAIR:rows] = jnp.zeros((PAIR, rows - PAIR), BF16)
    slopes[0:PAIR, PAIR:rows] = jnp.zeros((PAIR, rows - PAIR), BF16)

    def attend(block):
        for half in range(2):
            at = half * HEAD
            head = 2 * block + half
            rate = rate_of(block, half)
            query, key, value = [slice(kind * PAIR + at, kind * PAIR + at + HEAD) for kind in range(3)]
            mine_columns = slice(head * HEAD, head * HEAD + HEAD)
            for top in range(0, rows, PAIR):
                width = top + PAIR
                scores[0:PAIR, 0:width] = dots(acts[block, top:width, query], acts[block, 0:width, key], NT)
                scores[PAIR : 2 * PAIR, 0:width] = dots(backs[block, top:width, value], acts[block, 0:width, value], NT)

                def weigh(part, start, width=width, top=top):
                    below = pl.ds(pl.multiple_of(start + PAIR, BLOCK), BLOCK)
                    there = pl.ds(pl.multiple_of(start + top, BLOCK), BLOCK)
                    for left in range(0, width, HEAD):
                        apart = distance[there, left : left + HEAD]
                        fade = jnp.where(apart >= 0.0, jnp.exp(-rate * apart), 0.0)
                        weights[there, left : left + HEAD] = (scores[part, left : left + HEAD] * fade).astype(BF16)
                        grad = scores[below, left : left + HEAD].astype(BF16).astype(F32)
                        slopes[there, left : left + HEAD] = (grad * fade).astype(BF16)

                every_rows(PAIR, weigh)
                wide[top:width, mine_columns] += dots(slopes[top:width, 0:width], acts[block, 0:width, key], NN)
            inner = dots(weights[...], backs[block, :, value], TN)
            acts[block, :, 3 * PAIR + at : 3 * PAIR + at + HEAD] = inner.astype(BF16)
            inner = dots(slopes[...], acts[block, :, query], TN)
            backs[block, :, key] = inner.astype(BF16)

            def turn_back(part, start):
                turned = rotated(wide[part, mine_columns], cosine[part, :], -sine[part, :])
                backs[block, part, query] = (turned * pack[block, part, query].astype(F32)).astype(BF16)

            every_rows(rows, turn_back)

    for block in range(TP):
        attend(block)
        produce(4 + block)
        prefetch(5 + block)
        relay(2, 12)

    add_chips()
    produce(8)
    prefetch(9)
    relay(2, 12)
    finish_states()

    for block in range(TP):
        for half in range(2):
            at = half * HEAD
            head = 2 * block + half
            query, key, value = [slice(kind * PAIR + at, kind * PAIR + at + HEAD) for kind in range(3)]
            scores[:, 0:HEAD] = dots(acts[block, :, value], later[head], NT)
            scores[:, HEAD : 2 * HEAD] = dots(acts[block, :, key], later[head], NN)

            def finish_rows(part, start, block=block, half=half, at=at, key=key, value=value):
                number = row_numbers(start)
                valid = jnp.where(jnp.where(number >= edge, 1, 0) == last, 1.0, 0.0)
                fade = jnp.exp(-rate_of(block, half) * (rows - 1 - number).astype(F32)) * valid
                keys = backs[block, part, key].astype(F32) + fade * scores[part, 0:HEAD]
                turned = rotated(keys, cosine[part, :], -sine[part, :])
                backs[block, part, key] = (turned * pack[block, part, key].astype(F32)).astype(BF16)
                values = acts[block, part, 3 * PAIR + at : 3 * PAIR + at + HEAD].astype(F32)
                backs[block, part, value] = (values + fade * scores[part, HEAD : 2 * HEAD]).astype(BF16)

            every_rows(rows, finish_rows)
        backs_keep_copy(block).start()
        backs_copy(block).start()
        for part in range(2):
            index = at_tile + 2 * block + part
            term = dots(backs[block, :, part * half_d : part * half_d + half_d], tile(index), NN)
            if block or part:
                wide[...] += term
            else:
                wide[...] = term
            tile_next(index)
        if block == 0:
            for index in range(SEQ):
                hidden_load(index).start()
        if block == 1:
            produce(9)
            prefetch(10)
    relay(12, 12)
    for index in range(SEQ):
        hidden_load(index).wait()

    def input_rows(part, start):
        values = acts[0, part, :].astype(F32)
        scale = lax.rsqrt(jnp.mean(values * values, axis=-1, keepdims=True) + EPSILON)
        unit = values * scale
        grad = wide[part, :]
        inner = jnp.mean(grad * unit, axis=-1, keepdims=True)
        grad = mid[part, :] + scale * (grad - unit * inner)
        for index in range(SEQ):
            acts[1, part, plain(index)] = grad[:, place_of(index)].astype(BF16)

    for p in range(PIECES):

        @pl.loop(0, piece_rows // BLOCK)
        def _(block, p=p):
            start = p * piece_rows + block * BLOCK
            input_rows(pl.ds(pl.multiple_of(start, BLOCK), BLOCK), start)

        if p < EARLY:
            share_start(1, p)
    for index in range(BEFORE, ITEMS):
        produce(index)
        if index + 1 < ITEMS:
            prefetch(index + 1)
        if EARLY <= index - BEFORE + EARLY < PIECES:
            share_start(1, index - BEFORE + EARLY)
        if index >= BEFORE + WAIT_1:
            relay(2, 20)
        if index >= BEFORE + WAIT_2:
            relay(1)
    for now in range(ITEMS, ITEMS + LAG_5):
        advance(now)
        relay(1)
    relay(len(relays))

    half_copy().wait_send()
    for block in range(TP):
        backs_copy(block).wait_send()
    close_states()
    for index, (kind, step) in enumerate(items):
        if index >= ITEMS - HELD:
            for copy in to_second(index):
                copy.wait_send()
        to_first(index).wait_send()
        if step:
            along(index, True).wait_send()
    for a in range(2):
        for p in range(PIECES):
            share_keep(a, p).wait()

            @pl.when(t < TP - 1)
            def _(a=a, p=p):
                share_copy(a, p, t, own_piece(a, p), True).wait_send()

            @pl.when(t > 0)
            def _(a=a, p=p):
                share_copy(a, p, t, own_piece(a, p), False).wait_send()
    for a, p, step in relays:
        owner = nearest(t, step)
        passed = passes(owner, True) | passes(owner, False)

        @pl.when(jnp.logical_not(passed))
        def _(a=a, p=p, owner=owner):
            share_copy(a, p, owner, piece(a, owner, p), True).wait_recv()

        for up in (True, False):

            @pl.when(passes(owner, up))
            def _(a=a, p=p, owner=owner, up=up):
                share_copy(a, p, owner, piece(a, owner, p), up).wait_send()


def backward(units, whole, kept, output, hidden_in, out_cotangent, incoming, inv_mix, inv_second, rates, cosine, sine, bounds):
    rows = output.shape[0]
    sizes = tuple(weight.shape[0] // TP for weight in whole) + (units,)
    dma = pltpu.SemaphoreType.DMA
    vmem = pl.BlockSpec(memory_space=pltpu.VMEM)
    anywhere = pl.BlockSpec(memory_space=pl.ANY)
    half_d = D // 2
    shape = jax.ShapeDtypeStruct
    tall = lambda height: shape((height, STRIPE), F32)
    scratch = [
        pltpu.VMEM((3, half_d, D), BF16),
        *[pltpu.VMEM((rows, D), BF16)] * 4,
        pltpu.VMEM((4, rows, half_d), BF16),
        *[pltpu.VMEM((TP, rows, 4 * PAIR), BF16)] * 3,
        pltpu.VMEM((rows, D), F32),
        pltpu.VMEM((rows, D), F32),
        pltpu.VMEM((rows, rows), F32),
        pltpu.VMEM((rows, rows), F32),
        pltpu.VMEM((rows, rows), BF16),
        pltpu.VMEM((rows, rows), BF16),
        pltpu.VMEM((rows, HEAD), BF16),
        pltpu.VMEM((2, 2, rows, units), BF16),
        pltpu.VMEM((HELD, 4, units, STRIPE), BF16),
        *state_scratch(),
    ]
    for count, height, extra in ((3 * TP, units, 3), (TP, sizes[1], 1), (2 * TP, half_d, 2)):
        scratch += [
            pltpu.VMEM((count, 2, height, STRIPE), BF16),
            pltpu.VMEM((count, height, STRIPE), BF16),
            pltpu.VMEM((count + extra, height, STRIPE), BF16),
        ]
    scratch += [
        dma((3,)),
        dma((2,)),
        dma((3,)),
        dma((TP,)),
        dma((TP,)),
        dma((TP,)),
        dma((5,)),
        dma((SEQ,)),
        dma((SEQ,)),
        dma((2, 2)),
        dma((ITEMS, 2)),
        dma((ITEMS, 2)),
        dma((ITEMS,)),
        dma((ITEMS,)),
        dma((ITEMS,)),
        dma((KINDS, TP)),
        dma((KINDS, TP)),
        dma((2, PIECES)),
        dma((2, PIECES, TP)),
        dma((2, PIECES, TP)),
        dma((2, PIECES, TP)),
    ]
    return pl.pallas_call(
        functools.partial(backward_kernel, rows, sizes),
        out_shape=[tall(units), tall(units), tall(units), tall(sizes[1]), tall(sizes[0])]
        + [shape((TP, rows, D), BF16)] * 2
        + [shape((TP, rows, 4 * PAIR), BF16)] * 2,
        in_specs=[anywhere] * 20 + [vmem] * 6 + [pl.BlockSpec(memory_space=pltpu.SMEM)],
        out_specs=[vmem] * 5 + [anywhere] * 4,
        scratch_shapes=scratch,
        compiler_params=pltpu.CompilerParams(
            collective_id=1, has_side_effects=True, vmem_limit_bytes=63 * 2**20
        ),
        name="backward",
    )(*whole, *kept, output, hidden_in, out_cotangent, incoming, inv_mix, inv_second, rates, cosine, sine, bounds)


def finish_kernel(output_in, input_in, qkvg_in, tall_in, output, input_grad, *refs):
    output[...] = output_in[...]
    input_grad[...] = input_in[...].astype(F32)

    @pl.when(pl.program_id(0) == 0)
    def _():
        for kind in range(4):
            refs[kind][...] = qkvg_in[kind * PAIR : kind * PAIR + PAIR, :].T
        refs[4][...] = tall_in[...]


def finish(output, input_grad, qkvg_grad, out_grad):
    rows = output.shape[1]
    steps = 2
    block = lambda: pl.BlockSpec((1, rows // steps, D), lambda step: (step // steps, step % steps, 0))
    fixed = lambda *shape: pl.BlockSpec(shape, lambda step: (0, 0))
    shape = jax.ShapeDtypeStruct
    return pl.pallas_call(
        finish_kernel,
        grid=(TP * steps,),
        out_shape=[
            shape(output.shape, BF16),
            shape(input_grad.shape, F32),
            *[shape((STRIPE, PAIR), F32)] * 4,
            shape(out_grad.shape, F32),
        ],
        in_specs=[block(), block(), fixed(4 * PAIR, STRIPE), fixed(*out_grad.shape)],
        out_specs=[block(), block(), *[fixed(STRIPE, PAIR)] * 4, fixed(*out_grad.shape)],
        name="finish",
    )(output, input_grad, qkvg_grad, out_grad)


def entering(value, axis, join, neutral, backward):
    count, mine = (lax.axis_size(axis), lax.axis_index(axis))
    pieces = jax.tree.map(lambda part: lax.all_gather(part, axis), value)
    if backward:
        pieces = jax.tree.map(lambda part: part[::-1], pieces)
        mine = count - 1 - mine
    subtotal = jax.tree.map(
        lambda part, zero: jnp.full_like(part, 0) + jnp.asarray(zero, part.dtype), value, neutral
    )

    def step(position, subtotal):
        longer = join(subtotal, jax.tree.map(lambda part: part[position], pieces))
        return jax.tree.map(lambda new, old: jnp.where(position < mine, new, old), longer, subtotal)

    return lax.fori_loop(0, count - 1, step, subtotal)


def swish_parts(pre_act):
    logistic = jax.nn.sigmoid(pre_act)
    return (pre_act * logistic, logistic * (1.0 + pre_act * (1.0 - logistic)))


def rotate(rows_in, cosine_table, sine_table, signed):
    halfway = rows_in.shape[-1] // 2
    front_half = rows_in[..., :halfway]
    back_half = rows_in[..., halfway:]
    return jnp.concatenate(
        [
            front_half * cosine_table - signed * back_half * sine_table,
            signed * front_half * sine_table + back_half * cosine_table,
        ],
        axis=-1,
    )


def combine_forward(earlier, following):
    return (earlier[0] * following[0], following[0][:, None, None] * earlier[1] + following[1])


def combine_backward(farther, nearer):
    return (farther[0] * nearer[0], nearer[1] + nearer[0][:, None, None] * farther[1])


def collect_weights(
    query_weight,
    key_weight,
    value_weight,
    gate_weight,
    out_weight,
    left_weight,
    right_weight,
    down_weight,
):
    return (
        lax.all_gather(query_weight, "seq", axis=0, tiled=True),
        lax.all_gather(key_weight, "seq", axis=0, tiled=True),
        lax.all_gather(value_weight, "seq", axis=0, tiled=True),
        lax.all_gather(gate_weight, "seq", axis=0, tiled=True),
        lax.all_gather(out_weight, "seq", axis=1, tiled=True),
        lax.all_gather(left_weight, "seq", axis=0, tiled=True),
        lax.all_gather(right_weight, "seq", axis=0, tiled=True),
        lax.all_gather(down_weight, "seq", axis=1, tiled=True),
    )


def state_prefix(factor, local_state):
    neutral = (jnp.ones_like(factor), jnp.zeros_like(local_state))
    return entering((factor, local_state), "seq", combine_forward, neutral, False)[1]


def state_suffix(factor, state_grad):
    neutral = (jnp.ones_like(factor), jnp.zeros_like(state_grad))
    return entering((factor, state_grad), "seq", combine_backward, neutral, True)[1]


def body(
    hidden_in,
    query_weight,
    key_weight,
    value_weight,
    gate_weight,
    out_weight,
    left_weight,
    right_weight,
    down_weight,
    decay_rate,
    seq_bounds,
    out_cotangent,
):
    row_count = hidden_in.shape[1]
    batch_count = hidden_in.shape[0]
    local_heads = decay_rate.shape[0]
    heads_shape = (row_count, local_heads, HEAD)
    device = lax.axis_index("seq")
    offsets = jnp.arange(row_count, dtype=jnp.int32)
    positions = device * row_count + offsets
    frequency = jnp.exp(
        jnp.arange(HEAD // 2, dtype=jnp.float32) * (-2.0 * math.log(10000.0) / HEAD)
    )
    angles = positions.astype(jnp.float32)[:, None] * frequency[None, :]
    cosine_table = jnp.cos(angles)[:, None, :]
    sine_table = jnp.sin(angles)[:, None, :]
    local_f = offsets.astype(jnp.float32)
    distance = local_f[:, None] - local_f[None, :]
    causal = distance >= 0.0
    distance_pos = jnp.maximum(distance, 0.0)
    accum = None
    outputs = []
    in_grads = []
    for batch_index in range(batch_count):
        gathered = collect_weights(
            query_weight,
            key_weight,
            value_weight,
            gate_weight,
            out_weight,
            left_weight,
            right_weight,
            down_weight,
        )
        query_full, key_full, value_full, gate_full, out_full, left_full, right_full, down_full = (
            gathered
        )
        boundary = seq_bounds[batch_index]
        segment = (positions >= boundary).astype(jnp.int32)
        before = (device * row_count - 1 >= boundary).astype(jnp.int32)
        last_segment = segment[row_count - 1]
        allowed = causal & (segment[:, None] == segment[None, :])
        decay = jnp.where(
            allowed[None], jnp.exp(-decay_rate[:, None, None] * distance_pos[None]), 0.0
        )
        coef_in = (
            jnp.exp(-decay_rate[None, :] * (local_f[:, None] + 1.0))
            * (segment == before).astype(jnp.float32)[:, None]
        )
        weight_loc = (
            jnp.exp(-decay_rate[None, :] * (row_count - 1.0 - local_f)[:, None])
            * (segment == last_segment).astype(jnp.float32)[:, None]
        )
        factor = jnp.where(last_segment == before, jnp.exp(-decay_rate * row_count), 0.0)
        input_rows = hidden_in[batch_index].astype(jnp.float32)
        inv_first = lax.rsqrt(jnp.mean(input_rows * input_rows, axis=-1, keepdims=True) + EPSILON)
        unit_first = input_rows * inv_first
        normed_first = unit_first.astype(jnp.bfloat16)
        query_pre = jnp.dot(normed_first, query_full, preferred_element_type=jnp.float32)
        key_pre = jnp.dot(normed_first, key_full, preferred_element_type=jnp.float32)
        value_pre = jnp.dot(normed_first, value_full, preferred_element_type=jnp.float32)
        gate_pre = jnp.dot(normed_first, gate_full, preferred_element_type=jnp.float32)
        query_act, query_slope = swish_parts(query_pre)
        key_act, key_slope = swish_parts(key_pre)
        query_rot = rotate(query_act.reshape(heads_shape), cosine_table, sine_table, 1.0).astype(
            jnp.bfloat16
        )
        key_rot = rotate(key_act.reshape(heads_shape), cosine_table, sine_table, 1.0).astype(
            jnp.bfloat16
        )
        value_rows = value_pre.astype(jnp.bfloat16).reshape(heads_shape)
        query_wide = query_rot.astype(jnp.float32)
        key_wide = key_rot.astype(jnp.float32)
        value_wide = value_rows.astype(jnp.float32)
        scores = jnp.einsum("ihe,jhe->hij", query_rot, key_rot, preferred_element_type=jnp.float32)
        attn_weights = (scores * decay).astype(jnp.bfloat16)
        inner_out = jnp.einsum(
            "hij,jhe->ihe", attn_weights, value_rows, preferred_element_type=jnp.float32
        )
        local_state = jnp.einsum(
            "jhe,jhf->hef",
            key_wide * weight_loc[:, :, None],
            value_wide,
            precision=HIGHEST_PRECISION,
        )
        incoming = state_prefix(factor, local_state)
        outer_out = coef_in[:, :, None] * jnp.einsum(
            "ihe,hef->ihf", query_wide, incoming, precision=HIGHEST_PRECISION
        )
        mixed_heads = (inner_out + outer_out).reshape(row_count, local_heads * HEAD)
        total_sq = lax.psum(jnp.sum(mixed_heads * mixed_heads, axis=-1), "tp")
        inv_mix = lax.rsqrt(total_sq / D + EPSILON)[:, None]
        unit_mix = mixed_heads * inv_mix
        gate_mix = (unit_mix * gate_pre).astype(jnp.bfloat16)
        attn_sum = lax.psum(jnp.dot(gate_mix, out_full, preferred_element_type=jnp.float32), "tp")
        resid_mid = input_rows + attn_sum
        inv_second = lax.rsqrt(jnp.mean(resid_mid * resid_mid, axis=-1, keepdims=True) + EPSILON)
        unit_second = resid_mid * inv_second
        normed_second = unit_second.astype(jnp.bfloat16)
        left_pre = jnp.dot(normed_second, left_full, preferred_element_type=jnp.float32)
        right_pre = jnp.dot(normed_second, right_full, preferred_element_type=jnp.float32)
        glu_product = (left_pre * right_pre).astype(jnp.bfloat16)
        glu_out = lax.psum(
            jnp.dot(glu_product, down_full, preferred_element_type=jnp.float32), "tp"
        )
        outputs.append((resid_mid + glu_out).astype(jnp.bfloat16))
        glu_cot = out_cotangent[batch_index]
        product_grad = jnp.einsum(
            "cd,fd->cf", glu_cot, down_full, preferred_element_type=jnp.float32
        )
        left_back = (product_grad * right_pre).astype(jnp.bfloat16)
        right_back = (product_grad * left_pre).astype(jnp.bfloat16)
        second_part = jnp.einsum(
            "cf,df->cd", left_back, left_full, preferred_element_type=jnp.float32
        ) + jnp.einsum("cf,df->cd", right_back, right_full, preferred_element_type=jnp.float32)
        second_back = lax.psum(second_part, "tp")
        mid_grad = glu_cot.astype(jnp.float32) + inv_second * (
            second_back - unit_second * jnp.mean(second_back * unit_second, axis=-1, keepdims=True)
        )
        attn_cot = mid_grad.astype(jnp.bfloat16)
        gate_mix_grad = jnp.einsum(
            "cd,kd->ck", attn_cot, out_full, preferred_element_type=jnp.float32
        )
        gate_back = (gate_mix_grad * unit_mix).astype(jnp.bfloat16)
        unit_mix_grad = gate_mix_grad * gate_pre
        mix_dot = lax.psum(jnp.sum(unit_mix_grad * unit_mix, axis=-1), "tp")
        heads_grad = (
            (inv_mix * (unit_mix_grad - unit_mix * (mix_dot / D)[:, None]))
            .astype(jnp.bfloat16)
            .reshape(heads_shape)
        )
        pair_grad = jnp.einsum(
            "ihe,jhe->hij", heads_grad, value_rows, preferred_element_type=jnp.float32
        ).astype(jnp.bfloat16)
        score_grad = pair_grad.astype(jnp.float32) * decay
        query_inner = jnp.einsum("hij,jhe->ihe", score_grad, key_wide, precision=HIGHEST_PRECISION)
        key_inner = jnp.einsum("hij,ihe->jhe", score_grad, query_wide, precision=HIGHEST_PRECISION)
        value_inner = jnp.einsum(
            "hij,ihe->jhe", attn_weights, heads_grad, preferred_element_type=jnp.float32
        )
        scaled_grad = heads_grad.astype(jnp.float32) * coef_in[:, :, None]
        query_outer = jnp.einsum("ihf,hef->ihe", scaled_grad, incoming, precision=HIGHEST_PRECISION)
        state_grad = jnp.einsum(
            "ihe,ihf->hef", query_wide, scaled_grad, precision=HIGHEST_PRECISION
        )
        later_grad = state_suffix(factor, state_grad)
        key_state = weight_loc[:, :, None] * jnp.einsum(
            "jhf,hef->jhe", value_wide, later_grad, precision=HIGHEST_PRECISION
        )
        value_state = weight_loc[:, :, None] * jnp.einsum(
            "jhe,hef->jhf", key_wide, later_grad, precision=HIGHEST_PRECISION
        )
        query_back = (
            rotate(query_inner + query_outer, cosine_table, sine_table, -1.0).reshape(row_count, -1)
            * query_slope
        ).astype(jnp.bfloat16)
        key_back = (
            rotate(key_inner + key_state, cosine_table, sine_table, -1.0).reshape(row_count, -1)
            * key_slope
        ).astype(jnp.bfloat16)
        value_back = (value_inner + value_state).reshape(row_count, -1).astype(jnp.bfloat16)
        fresh = (
            jnp.einsum("cd,ck->dk", normed_first, query_back, preferred_element_type=jnp.float32),
            jnp.einsum("cd,ck->dk", normed_first, key_back, preferred_element_type=jnp.float32),
            jnp.einsum("cd,ck->dk", normed_first, value_back, preferred_element_type=jnp.float32),
            jnp.einsum("cd,ck->dk", normed_first, gate_back, preferred_element_type=jnp.float32),
            jnp.einsum("ck,cd->kd", gate_mix, attn_cot, preferred_element_type=jnp.float32),
            jnp.einsum("cd,cf->df", normed_second, left_back, preferred_element_type=jnp.float32),
            jnp.einsum("cd,cf->df", normed_second, right_back, preferred_element_type=jnp.float32),
            jnp.einsum("cf,cd->fd", glu_product, glu_cot, preferred_element_type=jnp.float32),
        )
        if accum is None:
            accum = list(fresh)
        else:
            accum = [older + newer for older, newer in zip(accum, fresh)]
        total = jnp.einsum("ck,dk->cd", query_back, query_full, preferred_element_type=jnp.float32)
        total = total + jnp.einsum(
            "ck,dk->cd", key_back, key_full, preferred_element_type=jnp.float32
        )
        total = total + jnp.einsum(
            "ck,dk->cd", value_back, value_full, preferred_element_type=jnp.float32
        )
        first_back = lax.psum(
            total
            + jnp.einsum("ck,dk->cd", gate_back, gate_full, preferred_element_type=jnp.float32),
            "tp",
        )
        input_back = mid_grad + inv_first * (
            first_back - unit_first * jnp.mean(first_back * unit_first, axis=-1, keepdims=True)
        )
        in_grads.append(input_back)
    summed = (
        lax.psum_scatter(accum[0], "seq", scatter_dimension=0, tiled=True),
        lax.psum_scatter(accum[1], "seq", scatter_dimension=0, tiled=True),
        lax.psum_scatter(accum[2], "seq", scatter_dimension=0, tiled=True),
        lax.psum_scatter(accum[3], "seq", scatter_dimension=0, tiled=True),
        lax.psum_scatter(accum[4], "seq", scatter_dimension=1, tiled=True),
        lax.psum_scatter(accum[5], "seq", scatter_dimension=0, tiled=True),
        lax.psum_scatter(accum[6], "seq", scatter_dimension=0, tiled=True),
        lax.psum_scatter(accum[7], "seq", scatter_dimension=1, tiled=True),
    )
    return (
        jnp.stack(outputs),
        jnp.stack(in_grads),
        summed[0],
        summed[1],
        summed[2],
        summed[3],
        summed[4],
        summed[5],
        summed[6],
        summed[7],
    )


def fused_body(
    hidden_in,
    query_weight,
    key_weight,
    value_weight,
    gate_weight,
    out_weight,
    left_weight,
    right_weight,
    down_weight,
    decay_rate,
    seq_bounds,
    out_cotangent,
):
    row_count = hidden_in.shape[1]
    device = lax.axis_index("seq")
    positions = device * row_count + jnp.arange(row_count, dtype=jnp.int32)
    frequency = jnp.exp(jnp.arange(HEAD // 2, dtype=F32) * (-2.0 * math.log(10000.0) / HEAD))
    angles = positions.astype(F32)[:, None] * jnp.tile(frequency, 2)[None, :]
    sign = jnp.where(jnp.arange(HEAD) < HEAD // 2, -1.0, 1.0).astype(F32)
    cosine, sine = jnp.cos(angles), jnp.sin(angles) * sign[None, :]
    results = forward(
        (query_weight, key_weight, value_weight, gate_weight),
        (out_weight, left_weight.T, right_weight.T, down_weight),
        hidden_in,
        out_cotangent,
        cosine,
        sine,
        decay_rate,
        seq_bounds,
    )
    whole, kept, (incoming, inv_mix, inv_second, rates, output) = results[:2], results[2:17], results[17:]
    down_grad, left_grad, right_grad, out_grad, qkvg_grad, output, input_grad = backward(
        down_weight.shape[0],
        whole,
        kept,
        output,
        hidden_in,
        out_cotangent,
        incoming,
        inv_mix,
        inv_second,
        rates,
        cosine,
        sine,
        seq_bounds,
    )[:7]
    output, input_grad, query_grad, key_grad, value_grad, gate_grad, out_grad = finish(
        output, input_grad, qkvg_grad, out_grad
    )
    return (
        output,
        input_grad,
        query_grad,
        key_grad,
        value_grad,
        gate_grad,
        out_grad,
        left_grad.T,
        right_grad.T,
        down_grad,
    )


def solution(mesh):
    fits = mesh.shape["seq"] == SEQ and mesh.shape["tp"] == TP
    return jax.shard_map(
        fused_body if fits else body,
        mesh=mesh,
        in_specs=(
            P(None, "seq", None),
            P("seq", "tp"),
            P("seq", "tp"),
            P("seq", "tp"),
            P("seq", "tp"),
            P("tp", "seq"),
            P("seq", "tp"),
            P("seq", "tp"),
            P("tp", "seq"),
            P("tp"),
            P(),
            P(None, "seq", None),
        ),
        out_specs=(
            P(None, "seq", None),
            P(None, "seq", None),
            P("seq", "tp"),
            P("seq", "tp"),
            P("seq", "tp"),
            P("seq", "tp"),
            P("tp", "seq"),
            P("seq", "tp"),
            P("seq", "tp"),
            P("tp", "seq"),
        ),
        check_vma=False,
    )
```

```python
import functools
import math

import jax
import jax.numpy as jnp
from jax import lax
from jax.experimental import pallas as pl
from jax.experimental.pallas import tpu as pltpu
from jax.sharding import PartitionSpec as P

D = 1024
HEAD = 128


EPSILON = 1e-06
HIGHEST_PRECISION = lax.Precision.HIGHEST
MESH = pl.DeviceIdType.MESH
BF16 = jnp.bfloat16
F32 = jnp.float32

SEQ = 8
TP = 4
STRIPE = 128
PAIR = 2 * HEAD
BLOCK = 32
NARROW = 128
WEIGH = 64

NN = ((1,), (0,))
NT = ((1,), (1,))
TN = ((0,), (0,))


def dots(left, right, dims):
    return lax.dot_general(left, right, (dims, ((), ())), preferred_element_type=F32)


def place():
    s, t = lax.axis_index("seq"), lax.axis_index("tp")
    core = s % 2
    column = (s // 2) % 2
    line = s // 4
    other = s + 1 - 2 * core
    across_x = s + 2 * (1 - 2 * column)
    across_y = s + 4 * (1 - 2 * line)
    first = across_x + core * (across_y - across_x)
    second = across_y + core * (across_x - across_y)
    diagonal = across_x + across_y - s
    return s, t, other, first, second, diagonal


def nearest(t, step):
    flip = t // 2
    low = t + flip * (3 - 2 * t)
    swap = low * (1 - step // 2)
    index = step + swap * (1 - 2 * step)
    return index + flip * (3 - 2 * index)


def stripe(index):
    return pl.ds(pl.multiple_of((index % 2 * (SEQ // 2) + index // 2) * STRIPE, STRIPE), STRIPE)


def plain(index):
    return slice(index * STRIPE, index * STRIPE + STRIPE)


def place_of(index):
    at = (index % 2 * (SEQ // 2) + index // 2) * STRIPE
    return slice(at, at + STRIPE)


def rows_of(index, size):
    return pl.ds(pl.multiple_of(index * size, size), size)


def remote(src, dst, send, receive, device):
    return pltpu.make_async_remote_copy(
        src_ref=src, dst_ref=dst, send_sem=send, recv_sem=receive, device_id=device, device_id_type=MESH
    )


def greet(s, t, around):
    barrier = pltpu.get_barrier_semaphore()
    for step in range(1, TP):
        pl.semaphore_signal(barrier, inc=1, device_id=(s, (t + step) % TP), device_id_type=MESH)
    for device in around:
        pl.semaphore_signal(barrier, inc=1, device_id=(device, t), device_id_type=MESH)
    pl.semaphore_wait(barrier, TP - 1 + len(around))


def every_rows(count, body, size=BLOCK):
    @pl.loop(0, count // size)
    def _(block):
        body(pl.ds(pl.multiple_of(block * size, size), size), block * size)


def flag(condition):
    return jnp.where(condition, 1.0, 0.0).astype(F32)


def rotated(values, cosine, sine):
    return values * cosine + pltpu.roll(values, HEAD // 2, 1) * sine


def state_exchange(rows, boundary, refs, rates, scale, toward, source_of):
    state, pair_land, chip_state, chip_land, partial, result, pair_sem, chip_send, chip_recv, partial_sem = refs
    s, t, other, first, second, diagonal = place()
    core, half = s % 2, TP
    around = (first, second, diagonal)
    ours, theirs = pl.ds(core * half, half), pl.ds((1 - core) * half, half)

    def pair_copy():
        return remote(state.at[theirs], pair_land, pair_sem.at[0], pair_sem.at[1], (other, t))

    def chip_copy(part):
        return remote(chip_state, chip_land.at[part], chip_send.at[part], chip_recv.at[part], (around[part], t))

    def partial_copy():
        return remote(partial, result.at[ours], partial_sem.at[0], partial_sem.at[1], (other, t))

    def rate_of(number):
        head = core * half + number
        return rates[head // 2, pl.ds(head % 2, 1), :]

    def begin():
        pair_copy().start()

    def add_pair():
        pair_copy().wait_recv()

        @pl.loop(0, half)
        def _(number):
            rate, target = rate_of(number), toward(s // 2)
            total = scale(target, s, rate) * state[core * half + number].astype(F32)
            total += scale(target, other, rate) * pair_land[number].astype(F32)
            chip_state[number] = total.astype(BF16)

        for part in range(3):
            chip_copy(part).start()

    def add_chips():
        for part in range(3):
            chip_copy(part).wait_recv()

        @pl.loop(0, half)
        def _(number):
            rate = rate_of(number)
            mine, its = state[core * half + number].astype(F32), pair_land[number].astype(F32)
            here = scale(s, s, rate) * mine + scale(s, other, rate) * its
            there = scale(other, s, rate) * mine + scale(other, other, rate) * its
            for part in range(3):
                values = chip_land[part, number].astype(F32)
                source = source_of(around[part] // 2)
                here += scale(s, source, rate) * values
                there += scale(other, source, rate) * values
            result[core * half + number] = here.astype(BF16)
            partial[number] = there.astype(BF16)

        partial_copy().start()

    def finish():
        partial_copy().wait_recv()

    def close():
        pair_copy().wait_send()
        for part in range(3):
            chip_copy(part).wait_send()
        partial_copy().wait_send()

    return begin, add_pair, add_chips, finish, close


def state_scratch():
    dma = pltpu.SemaphoreType.DMA
    return [
        pltpu.VMEM((2 * TP, HEAD, HEAD), BF16),
        pltpu.VMEM((TP, HEAD, HEAD), BF16),
        pltpu.VMEM((TP, HEAD, HEAD), BF16),
        pltpu.VMEM((3, TP, HEAD, HEAD), BF16),
        pltpu.VMEM((TP, HEAD, HEAD), BF16),
        pltpu.VMEM((2 * TP, HEAD, HEAD), BF16),
        dma((2,)),
        dma((3,)),
        dma((3,)),
        dma((2,)),
    ]


LAG_B, LAG_C = 2, 4

def forward_kernel(rows, sizes, *refs):
    heads_in, refs = refs[:4], refs[4:]
    shards, refs = refs[:4], refs[4:]
    (hidden_in, cot_in, cosine, sine, rate_in, bounds), refs = refs[:6], refs[6:]
    whole_out, refs = refs[:2], refs[2:]
    (acts_out, pack_out, normed_out, second_out, glu_out, left_out, right_out, glu_other, left_other, right_other,
     gated_other, normed_other, second_other, cot_other, back_out,
     incoming_out, inv_mix_out, inv_second_out, rate_out, result_out), refs = refs[:20], refs[20:]
    whole, refs = refs[:5], refs[5:]
    (acts, pack, normed, hidden, cot, second_normed, sides, back, wide, mixed, distance, scores, weights,
     inv_mix, inv_second, rates, heads_shard), refs = refs[:17], refs[17:]
    exchange, refs = refs[:10], refs[10:]
    state, incoming = exchange[0], exchange[5]
    shards = (heads_shard, *shards)
    (local_sem, up_sem, down_sem, line_sem, down_send, down_recv, send_sem, first_sem, second_sem, other_sem, rate_send, rate_recv,
     copy_sem, side_sem, side_send, side_recv, half_send, half_recv,
     hidden_sem, cot_sem) = refs
    s, t, other, first, second, diagonal = place()
    units, beside = sizes[2], wide.shape[1] // 3
    theirs = rows_of(1 - s % 2, D // 2)
    shift = other - s
    for kind in range(4):
        heads_shard[kind * PAIR : kind * PAIR + PAIR, :] = heads_in[kind][...].T
    greet(s, t, (other, first, second, diagonal))

    def hidden_load(index):
        return pltpu.make_async_copy(
            hidden_in.at[t, :, plain(index)], hidden.at[:, place_of(index)], hidden_sem.at[index]
        )

    def cot_load(index):
        return pltpu.make_async_copy(cot_in.at[t, :, plain(index)], cot.at[:, place_of(index)], cot_sem.at[index])

    def half_copy(part):
        src, dst = (
            (normed.at[:, theirs], normed_other),
            (second_normed.at[:, theirs], second_other),
            (cot.at[:, theirs], cot_other),
            (pack.at[:, :, 2 * PAIR : 3 * PAIR], gated_other),
        )[part]
        return remote(src, dst, half_send.at[part], half_recv.at[part], (other, t))

    for index in range(SEQ):
        hidden_load(index).start()

    cut = -(-units // (2 * HEAD)) * HEAD
    items = (
        [(0, 0), (4, 0)]
        + [(0, step) for step in range(1, TP)]
        + [(1, step) for step in range(TP)]
        + [(w, step) for step in range(TP) for w in (2, 3)]
    )
    items = [(w, step, 0, sizes[w]) for w, step in items]
    items[-1:] = [(3, TP - 1, 0, cut), (3, TP - 1, cut, units)]
    columns = (s, first, second, diagonal)

    def spot(w, owner, column, low=0, high=None):
        high = sizes[w] if high is None else high
        return whole[w].at[pl.ds(pl.multiple_of(owner * sizes[w] + low, 16), high - low), stripe(column)]

    def source(w, step, owner, low=0, high=None):
        if step:
            return spot(w, owner, s, low, high)
        return shards[w].at[pl.ds(low, (sizes[w] if high is None else high) - low), :]

    def own_copy(w):
        return pltpu.make_async_copy(shards[w], spot(w, t, s), local_sem.at[w])

    def plane_copies(index):
        w, step, low, high = items[index]
        owner = nearest(t, step)
        src, dst = source(w, step, owner, low, high), spot(w, owner, s, low, high)
        return (
            remote(src, dst, send_sem.at[index, 0], first_sem.at[index], (first, t)),
            remote(src, dst, send_sem.at[index, 1], second_sem.at[index, 0], (second, t)),
            remote(src, dst, send_sem.at[index, 2], other_sem.at[index, 0], (other, t)),
        )

    def found(index, column):
        w, step, low, high = items[index]
        return spot(w, nearest(t, step), column, low, high)

    def relay_copies(index):
        src = found(index, first)
        return (
            remote(src, src, send_sem.at[index, 3], second_sem.at[index, 1], (second, t)),
            remote(src, src, send_sem.at[index, 4], other_sem.at[index, 1], (other, t)),
        )

    def last_copies(index):
        near, far = found(index, second), found(index, diagonal)
        return (
            remote(near, near, send_sem.at[index, 5], other_sem.at[index, 2], (other, t)),
            remote(far, far, send_sem.at[index, 6], other_sem.at[index, 3], (other, t)),
        )

    def parcel(w, step, column, up):
        owner = nearest(t, step)
        dst = spot(w, owner, columns[column])
        src = shards[w] if step == 0 and column == 0 else dst
        sem, device = (up_sem, t + 1) if up else (down_sem, t - 1)
        return remote(src, dst, sem.at[w, owner, column], line_sem.at[w, owner, column], (s, device))

    def across(step, column):
        block = spot(4, nearest(t, step), columns[column])
        return remote(block, block, down_send.at[step, column], down_recv.at[step, column], (other, t))

    def goes(step, up):
        owner = nearest(t, step)
        if step == 0:
            return t < TP - 1 if up else t > 0
        return (owner < t) & (t < TP - 1) if up else (owner > t) & (t > 0)

    def set_out(w, column=0):
        for up in (True, False):

            @pl.when(goes(0, up))
            def _(up=up):
                parcel(w, 0, column, up).start()

    inside = (t > 0) & (t < TP - 1)

    def pass_on(w, step, column=0, where=None):
        def act():
            parcel(w, step, column, True).wait_recv()
            for up in (True, False):

                @pl.when(goes(step, up))
                def _(up=up):
                    parcel(w, step, column, up).start()

            if w == 4:
                across(step, column).start()

        if where is None:
            act()
        else:
            pl.when(where)(act)

    down_parcels = [(step, column) for step in range(1, TP) for column in range(4)]

    def line_pass(now, where):
        if now + 2 < len(items):
            w, step, low, high = items[now + 2]
            if step and low == 0:
                pass_on(w, step, 0, where)

    def down_pass(now):
        for at, where in ((now - 6, inside), (now - 8, jnp.logical_not(inside))):
            if 0 <= at < len(down_parcels):
                pass_on(4, *down_parcels[at], where)

    relayed, ended = [], []

    def stage_a(index):
        if items[index][1] == 0:
            own_copy(items[index][0]).start()
        for copy in plane_copies(index):
            copy.start()

    def stage_b(until):
        while len(relayed) <= min(until, len(items) - 1):
            index = len(relayed)
            relayed.append(index)
            block = found(index, first)
            remote(block, block, send_sem.at[index, 0], first_sem.at[index], (first, t)).wait_recv()
            for copy in relay_copies(index):
                copy.start()

    def stage_c(until):
        while len(ended) <= min(until, len(items) - 1):
            index = len(ended)
            ended.append(index)
            for part, column in enumerate((second, diagonal)):
                block = found(index, column)
                remote(block, block, send_sem.at[index, 1], second_sem.at[index, part], (second, t)).wait_recv()
            for copy in last_copies(index):
                copy.start()

    def tick(now):
        stage_b(now - LAG_B)
        if now < len(items):
            stage_a(now)
        stage_c(now - LAG_C)
        if now == 5:
            set_out(2)
            set_out(3)
            line_pass(now - 1, None)
            line_pass(now, inside)
        line_pass(now + 1, inside)
        line_pass(now, jnp.logical_not(inside))
        down_pass(now)

    keeps = []

    def keep(src, dst):
        copy = functools.partial(pltpu.make_async_copy, src, dst, copy_sem.at[len(keeps)])
        copy().start()
        keeps.append(copy)

    def ready(index):
        w, step, low, high = items[index]
        owner = nearest(t, step)
        if step == 0:
            own_copy(w).wait()
        for part, column in enumerate((other, second + shift, first + shift, diagonal + shift)):
            block = found(index, column)
            remote(block, block, send_sem.at[index, 2], other_sem.at[index, part], (other, t)).wait_recv()
        block = rows_of(owner, sizes[w])
        if w < 2:
            keep(whole[w].at[block, :], whole_out[w].at[block, :])
        return owner, block

    def down_ready(step):
        if step == 0:
            ready(1)
            return
        for column, index in enumerate((other, second + shift, first + shift, diagonal + shift)):
            block = spot(4, nearest(t, step), index)
            remote(block, block, down_send.at[step, column], down_recv.at[step, column], (other, t)).wait_recv()

    def rate_copy(step):
        return remote(rates.at[t], rates.at[t], rate_send.at[step - 1], rate_recv.at[step - 1], (s, (t + step) % TP))

    row = lax.broadcasted_iota(jnp.int32, (8, HEAD), 0)
    rates[t] = jnp.where(row == 0, rate_in[0], rate_in[1])
    for step in range(1, TP):
        rate_copy(step).start()
    stage_a(0)
    set_out(0)
    set_out(1)
    set_out(4)
    stage_a(1)
    boundary = bounds[t]
    edge = boundary - s * rows

    for index in range(SEQ):
        hidden_load(index).wait()
        cot_load(index).start()

    def prepare(part, start):
        values = hidden[part, :].astype(F32)
        scale = lax.rsqrt(jnp.mean(values * values, axis=-1, keepdims=True) + EPSILON)
        normed[part, :] = (values * scale).astype(BF16)
        row = lax.broadcasted_iota(jnp.int32, (BLOCK, rows), 0) + start
        column = lax.broadcasted_iota(jnp.int32, (BLOCK, rows), 1)
        apart = (column > row) | ((row >= edge) & (column < edge))
        distance[part, :] = jnp.where(apart, -1, row - column).astype(F32)

    every_rows(rows, prepare)
    keep(normed, normed_out)
    half_copy(0).start()
    for step in range(1, TP):
        here = rates.at[t]
        remote(here, here, rate_send.at[step - 1], rate_recv.at[step - 1], (s, t)).wait_recv()
    keep(rates, rate_out)

    before = jnp.where(s * rows - 1 >= boundary, 1, 0)
    last = jnp.where(s * rows + rows - 1 >= boundary, 1, 0)

    def rate_of(block, half):
        return rates[block, half : half + 1, :]

    def row_numbers(start, count):
        return lax.broadcasted_iota(jnp.int32, (count, HEAD), 0) + start

    def project(step, index):
        owner, block = ready(index)
        wide[:, 0:D] = dots(normed[...], whole[0][block, :], NT)

        def shape_rows(part, start):
            turn, lean = cosine[part, :], sine[part, :]
            for kind in range(2):
                for half in range(2):
                    at = kind * PAIR + half * HEAD
                    values = wide[part, at : at + HEAD]
                    logistic = 1.0 / (1.0 + jnp.exp(-values))
                    acts[owner, part, at : at + HEAD] = rotated(values * logistic, turn, lean).astype(BF16)
                    pack[owner, part, at : at + HEAD] = (
                        logistic * (1.0 + values * (1.0 - logistic))
                    ).astype(BF16)
            acts[owner, part, 2 * PAIR : 4 * PAIR] = wide[part, 2 * PAIR : 4 * PAIR].astype(BF16)
            number = row_numbers(start, WEIGH)
            valid = jnp.where(jnp.where(number >= edge, 1, 0) == last, 1.0, 0.0)
            for half in range(2):
                fade = jnp.exp(-rate_of(owner, half) * (rows - 1 - number).astype(F32)) * valid
                keys = acts[owner, part, PAIR + half * HEAD : PAIR + half * HEAD + HEAD].astype(F32)
                weights[part, half * HEAD : half * HEAD + HEAD] = (keys * fade).astype(BF16)

        every_rows(rows, shape_rows, WEIGH)
        for half in range(2):
            at = half * HEAD
            state[owner * 2 + half] = dots(
                weights[:, at : at + HEAD], acts[owner, :, 2 * PAIR + at : 2 * PAIR + at + HEAD], TN
            ).astype(BF16)

    def attend(step):
        owner = nearest(t, step)
        for half in range(2):
            at = half * HEAD
            rate = rates[owner, half : half + 1, :]
            for top in range(0, rows, PAIR):
                width = top + PAIR
                scores[0:PAIR, 0:width] = dots(
                    acts[owner, top : top + PAIR, at : at + HEAD], acts[owner, 0:width, PAIR + at : PAIR + at + HEAD], NT
                )

                def weigh(part, start, width=width, top=top, rate=rate):
                    for left in range(0, width, HEAD):
                        apart = distance[pl.ds(pl.multiple_of(start + top, WEIGH), WEIGH), left : left + HEAD]
                        fade = jnp.where(apart >= 0.0, jnp.exp(-rate * apart), 0.0)
                        weights[part, left : left + HEAD] = (scores[part, left : left + HEAD] * fade).astype(BF16)

                every_rows(PAIR, weigh, WEIGH)
                column = pl.ds(pl.multiple_of(owner * PAIR + at, HEAD), HEAD)
                mixed[top : top + PAIR, column] = dots(
                    weights[0:PAIR, 0:width], acts[owner, 0:width, 2 * PAIR + at : 2 * PAIR + at + HEAD], NN
                )

    def prefix_scale(block, source_block, rate):
        same = jnp.where((source_block + 1) * rows - 1 >= boundary, 1, 0) == jnp.where(block * rows - 1 >= boundary, 1, 0)
        usable = flag(source_block < block) * flag(same)
        gap = jnp.maximum(block - 1 - source_block, 0).astype(F32)
        return jnp.exp(-rate * (rows * gap)) * usable

    begin_states, add_pair, add_chips, finish_states, close_states = state_exchange(
        rows, boundary, exchange, rates, prefix_scale, lambda chip: 2 * chip + 2, lambda chip: 2 * chip + 1
    )

    def mix():
        finish_states()
        keep(incoming, incoming_out)
        for block in range(TP):
            for half in range(2):
                at = half * HEAD
                scores[:, at : at + HEAD] = dots(acts[block, :, at : at + HEAD], incoming[2 * block + half], NN)

            def add_outer(part, start, block=block):
                number = row_numbers(start, NARROW)
                valid = jnp.where(jnp.where(number >= edge, 1, 0) == before, 1.0, 0.0)
                for half in range(2):
                    fade = jnp.exp(-rate_of(block, half) * (number + 1).astype(F32)) * valid
                    column = slice(block * PAIR + half * HEAD, block * PAIR + half * HEAD + HEAD)
                    mixed[part, column] += fade * scores[part, half * HEAD : half * HEAD + HEAD]

            every_rows(rows, add_outer, NARROW)

        def gate_rows(part, start):
            values = mixed[part, :]
            scale = lax.rsqrt(jnp.mean(values * values, axis=-1, keepdims=True) + EPSILON)
            inv_mix[part, :] = jnp.broadcast_to(scale, (BLOCK, HEAD))
            values = values * scale
            for block in range(TP):
                column = slice(block * PAIR, block * PAIR + PAIR)
                gate = acts[block, part, 3 * PAIR : 4 * PAIR].astype(F32)
                pack[block, part, 2 * PAIR : 3 * PAIR] = (values[:, column] * gate).astype(BF16)
                pack[block, part, 3 * PAIR : 4 * PAIR] = values[:, column].astype(BF16)

        every_rows(rows, gate_rows, BLOCK)
        keep(acts, acts_out)
        keep(pack, pack_out)
        half_copy(3).start()
        keep(inv_mix, inv_mix_out)

    def project_out():
        for block in range(TP):
            term = dots(pack[block, :, 2 * PAIR : 3 * PAIR], whole[1][block * PAIR : block * PAIR + PAIR, :], NN)
            if block:
                wide[:, 0:D] += term
            else:
                wide[:, 0:D] = term

        def norm_rows(part, start):
            values = hidden[part, :].astype(F32) + wide[part, 0:D]
            mixed[part, :] = values
            scale = lax.rsqrt(jnp.mean(values * values, axis=-1, keepdims=True) + EPSILON)
            inv_second[part, :] = jnp.broadcast_to(scale, (BLOCK, HEAD))
            second_normed[part, :] = (values * scale).astype(BF16)

        every_rows(rows, norm_rows)
        keep(second_normed, second_out)
        half_copy(1).start()
        keep(inv_second, inv_second_out)

    def left_side(index):
        owner, block = ready(index)
        down_ready(items[index][1])
        wide[:, 0:units] = dots(second_normed[...], whole[2][block, :], NT)
        wide[:, 2 * beside : 2 * beside + units] = dots(cot[...], whole[4][block, :], NT)

    def side_copies(slot, owner):
        return [
            pltpu.make_async_copy(sides.at[slot, part], out.at[owner], side_sem.at[slot, part])
            for part, out in enumerate((glu_out, left_out, right_out))
        ]

    def side_remotes(slot, step):
        owner = nearest(t, step)
        return [
            remote(sides.at[slot, part], out.at[owner], side_send.at[slot, part], side_recv.at[step, part], (other, t))
            for part, out in enumerate((glu_other, left_other, right_other))
        ]

    def right_side(index):
        owner, block = ready(index)
        w, step, low, high = items[index]
        part_rows = pl.ds(pl.multiple_of(owner * units + low, 16), high - low)
        wide[:, beside + low : beside + high] = dots(second_normed[...], whole[3][part_rows, :], NT)
        slot = step % 2
        if step >= 2 and low == 0:
            for copy in side_copies(slot, nearest(t, step - 2)):
                copy.wait()
            for copy in side_remotes(slot, step - 2):
                copy.wait_send()

        def multiply(part, start):
            left, right = wide[part, low:high], wide[part, beside + low : beside + high]
            grad = wide[part, 2 * beside + low : 2 * beside + high]
            sides[slot, 0, part, low:high] = (left * right).astype(BF16)
            sides[slot, 1, part, low:high] = (grad * right).astype(BF16)
            sides[slot, 2, part, low:high] = (grad * left).astype(BF16)

        every_rows(rows, multiply)
        if high == units:
            for copy in side_copies(slot, owner) + side_remotes(slot, step):
                copy.start()
        mixed[...] += dots(sides[slot, 0, :, low:high], whole[4][part_rows, :], NN)
        term = dots(sides[slot, 1, :, low:high], whole[2][part_rows, :], NN) + dots(
            sides[slot, 2, :, low:high], whole[3][part_rows, :], NN
        )
        if step:
            back[...] += term
        else:
            back[...] = term

    stage_b(0)
    pass_on(0, 1)
    stage_a(2)
    stage_b(1)
    set_out(4, 1)
    stage_c(0)
    pass_on(0, 2)
    stage_a(3)
    stage_b(2)
    stage_c(1)
    set_out(4, 2)
    set_out(4, 3)
    pass_on(0, 3)
    stage_a(4)
    project(0, 0)
    tick(5)
    for step in range(1, TP):
        tick(5 + step)
        project(step, 1 + step)
    begin_states()
    for index in range(SEQ):
        cot_load(index).wait()
    half_copy(2).start()
    tick(9)
    add_pair()
    attend(0)
    tick(10)
    attend(1)
    tick(11)
    attend(2)
    attend(3)
    add_chips()
    tick(12)
    for index in range(5, 5 + TP):
        ready(index)
    mix()
    tick(13)
    project_out()
    for index in range(5 + TP, len(items)):
        if index > 5 + TP:
            tick(index + LAG_C)
        (left_side, right_side)[items[index][0] - 2](index)

    def finish(part, start):
        for index in range(SEQ):
            result_out[part, plain(index)] = mixed[part, place_of(index)].astype(BF16)

    keep(back, back_out)
    every_rows(rows, finish)

    for step in range(1, TP):
        rate_copy(step).wait_send()
    close_states()
    for copy in keeps:
        copy().wait()
    for part in range(4):
        half_copy(part).wait()
    for step in range(TP):
        for copy in side_remotes(step % 2, step):
            copy.wait_recv()
            if step >= 2:
                copy.wait_send()
        if step >= 2:
            for copy in side_copies(step % 2, nearest(t, step)):
                copy.wait()
    for index in range(len(items)):
        for copy in plane_copies(index) + relay_copies(index) + last_copies(index):
            copy.wait_send()
    for w in range(5):
        for step in range(TP):
            for column in range(4 if w == 4 else 1):
                for up in (True, False):

                    @pl.when(goes(step, up))
                    def _(w=w, step=step, column=column, up=up):
                        parcel(w, step, column, up).wait_send()

                if w == 4 and step:
                    across(step, column).wait_send()


KEPT = 20


def forward(heads_in, shards, hidden, cot, cosine, sine, rate, bounds):
    rows = hidden.shape[1]
    sizes = (4 * PAIR, *(shard.shape[0] for shard in shards))
    units = sizes[2]
    beside = -(-units // HEAD) * HEAD
    items = 4 * TP + 2
    dma = pltpu.SemaphoreType.DMA
    vmem = pl.BlockSpec(memory_space=pltpu.VMEM)
    anywhere = pl.BlockSpec(memory_space=pl.ANY)
    heads = 2 * TP
    shape = jax.ShapeDtypeStruct
    outs = [
        *[shape((TP * size, D), BF16) for size in sizes[:2]],
        *[shape((TP, rows, 4 * PAIR), BF16)] * 2,
        *[shape((rows, D), BF16)] * 2,
        *[shape((TP, rows, units), BF16)] * 6,
        shape((TP, rows, PAIR), BF16),
        *[shape((rows, D // 2), BF16)] * 3,
        shape((rows, D), F32),
        shape((heads, HEAD, HEAD), BF16),
        shape((rows, HEAD), F32),
        shape((rows, HEAD), F32),
        shape((TP, 8, HEAD), F32),
        shape((rows, D), BF16),
    ]
    return pl.pallas_call(
        functools.partial(forward_kernel, rows, sizes),
        out_shape=outs,
        in_specs=[vmem] * 4 + [anywhere] * 6 + [vmem] * 2 + [pl.BlockSpec(memory_space=pltpu.SMEM)] * 2,
        out_specs=[anywhere] * (len(outs) - 1) + [vmem],
        scratch_shapes=[pltpu.VMEM((TP * size, D), BF16) for size in sizes]
        + [
            *[pltpu.VMEM((TP, rows, 4 * PAIR), BF16)] * 2,
            *[pltpu.VMEM((rows, D), BF16)] * 4,
            pltpu.VMEM((2, 3, rows, units), BF16),
            pltpu.VMEM((rows, D), F32),
            pltpu.VMEM((rows, 3 * beside), F32),
            pltpu.VMEM((rows, D), F32),
            pltpu.VMEM((rows, rows), F32),
            pltpu.VMEM((rows, rows), F32),
            pltpu.VMEM((rows, rows), BF16),
            pltpu.VMEM((rows, HEAD), F32),
            pltpu.VMEM((rows, HEAD), F32),
            pltpu.VMEM((TP, 8, HEAD), F32),
            pltpu.VMEM((4 * PAIR, STRIPE), BF16),
            *state_scratch(),
            dma((5,)),
            dma((5, TP, 4)),
            dma((5, TP, 4)),
            dma((5, TP, 4)),
            dma((TP, 4)),
            dma((TP, 4)),
            dma((items, 7)),
            dma((items,)),
            dma((items, 2)),
            dma((items, 4)),
            dma((TP - 1,)),
            dma((TP - 1,)),
            dma((KEPT,)),
            dma((2, 3)),
            dma((2, 3)),
            dma((TP, 3)),
            dma((4,)),
            dma((4,)),
            dma((SEQ,)),
            dma((SEQ,)),
        ],
        compiler_params=pltpu.CompilerParams(
            collective_id=0, has_side_effects=True, vmem_limit_bytes=63 * 2**20
        ),
        name="forward",
    )(*heads_in, *shards, hidden, cot, cosine, sine, rate, bounds)


PIECES = 4
HELD = 6
LAG_2, LAG_3, LAG_4, HOP, LAG_5 = 2, 4, 6, 2, 13
KINDS = 6
BEFORE, EARLY, WAIT_1, WAIT_2 = 10, 2, 3, 9
ITEMS = KINDS * TP


def add_rows(target, *terms):
    rows = target.shape[0]

    step = rows // 4

    @pl.loop(0, 4)
    def _(block):
        part = pl.ds(pl.multiple_of(block * step, 16), step)
        total = terms[0][part, :].astype(F32)
        for term in terms[1:]:
            total = total + term[part, :].astype(F32)
        target[part, :] = total.astype(target.dtype)


def backward_kernel(rows, sizes, *refs):
    whole, refs = refs[:2], refs[2:]
    (acts_in, pack_in, normed_in, second_in, glu_own, left_own, right_own, glu_other, left_other, right_other,
     gated_other, normed_other, second_other, cot_other, back_in, output_in, hidden_in, cot_in,
     incoming, inv_mix, inv_second, rates, cosine, sine, bounds), refs = refs[:25], refs[25:]
    (down_grad, left_grad, right_grad, out_grad, qkvg_grad, output_whole, input_whole,
     backs_own, backs_other), refs = refs[:9], refs[9:]
    (tiles, cot, second_normed, normed, attn_cot, halves, acts, pack, backs, mid, wide, distance, scores,
     weights, slopes, faded, lhs, held), refs = refs[:18], refs[18:]
    exchange, refs = refs[:10], refs[10:]
    state, later = exchange[0], exchange[5]
    lands, refs = refs[:9], refs[9:]
    (tile_sem, half_sem, half_load_sem, backs_keep, backs_send, backs_recv, load_sem, cot_sem, hidden_sem, lhs_sem, second_send, second_recv,
     first_send, first_recv, line_send, below_recv, above_recv, share_local, share_up, share_down, share_recv) = refs
    s, t, other, first, second, diagonal = place()
    core = s % 2
    units = sizes[2]
    half_d = D // 2
    ours, theirs = rows_of(core, half_d), rows_of(1 - core, half_d)
    boundary = bounds[t]
    edge = boundary - s * rows
    before = jnp.where(s * rows - 1 >= boundary, 1, 0)
    last = jnp.where(s * rows + rows - 1 >= boundary, 1, 0)
    around = (first, second, diagonal)
    order = [3, 2, 1, 0]
    local = pltpu.make_async_copy

    done = set()

    def once(key, wait):
        if key not in done:
            done.add(key)
            wait()

    greet(s, t, (other, first, second, diagonal))

    def cot_load(index):
        return local(cot_in.at[t, :, plain(index)], cot.at[:, place_of(index)], cot_sem.at[index])

    def hidden_load(index):
        return local(hidden_in.at[t, :, plain(index)], acts.at[0, :, place_of(index)], hidden_sem.at[index])

    def second_load():
        return local(second_in, second_normed, load_sem.at[0])

    def normed_load():
        return local(normed_in, normed, load_sem.at[1])

    def acts_load():
        return local(acts_in, acts, load_sem.at[2])

    def pack_load():
        return local(pack_in, pack, load_sem.at[3])

    def back_load():
        return local(back_in, mid, load_sem.at[4])

    def half_load(part):
        return local((cot_other, second_other, normed_other)[part], halves.at[part], half_load_sem.at[part])

    def half_copy():
        return remote(attn_cot.at[:, theirs], halves.at[3], half_sem.at[0], half_sem.at[1], (other, t))

    tile_list = [(1, part) for part in range(2)] + [(0, part) for part in range(2 * TP)]

    def tile_load(index):
        w, at = tile_list[index]
        return local(whole[w].at[pl.ds(at * half_d, half_d), :], tiles.at[index % 3], tile_sem.at[index % 3])

    def tile(index):
        tile_load(index).wait()
        return tiles[index % 3]

    def tile_next(index):
        if index + 3 < len(tile_list):
            tile_load(index + 3).start()

    def backs_keep_copy(block):
        return local(backs.at[block], backs_own.at[block], backs_keep.at[block])

    def backs_copy(block):
        return remote(backs.at[block], backs_other.at[block], backs_send.at[block], backs_recv.at[block], (other, t))

    piece_rows = rows // PIECES
    shares = ((output_in, output_whole), (acts.at[1], input_whole))

    def piece(a, owner, p):
        return shares[a][1].at[owner, pl.ds(p * piece_rows, piece_rows), :]

    def own_piece(a, p):
        return shares[a][0].at[pl.ds(p * piece_rows, piece_rows), :]

    def share_copy(a, p, owner, src, up):
        sem, target = (share_up, t + 1) if up else (share_down, t - 1)
        return remote(src, piece(a, owner, p), sem.at[a, p, owner], share_recv.at[a, p, owner], (s, target))

    def share_keep(a, p):
        return local(own_piece(a, p), piece(a, t, p), share_local.at[a, p])

    def share_start(a, p):
        @pl.when(t < TP - 1)
        def _():
            share_copy(a, p, t, own_piece(a, p), True).start()

        @pl.when(t > 0)
        def _():
            share_copy(a, p, t, own_piece(a, p), False).start()

        share_keep(a, p).start()

    relays = [
        (a, p, step) for a in range(2) for steps in ((1, 2), (3,)) for p in range(PIECES) for step in steps
    ]
    relayed = []

    def passes(owner, up):
        return (owner < t) & (t < TP - 1) if up else (owner > t) & (t > 0)

    def relay(limit, until=len(relays)):
        for _ in range(limit):
            if len(relayed) >= until:
                return
            a, p, step = relays[len(relayed)]
            relayed.append(1)
            owner = nearest(t, step)
            for up in (True, False):

                @pl.when(passes(owner, up))
                def _(up=up):
                    share_copy(a, p, owner, piece(a, owner, p), up).wait_recv()
                    share_copy(a, p, owner, piece(a, owner, p), up).start()

    items = (
        [(0, step) for step in order]
        + [(kind, step) for step in order for kind in (1, 2)]
        + [(3, step) for step in order]
        + [(kind, step) for step in order for kind in (4, 5)]
    )
    heights = (units, units, units, sizes[1], half_d, half_d)

    def lands_of(index):
        kind, step = items[index]
        owner = nearest(t, step)
        group, base, extra = ((0, kind * TP, 3 * TP + kind), (1, 0, TP), (2, (kind - 4) * TP, 2 * TP + kind - 4))[
            0 if kind < 3 else 1 if kind == 3 else 2
        ]
        return owner, lands[3 * group : 3 * group + 3], base + owner, extra

    def own_source(kind, owner):
        if kind == 0:
            return glu_own.at[owner], glu_other.at[owner]
        if kind == 1:
            return left_own.at[owner], left_other.at[owner]
        if kind == 2:
            return right_own.at[owner], right_other.at[owner]
        if kind == 3:
            return pack_in.at[owner, :, 2 * PAIR : 3 * PAIR], gated_other.at[owner]
        part = slice((kind - 4) * half_d, (kind - 3) * half_d)
        return backs_own.at[owner, :, part], backs_other.at[owner, :, part]

    def lhs_loads(index):
        kind, step = items[index]
        slot = index % 2
        return [
            local(src, lhs.at[slot, part, :, pl.ds(0, heights[kind])], lhs_sem.at[slot, part])
            for part, src in enumerate(own_source(kind, nearest(t, step)))
        ]

    def prefetch(index):
        kind, step = items[index]
        owner = nearest(t, step)
        if kind >= 4:
            once(("backs", step), lambda: backs_keep_copy(owner).wait())
            once(("backs_other", step), lambda: backs_copy(owner).wait_recv())
        for copy in lhs_loads(index):
            copy.start()

    def to_second(index):
        kind = items[index][0]
        owner, (second_land, first_land, line_land), at, extra = lands_of(index)
        return [
            remote(
                held.at[index % HELD, column // 2, pl.ds(0, heights[kind]), :],
                second_land.at[at, part],
                second_send.at[index, part],
                second_recv.at[index, part],
                (second, t),
            )
            for part, column in enumerate((diagonal, second))
        ]

    def to_first(index):
        owner, (second_land, first_land, line_land), at, extra = lands_of(index)
        return remote(second_land.at[at, 0], first_land.at[at], first_send.at[index], first_recv.at[index], (first, t))

    def along(index, up):
        kind = items[index][0]
        owner, (second_land, first_land, line_land), at, extra = lands_of(index)
        if up:
            return remote(
                first_land.at[at], line_land.at[at], line_send.at[index], below_recv.at[kind, owner], (s, t + 1)
            )
        final = jnp.where(owner == t - 1, 1, 0)
        return remote(
            first_land.at[at],
            line_land.at[at + final * (extra - at)],
            line_send.at[index],
            above_recv.at[kind, owner],
            (s, t - 1),
        )

    def held_rows(index, chip):
        return held.at[index % HELD, chip, pl.ds(0, heights[items[index][0]]), :]

    def advance(now):
        index = now - LAG_2
        if 0 <= index < ITEMS:
            owner, (second_land, first_land, line_land), at, extra = lands_of(index)
            for copy in to_second(index):
                copy.wait_recv()
            add_rows(second_land.at[at, 0], second_land.at[at, 0], held_rows(index, first // 2))
            to_first(index).start()
        index = now - LAG_3
        if 0 <= index < ITEMS:
            owner, (second_land, first_land, line_land), at, extra = lands_of(index)
            to_first(index).wait_recv()
            add_rows(first_land.at[at], first_land.at[at], held_rows(index, s // 2), second_land.at[at, 1])
        for hop in range(TP - 1):
            index = now - LAG_4 - HOP * hop
            if not 0 <= index < ITEMS or items[index][1] == 0:
                continue
            owner, (second_land, first_land, line_land), at, extra = lands_of(index)
            for up in (True, False):

                @pl.when((t == hop) & (owner > t) if up else (t == TP - 1 - hop) & (owner < t))
                def _(index=index, at=at, up=up, first_land=first_land, line_land=line_land, hop=hop):
                    if hop:
                        along(index, up).wait_recv()
                        add_rows(first_land.at[at], first_land.at[at], line_land.at[at])
                    along(index, up).start()

        index = now - LAG_5
        if 0 <= index < ITEMS:
            kind, step = items[index]
            owner, (second_land, first_land, line_land), at, extra = lands_of(index)
            if step == 0:
                target = (down_grad, left_grad, right_grad, out_grad, qkvg_grad, qkvg_grad)[kind]
                if kind >= 4:
                    target = target.at[(kind - 4) * half_d : (kind - 3) * half_d]

                @pl.when(t == 0)
                def _():
                    along(index, False).wait_recv()
                    add_rows(target, first_land.at[at], line_land.at[extra])

                @pl.when(t == TP - 1)
                def _():
                    along(index, True).wait_recv()
                    add_rows(target, first_land.at[at], line_land.at[at])

                @pl.when((t > 0) & (t < TP - 1))
                def _():
                    along(index, True).wait_recv()
                    along(index, False).wait_recv()
                    add_rows(target, first_land.at[at], line_land.at[at], line_land.at[extra])

    def produce(index):
        kind, step = items[index]
        height = heights[kind]
        right, part = ((cot, 0), (second_normed, 1), (second_normed, 1), (attn_cot, 3), (normed, 2), (normed, 2))[kind]
        once(("half", part), lambda: half_copy().wait_recv() if part == 3 else half_load(part).wait())
        if kind >= 4:
            once("normed", lambda: normed_load().wait())
        for copy in lhs_loads(index):
            copy.wait()
        if index >= HELD:
            for copy in to_second(index - HELD):
                copy.wait_send()
        slot = index % 2
        product = dots(lhs[slot, 0, :, 0:height], right[:, ours], TN) + dots(lhs[slot, 1, :, 0:height], halves[part], TN)
        for chip in range(4):
            held[index % HELD, chip, 0:height, :] = product[:, chip * STRIPE : chip * STRIPE + STRIPE].astype(BF16)
        for copy in to_second(index):
            copy.start()
        advance(index)

    for index in range(SEQ):
        cot_load(index).start()
    half_load(0).start()
    prefetch(0)
    for p in range(PIECES):
        share_start(0, p)
    back_load().start()
    second_load().start()
    half_load(1).start()
    for index in range(3):
        tile_load(index).start()
    acts_load().start()
    pack_load().start()
    normed_load().start()
    half_load(2).start()
    for index in range(SEQ):
        cot_load(index).wait()
    produce(0)
    prefetch(1)
    back_load().wait()
    second_load().wait()

    def middle(part, start):
        unit = second_normed[part, :].astype(F32)
        values = mid[part, :]
        inner = jnp.mean(values * unit, axis=-1, keepdims=True)
        values = cot[part, :].astype(F32) + inv_second[part, 0:1] * (values - unit * inner)
        mid[part, :] = values
        attn_cot[part, :] = values.astype(BF16)

    every_rows(rows, middle)
    half_copy().start()
    produce(1)
    prefetch(2)
    at_tile = 0
    for part in range(2):
        wide[:, part * half_d : part * half_d + half_d] = dots(attn_cot[...], tile(at_tile + part), NT)
        tile_next(at_tile + part)
    at_tile += 2
    acts_load().wait()
    pack_load().wait()

    def head_rows(part, start):
        total = jnp.zeros((BLOCK, 1), F32)
        for block in range(TP):
            values = wide[part, block * PAIR : block * PAIR + PAIR]
            gate = acts[block, part, 3 * PAIR : 4 * PAIR].astype(F32)
            unit = pack[block, part, 3 * PAIR : 4 * PAIR].astype(F32)
            total += jnp.sum(values * gate * unit, axis=-1, keepdims=True)
        total = total * (1.0 / D)
        scale = inv_mix[part, 0:1]
        for block in range(TP):
            values = wide[part, block * PAIR : block * PAIR + PAIR]
            gate = acts[block, part, 3 * PAIR : 4 * PAIR].astype(F32)
            unit = pack[block, part, 3 * PAIR : 4 * PAIR].astype(F32)
            backs[block, part, 3 * PAIR : 4 * PAIR] = (values * unit).astype(BF16)
            backs[block, part, 2 * PAIR : 3 * PAIR] = (scale * (values * gate - unit * total)).astype(BF16)
        row = lax.broadcasted_iota(jnp.int32, (BLOCK, rows), 0) + start
        column = lax.broadcasted_iota(jnp.int32, (BLOCK, rows), 1)
        apart = (column > row) | ((row >= edge) & (column < edge))
        distance[part, :] = jnp.where(apart, -1, row - column).astype(F32)

    every_rows(rows, head_rows)
    produce(2)
    prefetch(3)
    relay(2, 12)

    def rate_of(block, half):
        return rates[block, half : half + 1, :]

    def row_numbers(start):
        return lax.broadcasted_iota(jnp.int32, (NARROW, HEAD), 0) + start

    for block in range(TP):
        for half in range(2):
            at = half * HEAD

            def fade_rows(part, start, block=block, half=half, at=at):
                number = row_numbers(start)
                valid = jnp.where(jnp.where(number >= edge, 1, 0) == before, 1.0, 0.0)
                fade = jnp.exp(-rate_of(block, half) * (number + 1).astype(F32)) * valid
                values = backs[block, part, 2 * PAIR + at : 2 * PAIR + at + HEAD].astype(F32)
                faded[part, :] = (values * fade).astype(BF16)

            every_rows(rows, fade_rows, NARROW)
            head = 2 * block + half
            state[head] = dots(acts[block, :, at : at + HEAD], faded[...], TN).astype(BF16)
            wide[:, head * HEAD : head * HEAD + HEAD] = dots(faded[...], incoming[head], NT)

    def suffix_scale(block, source_block, rate):
        same = jnp.where(source_block * rows - 1 >= boundary, 1, 0) == jnp.where(block * rows + rows - 1 >= boundary, 1, 0)
        usable = flag(source_block > block) * flag(same)
        gap = jnp.maximum(source_block - 1 - block, 0).astype(F32)
        return jnp.exp(-rate * (rows * gap)) * usable

    begin_states, add_pair, add_chips, finish_states, close_states = state_exchange(
        rows, boundary, exchange, rates, suffix_scale, lambda chip: 2 * chip - 1, lambda chip: 2 * chip
    )
    begin_states()
    produce(3)
    prefetch(4)
    relay(2, 12)
    add_pair()
    weights[0:PAIR, PAIR:rows] = jnp.zeros((PAIR, rows - PAIR), BF16)
    slopes[0:PAIR, PAIR:rows] = jnp.zeros((PAIR, rows - PAIR), BF16)

    def attend(block):
        for half in range(2):
            at = half * HEAD
            head = 2 * block + half
            rate = rate_of(block, half)
            query, key, value = [slice(kind * PAIR + at, kind * PAIR + at + HEAD) for kind in range(3)]
            mine_columns = slice(head * HEAD, head * HEAD + HEAD)
            for top in range(0, rows, PAIR):
                width = top + PAIR
                scores[0:PAIR, 0:width] = dots(acts[block, top:width, query], acts[block, 0:width, key], NT)
                scores[PAIR : 2 * PAIR, 0:width] = dots(backs[block, top:width, value], acts[block, 0:width, value], NT)

                def weigh(part, start, width=width, top=top):
                    below = pl.ds(pl.multiple_of(start + PAIR, WEIGH), WEIGH)
                    there = pl.ds(pl.multiple_of(start + top, WEIGH), WEIGH)
                    for left in range(0, width, HEAD):
                        apart = distance[there, left : left + HEAD]
                        fade = jnp.where(apart >= 0.0, jnp.exp(-rate * apart), 0.0)
                        weights[there, left : left + HEAD] = (scores[part, left : left + HEAD] * fade).astype(BF16)
                        grad = scores[below, left : left + HEAD].astype(BF16).astype(F32)
                        slopes[there, left : left + HEAD] = (grad * fade).astype(BF16)

                every_rows(PAIR, weigh, WEIGH)
                wide[top:width, mine_columns] += dots(slopes[top:width, 0:width], acts[block, 0:width, key], NN)
            inner = dots(weights[...], backs[block, :, value], TN)
            acts[block, :, 3 * PAIR + at : 3 * PAIR + at + HEAD] = inner.astype(BF16)
            inner = dots(slopes[...], acts[block, :, query], TN)
            backs[block, :, key] = inner.astype(BF16)

            def turn_back(part, start):
                turned = rotated(wide[part, mine_columns], cosine[part, :], -sine[part, :])
                backs[block, part, query] = (turned * pack[block, part, query].astype(F32)).astype(BF16)

            every_rows(rows, turn_back, NARROW)

    for block in range(TP):
        attend(block)
        produce(4 + block)
        prefetch(5 + block)
        relay(2, 12)

    add_chips()
    produce(8)
    prefetch(9)
    relay(2, 12)
    finish_states()

    for block in range(TP):
        for half in range(2):
            at = half * HEAD
            head = 2 * block + half
            query, key, value = [slice(kind * PAIR + at, kind * PAIR + at + HEAD) for kind in range(3)]
            scores[:, 0:HEAD] = dots(acts[block, :, value], later[head], NT)
            scores[:, HEAD : 2 * HEAD] = dots(acts[block, :, key], later[head], NN)

            def finish_rows(part, start, block=block, half=half, at=at, key=key, value=value):
                number = row_numbers(start)
                valid = jnp.where(jnp.where(number >= edge, 1, 0) == last, 1.0, 0.0)
                fade = jnp.exp(-rate_of(block, half) * (rows - 1 - number).astype(F32)) * valid
                keys = backs[block, part, key].astype(F32) + fade * scores[part, 0:HEAD]
                turned = rotated(keys, cosine[part, :], -sine[part, :])
                backs[block, part, key] = (turned * pack[block, part, key].astype(F32)).astype(BF16)
                values = acts[block, part, 3 * PAIR + at : 3 * PAIR + at + HEAD].astype(F32)
                backs[block, part, value] = (values + fade * scores[part, HEAD : 2 * HEAD]).astype(BF16)

            every_rows(rows, finish_rows, NARROW)
        backs_keep_copy(block).start()
        backs_copy(block).start()
        for part in range(2):
            index = at_tile + 2 * block + part
            term = dots(backs[block, :, part * half_d : part * half_d + half_d], tile(index), NN)
            if block or part:
                wide[...] += term
            else:
                wide[...] = term
            tile_next(index)
        if block == 0:
            for index in range(SEQ):
                hidden_load(index).start()
        if block == 1:
            produce(9)
            prefetch(10)
    relay(12, 12)
    for index in range(SEQ):
        hidden_load(index).wait()

    def input_rows(part, start):
        values = acts[0, part, :].astype(F32)
        scale = lax.rsqrt(jnp.mean(values * values, axis=-1, keepdims=True) + EPSILON)
        unit = values * scale
        grad = wide[part, :]
        inner = jnp.mean(grad * unit, axis=-1, keepdims=True)
        grad = mid[part, :] + scale * (grad - unit * inner)
        for index in range(SEQ):
            acts[1, part, plain(index)] = grad[:, place_of(index)].astype(BF16)

    for p in range(PIECES):

        @pl.loop(0, piece_rows // BLOCK)
        def _(block, p=p):
            start = p * piece_rows + block * BLOCK
            input_rows(pl.ds(pl.multiple_of(start, BLOCK), BLOCK), start)

        if p < EARLY:
            share_start(1, p)
    for index in range(BEFORE, ITEMS):
        produce(index)
        if index + 1 < ITEMS:
            prefetch(index + 1)
        if EARLY <= index - BEFORE + EARLY < PIECES:
            share_start(1, index - BEFORE + EARLY)
        if index >= BEFORE + WAIT_1:
            relay(2, 20)
        if index >= BEFORE + WAIT_2:
            relay(1)
    for now in range(ITEMS, ITEMS + LAG_5):
        advance(now)
        relay(1)
    relay(len(relays))

    half_copy().wait_send()
    for block in range(TP):
        backs_copy(block).wait_send()
    close_states()
    for index, (kind, step) in enumerate(items):
        if index >= ITEMS - HELD:
            for copy in to_second(index):
                copy.wait_send()
        to_first(index).wait_send()
        if step:
            along(index, True).wait_send()
    for a in range(2):
        for p in range(PIECES):
            share_keep(a, p).wait()

            @pl.when(t < TP - 1)
            def _(a=a, p=p):
                share_copy(a, p, t, own_piece(a, p), True).wait_send()

            @pl.when(t > 0)
            def _(a=a, p=p):
                share_copy(a, p, t, own_piece(a, p), False).wait_send()
    for a, p, step in relays:
        owner = nearest(t, step)
        passed = passes(owner, True) | passes(owner, False)

        @pl.when(jnp.logical_not(passed))
        def _(a=a, p=p, owner=owner):
            share_copy(a, p, owner, piece(a, owner, p), True).wait_recv()

        for up in (True, False):

            @pl.when(passes(owner, up))
            def _(a=a, p=p, owner=owner, up=up):
                share_copy(a, p, owner, piece(a, owner, p), up).wait_send()


def backward(units, whole, kept, output, hidden_in, out_cotangent, incoming, inv_mix, inv_second, rates, cosine, sine, bounds):
    rows = output.shape[0]
    sizes = tuple(weight.shape[0] // TP for weight in whole) + (units,)
    dma = pltpu.SemaphoreType.DMA
    vmem = pl.BlockSpec(memory_space=pltpu.VMEM)
    anywhere = pl.BlockSpec(memory_space=pl.ANY)
    half_d = D // 2
    shape = jax.ShapeDtypeStruct
    tall = lambda height: shape((height, STRIPE), F32)
    scratch = [
        pltpu.VMEM((3, half_d, D), BF16),
        *[pltpu.VMEM((rows, D), BF16)] * 4,
        pltpu.VMEM((4, rows, half_d), BF16),
        *[pltpu.VMEM((TP, rows, 4 * PAIR), BF16)] * 3,
        pltpu.VMEM((rows, D), F32),
        pltpu.VMEM((rows, D), F32),
        pltpu.VMEM((rows, rows), F32),
        pltpu.VMEM((rows, rows), F32),
        pltpu.VMEM((rows, rows), BF16),
        pltpu.VMEM((rows, rows), BF16),
        pltpu.VMEM((rows, HEAD), BF16),
        pltpu.VMEM((2, 2, rows, units), BF16),
        pltpu.VMEM((HELD, 4, units, STRIPE), BF16),
        *state_scratch(),
    ]
    for count, height, extra in ((3 * TP, units, 3), (TP, sizes[1], 1), (2 * TP, half_d, 2)):
        scratch += [
            pltpu.VMEM((count, 2, height, STRIPE), BF16),
            pltpu.VMEM((count, height, STRIPE), BF16),
            pltpu.VMEM((count + extra, height, STRIPE), BF16),
        ]
    scratch += [
        dma((3,)),
        dma((2,)),
        dma((3,)),
        dma((TP,)),
        dma((TP,)),
        dma((TP,)),
        dma((5,)),
        dma((SEQ,)),
        dma((SEQ,)),
        dma((2, 2)),
        dma((ITEMS, 2)),
        dma((ITEMS, 2)),
        dma((ITEMS,)),
        dma((ITEMS,)),
        dma((ITEMS,)),
        dma((KINDS, TP)),
        dma((KINDS, TP)),
        dma((2, PIECES)),
        dma((2, PIECES, TP)),
        dma((2, PIECES, TP)),
        dma((2, PIECES, TP)),
    ]
    return pl.pallas_call(
        functools.partial(backward_kernel, rows, sizes),
        out_shape=[tall(units), tall(units), tall(units), tall(sizes[1]), tall(sizes[0])]
        + [shape((TP, rows, D), BF16)] * 2
        + [shape((TP, rows, 4 * PAIR), BF16)] * 2,
        in_specs=[anywhere] * 20 + [vmem] * 6 + [pl.BlockSpec(memory_space=pltpu.SMEM)],
        out_specs=[vmem] * 5 + [anywhere] * 4,
        scratch_shapes=scratch,
        compiler_params=pltpu.CompilerParams(
            collective_id=1, has_side_effects=True, vmem_limit_bytes=63 * 2**20
        ),
        name="backward",
    )(*whole, *kept, output, hidden_in, out_cotangent, incoming, inv_mix, inv_second, rates, cosine, sine, bounds)


def finish_kernel(input_in, qkvg_in, tall_in, input_grad, *refs):
    input_grad[...] = input_in[...].astype(F32)

    @pl.when(pl.program_id(0) == 0)
    def _():
        for kind in range(4):
            refs[kind][...] = qkvg_in[kind * PAIR : kind * PAIR + PAIR, :].T
        refs[4][...] = tall_in[...]


def finish(input_grad, qkvg_grad, out_grad):
    rows = input_grad.shape[1]
    block = lambda: pl.BlockSpec((1, rows, D), lambda step: (step, 0, 0))
    fixed = lambda *shape: pl.BlockSpec(shape, lambda step: (0, 0))
    shape = jax.ShapeDtypeStruct
    return pl.pallas_call(
        finish_kernel,
        grid=(TP,),
        out_shape=[
            shape(input_grad.shape, F32),
            *[shape((STRIPE, PAIR), F32)] * 4,
            shape(out_grad.shape, F32),
        ],
        in_specs=[block(), fixed(4 * PAIR, STRIPE), fixed(*out_grad.shape)],
        out_specs=[block(), *[fixed(STRIPE, PAIR)] * 4, fixed(*out_grad.shape)],
        compiler_params=pltpu.CompilerParams(vmem_limit_bytes=32 * 2**20),
        name="finish",
    )(input_grad, qkvg_grad, out_grad)


def entering(value, axis, join, neutral, backward):
    count, mine = (lax.axis_size(axis), lax.axis_index(axis))
    pieces = jax.tree.map(lambda part: lax.all_gather(part, axis), value)
    if backward:
        pieces = jax.tree.map(lambda part: part[::-1], pieces)
        mine = count - 1 - mine
    subtotal = jax.tree.map(
        lambda part, zero: jnp.full_like(part, 0) + jnp.asarray(zero, part.dtype), value, neutral
    )

    def step(position, subtotal):
        longer = join(subtotal, jax.tree.map(lambda part: part[position], pieces))
        return jax.tree.map(lambda new, old: jnp.where(position < mine, new, old), longer, subtotal)

    return lax.fori_loop(0, count - 1, step, subtotal)


def swish_parts(pre_act):
    logistic = jax.nn.sigmoid(pre_act)
    return (pre_act * logistic, logistic * (1.0 + pre_act * (1.0 - logistic)))


def rotate(rows_in, cosine_table, sine_table, signed):
    halfway = rows_in.shape[-1] // 2
    front_half = rows_in[..., :halfway]
    back_half = rows_in[..., halfway:]
    return jnp.concatenate(
        [
            front_half * cosine_table - signed * back_half * sine_table,
            signed * front_half * sine_table + back_half * cosine_table,
        ],
        axis=-1,
    )


def combine_forward(earlier, following):
    return (earlier[0] * following[0], following[0][:, None, None] * earlier[1] + following[1])


def combine_backward(farther, nearer):
    return (farther[0] * nearer[0], nearer[1] + nearer[0][:, None, None] * farther[1])


def collect_weights(
    query_weight,
    key_weight,
    value_weight,
    gate_weight,
    out_weight,
    left_weight,
    right_weight,
    down_weight,
):
    return (
        lax.all_gather(query_weight, "seq", axis=0, tiled=True),
        lax.all_gather(key_weight, "seq", axis=0, tiled=True),
        lax.all_gather(value_weight, "seq", axis=0, tiled=True),
        lax.all_gather(gate_weight, "seq", axis=0, tiled=True),
        lax.all_gather(out_weight, "seq", axis=1, tiled=True),
        lax.all_gather(left_weight, "seq", axis=0, tiled=True),
        lax.all_gather(right_weight, "seq", axis=0, tiled=True),
        lax.all_gather(down_weight, "seq", axis=1, tiled=True),
    )


def state_prefix(factor, local_state):
    neutral = (jnp.ones_like(factor), jnp.zeros_like(local_state))
    return entering((factor, local_state), "seq", combine_forward, neutral, False)[1]


def state_suffix(factor, state_grad):
    neutral = (jnp.ones_like(factor), jnp.zeros_like(state_grad))
    return entering((factor, state_grad), "seq", combine_backward, neutral, True)[1]


def body(
    hidden_in,
    query_weight,
    key_weight,
    value_weight,
    gate_weight,
    out_weight,
    left_weight,
    right_weight,
    down_weight,
    decay_rate,
    seq_bounds,
    out_cotangent,
):
    row_count = hidden_in.shape[1]
    batch_count = hidden_in.shape[0]
    local_heads = decay_rate.shape[0]
    heads_shape = (row_count, local_heads, HEAD)
    device = lax.axis_index("seq")
    offsets = jnp.arange(row_count, dtype=jnp.int32)
    positions = device * row_count + offsets
    frequency = jnp.exp(
        jnp.arange(HEAD // 2, dtype=jnp.float32) * (-2.0 * math.log(10000.0) / HEAD)
    )
    angles = positions.astype(jnp.float32)[:, None] * frequency[None, :]
    cosine_table = jnp.cos(angles)[:, None, :]
    sine_table = jnp.sin(angles)[:, None, :]
    local_f = offsets.astype(jnp.float32)
    distance = local_f[:, None] - local_f[None, :]
    causal = distance >= 0.0
    distance_pos = jnp.maximum(distance, 0.0)
    accum = None
    outputs = []
    in_grads = []
    for batch_index in range(batch_count):
        gathered = collect_weights(
            query_weight,
            key_weight,
            value_weight,
            gate_weight,
            out_weight,
            left_weight,
            right_weight,
            down_weight,
        )
        query_full, key_full, value_full, gate_full, out_full, left_full, right_full, down_full = (
            gathered
        )
        boundary = seq_bounds[batch_index]
        segment = (positions >= boundary).astype(jnp.int32)
        before = (device * row_count - 1 >= boundary).astype(jnp.int32)
        last_segment = segment[row_count - 1]
        allowed = causal & (segment[:, None] == segment[None, :])
        decay = jnp.where(
            allowed[None], jnp.exp(-decay_rate[:, None, None] * distance_pos[None]), 0.0
        )
        coef_in = (
            jnp.exp(-decay_rate[None, :] * (local_f[:, None] + 1.0))
            * (segment == before).astype(jnp.float32)[:, None]
        )
        weight_loc = (
            jnp.exp(-decay_rate[None, :] * (row_count - 1.0 - local_f)[:, None])
            * (segment == last_segment).astype(jnp.float32)[:, None]
        )
        factor = jnp.where(last_segment == before, jnp.exp(-decay_rate * row_count), 0.0)
        input_rows = hidden_in[batch_index].astype(jnp.float32)
        inv_first = lax.rsqrt(jnp.mean(input_rows * input_rows, axis=-1, keepdims=True) + EPSILON)
        unit_first = input_rows * inv_first
        normed_first = unit_first.astype(jnp.bfloat16)
        query_pre = jnp.dot(normed_first, query_full, preferred_element_type=jnp.float32)
        key_pre = jnp.dot(normed_first, key_full, preferred_element_type=jnp.float32)
        value_pre = jnp.dot(normed_first, value_full, preferred_element_type=jnp.float32)
        gate_pre = jnp.dot(normed_first, gate_full, preferred_element_type=jnp.float32)
        query_act, query_slope = swish_parts(query_pre)
        key_act, key_slope = swish_parts(key_pre)
        query_rot = rotate(query_act.reshape(heads_shape), cosine_table, sine_table, 1.0).astype(
            jnp.bfloat16
        )
        key_rot = rotate(key_act.reshape(heads_shape), cosine_table, sine_table, 1.0).astype(
            jnp.bfloat16
        )
        value_rows = value_pre.astype(jnp.bfloat16).reshape(heads_shape)
        query_wide = query_rot.astype(jnp.float32)
        key_wide = key_rot.astype(jnp.float32)
        value_wide = value_rows.astype(jnp.float32)
        scores = jnp.einsum("ihe,jhe->hij", query_rot, key_rot, preferred_element_type=jnp.float32)
        attn_weights = (scores * decay).astype(jnp.bfloat16)
        inner_out = jnp.einsum(
            "hij,jhe->ihe", attn_weights, value_rows, preferred_element_type=jnp.float32
        )
        local_state = jnp.einsum(
            "jhe,jhf->hef",
            key_wide * weight_loc[:, :, None],
            value_wide,
            precision=HIGHEST_PRECISION,
        )
        incoming = state_prefix(factor, local_state)
        outer_out = coef_in[:, :, None] * jnp.einsum(
            "ihe,hef->ihf", query_wide, incoming, precision=HIGHEST_PRECISION
        )
        mixed_heads = (inner_out + outer_out).reshape(row_count, local_heads * HEAD)
        total_sq = lax.psum(jnp.sum(mixed_heads * mixed_heads, axis=-1), "tp")
        inv_mix = lax.rsqrt(total_sq / D + EPSILON)[:, None]
        unit_mix = mixed_heads * inv_mix
        gate_mix = (unit_mix * gate_pre).astype(jnp.bfloat16)
        attn_sum = lax.psum(jnp.dot(gate_mix, out_full, preferred_element_type=jnp.float32), "tp")
        resid_mid = input_rows + attn_sum
        inv_second = lax.rsqrt(jnp.mean(resid_mid * resid_mid, axis=-1, keepdims=True) + EPSILON)
        unit_second = resid_mid * inv_second
        normed_second = unit_second.astype(jnp.bfloat16)
        left_pre = jnp.dot(normed_second, left_full, preferred_element_type=jnp.float32)
        right_pre = jnp.dot(normed_second, right_full, preferred_element_type=jnp.float32)
        glu_product = (left_pre * right_pre).astype(jnp.bfloat16)
        glu_out = lax.psum(
            jnp.dot(glu_product, down_full, preferred_element_type=jnp.float32), "tp"
        )
        outputs.append((resid_mid + glu_out).astype(jnp.bfloat16))
        glu_cot = out_cotangent[batch_index]
        product_grad = jnp.einsum(
            "cd,fd->cf", glu_cot, down_full, preferred_element_type=jnp.float32
        )
        left_back = (product_grad * right_pre).astype(jnp.bfloat16)
        right_back = (product_grad * left_pre).astype(jnp.bfloat16)
        second_part = jnp.einsum(
            "cf,df->cd", left_back, left_full, preferred_element_type=jnp.float32
        ) + jnp.einsum("cf,df->cd", right_back, right_full, preferred_element_type=jnp.float32)
        second_back = lax.psum(second_part, "tp")
        mid_grad = glu_cot.astype(jnp.float32) + inv_second * (
            second_back - unit_second * jnp.mean(second_back * unit_second, axis=-1, keepdims=True)
        )
        attn_cot = mid_grad.astype(jnp.bfloat16)
        gate_mix_grad = jnp.einsum(
            "cd,kd->ck", attn_cot, out_full, preferred_element_type=jnp.float32
        )
        gate_back = (gate_mix_grad * unit_mix).astype(jnp.bfloat16)
        unit_mix_grad = gate_mix_grad * gate_pre
        mix_dot = lax.psum(jnp.sum(unit_mix_grad * unit_mix, axis=-1), "tp")
        heads_grad = (
            (inv_mix * (unit_mix_grad - unit_mix * (mix_dot / D)[:, None]))
            .astype(jnp.bfloat16)
            .reshape(heads_shape)
        )
        pair_grad = jnp.einsum(
            "ihe,jhe->hij", heads_grad, value_rows, preferred_element_type=jnp.float32
        ).astype(jnp.bfloat16)
        score_grad = pair_grad.astype(jnp.float32) * decay
        query_inner = jnp.einsum("hij,jhe->ihe", score_grad, key_wide, precision=HIGHEST_PRECISION)
        key_inner = jnp.einsum("hij,ihe->jhe", score_grad, query_wide, precision=HIGHEST_PRECISION)
        value_inner = jnp.einsum(
            "hij,ihe->jhe", attn_weights, heads_grad, preferred_element_type=jnp.float32
        )
        scaled_grad = heads_grad.astype(jnp.float32) * coef_in[:, :, None]
        query_outer = jnp.einsum("ihf,hef->ihe", scaled_grad, incoming, precision=HIGHEST_PRECISION)
        state_grad = jnp.einsum(
            "ihe,ihf->hef", query_wide, scaled_grad, precision=HIGHEST_PRECISION
        )
        later_grad = state_suffix(factor, state_grad)
        key_state = weight_loc[:, :, None] * jnp.einsum(
            "jhf,hef->jhe", value_wide, later_grad, precision=HIGHEST_PRECISION
        )
        value_state = weight_loc[:, :, None] * jnp.einsum(
            "jhe,hef->jhf", key_wide, later_grad, precision=HIGHEST_PRECISION
        )
        query_back = (
            rotate(query_inner + query_outer, cosine_table, sine_table, -1.0).reshape(row_count, -1)
            * query_slope
        ).astype(jnp.bfloat16)
        key_back = (
            rotate(key_inner + key_state, cosine_table, sine_table, -1.0).reshape(row_count, -1)
            * key_slope
        ).astype(jnp.bfloat16)
        value_back = (value_inner + value_state).reshape(row_count, -1).astype(jnp.bfloat16)
        fresh = (
            jnp.einsum("cd,ck->dk", normed_first, query_back, preferred_element_type=jnp.float32),
            jnp.einsum("cd,ck->dk", normed_first, key_back, preferred_element_type=jnp.float32),
            jnp.einsum("cd,ck->dk", normed_first, value_back, preferred_element_type=jnp.float32),
            jnp.einsum("cd,ck->dk", normed_first, gate_back, preferred_element_type=jnp.float32),
            jnp.einsum("ck,cd->kd", gate_mix, attn_cot, preferred_element_type=jnp.float32),
            jnp.einsum("cd,cf->df", normed_second, left_back, preferred_element_type=jnp.float32),
            jnp.einsum("cd,cf->df", normed_second, right_back, preferred_element_type=jnp.float32),
            jnp.einsum("cf,cd->fd", glu_product, glu_cot, preferred_element_type=jnp.float32),
        )
        if accum is None:
            accum = list(fresh)
        else:
            accum = [older + newer for older, newer in zip(accum, fresh)]
        total = jnp.einsum("ck,dk->cd", query_back, query_full, preferred_element_type=jnp.float32)
        total = total + jnp.einsum(
            "ck,dk->cd", key_back, key_full, preferred_element_type=jnp.float32
        )
        total = total + jnp.einsum(
            "ck,dk->cd", value_back, value_full, preferred_element_type=jnp.float32
        )
        first_back = lax.psum(
            total
            + jnp.einsum("ck,dk->cd", gate_back, gate_full, preferred_element_type=jnp.float32),
            "tp",
        )
        input_back = mid_grad + inv_first * (
            first_back - unit_first * jnp.mean(first_back * unit_first, axis=-1, keepdims=True)
        )
        in_grads.append(input_back)
    summed = (
        lax.psum_scatter(accum[0], "seq", scatter_dimension=0, tiled=True),
        lax.psum_scatter(accum[1], "seq", scatter_dimension=0, tiled=True),
        lax.psum_scatter(accum[2], "seq", scatter_dimension=0, tiled=True),
        lax.psum_scatter(accum[3], "seq", scatter_dimension=0, tiled=True),
        lax.psum_scatter(accum[4], "seq", scatter_dimension=1, tiled=True),
        lax.psum_scatter(accum[5], "seq", scatter_dimension=0, tiled=True),
        lax.psum_scatter(accum[6], "seq", scatter_dimension=0, tiled=True),
        lax.psum_scatter(accum[7], "seq", scatter_dimension=1, tiled=True),
    )
    return (
        jnp.stack(outputs),
        jnp.stack(in_grads),
        summed[0],
        summed[1],
        summed[2],
        summed[3],
        summed[4],
        summed[5],
        summed[6],
        summed[7],
    )


def fused_body(
    hidden_in,
    query_weight,
    key_weight,
    value_weight,
    gate_weight,
    out_weight,
    left_weight,
    right_weight,
    down_weight,
    decay_rate,
    seq_bounds,
    out_cotangent,
):
    row_count = hidden_in.shape[1]
    device = lax.axis_index("seq")
    positions = device * row_count + jnp.arange(row_count, dtype=jnp.int32)
    frequency = jnp.exp(jnp.arange(HEAD // 2, dtype=F32) * (-2.0 * math.log(10000.0) / HEAD))
    angles = positions.astype(F32)[:, None] * jnp.tile(frequency, 2)[None, :]
    sign = jnp.where(jnp.arange(HEAD) < HEAD // 2, -1.0, 1.0).astype(F32)
    cosine, sine = jnp.cos(angles), jnp.sin(angles) * sign[None, :]
    results = forward(
        (query_weight, key_weight, value_weight, gate_weight),
        (out_weight, left_weight.T, right_weight.T, down_weight),
        hidden_in,
        out_cotangent,
        cosine,
        sine,
        decay_rate,
        seq_bounds,
    )
    whole, kept, (incoming, inv_mix, inv_second, rates, output) = results[:2], results[2:17], results[17:]
    down_grad, left_grad, right_grad, out_grad, qkvg_grad, output, input_grad = backward(
        down_weight.shape[0],
        whole,
        kept,
        output,
        hidden_in,
        out_cotangent,
        incoming,
        inv_mix,
        inv_second,
        rates,
        cosine,
        sine,
        seq_bounds,
    )[:7]
    input_grad, query_grad, key_grad, value_grad, gate_grad, out_grad = finish(input_grad, qkvg_grad, out_grad)
    return (
        output,
        input_grad,
        query_grad,
        key_grad,
        value_grad,
        gate_grad,
        out_grad,
        left_grad.T,
        right_grad.T,
        down_grad,
    )


def solution(mesh):
    fits = mesh.shape["seq"] == SEQ and mesh.shape["tp"] == TP
    return jax.shard_map(
        fused_body if fits else body,
        mesh=mesh,
        in_specs=(
            P(None, "seq", None),
            P("seq", "tp"),
            P("seq", "tp"),
            P("seq", "tp"),
            P("seq", "tp"),
            P("tp", "seq"),
            P("seq", "tp"),
            P("seq", "tp"),
            P("tp", "seq"),
            P("tp"),
            P(),
            P(None, "seq", None),
        ),
        out_specs=(
            P(None, "seq", None),
            P(None, "seq", None),
            P("seq", "tp"),
            P("seq", "tp"),
            P("seq", "tp"),
            P("seq", "tp"),
            P("tp", "seq"),
            P("seq", "tp"),
            P("seq", "tp"),
            P("tp", "seq"),
        ),
        check_vma=False,
    )
```

```python
import functools
import math

import jax
import jax.numpy as jnp
from jax import lax
from jax.experimental import pallas as pl
from jax.experimental.pallas import tpu as pltpu
from jax.sharding import PartitionSpec as P

D = 1024
HEAD = 128


EPSILON = 1e-06
HIGHEST_PRECISION = lax.Precision.HIGHEST
MESH = pl.DeviceIdType.MESH
BF16 = jnp.bfloat16
F32 = jnp.float32

SEQ = 8
TP = 4
STRIPE = 128
PAIR = 2 * HEAD
BLOCK = 32
NARROW = 128
WEIGH = 64

NN = ((1,), (0,))
NT = ((1,), (1,))
TN = ((0,), (0,))


def dots(left, right, dims):
    return lax.dot_general(left, right, (dims, ((), ())), preferred_element_type=F32)


def place():
    s, t = lax.axis_index("seq"), lax.axis_index("tp")
    core = s % 2
    column = (s // 2) % 2
    line = s // 4
    other = s + 1 - 2 * core
    across_x = s + 2 * (1 - 2 * column)
    across_y = s + 4 * (1 - 2 * line)
    first = across_x + core * (across_y - across_x)
    second = across_y + core * (across_x - across_y)
    diagonal = across_x + across_y - s
    return s, t, other, first, second, diagonal


def nearest(t, step):
    flip = t // 2
    low = t + flip * (3 - 2 * t)
    swap = low * (1 - step // 2)
    index = step + swap * (1 - 2 * step)
    return index + flip * (3 - 2 * index)


def stripe(index):
    return pl.ds(pl.multiple_of((index % 2 * (SEQ // 2) + index // 2) * STRIPE, STRIPE), STRIPE)


def plain(index):
    return slice(index * STRIPE, index * STRIPE + STRIPE)


def place_of(index):
    at = (index % 2 * (SEQ // 2) + index // 2) * STRIPE
    return slice(at, at + STRIPE)


def rows_of(index, size):
    return pl.ds(pl.multiple_of(index * size, size), size)


def remote(src, dst, send, receive, device):
    return pltpu.make_async_remote_copy(
        src_ref=src, dst_ref=dst, send_sem=send, recv_sem=receive, device_id=device, device_id_type=MESH
    )


def greet(s, t, around):
    barrier = pltpu.get_barrier_semaphore()
    for step in range(1, TP):
        pl.semaphore_signal(barrier, inc=1, device_id=(s, (t + step) % TP), device_id_type=MESH)
    for device in around:
        pl.semaphore_signal(barrier, inc=1, device_id=(device, t), device_id_type=MESH)
    pl.semaphore_wait(barrier, TP - 1 + len(around))


def every_rows(count, body, size=BLOCK):
    @pl.loop(0, count // size)
    def _(block):
        body(pl.ds(pl.multiple_of(block * size, size), size), block * size)


def flag(condition):
    return jnp.where(condition, 1.0, 0.0).astype(F32)


def rotated(values, cosine, sine):
    return values * cosine + pltpu.roll(values, HEAD // 2, 1) * sine


def state_exchange(rows, boundary, refs, rates, scale, toward, source_of):
    state, pair_land, chip_state, chip_land, partial, result, pair_sem, chip_send, chip_recv, partial_sem = refs
    s, t, other, first, second, diagonal = place()
    core, half = s % 2, TP
    around = (first, second, diagonal)
    ours, theirs = pl.ds(core * half, half), pl.ds((1 - core) * half, half)

    def pair_copy():
        return remote(state.at[theirs], pair_land, pair_sem.at[0], pair_sem.at[1], (other, t))

    def chip_copy(part):
        return remote(chip_state, chip_land.at[part], chip_send.at[part], chip_recv.at[part], (around[part], t))

    def partial_copy():
        return remote(partial, result.at[ours], partial_sem.at[0], partial_sem.at[1], (other, t))

    def rate_of(number):
        head = core * half + number
        return rates[head // 2, pl.ds(head % 2, 1), :]

    def begin():
        pair_copy().start()

    def add_pair():
        pair_copy().wait_recv()

        @pl.loop(0, half)
        def _(number):
            rate, target = rate_of(number), toward(s // 2)
            total = scale(target, s, rate) * state[core * half + number].astype(F32)
            total += scale(target, other, rate) * pair_land[number].astype(F32)
            chip_state[number] = total.astype(BF16)

        for part in range(3):
            chip_copy(part).start()

    def add_chips():
        for part in range(3):
            chip_copy(part).wait_recv()

        @pl.loop(0, half)
        def _(number):
            rate = rate_of(number)
            mine, its = state[core * half + number].astype(F32), pair_land[number].astype(F32)
            here = scale(s, s, rate) * mine + scale(s, other, rate) * its
            there = scale(other, s, rate) * mine + scale(other, other, rate) * its
            for part in range(3):
                values = chip_land[part, number].astype(F32)
                source = source_of(around[part] // 2)
                here += scale(s, source, rate) * values
                there += scale(other, source, rate) * values
            result[core * half + number] = here.astype(BF16)
            partial[number] = there.astype(BF16)

        partial_copy().start()

    def finish():
        partial_copy().wait_recv()

    def close():
        pair_copy().wait_send()
        for part in range(3):
            chip_copy(part).wait_send()
        partial_copy().wait_send()

    return begin, add_pair, add_chips, finish, close


def state_scratch():
    dma = pltpu.SemaphoreType.DMA
    return [
        pltpu.VMEM((2 * TP, HEAD, HEAD), BF16),
        pltpu.VMEM((TP, HEAD, HEAD), BF16),
        pltpu.VMEM((TP, HEAD, HEAD), BF16),
        pltpu.VMEM((3, TP, HEAD, HEAD), BF16),
        pltpu.VMEM((TP, HEAD, HEAD), BF16),
        pltpu.VMEM((2 * TP, HEAD, HEAD), BF16),
        dma((2,)),
        dma((3,)),
        dma((3,)),
        dma((2,)),
    ]


LAG_B, LAG_C = 2, 4

def forward_kernel(rows, sizes, *refs):
    heads_in, refs = refs[:4], refs[4:]
    shards, refs = refs[:4], refs[4:]
    (hidden_in, cot_in, cosine, sine, rate_in, bounds), refs = refs[:6], refs[6:]
    whole_out, refs = refs[:2], refs[2:]
    (acts_out, pack_out, normed_out, second_out, glu_out, left_out, right_out, glu_other, left_other, right_other,
     gated_other, normed_other, second_other, cot_other, back_out,
     incoming_out, inv_mix_out, inv_second_out, rate_out, result_out), refs = refs[:20], refs[20:]
    whole, refs = refs[:5], refs[5:]
    (acts, pack, normed, hidden, cot, second_normed, sides, back, wide, mixed, distance, scores, weights,
     inv_mix, inv_second, rates, heads_shard), refs = refs[:17], refs[17:]
    exchange, refs = refs[:10], refs[10:]
    state, incoming = exchange[0], exchange[5]
    shards = (heads_shard, *shards)
    (local_sem, up_sem, down_sem, line_sem, down_send, down_recv, send_sem, first_sem, second_sem, other_sem, rate_send, rate_recv,
     copy_sem, side_sem, side_send, side_recv, half_send, half_recv,
     hidden_sem, cot_sem) = refs
    s, t, other, first, second, diagonal = place()
    units, beside = sizes[2], wide.shape[1] // 3
    theirs = rows_of(1 - s % 2, D // 2)
    shift = other - s
    for kind in range(4):
        heads_shard[kind * PAIR : kind * PAIR + PAIR, :] = heads_in[kind][...].T
    greet(s, t, (other, first, second, diagonal))

    def hidden_load(index):
        return pltpu.make_async_copy(
            hidden_in.at[t, :, plain(index)], hidden.at[:, place_of(index)], hidden_sem.at[index]
        )

    def cot_load(index):
        return pltpu.make_async_copy(cot_in.at[t, :, plain(index)], cot.at[:, place_of(index)], cot_sem.at[index])

    def half_copy(part):
        src, dst = (
            (normed.at[:, theirs], normed_other),
            (second_normed.at[:, theirs], second_other),
            (cot.at[:, theirs], cot_other),
            (pack.at[:, :, 2 * PAIR : 3 * PAIR], gated_other),
        )[part]
        return remote(src, dst, half_send.at[part], half_recv.at[part], (other, t))

    for index in range(SEQ):
        hidden_load(index).start()

    cut = -(-units // (2 * HEAD)) * HEAD
    items = (
        [(0, 0), (4, 0)]
        + [(0, step) for step in range(1, TP)]
        + [(1, step) for step in range(TP)]
        + [(w, step) for step in range(TP) for w in (2, 3)]
    )
    items = [(w, step, 0, sizes[w]) for w, step in items]
    items[-1:] = [(3, TP - 1, 0, cut), (3, TP - 1, cut, units)]
    columns = (s, first, second, diagonal)

    def spot(w, owner, column, low=0, high=None):
        high = sizes[w] if high is None else high
        return whole[w].at[pl.ds(pl.multiple_of(owner * sizes[w] + low, 16), high - low), stripe(column)]

    def source(w, step, owner, low=0, high=None):
        if step:
            return spot(w, owner, s, low, high)
        return shards[w].at[pl.ds(low, (sizes[w] if high is None else high) - low), :]

    def own_copy(w):
        return pltpu.make_async_copy(shards[w], spot(w, t, s), local_sem.at[w])

    def plane_copies(index):
        w, step, low, high = items[index]
        owner = nearest(t, step)
        src, dst = source(w, step, owner, low, high), spot(w, owner, s, low, high)
        return (
            remote(src, dst, send_sem.at[index, 0], first_sem.at[index], (first, t)),
            remote(src, dst, send_sem.at[index, 1], second_sem.at[index, 0], (second, t)),
            remote(src, dst, send_sem.at[index, 2], other_sem.at[index, 0], (other, t)),
        )

    def found(index, column):
        w, step, low, high = items[index]
        return spot(w, nearest(t, step), column, low, high)

    def relay_copies(index):
        src = found(index, first)
        return (
            remote(src, src, send_sem.at[index, 3], second_sem.at[index, 1], (second, t)),
            remote(src, src, send_sem.at[index, 4], other_sem.at[index, 1], (other, t)),
        )

    def last_copies(index):
        near, far = found(index, second), found(index, diagonal)
        return (
            remote(near, near, send_sem.at[index, 5], other_sem.at[index, 2], (other, t)),
            remote(far, far, send_sem.at[index, 6], other_sem.at[index, 3], (other, t)),
        )

    def parcel(w, step, column, up):
        owner = nearest(t, step)
        dst = spot(w, owner, columns[column])
        src = shards[w] if step == 0 and column == 0 else dst
        sem, device = (up_sem, t + 1) if up else (down_sem, t - 1)
        return remote(src, dst, sem.at[w, owner, column], line_sem.at[w, owner, column], (s, device))

    def across(step, column):
        block = spot(4, nearest(t, step), columns[column])
        return remote(block, block, down_send.at[step, column], down_recv.at[step, column], (other, t))

    def goes(step, up):
        owner = nearest(t, step)
        if step == 0:
            return t < TP - 1 if up else t > 0
        return (owner < t) & (t < TP - 1) if up else (owner > t) & (t > 0)

    def set_out(w, column=0):
        for up in (True, False):

            @pl.when(goes(0, up))
            def _(up=up):
                parcel(w, 0, column, up).start()

    inside = (t > 0) & (t < TP - 1)

    def pass_on(w, step, column=0, where=None):
        def act():
            parcel(w, step, column, True).wait_recv()
            for up in (True, False):

                @pl.when(goes(step, up))
                def _(up=up):
                    parcel(w, step, column, up).start()

            if w == 4:
                across(step, column).start()

        if where is None:
            act()
        else:
            pl.when(where)(act)

    down_parcels = [(step, column) for step in range(1, TP) for column in range(4)]

    def line_pass(now, where):
        if now + 2 < len(items):
            w, step, low, high = items[now + 2]
            if step and low == 0:
                pass_on(w, step, 0, where)

    def down_pass(now):
        for at, where in ((now - 6, inside), (now - 8, jnp.logical_not(inside))):
            if 0 <= at < len(down_parcels):
                pass_on(4, *down_parcels[at], where)

    relayed, ended = [], []

    def stage_a(index):
        if items[index][1] == 0:
            own_copy(items[index][0]).start()
        for copy in plane_copies(index):
            copy.start()

    def stage_b(until):
        while len(relayed) <= min(until, len(items) - 1):
            index = len(relayed)
            relayed.append(index)
            block = found(index, first)
            remote(block, block, send_sem.at[index, 0], first_sem.at[index], (first, t)).wait_recv()
            for copy in relay_copies(index):
                copy.start()

    def stage_c(until):
        while len(ended) <= min(until, len(items) - 1):
            index = len(ended)
            ended.append(index)
            for part, column in enumerate((second, diagonal)):
                block = found(index, column)
                remote(block, block, send_sem.at[index, 1], second_sem.at[index, part], (second, t)).wait_recv()
            for copy in last_copies(index):
                copy.start()

    def tick(now):
        stage_b(now - LAG_B)
        if now < len(items):
            stage_a(now)
        stage_c(now - LAG_C)
        if now == 5:
            set_out(2)
            set_out(3)
            line_pass(now - 1, None)
            line_pass(now, inside)
        line_pass(now + 1, inside)
        line_pass(now, jnp.logical_not(inside))
        down_pass(now)

    keeps = []

    def keep(src, dst):
        copy = functools.partial(pltpu.make_async_copy, src, dst, copy_sem.at[len(keeps)])
        copy().start()
        keeps.append(copy)

    def ready(index):
        w, step, low, high = items[index]
        owner = nearest(t, step)
        if step == 0:
            own_copy(w).wait()
        for part, column in enumerate((other, second + shift, first + shift, diagonal + shift)):
            block = found(index, column)
            remote(block, block, send_sem.at[index, 2], other_sem.at[index, part], (other, t)).wait_recv()
        block = rows_of(owner, sizes[w])
        if w < 2:
            keep(whole[w].at[block, :], whole_out[w].at[block, :])
        return owner, block

    def down_ready(step):
        if step == 0:
            ready(1)
            return
        for column, index in enumerate((other, second + shift, first + shift, diagonal + shift)):
            block = spot(4, nearest(t, step), index)
            remote(block, block, down_send.at[step, column], down_recv.at[step, column], (other, t)).wait_recv()

    def rate_copy(step):
        return remote(rates.at[t], rates.at[t], rate_send.at[step - 1], rate_recv.at[step - 1], (s, (t + step) % TP))

    row = lax.broadcasted_iota(jnp.int32, (8, HEAD), 0)
    rates[t] = jnp.where(row == 0, rate_in[0], rate_in[1])
    for step in range(1, TP):
        rate_copy(step).start()
    stage_a(0)
    set_out(0)
    set_out(1)
    set_out(4)
    stage_a(1)
    boundary = bounds[t]
    edge = boundary - s * rows

    for index in range(SEQ):
        hidden_load(index).wait()
        cot_load(index).start()

    def prepare(part, start):
        values = hidden[part, :].astype(F32)
        scale = lax.rsqrt(jnp.mean(values * values, axis=-1, keepdims=True) + EPSILON)
        normed[part, :] = (values * scale).astype(BF16)
        row = lax.broadcasted_iota(jnp.int32, (BLOCK, rows), 0) + start
        column = lax.broadcasted_iota(jnp.int32, (BLOCK, rows), 1)
        apart = (column > row) | ((row >= edge) & (column < edge))
        distance[part, :] = jnp.where(apart, -1, row - column).astype(F32)

    every_rows(rows, prepare)
    keep(normed, normed_out)
    half_copy(0).start()
    for step in range(1, TP):
        here = rates.at[t]
        remote(here, here, rate_send.at[step - 1], rate_recv.at[step - 1], (s, t)).wait_recv()
    keep(rates, rate_out)

    before = jnp.where(s * rows - 1 >= boundary, 1, 0)
    last = jnp.where(s * rows + rows - 1 >= boundary, 1, 0)

    def rate_of(block, half):
        return rates[block, half : half + 1, :]

    def row_numbers(start, count):
        return lax.broadcasted_iota(jnp.int32, (count, HEAD), 0) + start

    def project(step, index):
        owner, block = ready(index)
        wide[:, 0:D] = dots(normed[...], whole[0][block, :], NT)

        def shape_rows(part, start):
            turn, lean = cosine[part, :], sine[part, :]
            for kind in range(2):
                for half in range(2):
                    at = kind * PAIR + half * HEAD
                    values = wide[part, at : at + HEAD]
                    logistic = 1.0 / (1.0 + jnp.exp(-values))
                    acts[owner, part, at : at + HEAD] = rotated(values * logistic, turn, lean).astype(BF16)
                    pack[owner, part, at : at + HEAD] = (
                        logistic * (1.0 + values * (1.0 - logistic))
                    ).astype(BF16)
            acts[owner, part, 2 * PAIR : 4 * PAIR] = wide[part, 2 * PAIR : 4 * PAIR].astype(BF16)
            number = row_numbers(start, WEIGH)
            valid = jnp.where(jnp.where(number >= edge, 1, 0) == last, 1.0, 0.0)
            for half in range(2):
                fade = jnp.exp(-rate_of(owner, half) * (rows - 1 - number).astype(F32)) * valid
                keys = acts[owner, part, PAIR + half * HEAD : PAIR + half * HEAD + HEAD].astype(F32)
                weights[part, half * HEAD : half * HEAD + HEAD] = (keys * fade).astype(BF16)

        every_rows(rows, shape_rows, WEIGH)
        for half in range(2):
            at = half * HEAD
            state[owner * 2 + half] = dots(
                weights[:, at : at + HEAD], acts[owner, :, 2 * PAIR + at : 2 * PAIR + at + HEAD], TN
            ).astype(BF16)

    def attend(step):
        owner = nearest(t, step)
        for half in range(2):
            at = half * HEAD
            rate = rates[owner, half : half + 1, :]
            for top in range(0, rows, PAIR):
                width = top + PAIR
                scores[0:PAIR, 0:width] = dots(
                    acts[owner, top : top + PAIR, at : at + HEAD], acts[owner, 0:width, PAIR + at : PAIR + at + HEAD], NT
                )

                def weigh(part, start, width=width, top=top, rate=rate):
                    for left in range(0, width, HEAD):
                        apart = distance[pl.ds(pl.multiple_of(start + top, WEIGH), WEIGH), left : left + HEAD]
                        fade = jnp.where(apart >= 0.0, jnp.exp(-rate * apart), 0.0)
                        weights[part, left : left + HEAD] = (scores[part, left : left + HEAD] * fade).astype(BF16)

                every_rows(PAIR, weigh, WEIGH)
                column = pl.ds(pl.multiple_of(owner * PAIR + at, HEAD), HEAD)
                mixed[top : top + PAIR, column] = dots(
                    weights[0:PAIR, 0:width], acts[owner, 0:width, 2 * PAIR + at : 2 * PAIR + at + HEAD], NN
                )

    def prefix_scale(block, source_block, rate):
        same = jnp.where((source_block + 1) * rows - 1 >= boundary, 1, 0) == jnp.where(block * rows - 1 >= boundary, 1, 0)
        usable = flag(source_block < block) * flag(same)
        gap = jnp.maximum(block - 1 - source_block, 0).astype(F32)
        return jnp.exp(-rate * (rows * gap)) * usable

    begin_states, add_pair, add_chips, finish_states, close_states = state_exchange(
        rows, boundary, exchange, rates, prefix_scale, lambda chip: 2 * chip + 2, lambda chip: 2 * chip + 1
    )

    def mix():
        finish_states()
        keep(incoming, incoming_out)
        for block in range(TP):
            for half in range(2):
                at = half * HEAD
                scores[:, at : at + HEAD] = dots(acts[block, :, at : at + HEAD], incoming[2 * block + half], NN)

            def add_outer(part, start, block=block):
                number = row_numbers(start, NARROW)
                valid = jnp.where(jnp.where(number >= edge, 1, 0) == before, 1.0, 0.0)
                for half in range(2):
                    fade = jnp.exp(-rate_of(block, half) * (number + 1).astype(F32)) * valid
                    column = slice(block * PAIR + half * HEAD, block * PAIR + half * HEAD + HEAD)
                    mixed[part, column] += fade * scores[part, half * HEAD : half * HEAD + HEAD]

            every_rows(rows, add_outer, NARROW)

        def gate_rows(part, start):
            values = mixed[part, :]
            scale = lax.rsqrt(jnp.mean(values * values, axis=-1, keepdims=True) + EPSILON)
            inv_mix[part, :] = jnp.broadcast_to(scale, (BLOCK, HEAD))
            values = values * scale
            for block in range(TP):
                column = slice(block * PAIR, block * PAIR + PAIR)
                gate = acts[block, part, 3 * PAIR : 4 * PAIR].astype(F32)
                pack[block, part, 2 * PAIR : 3 * PAIR] = (values[:, column] * gate).astype(BF16)
                pack[block, part, 3 * PAIR : 4 * PAIR] = values[:, column].astype(BF16)

        every_rows(rows, gate_rows, BLOCK)
        keep(acts, acts_out)
        keep(pack, pack_out)
        half_copy(3).start()
        keep(inv_mix, inv_mix_out)

    def project_out():
        for block in range(TP):
            term = dots(pack[block, :, 2 * PAIR : 3 * PAIR], whole[1][block * PAIR : block * PAIR + PAIR, :], NN)
            if block:
                wide[:, 0:D] += term
            else:
                wide[:, 0:D] = term

        def norm_rows(part, start):
            values = hidden[part, :].astype(F32) + wide[part, 0:D]
            mixed[part, :] = values
            scale = lax.rsqrt(jnp.mean(values * values, axis=-1, keepdims=True) + EPSILON)
            inv_second[part, :] = jnp.broadcast_to(scale, (BLOCK, HEAD))
            second_normed[part, :] = (values * scale).astype(BF16)

        every_rows(rows, norm_rows)
        keep(second_normed, second_out)
        half_copy(1).start()
        keep(inv_second, inv_second_out)

    def left_side(index):
        owner, block = ready(index)
        down_ready(items[index][1])
        wide[:, 0:units] = dots(second_normed[...], whole[2][block, :], NT)
        wide[:, 2 * beside : 2 * beside + units] = dots(cot[...], whole[4][block, :], NT)

    def side_copies(slot, owner):
        return [
            pltpu.make_async_copy(sides.at[slot, part], out.at[owner], side_sem.at[slot, part])
            for part, out in enumerate((glu_out, left_out, right_out))
        ]

    def side_remotes(slot, step):
        owner = nearest(t, step)
        return [
            remote(sides.at[slot, part], out.at[owner], side_send.at[slot, part], side_recv.at[step, part], (other, t))
            for part, out in enumerate((glu_other, left_other, right_other))
        ]

    def right_side(index):
        owner, block = ready(index)
        w, step, low, high = items[index]
        part_rows = pl.ds(pl.multiple_of(owner * units + low, 16), high - low)
        wide[:, beside + low : beside + high] = dots(second_normed[...], whole[3][part_rows, :], NT)
        slot = step % 2
        if step >= 2 and low == 0:
            for copy in side_copies(slot, nearest(t, step - 2)):
                copy.wait()
            for copy in side_remotes(slot, step - 2):
                copy.wait_send()

        def multiply(part, start):
            left, right = wide[part, low:high], wide[part, beside + low : beside + high]
            grad = wide[part, 2 * beside + low : 2 * beside + high]
            sides[slot, 0, part, low:high] = (left * right).astype(BF16)
            sides[slot, 1, part, low:high] = (grad * right).astype(BF16)
            sides[slot, 2, part, low:high] = (grad * left).astype(BF16)

        every_rows(rows, multiply)
        if high == units:
            for copy in side_copies(slot, owner) + side_remotes(slot, step):
                copy.start()
        mixed[...] += dots(sides[slot, 0, :, low:high], whole[4][part_rows, :], NN)
        term = dots(sides[slot, 1, :, low:high], whole[2][part_rows, :], NN) + dots(
            sides[slot, 2, :, low:high], whole[3][part_rows, :], NN
        )
        if step:
            back[...] += term
        else:
            back[...] = term

    stage_b(0)
    pass_on(0, 1)
    stage_a(2)
    stage_b(1)
    set_out(4, 1)
    stage_c(0)
    pass_on(0, 2)
    stage_a(3)
    stage_b(2)
    stage_c(1)
    set_out(4, 2)
    set_out(4, 3)
    pass_on(0, 3)
    stage_a(4)
    project(0, 0)
    tick(5)
    for step in range(1, TP):
        tick(5 + step)
        project(step, 1 + step)
    begin_states()
    for index in range(SEQ):
        cot_load(index).wait()
    half_copy(2).start()
    tick(9)
    add_pair()
    attend(0)
    tick(10)
    attend(1)
    tick(11)
    attend(2)
    attend(3)
    add_chips()
    tick(12)
    for index in range(5, 5 + TP):
        ready(index)
    mix()
    tick(13)
    project_out()
    for index in range(5 + TP, len(items)):
        if index > 5 + TP:
            tick(index + LAG_C)
        (left_side, right_side)[items[index][0] - 2](index)

    def finish(part, start):
        for index in range(SEQ):
            result_out[part, plain(index)] = mixed[part, place_of(index)].astype(BF16)

    keep(back, back_out)
    every_rows(rows, finish)

    for step in range(1, TP):
        rate_copy(step).wait_send()
    close_states()
    for copy in keeps:
        copy().wait()
    for part in range(4):
        half_copy(part).wait()
    for step in range(TP):
        for copy in side_remotes(step % 2, step):
            copy.wait_recv()
            if step >= 2:
                copy.wait_send()
        if step >= 2:
            for copy in side_copies(step % 2, nearest(t, step)):
                copy.wait()
    for index in range(len(items)):
        for copy in plane_copies(index) + relay_copies(index) + last_copies(index):
            copy.wait_send()
    for w in range(5):
        for step in range(TP):
            for column in range(4 if w == 4 else 1):
                for up in (True, False):

                    @pl.when(goes(step, up))
                    def _(w=w, step=step, column=column, up=up):
                        parcel(w, step, column, up).wait_send()

                if w == 4 and step:
                    across(step, column).wait_send()


KEPT = 20


def forward(heads_in, shards, hidden, cot, cosine, sine, rate, bounds):
    rows = hidden.shape[1]
    sizes = (4 * PAIR, *(shard.shape[0] for shard in shards))
    units = sizes[2]
    beside = -(-units // HEAD) * HEAD
    items = 4 * TP + 2
    dma = pltpu.SemaphoreType.DMA
    vmem = pl.BlockSpec(memory_space=pltpu.VMEM)
    anywhere = pl.BlockSpec(memory_space=pl.ANY)
    heads = 2 * TP
    shape = jax.ShapeDtypeStruct
    outs = [
        *[shape((TP * size, D), BF16) for size in sizes[:2]],
        *[shape((TP, rows, 4 * PAIR), BF16)] * 2,
        *[shape((rows, D), BF16)] * 2,
        *[shape((TP, rows, units), BF16)] * 6,
        shape((TP, rows, PAIR), BF16),
        *[shape((rows, D // 2), BF16)] * 3,
        shape((rows, D), F32),
        shape((heads, HEAD, HEAD), BF16),
        shape((rows, HEAD), F32),
        shape((rows, HEAD), F32),
        shape((TP, 8, HEAD), F32),
        shape((rows, D), BF16),
    ]
    return pl.pallas_call(
        functools.partial(forward_kernel, rows, sizes),
        out_shape=outs,
        in_specs=[vmem] * 4 + [anywhere] * 6 + [vmem] * 2 + [pl.BlockSpec(memory_space=pltpu.SMEM)] * 2,
        out_specs=[anywhere] * (len(outs) - 1) + [vmem],
        scratch_shapes=[pltpu.VMEM((TP * size, D), BF16) for size in sizes]
        + [
            *[pltpu.VMEM((TP, rows, 4 * PAIR), BF16)] * 2,
            *[pltpu.VMEM((rows, D), BF16)] * 4,
            pltpu.VMEM((2, 3, rows, units), BF16),
            pltpu.VMEM((rows, D), F32),
            pltpu.VMEM((rows, 3 * beside), F32),
            pltpu.VMEM((rows, D), F32),
            pltpu.VMEM((rows, rows), F32),
            pltpu.VMEM((rows, rows), F32),
            pltpu.VMEM((rows, rows), BF16),
            pltpu.VMEM((rows, HEAD), F32),
            pltpu.VMEM((rows, HEAD), F32),
            pltpu.VMEM((TP, 8, HEAD), F32),
            pltpu.VMEM((4 * PAIR, STRIPE), BF16),
            *state_scratch(),
            dma((5,)),
            dma((5, TP, 4)),
            dma((5, TP, 4)),
            dma((5, TP, 4)),
            dma((TP, 4)),
            dma((TP, 4)),
            dma((items, 7)),
            dma((items,)),
            dma((items, 2)),
            dma((items, 4)),
            dma((TP - 1,)),
            dma((TP - 1,)),
            dma((KEPT,)),
            dma((2, 3)),
            dma((2, 3)),
            dma((TP, 3)),
            dma((4,)),
            dma((4,)),
            dma((SEQ,)),
            dma((SEQ,)),
        ],
        compiler_params=pltpu.CompilerParams(
            collective_id=0, has_side_effects=True, vmem_limit_bytes=63 * 2**20
        ),
        name="forward",
    )(*heads_in, *shards, hidden, cot, cosine, sine, rate, bounds)


PIECES = 4
HELD = 6
LAG_2, LAG_3, LAG_4, HOP, LAG_5 = 2, 4, 6, 2, 13
KINDS = 6
BEFORE, EARLY, WAIT_1, WAIT_2 = 10, 2, 3, 9
ITEMS = KINDS * TP


def add_rows(target, *terms):
    rows = target.shape[0]

    step = rows // 4

    @pl.loop(0, 4)
    def _(block):
        part = pl.ds(pl.multiple_of(block * step, 16), step)
        total = terms[0][part, :].astype(F32)
        for term in terms[1:]:
            total = total + term[part, :].astype(F32)
        target[part, :] = total.astype(target.dtype)


def backward_kernel(rows, sizes, *refs):
    whole, refs = refs[:2], refs[2:]
    (acts_in, pack_in, normed_in, second_in, glu_own, left_own, right_own, glu_other, left_other, right_other,
     gated_other, normed_other, second_other, cot_other, back_in, output_in, hidden_in, cot_in,
     incoming, inv_mix, inv_second, rates, cosine, sine, bounds), refs = refs[:25], refs[25:]
    (tall, output_whole, input_whole, backs_own, backs_other), refs = refs[:5], refs[5:]
    (tiles, cot, second_normed, normed, attn_cot, halves, acts, pack, backs, mid, wide, distance, scores,
     weights, slopes, faded, lhs, held), refs = refs[:18], refs[18:]
    exchange, refs = refs[:10], refs[10:]
    state, later = exchange[0], exchange[5]
    lands, refs = refs[:9], refs[9:]
    (tile_sem, half_sem, half_load_sem, backs_keep, backs_send, backs_recv, load_sem, cot_sem, hidden_sem, lhs_sem, second_send, second_recv,
     first_send, first_recv, line_send, below_recv, above_recv, share_local, share_up, share_down, share_recv) = refs
    s, t, other, first, second, diagonal = place()
    core = s % 2
    units = sizes[2]
    half_d = D // 2
    ours, theirs = rows_of(core, half_d), rows_of(1 - core, half_d)
    boundary = bounds[t]
    edge = boundary - s * rows
    before = jnp.where(s * rows - 1 >= boundary, 1, 0)
    last = jnp.where(s * rows + rows - 1 >= boundary, 1, 0)
    around = (first, second, diagonal)
    order = [3, 2, 1, 0]
    local = pltpu.make_async_copy

    done = set()

    def once(key, wait):
        if key not in done:
            done.add(key)
            wait()

    greet(s, t, (other, first, second, diagonal))

    def cot_load(index):
        return local(cot_in.at[t, :, plain(index)], cot.at[:, place_of(index)], cot_sem.at[index])

    def hidden_load(index):
        return local(hidden_in.at[t, :, plain(index)], acts.at[0, :, place_of(index)], hidden_sem.at[index])

    def second_load():
        return local(second_in, second_normed, load_sem.at[0])

    def normed_load():
        return local(normed_in, normed, load_sem.at[1])

    def acts_load():
        return local(acts_in, acts, load_sem.at[2])

    def pack_load():
        return local(pack_in, pack, load_sem.at[3])

    def back_load():
        return local(back_in, mid, load_sem.at[4])

    def half_load(part):
        return local((cot_other, second_other, normed_other)[part], halves.at[part], half_load_sem.at[part])

    def half_copy():
        return remote(attn_cot.at[:, theirs], halves.at[3], half_sem.at[0], half_sem.at[1], (other, t))

    tile_list = [(1, part) for part in range(2)] + [(0, part) for part in range(2 * TP)]

    def tile_load(index):
        w, at = tile_list[index]
        return local(whole[w].at[pl.ds(at * half_d, half_d), :], tiles.at[index % 3], tile_sem.at[index % 3])

    def tile(index):
        tile_load(index).wait()
        return tiles[index % 3]

    def tile_next(index):
        if index + 3 < len(tile_list):
            tile_load(index + 3).start()

    def backs_keep_copy(block):
        return local(backs.at[block], backs_own.at[block], backs_keep.at[block])

    def backs_copy(block):
        return remote(backs.at[block], backs_other.at[block], backs_send.at[block], backs_recv.at[block], (other, t))

    piece_rows = rows // PIECES
    shares = ((output_in, output_whole), (acts.at[1], input_whole))

    def piece(a, owner, p):
        return shares[a][1].at[owner, pl.ds(p * piece_rows, piece_rows), :]

    def own_piece(a, p):
        return shares[a][0].at[pl.ds(p * piece_rows, piece_rows), :]

    def share_copy(a, p, owner, src, up):
        sem, target = (share_up, t + 1) if up else (share_down, t - 1)
        return remote(src, piece(a, owner, p), sem.at[a, p, owner], share_recv.at[a, p, owner], (s, target))

    def share_keep(a, p):
        return local(own_piece(a, p), piece(a, t, p), share_local.at[a, p])

    def share_start(a, p):
        @pl.when(t < TP - 1)
        def _():
            share_copy(a, p, t, own_piece(a, p), True).start()

        @pl.when(t > 0)
        def _():
            share_copy(a, p, t, own_piece(a, p), False).start()

        share_keep(a, p).start()

    relays = [
        (a, p, step) for a in range(2) for steps in ((1, 2), (3,)) for p in range(PIECES) for step in steps
    ]
    relayed = []

    def passes(owner, up):
        return (owner < t) & (t < TP - 1) if up else (owner > t) & (t > 0)

    def relay(limit, until=len(relays)):
        for _ in range(limit):
            if len(relayed) >= until:
                return
            a, p, step = relays[len(relayed)]
            relayed.append(1)
            owner = nearest(t, step)
            for up in (True, False):

                @pl.when(passes(owner, up))
                def _(up=up):
                    share_copy(a, p, owner, piece(a, owner, p), up).wait_recv()
                    share_copy(a, p, owner, piece(a, owner, p), up).start()

    items = (
        [(0, step) for step in order]
        + [(kind, step) for step in order for kind in (1, 2)]
        + [(3, step) for step in order]
        + [(kind, step) for step in order for kind in (4, 5)]
    )
    heights = (units, units, units, sizes[1], half_d, half_d)

    def lands_of(index):
        kind, step = items[index]
        owner = nearest(t, step)
        group, base, extra = ((0, kind * TP, 3 * TP + kind), (1, 0, TP), (2, (kind - 4) * TP, 2 * TP + kind - 4))[
            0 if kind < 3 else 1 if kind == 3 else 2
        ]
        return owner, lands[3 * group : 3 * group + 3], base + owner, extra

    def own_source(kind, owner):
        if kind == 0:
            return glu_own.at[owner], glu_other.at[owner]
        if kind == 1:
            return left_own.at[owner], left_other.at[owner]
        if kind == 2:
            return right_own.at[owner], right_other.at[owner]
        if kind == 3:
            return pack_in.at[owner, :, 2 * PAIR : 3 * PAIR], gated_other.at[owner]
        part = slice((kind - 4) * half_d, (kind - 3) * half_d)
        return backs_own.at[owner, :, part], backs_other.at[owner, :, part]

    def lhs_loads(index):
        kind, step = items[index]
        slot = index % 2
        return [
            local(src, lhs.at[slot, part, :, pl.ds(0, heights[kind])], lhs_sem.at[slot, part])
            for part, src in enumerate(own_source(kind, nearest(t, step)))
        ]

    def prefetch(index):
        kind, step = items[index]
        owner = nearest(t, step)
        if kind >= 4:
            once(("backs", step), lambda: backs_keep_copy(owner).wait())
            once(("backs_other", step), lambda: backs_copy(owner).wait_recv())
        for copy in lhs_loads(index):
            copy.start()

    def to_second(index):
        kind = items[index][0]
        owner, (second_land, first_land, line_land), at, extra = lands_of(index)
        return [
            remote(
                held.at[index % HELD, column // 2, pl.ds(0, heights[kind]), :],
                second_land.at[at, part],
                second_send.at[index, part],
                second_recv.at[index, part],
                (second, t),
            )
            for part, column in enumerate((diagonal, second))
        ]

    def to_first(index):
        owner, (second_land, first_land, line_land), at, extra = lands_of(index)
        return remote(second_land.at[at, 0], first_land.at[at], first_send.at[index], first_recv.at[index], (first, t))

    def along(index, up):
        kind = items[index][0]
        owner, (second_land, first_land, line_land), at, extra = lands_of(index)
        if up:
            return remote(
                first_land.at[at], line_land.at[at], line_send.at[index], below_recv.at[kind, owner], (s, t + 1)
            )
        final = jnp.where(owner == t - 1, 1, 0)
        return remote(
            first_land.at[at],
            line_land.at[at + final * (extra - at)],
            line_send.at[index],
            above_recv.at[kind, owner],
            (s, t - 1),
        )

    def held_rows(index, chip):
        return held.at[index % HELD, chip, pl.ds(0, heights[items[index][0]]), :]

    def advance(now):
        index = now - LAG_2
        if 0 <= index < ITEMS:
            owner, (second_land, first_land, line_land), at, extra = lands_of(index)
            for copy in to_second(index):
                copy.wait_recv()
            add_rows(second_land.at[at, 0], second_land.at[at, 0], held_rows(index, first // 2))
            to_first(index).start()
        index = now - LAG_3
        if 0 <= index < ITEMS:
            owner, (second_land, first_land, line_land), at, extra = lands_of(index)
            to_first(index).wait_recv()
            add_rows(first_land.at[at], first_land.at[at], held_rows(index, s // 2), second_land.at[at, 1])
        for hop in range(TP - 1):
            index = now - LAG_4 - HOP * hop
            if not 0 <= index < ITEMS or items[index][1] == 0:
                continue
            owner, (second_land, first_land, line_land), at, extra = lands_of(index)
            for up in (True, False):

                @pl.when((t == hop) & (owner > t) if up else (t == TP - 1 - hop) & (owner < t))
                def _(index=index, at=at, up=up, first_land=first_land, line_land=line_land, hop=hop):
                    if hop:
                        along(index, up).wait_recv()
                        add_rows(first_land.at[at], first_land.at[at], line_land.at[at])
                    along(index, up).start()

        index = now - LAG_5
        if 0 <= index < ITEMS:
            kind, step = items[index]
            owner, (second_land, first_land, line_land), at, extra = lands_of(index)
            if step == 0:
                above = sum(heights[:kind])
                target = tall.at[above : above + heights[kind]]

                @pl.when(t == 0)
                def _():
                    along(index, False).wait_recv()
                    add_rows(target, first_land.at[at], line_land.at[extra])

                @pl.when(t == TP - 1)
                def _():
                    along(index, True).wait_recv()
                    add_rows(target, first_land.at[at], line_land.at[at])

                @pl.when((t > 0) & (t < TP - 1))
                def _():
                    along(index, True).wait_recv()
                    along(index, False).wait_recv()
                    add_rows(target, first_land.at[at], line_land.at[at], line_land.at[extra])

    def produce(index):
        kind, step = items[index]
        height = heights[kind]
        right, part = ((cot, 0), (second_normed, 1), (second_normed, 1), (attn_cot, 3), (normed, 2), (normed, 2))[kind]
        once(("half", part), lambda: half_copy().wait_recv() if part == 3 else half_load(part).wait())
        if kind >= 4:
            once("normed", lambda: normed_load().wait())
        for copy in lhs_loads(index):
            copy.wait()
        if index >= HELD:
            for copy in to_second(index - HELD):
                copy.wait_send()
        slot = index % 2
        product = dots(lhs[slot, 0, :, 0:height], right[:, ours], TN) + dots(lhs[slot, 1, :, 0:height], halves[part], TN)
        for chip in range(4):
            held[index % HELD, chip, 0:height, :] = product[:, chip * STRIPE : chip * STRIPE + STRIPE].astype(BF16)
        for copy in to_second(index):
            copy.start()
        advance(index)

    for index in range(SEQ):
        cot_load(index).start()
    half_load(0).start()
    prefetch(0)
    for p in range(PIECES):
        share_start(0, p)
    back_load().start()
    second_load().start()
    half_load(1).start()
    for index in range(3):
        tile_load(index).start()
    acts_load().start()
    pack_load().start()
    normed_load().start()
    half_load(2).start()
    for index in range(SEQ):
        cot_load(index).wait()
    produce(0)
    prefetch(1)
    back_load().wait()
    second_load().wait()

    def middle(part, start):
        unit = second_normed[part, :].astype(F32)
        values = mid[part, :]
        inner = jnp.mean(values * unit, axis=-1, keepdims=True)
        values = cot[part, :].astype(F32) + inv_second[part, 0:1] * (values - unit * inner)
        mid[part, :] = values
        attn_cot[part, :] = values.astype(BF16)

    every_rows(rows, middle)
    half_copy().start()
    produce(1)
    prefetch(2)
    at_tile = 0
    for part in range(2):
        wide[:, part * half_d : part * half_d + half_d] = dots(attn_cot[...], tile(at_tile + part), NT)
        tile_next(at_tile + part)
    at_tile += 2
    acts_load().wait()
    pack_load().wait()

    def head_rows(part, start):
        total = jnp.zeros((BLOCK, 1), F32)
        for block in range(TP):
            values = wide[part, block * PAIR : block * PAIR + PAIR]
            gate = acts[block, part, 3 * PAIR : 4 * PAIR].astype(F32)
            unit = pack[block, part, 3 * PAIR : 4 * PAIR].astype(F32)
            total += jnp.sum(values * gate * unit, axis=-1, keepdims=True)
        total = total * (1.0 / D)
        scale = inv_mix[part, 0:1]
        for block in range(TP):
            values = wide[part, block * PAIR : block * PAIR + PAIR]
            gate = acts[block, part, 3 * PAIR : 4 * PAIR].astype(F32)
            unit = pack[block, part, 3 * PAIR : 4 * PAIR].astype(F32)
            backs[block, part, 3 * PAIR : 4 * PAIR] = (values * unit).astype(BF16)
            backs[block, part, 2 * PAIR : 3 * PAIR] = (scale * (values * gate - unit * total)).astype(BF16)
        row = lax.broadcasted_iota(jnp.int32, (BLOCK, rows), 0) + start
        column = lax.broadcasted_iota(jnp.int32, (BLOCK, rows), 1)
        apart = (column > row) | ((row >= edge) & (column < edge))
        distance[part, :] = jnp.where(apart, -1, row - column).astype(F32)

    every_rows(rows, head_rows)
    produce(2)
    prefetch(3)
    relay(2, 12)

    def rate_of(block, half):
        return rates[block, half : half + 1, :]

    def row_numbers(start):
        return lax.broadcasted_iota(jnp.int32, (NARROW, HEAD), 0) + start

    for block in range(TP):
        for half in range(2):
            at = half * HEAD

            def fade_rows(part, start, block=block, half=half, at=at):
                number = row_numbers(start)
                valid = jnp.where(jnp.where(number >= edge, 1, 0) == before, 1.0, 0.0)
                fade = jnp.exp(-rate_of(block, half) * (number + 1).astype(F32)) * valid
                values = backs[block, part, 2 * PAIR + at : 2 * PAIR + at + HEAD].astype(F32)
                faded[part, :] = (values * fade).astype(BF16)

            every_rows(rows, fade_rows, NARROW)
            head = 2 * block + half
            state[head] = dots(acts[block, :, at : at + HEAD], faded[...], TN).astype(BF16)
            wide[:, head * HEAD : head * HEAD + HEAD] = dots(faded[...], incoming[head], NT)

    def suffix_scale(block, source_block, rate):
        same = jnp.where(source_block * rows - 1 >= boundary, 1, 0) == jnp.where(block * rows + rows - 1 >= boundary, 1, 0)
        usable = flag(source_block > block) * flag(same)
        gap = jnp.maximum(source_block - 1 - block, 0).astype(F32)
        return jnp.exp(-rate * (rows * gap)) * usable

    begin_states, add_pair, add_chips, finish_states, close_states = state_exchange(
        rows, boundary, exchange, rates, suffix_scale, lambda chip: 2 * chip - 1, lambda chip: 2 * chip
    )
    begin_states()
    produce(3)
    prefetch(4)
    relay(2, 12)
    add_pair()
    weights[0:PAIR, PAIR:rows] = jnp.zeros((PAIR, rows - PAIR), BF16)
    slopes[0:PAIR, PAIR:rows] = jnp.zeros((PAIR, rows - PAIR), BF16)

    def attend(block):
        for half in range(2):
            at = half * HEAD
            head = 2 * block + half
            rate = rate_of(block, half)
            query, key, value = [slice(kind * PAIR + at, kind * PAIR + at + HEAD) for kind in range(3)]
            mine_columns = slice(head * HEAD, head * HEAD + HEAD)
            for top in range(0, rows, PAIR):
                width = top + PAIR
                scores[0:PAIR, 0:width] = dots(acts[block, top:width, query], acts[block, 0:width, key], NT)
                scores[PAIR : 2 * PAIR, 0:width] = dots(backs[block, top:width, value], acts[block, 0:width, value], NT)

                def weigh(part, start, width=width, top=top):
                    below = pl.ds(pl.multiple_of(start + PAIR, WEIGH), WEIGH)
                    there = pl.ds(pl.multiple_of(start + top, WEIGH), WEIGH)
                    for left in range(0, width, HEAD):
                        apart = distance[there, left : left + HEAD]
                        fade = jnp.where(apart >= 0.0, jnp.exp(-rate * apart), 0.0)
                        weights[there, left : left + HEAD] = (scores[part, left : left + HEAD] * fade).astype(BF16)
                        grad = scores[below, left : left + HEAD].astype(BF16).astype(F32)
                        slopes[there, left : left + HEAD] = (grad * fade).astype(BF16)

                every_rows(PAIR, weigh, WEIGH)
                wide[top:width, mine_columns] += dots(slopes[top:width, 0:width], acts[block, 0:width, key], NN)
            inner = dots(weights[...], backs[block, :, value], TN)
            acts[block, :, 3 * PAIR + at : 3 * PAIR + at + HEAD] = inner.astype(BF16)
            inner = dots(slopes[...], acts[block, :, query], TN)
            backs[block, :, key] = inner.astype(BF16)

            def turn_back(part, start):
                turned = rotated(wide[part, mine_columns], cosine[part, :], -sine[part, :])
                backs[block, part, query] = (turned * pack[block, part, query].astype(F32)).astype(BF16)

            every_rows(rows, turn_back, NARROW)

    for block in range(TP):
        attend(block)
        produce(4 + block)
        prefetch(5 + block)
        relay(2, 12)

    add_chips()
    produce(8)
    prefetch(9)
    relay(2, 12)
    finish_states()

    for block in range(TP):
        for half in range(2):
            at = half * HEAD
            head = 2 * block + half
            query, key, value = [slice(kind * PAIR + at, kind * PAIR + at + HEAD) for kind in range(3)]
            scores[:, 0:HEAD] = dots(acts[block, :, value], later[head], NT)
            scores[:, HEAD : 2 * HEAD] = dots(acts[block, :, key], later[head], NN)

            def finish_rows(part, start, block=block, half=half, at=at, key=key, value=value):
                number = row_numbers(start)
                valid = jnp.where(jnp.where(number >= edge, 1, 0) == last, 1.0, 0.0)
                fade = jnp.exp(-rate_of(block, half) * (rows - 1 - number).astype(F32)) * valid
                keys = backs[block, part, key].astype(F32) + fade * scores[part, 0:HEAD]
                turned = rotated(keys, cosine[part, :], -sine[part, :])
                backs[block, part, key] = (turned * pack[block, part, key].astype(F32)).astype(BF16)
                values = acts[block, part, 3 * PAIR + at : 3 * PAIR + at + HEAD].astype(F32)
                backs[block, part, value] = (values + fade * scores[part, HEAD : 2 * HEAD]).astype(BF16)

            every_rows(rows, finish_rows, NARROW)
        backs_keep_copy(block).start()
        backs_copy(block).start()
        for part in range(2):
            index = at_tile + 2 * block + part
            term = dots(backs[block, :, part * half_d : part * half_d + half_d], tile(index), NN)
            if block or part:
                wide[...] += term
            else:
                wide[...] = term
            tile_next(index)
        if block == 0:
            for index in range(SEQ):
                hidden_load(index).start()
        if block == 1:
            produce(9)
            prefetch(10)
    relay(12, 12)
    for index in range(SEQ):
        hidden_load(index).wait()

    def input_rows(part, start):
        values = acts[0, part, :].astype(F32)
        scale = lax.rsqrt(jnp.mean(values * values, axis=-1, keepdims=True) + EPSILON)
        unit = values * scale
        grad = wide[part, :]
        inner = jnp.mean(grad * unit, axis=-1, keepdims=True)
        grad = mid[part, :] + scale * (grad - unit * inner)
        for index in range(SEQ):
            acts[1, part, plain(index)] = grad[:, place_of(index)].astype(BF16)

    for p in range(PIECES):

        @pl.loop(0, piece_rows // BLOCK)
        def _(block, p=p):
            start = p * piece_rows + block * BLOCK
            input_rows(pl.ds(pl.multiple_of(start, BLOCK), BLOCK), start)

        if p < EARLY:
            share_start(1, p)
    for index in range(BEFORE, ITEMS):
        produce(index)
        if index + 1 < ITEMS:
            prefetch(index + 1)
        if EARLY <= index - BEFORE + EARLY < PIECES:
            share_start(1, index - BEFORE + EARLY)
        if index >= BEFORE + WAIT_1:
            relay(2, 20)
        if index >= BEFORE + WAIT_2:
            relay(1)
    for now in range(ITEMS, ITEMS + LAG_5):
        advance(now)
        relay(1)
    relay(len(relays))

    half_copy().wait_send()
    for block in range(TP):
        backs_copy(block).wait_send()
    close_states()
    for index, (kind, step) in enumerate(items):
        if index >= ITEMS - HELD:
            for copy in to_second(index):
                copy.wait_send()
        to_first(index).wait_send()
        if step:
            along(index, True).wait_send()
    for a in range(2):
        for p in range(PIECES):
            share_keep(a, p).wait()

            @pl.when(t < TP - 1)
            def _(a=a, p=p):
                share_copy(a, p, t, own_piece(a, p), True).wait_send()

            @pl.when(t > 0)
            def _(a=a, p=p):
                share_copy(a, p, t, own_piece(a, p), False).wait_send()
    for a, p, step in relays:
        owner = nearest(t, step)
        passed = passes(owner, True) | passes(owner, False)

        @pl.when(jnp.logical_not(passed))
        def _(a=a, p=p, owner=owner):
            share_copy(a, p, owner, piece(a, owner, p), True).wait_recv()

        for up in (True, False):

            @pl.when(passes(owner, up))
            def _(a=a, p=p, owner=owner, up=up):
                share_copy(a, p, owner, piece(a, owner, p), up).wait_send()


def backward(units, whole, kept, output, hidden_in, out_cotangent, incoming, inv_mix, inv_second, rates, cosine, sine, bounds):
    rows = output.shape[0]
    sizes = tuple(weight.shape[0] // TP for weight in whole) + (units,)
    dma = pltpu.SemaphoreType.DMA
    vmem = pl.BlockSpec(memory_space=pltpu.VMEM)
    anywhere = pl.BlockSpec(memory_space=pl.ANY)
    half_d = D // 2
    shape = jax.ShapeDtypeStruct
    scratch = [
        pltpu.VMEM((3, half_d, D), BF16),
        *[pltpu.VMEM((rows, D), BF16)] * 4,
        pltpu.VMEM((4, rows, half_d), BF16),
        *[pltpu.VMEM((TP, rows, 4 * PAIR), BF16)] * 3,
        pltpu.VMEM((rows, D), F32),
        pltpu.VMEM((rows, D), F32),
        pltpu.VMEM((rows, rows), F32),
        pltpu.VMEM((rows, rows), F32),
        pltpu.VMEM((rows, rows), BF16),
        pltpu.VMEM((rows, rows), BF16),
        pltpu.VMEM((rows, HEAD), BF16),
        pltpu.VMEM((2, 2, rows, units), BF16),
        pltpu.VMEM((HELD, 4, units, STRIPE), BF16),
        *state_scratch(),
    ]
    for count, height, extra in ((3 * TP, units, 3), (TP, sizes[1], 1), (2 * TP, half_d, 2)):
        scratch += [
            pltpu.VMEM((count, 2, height, STRIPE), BF16),
            pltpu.VMEM((count, height, STRIPE), BF16),
            pltpu.VMEM((count + extra, height, STRIPE), BF16),
        ]
    scratch += [
        dma((3,)),
        dma((2,)),
        dma((3,)),
        dma((TP,)),
        dma((TP,)),
        dma((TP,)),
        dma((5,)),
        dma((SEQ,)),
        dma((SEQ,)),
        dma((2, 2)),
        dma((ITEMS, 2)),
        dma((ITEMS, 2)),
        dma((ITEMS,)),
        dma((ITEMS,)),
        dma((ITEMS,)),
        dma((KINDS, TP)),
        dma((KINDS, TP)),
        dma((2, PIECES)),
        dma((2, PIECES, TP)),
        dma((2, PIECES, TP)),
        dma((2, PIECES, TP)),
    ]
    return pl.pallas_call(
        functools.partial(backward_kernel, rows, sizes),
        out_shape=[shape((3 * units + sizes[1] + sizes[0], STRIPE), F32)]
        + [shape((TP, rows, D), BF16)] * 2
        + [shape((TP, rows, 4 * PAIR), BF16)] * 2,
        in_specs=[anywhere] * 20 + [vmem] * 6 + [pl.BlockSpec(memory_space=pltpu.SMEM)],
        out_specs=[vmem] + [anywhere] * 4,
        scratch_shapes=scratch,
        compiler_params=pltpu.CompilerParams(
            collective_id=1, has_side_effects=True, vmem_limit_bytes=63 * 2**20
        ),
        name="backward",
    )(*whole, *kept, output, hidden_in, out_cotangent, incoming, inv_mix, inv_second, rates, cosine, sine, bounds)


def finish_kernel(units, input_in, tall, output_in, input_grad, output, *refs):
    grads, (held, sem) = refs[:8], refs[8:]
    step = pl.program_id(0)

    def load(block):
        return pltpu.make_async_copy(output_in.at[block], held.at[block], sem.at[0, block])

    def store(block):
        return pltpu.make_async_copy(held.at[block], output.at[block], sem.at[1, block])

    @pl.when(step == 0)
    def _():
        for block in range(TP):
            load(block).start()
        for kind in range(3):
            grads[kind][...] = tall[kind * units : kind * units + units, :]
        grads[3][...] = tall[3 * units : 3 * units + PAIR, :]
        for kind in range(4):
            above = 3 * units + PAIR + kind * PAIR
            grads[4 + kind][...] = tall[above : above + PAIR, :].T

    input_grad[...] = input_in[...].astype(F32)

    for block in range(TP):

        @pl.when(step == block)
        def _(block=block):
            load(block).wait()
            store(block).start()

    @pl.when(step == TP - 1)
    def _():
        for block in range(TP):
            store(block).wait()


def finish(units, input_grad, tall, output):
    rows = input_grad.shape[1]
    block = lambda: pl.BlockSpec((1, rows, D), lambda step: (step, 0, 0))
    fixed = lambda *shape: pl.BlockSpec(shape, lambda step: (0, 0))
    anywhere = pl.BlockSpec(memory_space=pl.ANY)
    shape = jax.ShapeDtypeStruct
    shapes = [(units, STRIPE)] * 3 + [(PAIR, STRIPE)] + [(STRIPE, PAIR)] * 4
    return pl.pallas_call(
        functools.partial(finish_kernel, units),
        grid=(TP,),
        out_shape=[shape(input_grad.shape, F32), shape(output.shape, BF16), *[shape(each, F32) for each in shapes]],
        in_specs=[block(), fixed(*tall.shape), anywhere],
        out_specs=[block(), anywhere, *[fixed(*each) for each in shapes]],
        scratch_shapes=[pltpu.VMEM(output.shape, BF16), pltpu.SemaphoreType.DMA((2, TP))],
        compiler_params=pltpu.CompilerParams(vmem_limit_bytes=62 * 2**20),
        name="finish",
    )(input_grad, tall, output)


def entering(value, axis, join, neutral, backward):
    count, mine = (lax.axis_size(axis), lax.axis_index(axis))
    pieces = jax.tree.map(lambda part: lax.all_gather(part, axis), value)
    if backward:
        pieces = jax.tree.map(lambda part: part[::-1], pieces)
        mine = count - 1 - mine
    subtotal = jax.tree.map(
        lambda part, zero: jnp.full_like(part, 0) + jnp.asarray(zero, part.dtype), value, neutral
    )

    def step(position, subtotal):
        longer = join(subtotal, jax.tree.map(lambda part: part[position], pieces))
        return jax.tree.map(lambda new, old: jnp.where(position < mine, new, old), longer, subtotal)

    return lax.fori_loop(0, count - 1, step, subtotal)


def swish_parts(pre_act):
    logistic = jax.nn.sigmoid(pre_act)
    return (pre_act * logistic, logistic * (1.0 + pre_act * (1.0 - logistic)))


def rotate(rows_in, cosine_table, sine_table, signed):
    halfway = rows_in.shape[-1] // 2
    front_half = rows_in[..., :halfway]
    back_half = rows_in[..., halfway:]
    return jnp.concatenate(
        [
            front_half * cosine_table - signed * back_half * sine_table,
            signed * front_half * sine_table + back_half * cosine_table,
        ],
        axis=-1,
    )


def combine_forward(earlier, following):
    return (earlier[0] * following[0], following[0][:, None, None] * earlier[1] + following[1])


def combine_backward(farther, nearer):
    return (farther[0] * nearer[0], nearer[1] + nearer[0][:, None, None] * farther[1])


def collect_weights(
    query_weight,
    key_weight,
    value_weight,
    gate_weight,
    out_weight,
    left_weight,
    right_weight,
    down_weight,
):
    return (
        lax.all_gather(query_weight, "seq", axis=0, tiled=True),
        lax.all_gather(key_weight, "seq", axis=0, tiled=True),
        lax.all_gather(value_weight, "seq", axis=0, tiled=True),
        lax.all_gather(gate_weight, "seq", axis=0, tiled=True),
        lax.all_gather(out_weight, "seq", axis=1, tiled=True),
        lax.all_gather(left_weight, "seq", axis=0, tiled=True),
        lax.all_gather(right_weight, "seq", axis=0, tiled=True),
        lax.all_gather(down_weight, "seq", axis=1, tiled=True),
    )


def state_prefix(factor, local_state):
    neutral = (jnp.ones_like(factor), jnp.zeros_like(local_state))
    return entering((factor, local_state), "seq", combine_forward, neutral, False)[1]


def state_suffix(factor, state_grad):
    neutral = (jnp.ones_like(factor), jnp.zeros_like(state_grad))
    return entering((factor, state_grad), "seq", combine_backward, neutral, True)[1]


def body(
    hidden_in,
    query_weight,
    key_weight,
    value_weight,
    gate_weight,
    out_weight,
    left_weight,
    right_weight,
    down_weight,
    decay_rate,
    seq_bounds,
    out_cotangent,
):
    row_count = hidden_in.shape[1]
    batch_count = hidden_in.shape[0]
    local_heads = decay_rate.shape[0]
    heads_shape = (row_count, local_heads, HEAD)
    device = lax.axis_index("seq")
    offsets = jnp.arange(row_count, dtype=jnp.int32)
    positions = device * row_count + offsets
    frequency = jnp.exp(
        jnp.arange(HEAD // 2, dtype=jnp.float32) * (-2.0 * math.log(10000.0) / HEAD)
    )
    angles = positions.astype(jnp.float32)[:, None] * frequency[None, :]
    cosine_table = jnp.cos(angles)[:, None, :]
    sine_table = jnp.sin(angles)[:, None, :]
    local_f = offsets.astype(jnp.float32)
    distance = local_f[:, None] - local_f[None, :]
    causal = distance >= 0.0
    distance_pos = jnp.maximum(distance, 0.0)
    accum = None
    outputs = []
    in_grads = []
    for batch_index in range(batch_count):
        gathered = collect_weights(
            query_weight,
            key_weight,
            value_weight,
            gate_weight,
            out_weight,
            left_weight,
            right_weight,
            down_weight,
        )
        query_full, key_full, value_full, gate_full, out_full, left_full, right_full, down_full = (
            gathered
        )
        boundary = seq_bounds[batch_index]
        segment = (positions >= boundary).astype(jnp.int32)
        before = (device * row_count - 1 >= boundary).astype(jnp.int32)
        last_segment = segment[row_count - 1]
        allowed = causal & (segment[:, None] == segment[None, :])
        decay = jnp.where(
            allowed[None], jnp.exp(-decay_rate[:, None, None] * distance_pos[None]), 0.0
        )
        coef_in = (
            jnp.exp(-decay_rate[None, :] * (local_f[:, None] + 1.0))
            * (segment == before).astype(jnp.float32)[:, None]
        )
        weight_loc = (
            jnp.exp(-decay_rate[None, :] * (row_count - 1.0 - local_f)[:, None])
            * (segment == last_segment).astype(jnp.float32)[:, None]
        )
        factor = jnp.where(last_segment == before, jnp.exp(-decay_rate * row_count), 0.0)
        input_rows = hidden_in[batch_index].astype(jnp.float32)
        inv_first = lax.rsqrt(jnp.mean(input_rows * input_rows, axis=-1, keepdims=True) + EPSILON)
        unit_first = input_rows * inv_first
        normed_first = unit_first.astype(jnp.bfloat16)
        query_pre = jnp.dot(normed_first, query_full, preferred_element_type=jnp.float32)
        key_pre = jnp.dot(normed_first, key_full, preferred_element_type=jnp.float32)
        value_pre = jnp.dot(normed_first, value_full, preferred_element_type=jnp.float32)
        gate_pre = jnp.dot(normed_first, gate_full, preferred_element_type=jnp.float32)
        query_act, query_slope = swish_parts(query_pre)
        key_act, key_slope = swish_parts(key_pre)
        query_rot = rotate(query_act.reshape(heads_shape), cosine_table, sine_table, 1.0).astype(
            jnp.bfloat16
        )
        key_rot = rotate(key_act.reshape(heads_shape), cosine_table, sine_table, 1.0).astype(
            jnp.bfloat16
        )
        value_rows = value_pre.astype(jnp.bfloat16).reshape(heads_shape)
        query_wide = query_rot.astype(jnp.float32)
        key_wide = key_rot.astype(jnp.float32)
        value_wide = value_rows.astype(jnp.float32)
        scores = jnp.einsum("ihe,jhe->hij", query_rot, key_rot, preferred_element_type=jnp.float32)
        attn_weights = (scores * decay).astype(jnp.bfloat16)
        inner_out = jnp.einsum(
            "hij,jhe->ihe", attn_weights, value_rows, preferred_element_type=jnp.float32
        )
        local_state = jnp.einsum(
            "jhe,jhf->hef",
            key_wide * weight_loc[:, :, None],
            value_wide,
            precision=HIGHEST_PRECISION,
        )
        incoming = state_prefix(factor, local_state)
        outer_out = coef_in[:, :, None] * jnp.einsum(
            "ihe,hef->ihf", query_wide, incoming, precision=HIGHEST_PRECISION
        )
        mixed_heads = (inner_out + outer_out).reshape(row_count, local_heads * HEAD)
        total_sq = lax.psum(jnp.sum(mixed_heads * mixed_heads, axis=-1), "tp")
        inv_mix = lax.rsqrt(total_sq / D + EPSILON)[:, None]
        unit_mix = mixed_heads * inv_mix
        gate_mix = (unit_mix * gate_pre).astype(jnp.bfloat16)
        attn_sum = lax.psum(jnp.dot(gate_mix, out_full, preferred_element_type=jnp.float32), "tp")
        resid_mid = input_rows + attn_sum
        inv_second = lax.rsqrt(jnp.mean(resid_mid * resid_mid, axis=-1, keepdims=True) + EPSILON)
        unit_second = resid_mid * inv_second
        normed_second = unit_second.astype(jnp.bfloat16)
        left_pre = jnp.dot(normed_second, left_full, preferred_element_type=jnp.float32)
        right_pre = jnp.dot(normed_second, right_full, preferred_element_type=jnp.float32)
        glu_product = (left_pre * right_pre).astype(jnp.bfloat16)
        glu_out = lax.psum(
            jnp.dot(glu_product, down_full, preferred_element_type=jnp.float32), "tp"
        )
        outputs.append((resid_mid + glu_out).astype(jnp.bfloat16))
        glu_cot = out_cotangent[batch_index]
        product_grad = jnp.einsum(
            "cd,fd->cf", glu_cot, down_full, preferred_element_type=jnp.float32
        )
        left_back = (product_grad * right_pre).astype(jnp.bfloat16)
        right_back = (product_grad * left_pre).astype(jnp.bfloat16)
        second_part = jnp.einsum(
            "cf,df->cd", left_back, left_full, preferred_element_type=jnp.float32
        ) + jnp.einsum("cf,df->cd", right_back, right_full, preferred_element_type=jnp.float32)
        second_back = lax.psum(second_part, "tp")
        mid_grad = glu_cot.astype(jnp.float32) + inv_second * (
            second_back - unit_second * jnp.mean(second_back * unit_second, axis=-1, keepdims=True)
        )
        attn_cot = mid_grad.astype(jnp.bfloat16)
        gate_mix_grad = jnp.einsum(
            "cd,kd->ck", attn_cot, out_full, preferred_element_type=jnp.float32
        )
        gate_back = (gate_mix_grad * unit_mix).astype(jnp.bfloat16)
        unit_mix_grad = gate_mix_grad * gate_pre
        mix_dot = lax.psum(jnp.sum(unit_mix_grad * unit_mix, axis=-1), "tp")
        heads_grad = (
            (inv_mix * (unit_mix_grad - unit_mix * (mix_dot / D)[:, None]))
            .astype(jnp.bfloat16)
            .reshape(heads_shape)
        )
        pair_grad = jnp.einsum(
            "ihe,jhe->hij", heads_grad, value_rows, preferred_element_type=jnp.float32
        ).astype(jnp.bfloat16)
        score_grad = pair_grad.astype(jnp.float32) * decay
        query_inner = jnp.einsum("hij,jhe->ihe", score_grad, key_wide, precision=HIGHEST_PRECISION)
        key_inner = jnp.einsum("hij,ihe->jhe", score_grad, query_wide, precision=HIGHEST_PRECISION)
        value_inner = jnp.einsum(
            "hij,ihe->jhe", attn_weights, heads_grad, preferred_element_type=jnp.float32
        )
        scaled_grad = heads_grad.astype(jnp.float32) * coef_in[:, :, None]
        query_outer = jnp.einsum("ihf,hef->ihe", scaled_grad, incoming, precision=HIGHEST_PRECISION)
        state_grad = jnp.einsum(
            "ihe,ihf->hef", query_wide, scaled_grad, precision=HIGHEST_PRECISION
        )
        later_grad = state_suffix(factor, state_grad)
        key_state = weight_loc[:, :, None] * jnp.einsum(
            "jhf,hef->jhe", value_wide, later_grad, precision=HIGHEST_PRECISION
        )
        value_state = weight_loc[:, :, None] * jnp.einsum(
            "jhe,hef->jhf", key_wide, later_grad, precision=HIGHEST_PRECISION
        )
        query_back = (
            rotate(query_inner + query_outer, cosine_table, sine_table, -1.0).reshape(row_count, -1)
            * query_slope
        ).astype(jnp.bfloat16)
        key_back = (
            rotate(key_inner + key_state, cosine_table, sine_table, -1.0).reshape(row_count, -1)
            * key_slope
        ).astype(jnp.bfloat16)
        value_back = (value_inner + value_state).reshape(row_count, -1).astype(jnp.bfloat16)
        fresh = (
            jnp.einsum("cd,ck->dk", normed_first, query_back, preferred_element_type=jnp.float32),
            jnp.einsum("cd,ck->dk", normed_first, key_back, preferred_element_type=jnp.float32),
            jnp.einsum("cd,ck->dk", normed_first, value_back, preferred_element_type=jnp.float32),
            jnp.einsum("cd,ck->dk", normed_first, gate_back, preferred_element_type=jnp.float32),
            jnp.einsum("ck,cd->kd", gate_mix, attn_cot, preferred_element_type=jnp.float32),
            jnp.einsum("cd,cf->df", normed_second, left_back, preferred_element_type=jnp.float32),
            jnp.einsum("cd,cf->df", normed_second, right_back, preferred_element_type=jnp.float32),
            jnp.einsum("cf,cd->fd", glu_product, glu_cot, preferred_element_type=jnp.float32),
        )
        if accum is None:
            accum = list(fresh)
        else:
            accum = [older + newer for older, newer in zip(accum, fresh)]
        total = jnp.einsum("ck,dk->cd", query_back, query_full, preferred_element_type=jnp.float32)
        total = total + jnp.einsum(
            "ck,dk->cd", key_back, key_full, preferred_element_type=jnp.float32
        )
        total = total + jnp.einsum(
            "ck,dk->cd", value_back, value_full, preferred_element_type=jnp.float32
        )
        first_back = lax.psum(
            total
            + jnp.einsum("ck,dk->cd", gate_back, gate_full, preferred_element_type=jnp.float32),
            "tp",
        )
        input_back = mid_grad + inv_first * (
            first_back - unit_first * jnp.mean(first_back * unit_first, axis=-1, keepdims=True)
        )
        in_grads.append(input_back)
    summed = (
        lax.psum_scatter(accum[0], "seq", scatter_dimension=0, tiled=True),
        lax.psum_scatter(accum[1], "seq", scatter_dimension=0, tiled=True),
        lax.psum_scatter(accum[2], "seq", scatter_dimension=0, tiled=True),
        lax.psum_scatter(accum[3], "seq", scatter_dimension=0, tiled=True),
        lax.psum_scatter(accum[4], "seq", scatter_dimension=1, tiled=True),
        lax.psum_scatter(accum[5], "seq", scatter_dimension=0, tiled=True),
        lax.psum_scatter(accum[6], "seq", scatter_dimension=0, tiled=True),
        lax.psum_scatter(accum[7], "seq", scatter_dimension=1, tiled=True),
    )
    return (
        jnp.stack(outputs),
        jnp.stack(in_grads),
        summed[0],
        summed[1],
        summed[2],
        summed[3],
        summed[4],
        summed[5],
        summed[6],
        summed[7],
    )


def fused_body(
    hidden_in,
    query_weight,
    key_weight,
    value_weight,
    gate_weight,
    out_weight,
    left_weight,
    right_weight,
    down_weight,
    decay_rate,
    seq_bounds,
    out_cotangent,
):
    row_count = hidden_in.shape[1]
    device = lax.axis_index("seq")
    positions = device * row_count + jnp.arange(row_count, dtype=jnp.int32)
    frequency = jnp.exp(jnp.arange(HEAD // 2, dtype=F32) * (-2.0 * math.log(10000.0) / HEAD))
    angles = positions.astype(F32)[:, None] * jnp.tile(frequency, 2)[None, :]
    sign = jnp.where(jnp.arange(HEAD) < HEAD // 2, -1.0, 1.0).astype(F32)
    cosine, sine = jnp.cos(angles), jnp.sin(angles) * sign[None, :]
    results = forward(
        (query_weight, key_weight, value_weight, gate_weight),
        (out_weight, left_weight.T, right_weight.T, down_weight),
        hidden_in,
        out_cotangent,
        cosine,
        sine,
        decay_rate,
        seq_bounds,
    )
    whole, kept, (incoming, inv_mix, inv_second, rates, output) = results[:2], results[2:17], results[17:]
    tall, output, input_grad = backward(
        down_weight.shape[0],
        whole,
        kept,
        output,
        hidden_in,
        out_cotangent,
        incoming,
        inv_mix,
        inv_second,
        rates,
        cosine,
        sine,
        seq_bounds,
    )[:3]
    (input_grad, output, down_grad, left_grad, right_grad, out_grad,
     query_grad, key_grad, value_grad, gate_grad) = finish(down_weight.shape[0], input_grad, tall, output)
    return (
        output,
        input_grad,
        query_grad,
        key_grad,
        value_grad,
        gate_grad,
        out_grad,
        left_grad.T,
        right_grad.T,
        down_grad,
    )


def solution(mesh):
    fits = mesh.shape["seq"] == SEQ and mesh.shape["tp"] == TP
    return jax.shard_map(
        fused_body if fits else body,
        mesh=mesh,
        in_specs=(
            P(None, "seq", None),
            P("seq", "tp"),
            P("seq", "tp"),
            P("seq", "tp"),
            P("seq", "tp"),
            P("tp", "seq"),
            P("seq", "tp"),
            P("seq", "tp"),
            P("tp", "seq"),
            P("tp"),
            P(),
            P(None, "seq", None),
        ),
        out_specs=(
            P(None, "seq", None),
            P(None, "seq", None),
            P("seq", "tp"),
            P("seq", "tp"),
            P("seq", "tp"),
            P("seq", "tp"),
            P("tp", "seq"),
            P("seq", "tp"),
            P("seq", "tp"),
            P("tp", "seq"),
        ),
        check_vma=False,
    )
```

```python
import functools
import math

import jax
import jax.numpy as jnp
from jax import lax
from jax.experimental import pallas as pl
from jax.experimental.pallas import tpu as pltpu
from jax.sharding import PartitionSpec as P

D = 1024
HEAD = 128


EPSILON = 1e-06
HIGHEST_PRECISION = lax.Precision.HIGHEST
MESH = pl.DeviceIdType.MESH
BF16 = jnp.bfloat16
F32 = jnp.float32

SEQ = 8
TP = 4
STRIPE = 128
PAIR = 2 * HEAD
BLOCK = 32
NARROW = 128
WEIGH = 64

NN = ((1,), (0,))
NT = ((1,), (1,))
TN = ((0,), (0,))


def dots(left, right, dims):
    return lax.dot_general(left, right, (dims, ((), ())), preferred_element_type=F32)


def place():
    s, t = lax.axis_index("seq"), lax.axis_index("tp")
    core = s % 2
    column = (s // 2) % 2
    line = s // 4
    other = s + 1 - 2 * core
    across_x = s + 2 * (1 - 2 * column)
    across_y = s + 4 * (1 - 2 * line)
    first = across_x + core * (across_y - across_x)
    second = across_y + core * (across_x - across_y)
    diagonal = across_x + across_y - s
    return s, t, other, first, second, diagonal


def nearest(t, step):
    flip = t // 2
    low = t + flip * (3 - 2 * t)
    swap = low * (1 - step // 2)
    index = step + swap * (1 - 2 * step)
    return index + flip * (3 - 2 * index)


def stripe(index):
    return pl.ds(pl.multiple_of((index % 2 * (SEQ // 2) + index // 2) * STRIPE, STRIPE), STRIPE)


def plain(index):
    return slice(index * STRIPE, index * STRIPE + STRIPE)


def place_of(index):
    at = (index % 2 * (SEQ // 2) + index // 2) * STRIPE
    return slice(at, at + STRIPE)


def rows_of(index, size):
    return pl.ds(pl.multiple_of(index * size, size), size)


def remote(src, dst, send, receive, device):
    return pltpu.make_async_remote_copy(
        src_ref=src, dst_ref=dst, send_sem=send, recv_sem=receive, device_id=device, device_id_type=MESH
    )


def greet(s, t, around):
    barrier = pltpu.get_barrier_semaphore()
    for step in range(1, TP):
        pl.semaphore_signal(barrier, inc=1, device_id=(s, (t + step) % TP), device_id_type=MESH)
    for device in around:
        pl.semaphore_signal(barrier, inc=1, device_id=(device, t), device_id_type=MESH)
    pl.semaphore_wait(barrier, TP - 1 + len(around))


def every_rows(count, body, size=BLOCK):
    @pl.loop(0, count // size)
    def _(block):
        body(pl.ds(pl.multiple_of(block * size, size), size), block * size)


def flag(condition):
    return jnp.where(condition, 1.0, 0.0).astype(F32)


def rotated(values, cosine, sine):
    return values * cosine + pltpu.roll(values, HEAD // 2, 1) * sine


def state_exchange(rows, boundary, refs, rates, scale, toward, source_of):
    state, pair_land, chip_state, chip_land, partial, result, pair_sem, chip_send, chip_recv, partial_sem = refs
    s, t, other, first, second, diagonal = place()
    core, half = s % 2, TP
    around = (first, second, diagonal)
    ours, theirs = pl.ds(core * half, half), pl.ds((1 - core) * half, half)

    def pair_copy():
        return remote(state.at[theirs], pair_land, pair_sem.at[0], pair_sem.at[1], (other, t))

    def chip_copy(part):
        return remote(chip_state, chip_land.at[part], chip_send.at[part], chip_recv.at[part], (around[part], t))

    def partial_copy():
        return remote(partial, result.at[ours], partial_sem.at[0], partial_sem.at[1], (other, t))

    def rate_of(number):
        head = core * half + number
        return rates[head // 2, pl.ds(head % 2, 1), :]

    def begin():
        pair_copy().start()

    def add_pair():
        pair_copy().wait_recv()

        @pl.loop(0, half)
        def _(number):
            rate, target = rate_of(number), toward(s // 2)
            total = scale(target, s, rate) * state[core * half + number].astype(F32)
            total += scale(target, other, rate) * pair_land[number].astype(F32)
            chip_state[number] = total.astype(BF16)

        for part in range(3):
            chip_copy(part).start()

    def add_chips():
        for part in range(3):
            chip_copy(part).wait_recv()

        @pl.loop(0, half)
        def _(number):
            rate = rate_of(number)
            mine, its = state[core * half + number].astype(F32), pair_land[number].astype(F32)
            here = scale(s, s, rate) * mine + scale(s, other, rate) * its
            there = scale(other, s, rate) * mine + scale(other, other, rate) * its
            for part in range(3):
                values = chip_land[part, number].astype(F32)
                source = source_of(around[part] // 2)
                here += scale(s, source, rate) * values
                there += scale(other, source, rate) * values
            result[core * half + number] = here.astype(BF16)
            partial[number] = there.astype(BF16)

        partial_copy().start()

    def finish():
        partial_copy().wait_recv()

    def close():
        pair_copy().wait_send()
        for part in range(3):
            chip_copy(part).wait_send()
        partial_copy().wait_send()

    return begin, add_pair, add_chips, finish, close


def state_scratch():
    dma = pltpu.SemaphoreType.DMA
    return [
        pltpu.VMEM((2 * TP, HEAD, HEAD), BF16),
        pltpu.VMEM((TP, HEAD, HEAD), BF16),
        pltpu.VMEM((TP, HEAD, HEAD), BF16),
        pltpu.VMEM((3, TP, HEAD, HEAD), BF16),
        pltpu.VMEM((TP, HEAD, HEAD), BF16),
        pltpu.VMEM((2 * TP, HEAD, HEAD), BF16),
        dma((2,)),
        dma((3,)),
        dma((3,)),
        dma((2,)),
    ]


LAG_B, LAG_C = 2, 4

def forward_kernel(rows, sizes, *refs):
    heads_in, refs = refs[:4], refs[4:]
    shards, refs = refs[:4], refs[4:]
    (hidden_in, cot_in, cosine, sine, rate_in, bounds), refs = refs[:6], refs[6:]
    whole_out, refs = refs[:2], refs[2:]
    (acts_out, pack_out, normed_out, second_out, glu_out, left_out, right_out, glu_other, left_other, right_other,
     gated_other, normed_other, second_other, cot_other, back_out,
     incoming_out, inv_mix_out, inv_second_out, rate_out, result_out), refs = refs[:20], refs[20:]
    whole, refs = refs[:5], refs[5:]
    (acts, pack, normed, hidden, cot, second_normed, sides, back, wide, mixed, distance, scores, weights,
     inv_mix, inv_second, rates, heads_shard), refs = refs[:17], refs[17:]
    exchange, refs = refs[:10], refs[10:]
    state, incoming = exchange[0], exchange[5]
    shards = (heads_shard, *shards)
    (local_sem, up_sem, down_sem, line_sem, down_send, down_recv, send_sem, first_sem, second_sem, other_sem, rate_send, rate_recv,
     copy_sem, side_sem, side_send, side_recv, half_send, half_recv,
     hidden_sem, cot_sem) = refs
    s, t, other, first, second, diagonal = place()
    units, beside = sizes[2], wide.shape[1] // 3
    theirs = rows_of(1 - s % 2, D // 2)
    shift = other - s
    for kind in range(4):
        heads_shard[kind * PAIR : kind * PAIR + PAIR, :] = heads_in[kind][...].T
    greet(s, t, (other, first, second, diagonal))

    def hidden_load(index):
        return pltpu.make_async_copy(
            hidden_in.at[t, :, plain(index)], hidden.at[:, place_of(index)], hidden_sem.at[index]
        )

    def cot_load(index):
        return pltpu.make_async_copy(cot_in.at[t, :, plain(index)], cot.at[:, place_of(index)], cot_sem.at[index])

    def half_copy(part):
        src, dst = (
            (normed.at[:, theirs], normed_other),
            (second_normed.at[:, theirs], second_other),
            (cot.at[:, theirs], cot_other),
            (pack.at[:, :, 2 * PAIR : 3 * PAIR], gated_other),
        )[part]
        return remote(src, dst, half_send.at[part], half_recv.at[part], (other, t))

    for index in range(SEQ):
        hidden_load(index).start()

    cut = -(-units // (2 * HEAD)) * HEAD
    items = (
        [(0, 0), (4, 0)]
        + [(0, step) for step in range(1, TP)]
        + [(1, step) for step in range(TP)]
        + [(w, step) for step in range(TP) for w in (2, 3)]
    )
    items = [(w, step, 0, sizes[w]) for w, step in items]
    items[-1:] = [(3, TP - 1, 0, cut), (3, TP - 1, cut, units)]
    columns = (s, first, second, diagonal)

    def spot(w, owner, column, low=0, high=None):
        high = sizes[w] if high is None else high
        return whole[w].at[pl.ds(pl.multiple_of(owner * sizes[w] + low, 16), high - low), stripe(column)]

    def source(w, step, owner, low=0, high=None):
        if step:
            return spot(w, owner, s, low, high)
        return shards[w].at[pl.ds(low, (sizes[w] if high is None else high) - low), :]

    def own_copy(w):
        return pltpu.make_async_copy(shards[w], spot(w, t, s), local_sem.at[w])

    def plane_copies(index):
        w, step, low, high = items[index]
        owner = nearest(t, step)
        src, dst = source(w, step, owner, low, high), spot(w, owner, s, low, high)
        return (
            remote(src, dst, send_sem.at[index, 0], first_sem.at[index], (first, t)),
            remote(src, dst, send_sem.at[index, 1], second_sem.at[index, 0], (second, t)),
            remote(src, dst, send_sem.at[index, 2], other_sem.at[index, 0], (other, t)),
        )

    def found(index, column):
        w, step, low, high = items[index]
        return spot(w, nearest(t, step), column, low, high)

    def relay_copies(index):
        src = found(index, first)
        return (
            remote(src, src, send_sem.at[index, 3], second_sem.at[index, 1], (second, t)),
            remote(src, src, send_sem.at[index, 4], other_sem.at[index, 1], (other, t)),
        )

    def last_copies(index):
        near, far = found(index, second), found(index, diagonal)
        return (
            remote(near, near, send_sem.at[index, 5], other_sem.at[index, 2], (other, t)),
            remote(far, far, send_sem.at[index, 6], other_sem.at[index, 3], (other, t)),
        )

    def parcel(w, step, column, up):
        owner = nearest(t, step)
        dst = spot(w, owner, columns[column])
        src = shards[w] if step == 0 and column == 0 else dst
        sem, device = (up_sem, t + 1) if up else (down_sem, t - 1)
        return remote(src, dst, sem.at[w, owner, column], line_sem.at[w, owner, column], (s, device))

    def across(step, column):
        block = spot(4, nearest(t, step), columns[column])
        return remote(block, block, down_send.at[step, column], down_recv.at[step, column], (other, t))

    def goes(step, up):
        owner = nearest(t, step)
        if step == 0:
            return t < TP - 1 if up else t > 0
        return (owner < t) & (t < TP - 1) if up else (owner > t) & (t > 0)

    def set_out(w, column=0):
        for up in (True, False):

            @pl.when(goes(0, up))
            def _(up=up):
                parcel(w, 0, column, up).start()

    inside = (t > 0) & (t < TP - 1)

    def pass_on(w, step, column=0, where=None):
        def act():
            parcel(w, step, column, True).wait_recv()
            for up in (True, False):

                @pl.when(goes(step, up))
                def _(up=up):
                    parcel(w, step, column, up).start()

            if w == 4:
                across(step, column).start()

        if where is None:
            act()
        else:
            pl.when(where)(act)

    down_parcels = [(step, column) for step in range(1, TP) for column in range(4)]

    def line_pass(now, where):
        if now + 2 < len(items):
            w, step, low, high = items[now + 2]
            if step and low == 0:
                pass_on(w, step, 0, where)

    def down_pass(now):
        for at, where in ((now - 6, inside), (now - 8, jnp.logical_not(inside))):
            if 0 <= at < len(down_parcels):
                pass_on(4, *down_parcels[at], where)

    relayed, ended = [], []

    def stage_a(index):
        if items[index][1] == 0:
            own_copy(items[index][0]).start()
        for copy in plane_copies(index):
            copy.start()

    def stage_b(until):
        while len(relayed) <= min(until, len(items) - 1):
            index = len(relayed)
            relayed.append(index)
            block = found(index, first)
            remote(block, block, send_sem.at[index, 0], first_sem.at[index], (first, t)).wait_recv()
            for copy in relay_copies(index):
                copy.start()

    def stage_c(until):
        while len(ended) <= min(until, len(items) - 1):
            index = len(ended)
            ended.append(index)
            for part, column in enumerate((second, diagonal)):
                block = found(index, column)
                remote(block, block, send_sem.at[index, 1], second_sem.at[index, part], (second, t)).wait_recv()
            for copy in last_copies(index):
                copy.start()

    def tick(now):
        stage_b(now - LAG_B)
        if now < len(items):
            stage_a(now)
        stage_c(now - LAG_C)
        if now == 5:
            set_out(2)
            set_out(3)
            line_pass(now - 1, None)
            line_pass(now, inside)
        line_pass(now + 1, inside)
        line_pass(now, jnp.logical_not(inside))
        down_pass(now)

    keeps = []

    def keep(src, dst):
        copy = functools.partial(pltpu.make_async_copy, src, dst, copy_sem.at[len(keeps)])
        copy().start()
        keeps.append(copy)

    def ready(index):
        w, step, low, high = items[index]
        owner = nearest(t, step)
        if step == 0:
            own_copy(w).wait()
        for part, column in enumerate((other, second + shift, first + shift, diagonal + shift)):
            block = found(index, column)
            remote(block, block, send_sem.at[index, 2], other_sem.at[index, part], (other, t)).wait_recv()
        block = rows_of(owner, sizes[w])
        if w < 2:
            keep(whole[w].at[block, :], whole_out[w].at[block, :])
        return owner, block

    def down_ready(step):
        if step == 0:
            ready(1)
            return
        for column, index in enumerate((other, second + shift, first + shift, diagonal + shift)):
            block = spot(4, nearest(t, step), index)
            remote(block, block, down_send.at[step, column], down_recv.at[step, column], (other, t)).wait_recv()

    def rate_copy(step):
        return remote(rates.at[t], rates.at[t], rate_send.at[step - 1], rate_recv.at[step - 1], (s, (t + step) % TP))

    row = lax.broadcasted_iota(jnp.int32, (8, HEAD), 0)
    rates[t] = jnp.where(row == 0, rate_in[0], rate_in[1])
    for step in range(1, TP):
        rate_copy(step).start()
    stage_a(0)
    set_out(0)
    set_out(1)
    set_out(4)
    stage_a(1)
    boundary = bounds[t]
    edge = boundary - s * rows

    for index in range(SEQ):
        hidden_load(index).wait()
        cot_load(index).start()

    def prepare(part, start):
        values = hidden[part, :].astype(F32)
        scale = lax.rsqrt(jnp.mean(values * values, axis=-1, keepdims=True) + EPSILON)
        normed[part, :] = (values * scale).astype(BF16)
        row = lax.broadcasted_iota(jnp.int32, (BLOCK, rows), 0) + start
        column = lax.broadcasted_iota(jnp.int32, (BLOCK, rows), 1)
        apart = (column > row) | ((row >= edge) & (column < edge))
        distance[part, :] = jnp.where(apart, -1, row - column).astype(F32)

    every_rows(rows, prepare)
    keep(normed, normed_out)
    half_copy(0).start()
    for step in range(1, TP):
        here = rates.at[t]
        remote(here, here, rate_send.at[step - 1], rate_recv.at[step - 1], (s, t)).wait_recv()
    keep(rates, rate_out)

    before = jnp.where(s * rows - 1 >= boundary, 1, 0)
    last = jnp.where(s * rows + rows - 1 >= boundary, 1, 0)

    def rate_of(block, half):
        return rates[block, half : half + 1, :]

    def row_numbers(start, count):
        return lax.broadcasted_iota(jnp.int32, (count, HEAD), 0) + start

    def project(step, index):
        owner, block = ready(index)
        wide[:, 0:D] = dots(normed[...], whole[0][block, :], NT)

        def shape_rows(part, start):
            turn, lean = cosine[part, :], sine[part, :]
            for kind in range(2):
                for half in range(2):
                    at = kind * PAIR + half * HEAD
                    values = wide[part, at : at + HEAD]
                    logistic = 1.0 / (1.0 + jnp.exp(-values))
                    acts[owner, part, at : at + HEAD] = rotated(values * logistic, turn, lean).astype(BF16)
                    pack[owner, part, at : at + HEAD] = (
                        logistic * (1.0 + values * (1.0 - logistic))
                    ).astype(BF16)
            acts[owner, part, 2 * PAIR : 4 * PAIR] = wide[part, 2 * PAIR : 4 * PAIR].astype(BF16)
            number = row_numbers(start, WEIGH)
            valid = jnp.where(jnp.where(number >= edge, 1, 0) == last, 1.0, 0.0)
            for half in range(2):
                fade = jnp.exp(-rate_of(owner, half) * (rows - 1 - number).astype(F32)) * valid
                keys = acts[owner, part, PAIR + half * HEAD : PAIR + half * HEAD + HEAD].astype(F32)
                weights[part, half * HEAD : half * HEAD + HEAD] = (keys * fade).astype(BF16)

        every_rows(rows, shape_rows, WEIGH)
        for half in range(2):
            at = half * HEAD
            state[owner * 2 + half] = dots(
                weights[:, at : at + HEAD], acts[owner, :, 2 * PAIR + at : 2 * PAIR + at + HEAD], TN
            ).astype(BF16)

    def attend(step):
        owner = nearest(t, step)
        for half in range(2):
            at = half * HEAD
            rate = rates[owner, half : half + 1, :]
            for top in range(0, rows, PAIR):
                width = top + PAIR
                scores[0:PAIR, 0:width] = dots(
                    acts[owner, top : top + PAIR, at : at + HEAD], acts[owner, 0:width, PAIR + at : PAIR + at + HEAD], NT
                )

                def weigh(part, start, width=width, top=top, rate=rate):
                    for left in range(0, width, HEAD):
                        apart = distance[pl.ds(pl.multiple_of(start + top, WEIGH), WEIGH), left : left + HEAD]
                        fade = jnp.where(apart >= 0.0, jnp.exp(-rate * apart), 0.0)
                        weights[part, left : left + HEAD] = (scores[part, left : left + HEAD] * fade).astype(BF16)

                every_rows(PAIR, weigh, WEIGH)
                column = pl.ds(pl.multiple_of(owner * PAIR + at, HEAD), HEAD)
                mixed[top : top + PAIR, column] = dots(
                    weights[0:PAIR, 0:width], acts[owner, 0:width, 2 * PAIR + at : 2 * PAIR + at + HEAD], NN
                )

    def prefix_scale(block, source_block, rate):
        same = jnp.where((source_block + 1) * rows - 1 >= boundary, 1, 0) == jnp.where(block * rows - 1 >= boundary, 1, 0)
        usable = flag(source_block < block) * flag(same)
        gap = jnp.maximum(block - 1 - source_block, 0).astype(F32)
        return jnp.exp(-rate * (rows * gap)) * usable

    begin_states, add_pair, add_chips, finish_states, close_states = state_exchange(
        rows, boundary, exchange, rates, prefix_scale, lambda chip: 2 * chip + 2, lambda chip: 2 * chip + 1
    )

    def mix():
        finish_states()
        keep(incoming, incoming_out)
        for block in range(TP):
            for half in range(2):
                at = half * HEAD
                scores[:, at : at + HEAD] = dots(acts[block, :, at : at + HEAD], incoming[2 * block + half], NN)

            def add_outer(part, start, block=block):
                number = row_numbers(start, NARROW)
                valid = jnp.where(jnp.where(number >= edge, 1, 0) == before, 1.0, 0.0)
                for half in range(2):
                    fade = jnp.exp(-rate_of(block, half) * (number + 1).astype(F32)) * valid
                    column = slice(block * PAIR + half * HEAD, block * PAIR + half * HEAD + HEAD)
                    mixed[part, column] += fade * scores[part, half * HEAD : half * HEAD + HEAD]

            every_rows(rows, add_outer, NARROW)

        def gate_rows(part, start):
            values = mixed[part, :]
            scale = lax.rsqrt(jnp.mean(values * values, axis=-1, keepdims=True) + EPSILON)
            inv_mix[part, :] = jnp.broadcast_to(scale, (BLOCK, HEAD))
            values = values * scale
            for block in range(TP):
                column = slice(block * PAIR, block * PAIR + PAIR)
                gate = acts[block, part, 3 * PAIR : 4 * PAIR].astype(F32)
                pack[block, part, 2 * PAIR : 3 * PAIR] = (values[:, column] * gate).astype(BF16)
                pack[block, part, 3 * PAIR : 4 * PAIR] = values[:, column].astype(BF16)

        every_rows(rows, gate_rows, BLOCK)
        keep(acts, acts_out)
        keep(pack, pack_out)
        half_copy(3).start()
        keep(inv_mix, inv_mix_out)

    def project_out():
        for block in range(TP):
            term = dots(pack[block, :, 2 * PAIR : 3 * PAIR], whole[1][block * PAIR : block * PAIR + PAIR, :], NN)
            if block:
                wide[:, 0:D] += term
            else:
                wide[:, 0:D] = term

        def norm_rows(part, start):
            values = hidden[part, :].astype(F32) + wide[part, 0:D]
            mixed[part, :] = values
            scale = lax.rsqrt(jnp.mean(values * values, axis=-1, keepdims=True) + EPSILON)
            inv_second[part, :] = jnp.broadcast_to(scale, (BLOCK, HEAD))
            second_normed[part, :] = (values * scale).astype(BF16)

        every_rows(rows, norm_rows)
        keep(second_normed, second_out)
        half_copy(1).start()
        keep(inv_second, inv_second_out)

    def left_side(index):
        owner, block = ready(index)
        down_ready(items[index][1])
        wide[:, 0:units] = dots(second_normed[...], whole[2][block, :], NT)
        wide[:, 2 * beside : 2 * beside + units] = dots(cot[...], whole[4][block, :], NT)

    def side_copies(slot, owner):
        return [
            pltpu.make_async_copy(sides.at[slot, part], out.at[owner], side_sem.at[slot, part])
            for part, out in enumerate((glu_out, left_out, right_out))
        ]

    def side_remotes(slot, step):
        owner = nearest(t, step)
        return [
            remote(sides.at[slot, part], out.at[owner], side_send.at[slot, part], side_recv.at[step, part], (other, t))
            for part, out in enumerate((glu_other, left_other, right_other))
        ]

    def right_side(index):
        owner, block = ready(index)
        w, step, low, high = items[index]
        part_rows = pl.ds(pl.multiple_of(owner * units + low, 16), high - low)
        wide[:, beside + low : beside + high] = dots(second_normed[...], whole[3][part_rows, :], NT)
        slot = step % 2
        if step >= 2 and low == 0:
            for copy in side_copies(slot, nearest(t, step - 2)):
                copy.wait()
            for copy in side_remotes(slot, step - 2):
                copy.wait_send()

        def multiply(part, start):
            left, right = wide[part, low:high], wide[part, beside + low : beside + high]
            grad = wide[part, 2 * beside + low : 2 * beside + high]
            sides[slot, 0, part, low:high] = (left * right).astype(BF16)
            sides[slot, 1, part, low:high] = (grad * right).astype(BF16)
            sides[slot, 2, part, low:high] = (grad * left).astype(BF16)

        every_rows(rows, multiply)
        if high == units:
            for copy in side_copies(slot, owner) + side_remotes(slot, step):
                copy.start()
        mixed[...] += dots(sides[slot, 0, :, low:high], whole[4][part_rows, :], NN)
        term = dots(sides[slot, 1, :, low:high], whole[2][part_rows, :], NN) + dots(
            sides[slot, 2, :, low:high], whole[3][part_rows, :], NN
        )
        if step:
            back[...] += term
        else:
            back[...] = term

    stage_b(0)
    pass_on(0, 1)
    stage_a(2)
    stage_b(1)
    set_out(4, 1)
    stage_c(0)
    pass_on(0, 2)
    stage_a(3)
    stage_b(2)
    stage_c(1)
    set_out(4, 2)
    set_out(4, 3)
    pass_on(0, 3)
    stage_a(4)
    project(0, 0)
    tick(5)
    for step in range(1, TP):
        tick(5 + step)
        project(step, 1 + step)
    begin_states()
    for index in range(SEQ):
        cot_load(index).wait()
    half_copy(2).start()
    tick(9)
    add_pair()
    attend(0)
    tick(10)
    attend(1)
    tick(11)
    attend(2)
    attend(3)
    add_chips()
    tick(12)
    for index in range(5, 5 + TP):
        ready(index)
    mix()
    tick(13)
    project_out()
    for index in range(5 + TP, len(items)):
        if index > 5 + TP:
            tick(index + LAG_C)
        (left_side, right_side)[items[index][0] - 2](index)

    def finish(part, start):
        for index in range(SEQ):
            result_out[part, plain(index)] = mixed[part, place_of(index)].astype(BF16)

    keep(back, back_out)
    every_rows(rows, finish)

    for step in range(1, TP):
        rate_copy(step).wait_send()
    close_states()
    for copy in keeps:
        copy().wait()
    for part in range(4):
        half_copy(part).wait()
    for step in range(TP):
        for copy in side_remotes(step % 2, step):
            copy.wait_recv()
            if step >= 2:
                copy.wait_send()
        if step >= 2:
            for copy in side_copies(step % 2, nearest(t, step)):
                copy.wait()
    for index in range(len(items)):
        for copy in plane_copies(index) + relay_copies(index) + last_copies(index):
            copy.wait_send()
    for w in range(5):
        for step in range(TP):
            for column in range(4 if w == 4 else 1):
                for up in (True, False):

                    @pl.when(goes(step, up))
                    def _(w=w, step=step, column=column, up=up):
                        parcel(w, step, column, up).wait_send()

                if w == 4 and step:
                    across(step, column).wait_send()


KEPT = 20


def forward(heads_in, shards, hidden, cot, cosine, sine, rate, bounds):
    rows = hidden.shape[1]
    sizes = (4 * PAIR, *(shard.shape[0] for shard in shards))
    units = sizes[2]
    beside = -(-units // HEAD) * HEAD
    items = 4 * TP + 2
    dma = pltpu.SemaphoreType.DMA
    vmem = pl.BlockSpec(memory_space=pltpu.VMEM)
    anywhere = pl.BlockSpec(memory_space=pl.ANY)
    heads = 2 * TP
    shape = jax.ShapeDtypeStruct
    outs = [
        *[shape((TP * size, D), BF16) for size in sizes[:2]],
        *[shape((TP, rows, 4 * PAIR), BF16)] * 2,
        *[shape((rows, D), BF16)] * 2,
        *[shape((TP, rows, units), BF16)] * 6,
        shape((TP, rows, PAIR), BF16),
        *[shape((rows, D // 2), BF16)] * 3,
        shape((rows, D), F32),
        shape((heads, HEAD, HEAD), BF16),
        shape((rows, HEAD), F32),
        shape((rows, HEAD), F32),
        shape((TP, 8, HEAD), F32),
        shape((rows, D), BF16),
    ]
    return pl.pallas_call(
        functools.partial(forward_kernel, rows, sizes),
        out_shape=outs,
        in_specs=[vmem] * 4 + [anywhere] * 6 + [vmem] * 2 + [pl.BlockSpec(memory_space=pltpu.SMEM)] * 2,
        out_specs=[anywhere] * (len(outs) - 1) + [vmem],
        scratch_shapes=[pltpu.VMEM((TP * size, D), BF16) for size in sizes]
        + [
            *[pltpu.VMEM((TP, rows, 4 * PAIR), BF16)] * 2,
            *[pltpu.VMEM((rows, D), BF16)] * 4,
            pltpu.VMEM((2, 3, rows, units), BF16),
            pltpu.VMEM((rows, D), F32),
            pltpu.VMEM((rows, 3 * beside), F32),
            pltpu.VMEM((rows, D), F32),
            pltpu.VMEM((rows, rows), F32),
            pltpu.VMEM((rows, rows), F32),
            pltpu.VMEM((rows, rows), BF16),
            pltpu.VMEM((rows, HEAD), F32),
            pltpu.VMEM((rows, HEAD), F32),
            pltpu.VMEM((TP, 8, HEAD), F32),
            pltpu.VMEM((4 * PAIR, STRIPE), BF16),
            *state_scratch(),
            dma((5,)),
            dma((5, TP, 4)),
            dma((5, TP, 4)),
            dma((5, TP, 4)),
            dma((TP, 4)),
            dma((TP, 4)),
            dma((items, 7)),
            dma((items,)),
            dma((items, 2)),
            dma((items, 4)),
            dma((TP - 1,)),
            dma((TP - 1,)),
            dma((KEPT,)),
            dma((2, 3)),
            dma((2, 3)),
            dma((TP, 3)),
            dma((4,)),
            dma((4,)),
            dma((SEQ,)),
            dma((SEQ,)),
        ],
        compiler_params=pltpu.CompilerParams(
            collective_id=0, has_side_effects=True, vmem_limit_bytes=63 * 2**20
        ),
        name="forward",
    )(*heads_in, *shards, hidden, cot, cosine, sine, rate, bounds)


PIECES = 4
HELD = 6
LAG_2, LAG_3, LAG_4, HOP, LAG_5 = 2, 4, 6, 2, 13
KINDS = 6
BEFORE, EARLY, WAIT_1, WAIT_2 = 10, 2, 3, 9
ITEMS = KINDS * TP


def add_rows(target, *terms):
    rows = target.shape[0]

    step = rows // 4

    @pl.loop(0, 4)
    def _(block):
        part = pl.ds(pl.multiple_of(block * step, 16), step)
        total = terms[0][part, :].astype(F32)
        for term in terms[1:]:
            total = total + term[part, :].astype(F32)
        target[part, :] = total.astype(target.dtype)


def backward_kernel(rows, sizes, *refs):
    whole, refs = refs[:2], refs[2:]
    (acts_in, pack_in, normed_in, second_in, glu_own, left_own, right_own, glu_other, left_other, right_other,
     gated_other, normed_other, second_other, cot_other, back_in, output_in, hidden_in, cot_in,
     incoming, inv_mix, inv_second, rates, cosine, sine, bounds), refs = refs[:25], refs[25:]
    (tall, output_whole, input_whole, backs_own, backs_other), refs = refs[:5], refs[5:]
    (tiles, cot, second_normed, normed, attn_cot, halves, acts, pack, backs, mid, wide, distance, scores,
     weights, slopes, faded, lhs, held), refs = refs[:18], refs[18:]
    exchange, refs = refs[:10], refs[10:]
    state, later = exchange[0], exchange[5]
    lands, refs = refs[:9], refs[9:]
    (tile_sem, half_sem, half_load_sem, backs_keep, backs_send, backs_recv, load_sem, cot_sem, hidden_sem, lhs_sem, second_send, second_recv,
     first_send, first_recv, line_send, below_recv, above_recv, share_local, share_up, share_down, share_recv) = refs
    s, t, other, first, second, diagonal = place()
    core = s % 2
    units = sizes[2]
    half_d = D // 2
    ours, theirs = rows_of(core, half_d), rows_of(1 - core, half_d)
    boundary = bounds[t]
    edge = boundary - s * rows
    before = jnp.where(s * rows - 1 >= boundary, 1, 0)
    last = jnp.where(s * rows + rows - 1 >= boundary, 1, 0)
    around = (first, second, diagonal)
    order = [3, 2, 1, 0]
    local = pltpu.make_async_copy

    done = set()

    def once(key, wait):
        if key not in done:
            done.add(key)
            wait()

    greet(s, t, (other, first, second, diagonal))

    def cot_load(index):
        return local(cot_in.at[t, :, plain(index)], cot.at[:, place_of(index)], cot_sem.at[index])

    def hidden_load(index):
        return local(hidden_in.at[t, :, plain(index)], acts.at[0, :, place_of(index)], hidden_sem.at[index])

    def second_load():
        return local(second_in, second_normed, load_sem.at[0])

    def normed_load():
        return local(normed_in, normed, load_sem.at[1])

    def acts_load():
        return local(acts_in, acts, load_sem.at[2])

    def pack_load():
        return local(pack_in, pack, load_sem.at[3])

    def back_load():
        return local(back_in, mid, load_sem.at[4])

    def half_load(part):
        return local((cot_other, second_other, normed_other)[part], halves.at[part], half_load_sem.at[part])

    def half_copy():
        return remote(attn_cot.at[:, theirs], halves.at[3], half_sem.at[0], half_sem.at[1], (other, t))

    tile_list = [(1, part) for part in range(2)] + [(0, part) for part in range(2 * TP)]

    def tile_load(index):
        w, at = tile_list[index]
        return local(whole[w].at[pl.ds(at * half_d, half_d), :], tiles.at[index % 3], tile_sem.at[index % 3])

    def tile(index):
        tile_load(index).wait()
        return tiles[index % 3]

    def tile_next(index):
        if index + 3 < len(tile_list):
            tile_load(index + 3).start()

    def backs_keep_copy(block):
        return local(backs.at[block], backs_own.at[block], backs_keep.at[block])

    def backs_copy(block):
        return remote(backs.at[block], backs_other.at[block], backs_send.at[block], backs_recv.at[block], (other, t))

    piece_rows = rows // PIECES
    shares = ((output_in, output_whole), (acts.at[1], input_whole))

    def piece(a, owner, p):
        return shares[a][1].at[owner, pl.ds(p * piece_rows, piece_rows), :]

    def own_piece(a, p):
        return shares[a][0].at[pl.ds(p * piece_rows, piece_rows), :]

    def share_copy(a, p, owner, src, up):
        sem, target = (share_up, t + 1) if up else (share_down, t - 1)
        return remote(src, piece(a, owner, p), sem.at[a, p, owner], share_recv.at[a, p, owner], (s, target))

    def share_keep(a, p):
        return local(own_piece(a, p), piece(a, t, p), share_local.at[a, p])

    def share_start(a, p):
        @pl.when(t < TP - 1)
        def _():
            share_copy(a, p, t, own_piece(a, p), True).start()

        @pl.when(t > 0)
        def _():
            share_copy(a, p, t, own_piece(a, p), False).start()

        if a:
            share_keep(a, p).start()

    relays = [
        (a, p, step) for a in range(2) for steps in ((1, 2), (3,)) for p in range(PIECES) for step in steps
    ]
    relayed = []

    def passes(owner, up):
        return (owner < t) & (t < TP - 1) if up else (owner > t) & (t > 0)

    def relay(limit, until=len(relays)):
        for _ in range(limit):
            if len(relayed) >= until:
                return
            a, p, step = relays[len(relayed)]
            relayed.append(1)
            owner = nearest(t, step)
            for up in (True, False):

                @pl.when(passes(owner, up))
                def _(up=up):
                    share_copy(a, p, owner, piece(a, owner, p), up).wait_recv()
                    share_copy(a, p, owner, piece(a, owner, p), up).start()

    items = (
        [(0, step) for step in order]
        + [(kind, step) for step in order for kind in (1, 2)]
        + [(3, step) for step in order]
        + [(kind, step) for step in order for kind in (4, 5)]
    )
    heights = (units, units, units, sizes[1], half_d, half_d)

    def lands_of(index):
        kind, step = items[index]
        owner = nearest(t, step)
        group, base, extra = ((0, kind * TP, 3 * TP + kind), (1, 0, TP), (2, (kind - 4) * TP, 2 * TP + kind - 4))[
            0 if kind < 3 else 1 if kind == 3 else 2
        ]
        return owner, lands[3 * group : 3 * group + 3], base + owner, extra

    def own_source(kind, owner):
        if kind == 0:
            return glu_own.at[owner], glu_other.at[owner]
        if kind == 1:
            return left_own.at[owner], left_other.at[owner]
        if kind == 2:
            return right_own.at[owner], right_other.at[owner]
        if kind == 3:
            return pack_in.at[owner, :, 2 * PAIR : 3 * PAIR], gated_other.at[owner]
        part = slice((kind - 4) * half_d, (kind - 3) * half_d)
        return backs_own.at[owner, :, part], backs_other.at[owner, :, part]

    def lhs_loads(index):
        kind, step = items[index]
        slot = index % 2
        return [
            local(src, lhs.at[slot, part, :, pl.ds(0, heights[kind])], lhs_sem.at[slot, part])
            for part, src in enumerate(own_source(kind, nearest(t, step)))
        ]

    def prefetch(index):
        kind, step = items[index]
        owner = nearest(t, step)
        if kind >= 4:
            once(("backs", step), lambda: backs_keep_copy(owner).wait())
            once(("backs_other", step), lambda: backs_copy(owner).wait_recv())
        for copy in lhs_loads(index):
            copy.start()

    def to_second(index):
        kind = items[index][0]
        owner, (second_land, first_land, line_land), at, extra = lands_of(index)
        return [
            remote(
                held.at[index % HELD, column // 2, pl.ds(0, heights[kind]), :],
                second_land.at[at, part],
                second_send.at[index, part],
                second_recv.at[index, part],
                (second, t),
            )
            for part, column in enumerate((diagonal, second))
        ]

    def to_first(index):
        owner, (second_land, first_land, line_land), at, extra = lands_of(index)
        return remote(second_land.at[at, 0], first_land.at[at], first_send.at[index], first_recv.at[index], (first, t))

    def along(index, up):
        kind = items[index][0]
        owner, (second_land, first_land, line_land), at, extra = lands_of(index)
        if up:
            return remote(
                first_land.at[at], line_land.at[at], line_send.at[index], below_recv.at[kind, owner], (s, t + 1)
            )
        final = jnp.where(owner == t - 1, 1, 0)
        return remote(
            first_land.at[at],
            line_land.at[at + final * (extra - at)],
            line_send.at[index],
            above_recv.at[kind, owner],
            (s, t - 1),
        )

    def held_rows(index, chip):
        return held.at[index % HELD, chip, pl.ds(0, heights[items[index][0]]), :]

    def advance(now):
        index = now - LAG_2
        if 0 <= index < ITEMS:
            owner, (second_land, first_land, line_land), at, extra = lands_of(index)
            for copy in to_second(index):
                copy.wait_recv()
            add_rows(second_land.at[at, 0], second_land.at[at, 0], held_rows(index, first // 2))
            to_first(index).start()
        index = now - LAG_3
        if 0 <= index < ITEMS:
            owner, (second_land, first_land, line_land), at, extra = lands_of(index)
            to_first(index).wait_recv()
            add_rows(first_land.at[at], first_land.at[at], held_rows(index, s // 2), second_land.at[at, 1])
        for hop in range(TP - 1):
            index = now - LAG_4 - HOP * hop
            if not 0 <= index < ITEMS or items[index][1] == 0:
                continue
            owner, (second_land, first_land, line_land), at, extra = lands_of(index)
            for up in (True, False):

                @pl.when((t == hop) & (owner > t) if up else (t == TP - 1 - hop) & (owner < t))
                def _(index=index, at=at, up=up, first_land=first_land, line_land=line_land, hop=hop):
                    if hop:
                        along(index, up).wait_recv()
                        add_rows(first_land.at[at], first_land.at[at], line_land.at[at])
                    along(index, up).start()

        index = now - LAG_5
        if 0 <= index < ITEMS:
            kind, step = items[index]
            owner, (second_land, first_land, line_land), at, extra = lands_of(index)
            if step == 0:
                above = sum(heights[:kind])
                target = tall.at[above : above + heights[kind]]

                @pl.when(t == 0)
                def _():
                    along(index, False).wait_recv()
                    add_rows(target, first_land.at[at], line_land.at[extra])

                @pl.when(t == TP - 1)
                def _():
                    along(index, True).wait_recv()
                    add_rows(target, first_land.at[at], line_land.at[at])

                @pl.when((t > 0) & (t < TP - 1))
                def _():
                    along(index, True).wait_recv()
                    along(index, False).wait_recv()
                    add_rows(target, first_land.at[at], line_land.at[at], line_land.at[extra])

    def produce(index):
        kind, step = items[index]
        height = heights[kind]
        right, part = ((cot, 0), (second_normed, 1), (second_normed, 1), (attn_cot, 3), (normed, 2), (normed, 2))[kind]
        once(("half", part), lambda: half_copy().wait_recv() if part == 3 else half_load(part).wait())
        if kind >= 4:
            once("normed", lambda: normed_load().wait())
        for copy in lhs_loads(index):
            copy.wait()
        if index >= HELD:
            for copy in to_second(index - HELD):
                copy.wait_send()
        slot = index % 2
        product = dots(lhs[slot, 0, :, 0:height], right[:, ours], TN) + dots(lhs[slot, 1, :, 0:height], halves[part], TN)
        for chip in range(4):
            held[index % HELD, chip, 0:height, :] = product[:, chip * STRIPE : chip * STRIPE + STRIPE].astype(BF16)
        for copy in to_second(index):
            copy.start()
        advance(index)

    for index in range(SEQ):
        cot_load(index).start()
    half_load(0).start()
    prefetch(0)
    for p in range(PIECES):
        share_start(0, p)
    back_load().start()
    second_load().start()
    half_load(1).start()
    for index in range(3):
        tile_load(index).start()
    acts_load().start()
    pack_load().start()
    normed_load().start()
    half_load(2).start()
    for index in range(SEQ):
        cot_load(index).wait()
    produce(0)
    prefetch(1)
    back_load().wait()
    second_load().wait()

    def middle(part, start):
        unit = second_normed[part, :].astype(F32)
        values = mid[part, :]
        inner = jnp.mean(values * unit, axis=-1, keepdims=True)
        values = cot[part, :].astype(F32) + inv_second[part, 0:1] * (values - unit * inner)
        mid[part, :] = values
        attn_cot[part, :] = values.astype(BF16)

    every_rows(rows, middle)
    half_copy().start()
    produce(1)
    prefetch(2)
    at_tile = 0
    for part in range(2):
        wide[:, part * half_d : part * half_d + half_d] = dots(attn_cot[...], tile(at_tile + part), NT)
        tile_next(at_tile + part)
    at_tile += 2
    acts_load().wait()
    pack_load().wait()

    def head_rows(part, start):
        total = jnp.zeros((BLOCK, 1), F32)
        for block in range(TP):
            values = wide[part, block * PAIR : block * PAIR + PAIR]
            gate = acts[block, part, 3 * PAIR : 4 * PAIR].astype(F32)
            unit = pack[block, part, 3 * PAIR : 4 * PAIR].astype(F32)
            total += jnp.sum(values * gate * unit, axis=-1, keepdims=True)
        total = total * (1.0 / D)
        scale = inv_mix[part, 0:1]
        for block in range(TP):
            values = wide[part, block * PAIR : block * PAIR + PAIR]
            gate = acts[block, part, 3 * PAIR : 4 * PAIR].astype(F32)
            unit = pack[block, part, 3 * PAIR : 4 * PAIR].astype(F32)
            backs[block, part, 3 * PAIR : 4 * PAIR] = (values * unit).astype(BF16)
            backs[block, part, 2 * PAIR : 3 * PAIR] = (scale * (values * gate - unit * total)).astype(BF16)
        row = lax.broadcasted_iota(jnp.int32, (BLOCK, rows), 0) + start
        column = lax.broadcasted_iota(jnp.int32, (BLOCK, rows), 1)
        apart = (column > row) | ((row >= edge) & (column < edge))
        distance[part, :] = jnp.where(apart, -1, row - column).astype(F32)

    every_rows(rows, head_rows)
    produce(2)
    prefetch(3)
    relay(2, 12)

    def rate_of(block, half):
        return rates[block, half : half + 1, :]

    def row_numbers(start):
        return lax.broadcasted_iota(jnp.int32, (NARROW, HEAD), 0) + start

    for block in range(TP):
        for half in range(2):
            at = half * HEAD

            def fade_rows(part, start, block=block, half=half, at=at):
                number = row_numbers(start)
                valid = jnp.where(jnp.where(number >= edge, 1, 0) == before, 1.0, 0.0)
                fade = jnp.exp(-rate_of(block, half) * (number + 1).astype(F32)) * valid
                values = backs[block, part, 2 * PAIR + at : 2 * PAIR + at + HEAD].astype(F32)
                faded[part, :] = (values * fade).astype(BF16)

            every_rows(rows, fade_rows, NARROW)
            head = 2 * block + half
            state[head] = dots(acts[block, :, at : at + HEAD], faded[...], TN).astype(BF16)
            wide[:, head * HEAD : head * HEAD + HEAD] = dots(faded[...], incoming[head], NT)

    def suffix_scale(block, source_block, rate):
        same = jnp.where(source_block * rows - 1 >= boundary, 1, 0) == jnp.where(block * rows + rows - 1 >= boundary, 1, 0)
        usable = flag(source_block > block) * flag(same)
        gap = jnp.maximum(source_block - 1 - block, 0).astype(F32)
        return jnp.exp(-rate * (rows * gap)) * usable

    begin_states, add_pair, add_chips, finish_states, close_states = state_exchange(
        rows, boundary, exchange, rates, suffix_scale, lambda chip: 2 * chip - 1, lambda chip: 2 * chip
    )
    begin_states()
    produce(3)
    prefetch(4)
    relay(2, 12)
    add_pair()
    weights[0:PAIR, PAIR:rows] = jnp.zeros((PAIR, rows - PAIR), BF16)
    slopes[0:PAIR, PAIR:rows] = jnp.zeros((PAIR, rows - PAIR), BF16)

    def attend(block):
        for half in range(2):
            at = half * HEAD
            head = 2 * block + half
            rate = rate_of(block, half)
            query, key, value = [slice(kind * PAIR + at, kind * PAIR + at + HEAD) for kind in range(3)]
            mine_columns = slice(head * HEAD, head * HEAD + HEAD)
            for top in range(0, rows, PAIR):
                width = top + PAIR
                scores[0:PAIR, 0:width] = dots(acts[block, top:width, query], acts[block, 0:width, key], NT)
                scores[PAIR : 2 * PAIR, 0:width] = dots(backs[block, top:width, value], acts[block, 0:width, value], NT)

                def weigh(part, start, width=width, top=top):
                    below = pl.ds(pl.multiple_of(start + PAIR, WEIGH), WEIGH)
                    there = pl.ds(pl.multiple_of(start + top, WEIGH), WEIGH)
                    for left in range(0, width, HEAD):
                        apart = distance[there, left : left + HEAD]
                        fade = jnp.where(apart >= 0.0, jnp.exp(-rate * apart), 0.0)
                        weights[there, left : left + HEAD] = (scores[part, left : left + HEAD] * fade).astype(BF16)
                        grad = scores[below, left : left + HEAD].astype(BF16).astype(F32)
                        slopes[there, left : left + HEAD] = (grad * fade).astype(BF16)

                every_rows(PAIR, weigh, WEIGH)
                wide[top:width, mine_columns] += dots(slopes[top:width, 0:width], acts[block, 0:width, key], NN)
            inner = dots(weights[...], backs[block, :, value], TN)
            acts[block, :, 3 * PAIR + at : 3 * PAIR + at + HEAD] = inner.astype(BF16)
            inner = dots(slopes[...], acts[block, :, query], TN)
            backs[block, :, key] = inner.astype(BF16)

            def turn_back(part, start):
                turned = rotated(wide[part, mine_columns], cosine[part, :], -sine[part, :])
                backs[block, part, query] = (turned * pack[block, part, query].astype(F32)).astype(BF16)

            every_rows(rows, turn_back, NARROW)

    for block in range(TP):
        attend(block)
        produce(4 + block)
        prefetch(5 + block)
        relay(2, 12)

    add_chips()
    produce(8)
    prefetch(9)
    relay(2, 12)
    finish_states()

    for block in range(TP):
        for half in range(2):
            at = half * HEAD
            head = 2 * block + half
            query, key, value = [slice(kind * PAIR + at, kind * PAIR + at + HEAD) for kind in range(3)]
            scores[:, 0:HEAD] = dots(acts[block, :, value], later[head], NT)
            scores[:, HEAD : 2 * HEAD] = dots(acts[block, :, key], later[head], NN)

            def finish_rows(part, start, block=block, half=half, at=at, key=key, value=value):
                number = row_numbers(start)
                valid = jnp.where(jnp.where(number >= edge, 1, 0) == last, 1.0, 0.0)
                fade = jnp.exp(-rate_of(block, half) * (rows - 1 - number).astype(F32)) * valid
                keys = backs[block, part, key].astype(F32) + fade * scores[part, 0:HEAD]
                turned = rotated(keys, cosine[part, :], -sine[part, :])
                backs[block, part, key] = (turned * pack[block, part, key].astype(F32)).astype(BF16)
                values = acts[block, part, 3 * PAIR + at : 3 * PAIR + at + HEAD].astype(F32)
                backs[block, part, value] = (values + fade * scores[part, HEAD : 2 * HEAD]).astype(BF16)

            every_rows(rows, finish_rows, NARROW)
        backs_keep_copy(block).start()
        backs_copy(block).start()
        for part in range(2):
            index = at_tile + 2 * block + part
            term = dots(backs[block, :, part * half_d : part * half_d + half_d], tile(index), NN)
            if block or part:
                wide[...] += term
            else:
                wide[...] = term
            tile_next(index)
        if block == 0:
            for index in range(SEQ):
                hidden_load(index).start()
        if block == 1:
            produce(9)
            prefetch(10)
    relay(12, 12)
    for index in range(SEQ):
        hidden_load(index).wait()

    def input_rows(part, start):
        values = acts[0, part, :].astype(F32)
        scale = lax.rsqrt(jnp.mean(values * values, axis=-1, keepdims=True) + EPSILON)
        unit = values * scale
        grad = wide[part, :]
        inner = jnp.mean(grad * unit, axis=-1, keepdims=True)
        grad = mid[part, :] + scale * (grad - unit * inner)
        for index in range(SEQ):
            acts[1, part, plain(index)] = grad[:, place_of(index)].astype(BF16)

    for p in range(PIECES):

        @pl.loop(0, piece_rows // BLOCK)
        def _(block, p=p):
            start = p * piece_rows + block * BLOCK
            input_rows(pl.ds(pl.multiple_of(start, BLOCK), BLOCK), start)

        if p < EARLY:
            share_start(1, p)
    for index in range(BEFORE, ITEMS):
        produce(index)
        if index + 1 < ITEMS:
            prefetch(index + 1)
        if EARLY <= index - BEFORE + EARLY < PIECES:
            share_start(1, index - BEFORE + EARLY)
        if index >= BEFORE + WAIT_1:
            relay(2, 20)
        if index >= BEFORE + WAIT_2:
            relay(1)
    for now in range(ITEMS, ITEMS + LAG_5):
        advance(now)
        relay(1)
    relay(len(relays))

    half_copy().wait_send()
    for block in range(TP):
        backs_copy(block).wait_send()
    close_states()
    for index, (kind, step) in enumerate(items):
        if index >= ITEMS - HELD:
            for copy in to_second(index):
                copy.wait_send()
        to_first(index).wait_send()
        if step:
            along(index, True).wait_send()
    for a in range(2):
        for p in range(PIECES):
            if a:
                share_keep(a, p).wait()

            @pl.when(t < TP - 1)
            def _(a=a, p=p):
                share_copy(a, p, t, own_piece(a, p), True).wait_send()

            @pl.when(t > 0)
            def _(a=a, p=p):
                share_copy(a, p, t, own_piece(a, p), False).wait_send()
    for a, p, step in relays:
        owner = nearest(t, step)
        passed = passes(owner, True) | passes(owner, False)

        @pl.when(jnp.logical_not(passed))
        def _(a=a, p=p, owner=owner):
            share_copy(a, p, owner, piece(a, owner, p), True).wait_recv()

        for up in (True, False):

            @pl.when(passes(owner, up))
            def _(a=a, p=p, owner=owner, up=up):
                share_copy(a, p, owner, piece(a, owner, p), up).wait_send()


def backward(units, whole, kept, output, hidden_in, out_cotangent, incoming, inv_mix, inv_second, rates, cosine, sine, bounds):
    rows = output.shape[0]
    sizes = tuple(weight.shape[0] // TP for weight in whole) + (units,)
    dma = pltpu.SemaphoreType.DMA
    vmem = pl.BlockSpec(memory_space=pltpu.VMEM)
    anywhere = pl.BlockSpec(memory_space=pl.ANY)
    half_d = D // 2
    shape = jax.ShapeDtypeStruct
    scratch = [
        pltpu.VMEM((3, half_d, D), BF16),
        *[pltpu.VMEM((rows, D), BF16)] * 4,
        pltpu.VMEM((4, rows, half_d), BF16),
        *[pltpu.VMEM((TP, rows, 4 * PAIR), BF16)] * 3,
        pltpu.VMEM((rows, D), F32),
        pltpu.VMEM((rows, D), F32),
        pltpu.VMEM((rows, rows), F32),
        pltpu.VMEM((rows, rows), F32),
        pltpu.VMEM((rows, rows), BF16),
        pltpu.VMEM((rows, rows), BF16),
        pltpu.VMEM((rows, HEAD), BF16),
        pltpu.VMEM((2, 2, rows, units), BF16),
        pltpu.VMEM((HELD, 4, units, STRIPE), BF16),
        *state_scratch(),
    ]
    for count, height, extra in ((3 * TP, units, 3), (TP, sizes[1], 1), (2 * TP, half_d, 2)):
        scratch += [
            pltpu.VMEM((count, 2, height, STRIPE), BF16),
            pltpu.VMEM((count, height, STRIPE), BF16),
            pltpu.VMEM((count + extra, height, STRIPE), BF16),
        ]
    scratch += [
        dma((3,)),
        dma((2,)),
        dma((3,)),
        dma((TP,)),
        dma((TP,)),
        dma((TP,)),
        dma((5,)),
        dma((SEQ,)),
        dma((SEQ,)),
        dma((2, 2)),
        dma((ITEMS, 2)),
        dma((ITEMS, 2)),
        dma((ITEMS,)),
        dma((ITEMS,)),
        dma((ITEMS,)),
        dma((KINDS, TP)),
        dma((KINDS, TP)),
        dma((2, PIECES)),
        dma((2, PIECES, TP)),
        dma((2, PIECES, TP)),
        dma((2, PIECES, TP)),
    ]
    return pl.pallas_call(
        functools.partial(backward_kernel, rows, sizes),
        out_shape=[shape((3 * units + sizes[1] + sizes[0], STRIPE), F32)]
        + [shape((TP, rows, D), BF16)] * 2
        + [shape((TP, rows, 4 * PAIR), BF16)] * 2,
        in_specs=[anywhere] * 20 + [vmem] * 6 + [pl.BlockSpec(memory_space=pltpu.SMEM)],
        out_specs=[vmem] + [anywhere] * 4,
        scratch_shapes=scratch,
        compiler_params=pltpu.CompilerParams(
            collective_id=1, has_side_effects=True, vmem_limit_bytes=63 * 2**20
        ),
        name="backward",
    )(*whole, *kept, output, hidden_in, out_cotangent, incoming, inv_mix, inv_second, rates, cosine, sine, bounds)


def finish_kernel(units, input_in, tall, output_in, own_in, input_grad, output, *refs):
    grads, (held, sem) = refs[:8], refs[8:]
    step = pl.program_id(0)
    t = lax.axis_index("tp")

    def load(block):
        return pltpu.make_async_copy(output_in.at[block], held.at[block], sem.at[0, block])

    def load_own(block):
        return pltpu.make_async_copy(own_in, held.at[block], sem.at[0, block])

    def store(block):
        return pltpu.make_async_copy(held.at[block], output.at[block], sem.at[1, block])

    @pl.when(step == 0)
    def _():
        for block in range(TP):
            pl.when(t != block)(lambda block=block: load(block).start())
            pl.when(t == block)(lambda block=block: load_own(block).start())
        for kind in range(3):
            grads[kind][...] = tall[kind * units : kind * units + units, :]
        grads[3][...] = tall[3 * units : 3 * units + PAIR, :]
        for kind in range(4):
            above = 3 * units + PAIR + kind * PAIR
            grads[4 + kind][...] = tall[above : above + PAIR, :].T

    input_grad[...] = input_in[...].astype(F32)

    for block in range(TP):

        @pl.when(step == block)
        def _(block=block):
            load(block).wait()
            store(block).start()

    @pl.when(step == TP - 1)
    def _():
        for block in range(TP):
            store(block).wait()


def finish(units, input_grad, tall, output, own):
    rows = input_grad.shape[1]
    block = lambda: pl.BlockSpec((1, rows, D), lambda step: (step, 0, 0))
    fixed = lambda *shape: pl.BlockSpec(shape, lambda step: (0, 0))
    anywhere = pl.BlockSpec(memory_space=pl.ANY)
    shape = jax.ShapeDtypeStruct
    shapes = [(units, STRIPE)] * 3 + [(PAIR, STRIPE)] + [(STRIPE, PAIR)] * 4
    return pl.pallas_call(
        functools.partial(finish_kernel, units),
        grid=(TP,),
        out_shape=[shape(input_grad.shape, F32), shape(output.shape, BF16), *[shape(each, F32) for each in shapes]],
        in_specs=[block(), fixed(*tall.shape), anywhere, anywhere],
        out_specs=[block(), anywhere, *[fixed(*each) for each in shapes]],
        scratch_shapes=[pltpu.VMEM(output.shape, BF16), pltpu.SemaphoreType.DMA((2, TP))],
        compiler_params=pltpu.CompilerParams(vmem_limit_bytes=62 * 2**20),
        name="finish",
    )(input_grad, tall, output, own)


def entering(value, axis, join, neutral, backward):
    count, mine = (lax.axis_size(axis), lax.axis_index(axis))
    pieces = jax.tree.map(lambda part: lax.all_gather(part, axis), value)
    if backward:
        pieces = jax.tree.map(lambda part: part[::-1], pieces)
        mine = count - 1 - mine
    subtotal = jax.tree.map(
        lambda part, zero: jnp.full_like(part, 0) + jnp.asarray(zero, part.dtype), value, neutral
    )

    def step(position, subtotal):
        longer = join(subtotal, jax.tree.map(lambda part: part[position], pieces))
        return jax.tree.map(lambda new, old: jnp.where(position < mine, new, old), longer, subtotal)

    return lax.fori_loop(0, count - 1, step, subtotal)


def swish_parts(pre_act):
    logistic = jax.nn.sigmoid(pre_act)
    return (pre_act * logistic, logistic * (1.0 + pre_act * (1.0 - logistic)))


def rotate(rows_in, cosine_table, sine_table, signed):
    halfway = rows_in.shape[-1] // 2
    front_half = rows_in[..., :halfway]
    back_half = rows_in[..., halfway:]
    return jnp.concatenate(
        [
            front_half * cosine_table - signed * back_half * sine_table,
            signed * front_half * sine_table + back_half * cosine_table,
        ],
        axis=-1,
    )


def combine_forward(earlier, following):
    return (earlier[0] * following[0], following[0][:, None, None] * earlier[1] + following[1])


def combine_backward(farther, nearer):
    return (farther[0] * nearer[0], nearer[1] + nearer[0][:, None, None] * farther[1])


def collect_weights(
    query_weight,
    key_weight,
    value_weight,
    gate_weight,
    out_weight,
    left_weight,
    right_weight,
    down_weight,
):
    return (
        lax.all_gather(query_weight, "seq", axis=0, tiled=True),
        lax.all_gather(key_weight, "seq", axis=0, tiled=True),
        lax.all_gather(value_weight, "seq", axis=0, tiled=True),
        lax.all_gather(gate_weight, "seq", axis=0, tiled=True),
        lax.all_gather(out_weight, "seq", axis=1, tiled=True),
        lax.all_gather(left_weight, "seq", axis=0, tiled=True),
        lax.all_gather(right_weight, "seq", axis=0, tiled=True),
        lax.all_gather(down_weight, "seq", axis=1, tiled=True),
    )


def state_prefix(factor, local_state):
    neutral = (jnp.ones_like(factor), jnp.zeros_like(local_state))
    return entering((factor, local_state), "seq", combine_forward, neutral, False)[1]


def state_suffix(factor, state_grad):
    neutral = (jnp.ones_like(factor), jnp.zeros_like(state_grad))
    return entering((factor, state_grad), "seq", combine_backward, neutral, True)[1]


def body(
    hidden_in,
    query_weight,
    key_weight,
    value_weight,
    gate_weight,
    out_weight,
    left_weight,
    right_weight,
    down_weight,
    decay_rate,
    seq_bounds,
    out_cotangent,
):
    row_count = hidden_in.shape[1]
    batch_count = hidden_in.shape[0]
    local_heads = decay_rate.shape[0]
    heads_shape = (row_count, local_heads, HEAD)
    device = lax.axis_index("seq")
    offsets = jnp.arange(row_count, dtype=jnp.int32)
    positions = device * row_count + offsets
    frequency = jnp.exp(
        jnp.arange(HEAD // 2, dtype=jnp.float32) * (-2.0 * math.log(10000.0) / HEAD)
    )
    angles = positions.astype(jnp.float32)[:, None] * frequency[None, :]
    cosine_table = jnp.cos(angles)[:, None, :]
    sine_table = jnp.sin(angles)[:, None, :]
    local_f = offsets.astype(jnp.float32)
    distance = local_f[:, None] - local_f[None, :]
    causal = distance >= 0.0
    distance_pos = jnp.maximum(distance, 0.0)
    accum = None
    outputs = []
    in_grads = []
    for batch_index in range(batch_count):
        gathered = collect_weights(
            query_weight,
            key_weight,
            value_weight,
            gate_weight,
            out_weight,
            left_weight,
            right_weight,
            down_weight,
        )
        query_full, key_full, value_full, gate_full, out_full, left_full, right_full, down_full = (
            gathered
        )
        boundary = seq_bounds[batch_index]
        segment = (positions >= boundary).astype(jnp.int32)
        before = (device * row_count - 1 >= boundary).astype(jnp.int32)
        last_segment = segment[row_count - 1]
        allowed = causal & (segment[:, None] == segment[None, :])
        decay = jnp.where(
            allowed[None], jnp.exp(-decay_rate[:, None, None] * distance_pos[None]), 0.0
        )
        coef_in = (
            jnp.exp(-decay_rate[None, :] * (local_f[:, None] + 1.0))
            * (segment == before).astype(jnp.float32)[:, None]
        )
        weight_loc = (
            jnp.exp(-decay_rate[None, :] * (row_count - 1.0 - local_f)[:, None])
            * (segment == last_segment).astype(jnp.float32)[:, None]
        )
        factor = jnp.where(last_segment == before, jnp.exp(-decay_rate * row_count), 0.0)
        input_rows = hidden_in[batch_index].astype(jnp.float32)
        inv_first = lax.rsqrt(jnp.mean(input_rows * input_rows, axis=-1, keepdims=True) + EPSILON)
        unit_first = input_rows * inv_first
        normed_first = unit_first.astype(jnp.bfloat16)
        query_pre = jnp.dot(normed_first, query_full, preferred_element_type=jnp.float32)
        key_pre = jnp.dot(normed_first, key_full, preferred_element_type=jnp.float32)
        value_pre = jnp.dot(normed_first, value_full, preferred_element_type=jnp.float32)
        gate_pre = jnp.dot(normed_first, gate_full, preferred_element_type=jnp.float32)
        query_act, query_slope = swish_parts(query_pre)
        key_act, key_slope = swish_parts(key_pre)
        query_rot = rotate(query_act.reshape(heads_shape), cosine_table, sine_table, 1.0).astype(
            jnp.bfloat16
        )
        key_rot = rotate(key_act.reshape(heads_shape), cosine_table, sine_table, 1.0).astype(
            jnp.bfloat16
        )
        value_rows = value_pre.astype(jnp.bfloat16).reshape(heads_shape)
        query_wide = query_rot.astype(jnp.float32)
        key_wide = key_rot.astype(jnp.float32)
        value_wide = value_rows.astype(jnp.float32)
        scores = jnp.einsum("ihe,jhe->hij", query_rot, key_rot, preferred_element_type=jnp.float32)
        attn_weights = (scores * decay).astype(jnp.bfloat16)
        inner_out = jnp.einsum(
            "hij,jhe->ihe", attn_weights, value_rows, preferred_element_type=jnp.float32
        )
        local_state = jnp.einsum(
            "jhe,jhf->hef",
            key_wide * weight_loc[:, :, None],
            value_wide,
            precision=HIGHEST_PRECISION,
        )
        incoming = state_prefix(factor, local_state)
        outer_out = coef_in[:, :, None] * jnp.einsum(
            "ihe,hef->ihf", query_wide, incoming, precision=HIGHEST_PRECISION
        )
        mixed_heads = (inner_out + outer_out).reshape(row_count, local_heads * HEAD)
        total_sq = lax.psum(jnp.sum(mixed_heads * mixed_heads, axis=-1), "tp")
        inv_mix = lax.rsqrt(total_sq / D + EPSILON)[:, None]
        unit_mix = mixed_heads * inv_mix
        gate_mix = (unit_mix * gate_pre).astype(jnp.bfloat16)
        attn_sum = lax.psum(jnp.dot(gate_mix, out_full, preferred_element_type=jnp.float32), "tp")
        resid_mid = input_rows + attn_sum
        inv_second = lax.rsqrt(jnp.mean(resid_mid * resid_mid, axis=-1, keepdims=True) + EPSILON)
        unit_second = resid_mid * inv_second
        normed_second = unit_second.astype(jnp.bfloat16)
        left_pre = jnp.dot(normed_second, left_full, preferred_element_type=jnp.float32)
        right_pre = jnp.dot(normed_second, right_full, preferred_element_type=jnp.float32)
        glu_product = (left_pre * right_pre).astype(jnp.bfloat16)
        glu_out = lax.psum(
            jnp.dot(glu_product, down_full, preferred_element_type=jnp.float32), "tp"
        )
        outputs.append((resid_mid + glu_out).astype(jnp.bfloat16))
        glu_cot = out_cotangent[batch_index]
        product_grad = jnp.einsum(
            "cd,fd->cf", glu_cot, down_full, preferred_element_type=jnp.float32
        )
        left_back = (product_grad * right_pre).astype(jnp.bfloat16)
        right_back = (product_grad * left_pre).astype(jnp.bfloat16)
        second_part = jnp.einsum(
            "cf,df->cd", left_back, left_full, preferred_element_type=jnp.float32
        ) + jnp.einsum("cf,df->cd", right_back, right_full, preferred_element_type=jnp.float32)
        second_back = lax.psum(second_part, "tp")
        mid_grad = glu_cot.astype(jnp.float32) + inv_second * (
            second_back - unit_second * jnp.mean(second_back * unit_second, axis=-1, keepdims=True)
        )
        attn_cot = mid_grad.astype(jnp.bfloat16)
        gate_mix_grad = jnp.einsum(
            "cd,kd->ck", attn_cot, out_full, preferred_element_type=jnp.float32
        )
        gate_back = (gate_mix_grad * unit_mix).astype(jnp.bfloat16)
        unit_mix_grad = gate_mix_grad * gate_pre
        mix_dot = lax.psum(jnp.sum(unit_mix_grad * unit_mix, axis=-1), "tp")
        heads_grad = (
            (inv_mix * (unit_mix_grad - unit_mix * (mix_dot / D)[:, None]))
            .astype(jnp.bfloat16)
            .reshape(heads_shape)
        )
        pair_grad = jnp.einsum(
            "ihe,jhe->hij", heads_grad, value_rows, preferred_element_type=jnp.float32
        ).astype(jnp.bfloat16)
        score_grad = pair_grad.astype(jnp.float32) * decay
        query_inner = jnp.einsum("hij,jhe->ihe", score_grad, key_wide, precision=HIGHEST_PRECISION)
        key_inner = jnp.einsum("hij,ihe->jhe", score_grad, query_wide, precision=HIGHEST_PRECISION)
        value_inner = jnp.einsum(
            "hij,ihe->jhe", attn_weights, heads_grad, preferred_element_type=jnp.float32
        )
        scaled_grad = heads_grad.astype(jnp.float32) * coef_in[:, :, None]
        query_outer = jnp.einsum("ihf,hef->ihe", scaled_grad, incoming, precision=HIGHEST_PRECISION)
        state_grad = jnp.einsum(
            "ihe,ihf->hef", query_wide, scaled_grad, precision=HIGHEST_PRECISION
        )
        later_grad = state_suffix(factor, state_grad)
        key_state = weight_loc[:, :, None] * jnp.einsum(
            "jhf,hef->jhe", value_wide, later_grad, precision=HIGHEST_PRECISION
        )
        value_state = weight_loc[:, :, None] * jnp.einsum(
            "jhe,hef->jhf", key_wide, later_grad, precision=HIGHEST_PRECISION
        )
        query_back = (
            rotate(query_inner + query_outer, cosine_table, sine_table, -1.0).reshape(row_count, -1)
            * query_slope
        ).astype(jnp.bfloat16)
        key_back = (
            rotate(key_inner + key_state, cosine_table, sine_table, -1.0).reshape(row_count, -1)
            * key_slope
        ).astype(jnp.bfloat16)
        value_back = (value_inner + value_state).reshape(row_count, -1).astype(jnp.bfloat16)
        fresh = (
            jnp.einsum("cd,ck->dk", normed_first, query_back, preferred_element_type=jnp.float32),
            jnp.einsum("cd,ck->dk", normed_first, key_back, preferred_element_type=jnp.float32),
            jnp.einsum("cd,ck->dk", normed_first, value_back, preferred_element_type=jnp.float32),
            jnp.einsum("cd,ck->dk", normed_first, gate_back, preferred_element_type=jnp.float32),
            jnp.einsum("ck,cd->kd", gate_mix, attn_cot, preferred_element_type=jnp.float32),
            jnp.einsum("cd,cf->df", normed_second, left_back, preferred_element_type=jnp.float32),
            jnp.einsum("cd,cf->df", normed_second, right_back, preferred_element_type=jnp.float32),
            jnp.einsum("cf,cd->fd", glu_product, glu_cot, preferred_element_type=jnp.float32),
        )
        if accum is None:
            accum = list(fresh)
        else:
            accum = [older + newer for older, newer in zip(accum, fresh)]
        total = jnp.einsum("ck,dk->cd", query_back, query_full, preferred_element_type=jnp.float32)
        total = total + jnp.einsum(
            "ck,dk->cd", key_back, key_full, preferred_element_type=jnp.float32
        )
        total = total + jnp.einsum(
            "ck,dk->cd", value_back, value_full, preferred_element_type=jnp.float32
        )
        first_back = lax.psum(
            total
            + jnp.einsum("ck,dk->cd", gate_back, gate_full, preferred_element_type=jnp.float32),
            "tp",
        )
        input_back = mid_grad + inv_first * (
            first_back - unit_first * jnp.mean(first_back * unit_first, axis=-1, keepdims=True)
        )
        in_grads.append(input_back)
    summed = (
        lax.psum_scatter(accum[0], "seq", scatter_dimension=0, tiled=True),
        lax.psum_scatter(accum[1], "seq", scatter_dimension=0, tiled=True),
        lax.psum_scatter(accum[2], "seq", scatter_dimension=0, tiled=True),
        lax.psum_scatter(accum[3], "seq", scatter_dimension=0, tiled=True),
        lax.psum_scatter(accum[4], "seq", scatter_dimension=1, tiled=True),
        lax.psum_scatter(accum[5], "seq", scatter_dimension=0, tiled=True),
        lax.psum_scatter(accum[6], "seq", scatter_dimension=0, tiled=True),
        lax.psum_scatter(accum[7], "seq", scatter_dimension=1, tiled=True),
    )
    return (
        jnp.stack(outputs),
        jnp.stack(in_grads),
        summed[0],
        summed[1],
        summed[2],
        summed[3],
        summed[4],
        summed[5],
        summed[6],
        summed[7],
    )


def fused_body(
    hidden_in,
    query_weight,
    key_weight,
    value_weight,
    gate_weight,
    out_weight,
    left_weight,
    right_weight,
    down_weight,
    decay_rate,
    seq_bounds,
    out_cotangent,
):
    row_count = hidden_in.shape[1]
    device = lax.axis_index("seq")
    positions = device * row_count + jnp.arange(row_count, dtype=jnp.int32)
    frequency = jnp.exp(jnp.arange(HEAD // 2, dtype=F32) * (-2.0 * math.log(10000.0) / HEAD))
    angles = positions.astype(F32)[:, None] * jnp.tile(frequency, 2)[None, :]
    sign = jnp.where(jnp.arange(HEAD) < HEAD // 2, -1.0, 1.0).astype(F32)
    cosine, sine = jnp.cos(angles), jnp.sin(angles) * sign[None, :]
    results = forward(
        (query_weight, key_weight, value_weight, gate_weight),
        (out_weight, left_weight.T, right_weight.T, down_weight),
        hidden_in,
        out_cotangent,
        cosine,
        sine,
        decay_rate,
        seq_bounds,
    )
    whole, kept, (incoming, inv_mix, inv_second, rates, output) = results[:2], results[2:17], results[17:]
    tall, shared, input_grad = backward(
        down_weight.shape[0],
        whole,
        kept,
        output,
        hidden_in,
        out_cotangent,
        incoming,
        inv_mix,
        inv_second,
        rates,
        cosine,
        sine,
        seq_bounds,
    )[:3]
    (input_grad, output, down_grad, left_grad, right_grad, out_grad,
     query_grad, key_grad, value_grad, gate_grad) = finish(
        down_weight.shape[0], input_grad, tall, shared, output
    )
    return (
        output,
        input_grad,
        query_grad,
        key_grad,
        value_grad,
        gate_grad,
        out_grad,
        left_grad.T,
        right_grad.T,
        down_grad,
    )


def solution(mesh):
    fits = mesh.shape["seq"] == SEQ and mesh.shape["tp"] == TP
    return jax.shard_map(
        fused_body if fits else body,
        mesh=mesh,
        in_specs=(
            P(None, "seq", None),
            P("seq", "tp"),
            P("seq", "tp"),
            P("seq", "tp"),
            P("seq", "tp"),
            P("tp", "seq"),
            P("seq", "tp"),
            P("seq", "tp"),
            P("tp", "seq"),
            P("tp"),
            P(),
            P(None, "seq", None),
        ),
        out_specs=(
            P(None, "seq", None),
            P(None, "seq", None),
            P("seq", "tp"),
            P("seq", "tp"),
            P("seq", "tp"),
            P("seq", "tp"),
            P("tp", "seq"),
            P("seq", "tp"),
            P("seq", "tp"),
            P("tp", "seq"),
        ),
        check_vma=False,
    )
```
